32 devices in a mesh: grp: 8 (over z, y), exp: 4 (over x, core).
Axes of the slice: x: 2, y: 2, z: 4, core: 2. Of those that a mesh axis runs over, the one named last changes fastest.
Arguments:
- tokens: bfloat16 [32, 192, 768], P(('grp', 'exp')), may hold values from -6 to 6
- seq_lengths: int32 [32], P('grp'), may hold values from 48 to 192, as said below
- deal_order: int32 [32], P('grp'), may hold values from 0 to 3, as said below
- expert_routes: int32 [32, 192, 2], P(('grp', 'exp')), may hold values from 0 to 3, as said below
- capacity_slots: int32 [32, 192, 2], P(('grp', 'exp')), may hold values from 0 to 143, as said below
- gate_weights: float32 [32, 192, 2], P(('grp', 'exp')), may hold values from 0.2 to 0.8
- cotangent: float32 [32, 192, 768], P(('grp', 'exp')), may hold values from -6 to 6
- projector: float32 [3, 768, 768], P(None, ('grp', 'exp')), may hold values from -0.3125 to 0.3125
- projector_mean: float32 [3, 768, 768], P(None, ('grp', 'exp')), may hold values from -256 to 256
- projector_square: float32 [3, 768, 768], P(None, ('grp', 'exp')), may hold values from 2211.84 to 8847.36
- collector: float32 [768, 768], P(('grp', 'exp')), may hold values from -0.875 to 0.875
- collector_first_moment: float32 [768, 768], P(('grp', 'exp')), may hold values from -96 to 96
- collector_second_moment: float32 [768, 768], P(('grp', 'exp')), may hold values from 245.76 to 983.04
- widener: float32 [2, 768, 2048], P(None, ('grp', 'exp')), may hold values from -0.21875 to 0.21875
- widener_mean: float32 [2, 768, 2048], P(None, ('grp', 'exp')), may hold values from -128 to 128
- widener_square: float32 [2, 768, 2048], P(None, ('grp', 'exp')), may hold values from 552.96 to 2211.84
- narrower: float32 [2048, 768], P(('grp', 'exp')), may hold values from -0.125 to 0.125
- narrower_mean: float32 [2048, 768], P(('grp', 'exp')), may hold values from -192 to 192
- narrower_square: float32 [2048, 768], P(('grp', 'exp')), may hold values from 983.04 to 3932.16
- norm_gains: float32 [2, 768], P(None, ('grp', 'exp')), may hold values from 0.5 to 1.5
- gains_mean: float32 [2, 768], P(None, ('grp', 'exp')), may hold values from -448 to 448
- gains_square: float32 [2, 768], P(None, ('grp', 'exp')), may hold values from 6144 to 24576
- expander: float32 [4, 2, 768, 2048], P('exp', None, 'grp'), may hold values from -0.21875 to 0.21875
- expander_mean: float32 [4, 2, 768, 2048], P('exp', None, 'grp'), may hold values from -48 to 48
- expander_square: float32 [4, 2, 768, 2048], P('exp', None, 'grp'), may hold values from 69.12 to 276.48
- reducer: float32 [4, 2048, 768], P('exp', 'grp'), may hold values from -0.125 to 0.125
- reducer_mean: float32 [4, 2048, 768], P('exp', 'grp'), may hold values from -80 to 80
- reducer_square: float32 [4, 2048, 768], P('exp', 'grp'), may hold values from 168.96 to 675.84
Outputs:
- block_output: float32 [32, 192, 768], P(('grp', 'exp'))
- input_grad: float32 [32, 192, 768], P(('grp', 'exp'))
- gate_grad: float32 [32, 192, 2], P(('grp', 'exp'))
- projector_moment: float32 [3, 768, 768], P(None, ('grp', 'exp'))
- projector_variance: float32 [3, 768, 768], P(None, ('grp', 'exp'))
- projector_weight: float32 [3, 768, 768], P(None, ('grp', 'exp'))
- collector_moment: float32 [768, 768], P(('grp', 'exp'))
- collector_variance: float32 [768, 768], P(('grp', 'exp'))
- collector_weight: float32 [768, 768], P(('grp', 'exp'))
- widener_moment: float32 [2, 768, 2048], P(None, ('grp', 'exp'))
- widener_variance: float32 [2, 768, 2048], P(None, ('grp', 'exp'))
- widener_weight: float32 [2, 768, 2048], P(None, ('grp', 'exp'))
- narrower_moment: float32 [2048, 768], P(('grp', 'exp'))
- narrower_variance: float32 [2048, 768], P(('grp', 'exp'))
- narrower_weight: float32 [2048, 768], P(('grp', 'exp'))
- gains_moment: float32 [2, 768], P(None, ('grp', 'exp'))
- gains_variance: float32 [2, 768], P(None, ('grp', 'exp'))
- gains_weight: float32 [2, 768], P(None, ('grp', 'exp'))
- expander_moment: float32 [4, 2, 768, 2048], P('exp', None, 'grp')
- expander_variance: float32 [4, 2, 768, 2048], P('exp', None, 'grp')
- expander_weight: float32 [4, 2, 768, 2048], P('exp', None, 'grp')
- reducer_moment: float32 [4, 2048, 768], P('exp', 'grp')
- reducer_variance: float32 [4, 2048, 768], P('exp', 'grp')
- reducer_weight: float32 [4, 2048, 768], P('exp', 'grp')
The draws below stay inside these ranges and needn't reach their ends.
Inputs may be any that keep to these rules, and one draw needn't show every extreme that they name: `seq_lengths`: in each aligned block of 4 sequences one has length 192. `deal_order`: each aligned block of 4 entries is a permutation of 0 .. 3. `expert_routes`: A token's two experts differ. Within one slot no expert is named more than 144 times; in each aligned block of 4 slots some expert is named 144 times in every slot. Within one slot, the pairs (expert_routes, capacity_slots) are all different.
All inputs are finite; a program needn't handle non-finite values.
Results may differ from the reference program's by a relative error of at most 0.019.
The reference program's roundings to bfloat16 on the way count: a program that leaves them out, or rounds other values in their place, can miss the bound.
Values may be sent and summed in bfloat16 or wider, within the bound.
A program may use at most 256 MiB of HBM per device.

```python
import math
import jax
import jax.numpy as jnp
from jax import lax

D = 768
HEAD_COUNT = 12
HEAD_FEATURES = 64
DENSE_FF = 2048
EXPERT_FF = 2048
TOKEN_SLOTS = 192
STEP = 5
SEQUENCE_COUNT = 32
EXPERTS = 4
CAP = 144
N_EXP = 4


def route_block(block_key, fullest):
    rank_key, swap_key, order_key = jax.random.split(block_key, 3)
    rest = 2 * TOKEN_SLOTS - CAP
    base_load = rest // (EXPERTS - 1)
    extra = rest - base_load * (EXPERTS - 1)
    labels = jnp.arange(EXPERTS, dtype=jnp.int32)
    ranks = jax.random.permutation(rank_key, EXPERTS).astype(jnp.int32)
    other_rank = ranks - (ranks > ranks[fullest]).astype(jnp.int32)
    loads = jnp.where(labels == fullest, CAP, base_load + (other_rank < extra).astype(jnp.int32))
    ends = jnp.cumsum(loads).astype(jnp.int32)
    starts = ends - loads
    places = jnp.arange(2 * TOKEN_SLOTS, dtype=jnp.int32)
    owner = jnp.sum((places[:, None] >= ends[None, :]).astype(jnp.int32), axis=1)
    offset = places - jnp.sum(jnp.where(owner[:, None] == labels[None, :], starts[None, :], 0), axis=1)
    swapped = jax.random.randint(swap_key, (TOKEN_SLOTS,), 0, 2) == 1
    first_expert = jnp.where(swapped, owner[TOKEN_SLOTS:], owner[:TOKEN_SLOTS])
    second_expert = jnp.where(swapped, owner[:TOKEN_SLOTS], owner[TOKEN_SLOTS:])
    first_slot = jnp.where(swapped, offset[TOKEN_SLOTS:], offset[:TOKEN_SLOTS])
    second_slot = jnp.where(swapped, offset[:TOKEN_SLOTS], offset[TOKEN_SLOTS:])
    shuffle = jax.random.permutation(order_key, TOKEN_SLOTS)
    routes = jnp.stack([first_expert, second_expert], axis=-1)[shuffle]
    slots = jnp.stack([first_slot, second_slot], axis=-1)[shuffle]
    return (routes.astype(jnp.int32), slots.astype(jnp.int32))


def route_plan(key):
    group_keys = jax.random.split(jax.random.fold_in(key, 101), SEQUENCE_COUNT // N_EXP)
    fullest = jax.vmap(lambda group_key: jax.random.randint(group_key, (), 0, EXPERTS))(group_keys)
    fullest = jnp.repeat(fullest.astype(jnp.int32), N_EXP)
    block_keys = jax.random.split(jax.random.fold_in(key, 102), SEQUENCE_COUNT)
    return jax.vmap(route_block)(block_keys, fullest)


def draw_expert_routes(key, part):
    routes, slots = route_plan(key)
    return routes


def draw_capacity_slots(key, part):
    routes, slots = route_plan(key)
    return slots


def draw_seq_lengths(key, part):
    key = jax.random.fold_in(key, 5)
    length_key, chosen_key = jax.random.split(key)
    lengths = jax.random.randint(length_key, (SEQUENCE_COUNT,), TOKEN_SLOTS // 4, TOKEN_SLOTS + 1)
    chosen = jax.random.randint(chosen_key, (SEQUENCE_COUNT // N_EXP,), 0, N_EXP)
    longest = jnp.arange(SEQUENCE_COUNT, dtype=jnp.int32) % N_EXP == jnp.repeat(chosen, N_EXP)
    return jnp.where(longest, TOKEN_SLOTS, lengths).astype(jnp.int32)


def draw_deal_order(key, part):
    key = jax.random.fold_in(key, 7)
    group_keys = jax.random.split(key, SEQUENCE_COUNT // N_EXP)
    orders = jax.vmap(lambda group_key: jax.random.permutation(group_key, N_EXP))(group_keys)
    return orders.reshape(-1).astype(jnp.int32)


def block_levels(stream_key, dims, cuts, smallest, largest):
    factor_of = 1.0
    for axis_at, blocks in cuts:
        draws = jax.random.uniform(jax.random.fold_in(jax.random.fold_in(stream_key, 6), axis_at), (blocks,), jnp.float32, smallest / len(cuts), largest / len(cuts))
        factor_of = factor_of * jnp.repeat(jnp.exp(draws), dims[axis_at] // blocks).reshape((-1,) + (1,) * (len(dims) - 1 - axis_at))
    return factor_of


def gaussian(stream_key, extent, deviation, bound, cuts=(), kind=jnp.bfloat16):
    loudness = block_levels(stream_key, extent, cuts, -0.22, 0.18) if cuts else 1.0
    array = jax.random.normal(stream_key, extent, jnp.float32) * deviation * loudness
    return jnp.minimum(jnp.maximum(array, -bound), bound).astype(kind)


def setup_inputs(seed: int = 0) -> dict:
    arg_keys = jax.random.split(jax.random.key(seed), 29)
    return {
        "tokens": gaussian(arg_keys[0], (SEQUENCE_COUNT, TOKEN_SLOTS, D), 1.0, 6.0, ((0, 32),)),
        "seq_lengths": draw_seq_lengths(jax.random.fold_in(arg_keys[28], 71), 0),
        "deal_order": draw_deal_order(jax.random.fold_in(arg_keys[28], 71), 0),
        "expert_routes": draw_expert_routes(jax.random.fold_in(arg_keys[28], 71), 0),
        "capacity_slots": draw_capacity_slots(jax.random.fold_in(arg_keys[28], 71), 0),
        "gate_weights": jnp.clip(0.2 + 0.6 * jax.random.uniform(arg_keys[5], (SEQUENCE_COUNT, TOKEN_SLOTS, 2), jnp.float32) ** block_levels(arg_keys[5], (SEQUENCE_COUNT, TOKEN_SLOTS, 2), ((0, 32),), -0.2, 0.2), 0.2, 0.8),
        "cotangent": gaussian(arg_keys[6], (SEQUENCE_COUNT, TOKEN_SLOTS, D), 1.0, 6.0, ((0, 32),), jnp.float32),
        "projector": gaussian(arg_keys[7], (3, D, D), (D // 2) ** -0.5, 0.3125, ((1, 32),), jnp.float32),
        "projector_mean": gaussian(arg_keys[8], (3, D, D), (0.6 * (SEQUENCE_COUNT * TOKEN_SLOTS) ** 0.5), 256.0, ((1, 32),), jnp.float32),
        "projector_square": jnp.clip(jnp.exp(math.log(8847.36) - 1.3862944 * jax.random.uniform(arg_keys[9], (3, D, D), jnp.float32) ** block_levels(arg_keys[9], (3, D, D), ((1, 32),), -0.2, 0.2)), 2211.84, 8847.36),
        "collector": gaussian(arg_keys[10], (D, D), (D // 16) ** -0.5, 0.875, ((0, 32),), jnp.float32),
        "collector_first_moment": gaussian(arg_keys[11], (D, D), (0.2 * (SEQUENCE_COUNT * TOKEN_SLOTS) ** 0.5), 96.0, ((0, 32),), jnp.float32),
        "collector_second_moment": jnp.clip(jnp.exp(math.log(983.04) - 1.3862944 * jax.random.uniform(arg_keys[12], (D, D), jnp.float32) ** block_levels(arg_keys[12], (D, D), ((0, 32),), -0.2, 0.2)), 245.76, 983.04),
        "widener": gaussian(arg_keys[13], (2, D, DENSE_FF), D ** -0.5, 0.21875, ((1, 32),), jnp.float32),
        "widener_mean": gaussian(arg_keys[14], (2, D, DENSE_FF), (0.3 * (SEQUENCE_COUNT * TOKEN_SLOTS) ** 0.5), 128.0, ((1, 32),), jnp.float32),
        "widener_square": jnp.clip(jnp.exp(math.log(2211.84) - 1.3862944 * jax.random.uniform(arg_keys[15], (2, D, DENSE_FF), jnp.float32) ** block_levels(arg_keys[15], (2, D, DENSE_FF), ((1, 32),), -0.2, 0.2)), 552.96, 2211.84),
        "narrower": gaussian(arg_keys[16], (DENSE_FF, D), DENSE_FF ** -0.5, 0.125, ((0, 32),), jnp.float32),
        "narrower_mean": gaussian(arg_keys[17], (DENSE_FF, D), (0.4 * (SEQUENCE_COUNT * TOKEN_SLOTS) ** 0.5), 192.0, ((0, 32),), jnp.float32),
        "narrower_square": jnp.clip(jnp.exp(math.log(3932.16) - 1.3862944 * jax.random.uniform(arg_keys[18], (DENSE_FF, D), jnp.float32) ** block_levels(arg_keys[18], (DENSE_FF, D), ((0, 32),), -0.2, 0.2)), 983.04, 3932.16),
        "norm_gains": jnp.clip(1.0 + 0.1 * jax.random.normal(arg_keys[19], (2, D), jnp.float32), 0.5, 1.5),
        "gains_mean": gaussian(arg_keys[20], (2, D), (1.0 * (SEQUENCE_COUNT * TOKEN_SLOTS) ** 0.5), 448.0, ((1, 32),), jnp.float32),
        "gains_square": jnp.clip(jnp.exp(math.log(24576.0) - 1.3862944 * jax.random.uniform(arg_keys[21], (2, D), jnp.float32) ** block_levels(arg_keys[21], (2, D), ((1, 32),), -0.2, 0.2)), 6144.0, 24576.0),
        "expander": gaussian(arg_keys[22], (EXPERTS, 2, D, EXPERT_FF), D ** -0.5, 0.21875, ((0, 4), (2, 8)), jnp.float32),
        "expander_mean": gaussian(arg_keys[23], (EXPERTS, 2, D, EXPERT_FF), (0.21 * (SEQUENCE_COUNT * TOKEN_SLOTS // EXPERTS) ** 0.5), 48.0, ((0, 4), (2, 8)), jnp.float32),
        "expander_square": jnp.clip(jnp.exp(math.log(276.48) - 1.3862944 * jax.random.uniform(arg_keys[24], (EXPERTS, 2, D, EXPERT_FF), jnp.float32) ** block_levels(arg_keys[24], (EXPERTS, 2, D, EXPERT_FF), ((0, 4), (2, 8)), -0.2, 0.2)), 69.12, 276.48),
        "reducer": gaussian(arg_keys[25], (EXPERTS, EXPERT_FF, D), EXPERT_FF ** -0.5, 0.125, ((0, 4), (1, 8)), jnp.float32),
        "reducer_mean": gaussian(arg_keys[26], (EXPERTS, EXPERT_FF, D), (0.33 * (SEQUENCE_COUNT * TOKEN_SLOTS // EXPERTS) ** 0.5), 80.0, ((0, 4), (1, 8)), jnp.float32),
        "reducer_square": jnp.clip(jnp.exp(math.log(675.84) - 1.3862944 * jax.random.uniform(arg_keys[27], (EXPERTS, EXPERT_FF, D), jnp.float32) ** block_levels(arg_keys[27], (EXPERTS, EXPERT_FF, D), ((0, 4), (1, 8)), -0.2, 0.2)), 168.96, 675.84),
    }


@jax.custom_vjp
def lower_precision(v):
    return lax.optimization_barrier(v.astype(jnp.bfloat16)).astype(jnp.float32)

@jax.custom_vjp
def lower_precision_backward(v):
    return v

def low_keep(v):
    return (lower_precision(v), None)

def low_pass(kept, grad):
    return (grad,)

def back_keep(v):
    return (v, None)

def back_low(kept, grad):
    return (lower_precision(grad),)
lower_precision.defvjp(low_keep, low_pass)
lower_precision_backward.defvjp(back_keep, back_low)

def product_rows(form, left, right):
    return jnp.einsum(form, left, right, precision=lax.Precision.HIGHEST)

def normed(values):
    return values * lax.rsqrt(lax.optimization_barrier(jnp.mean(values * values, axis=-1, keepdims=True)) + 1e-06)

def rotary(length):
    positions = jnp.arange(length, dtype=jnp.int32).astype(jnp.float32)
    half = HEAD_FEATURES // 2
    freqs = jnp.exp(-jnp.log(10000.0) * jnp.arange(half, dtype=jnp.int32).astype(jnp.float32) / half)
    angles = positions[:, None] * freqs[None, :]
    return (jnp.cos(angles)[:, None, :], jnp.sin(angles)[:, None, :])

def rotate(values, cosines, sines):
    half = values.shape[-1] // 2
    first = values[..., :half]
    second = values[..., half:]
    return jnp.concatenate([first * cosines - second * sines, second * cosines + first * sines], axis=-1)

def adamw_update(weight, moment, variance, gradient, rate):
    moment_new = 0.5 * moment + 0.5 * gradient
    variance_new = 0.5 * variance + 0.5 * gradient * gradient
    correct = 1.0 - 0.5 ** STEP
    stepped = moment_new / correct / (jnp.sqrt(variance_new / correct) + 1e-08) + 0.1 * weight
    return (moment_new, variance_new, weight - rate * stepped)

def reference(tokens, seq_lengths, deal_order, expert_routes, capacity_slots, gate_weights, cotangent, projector, projector_mean, projector_square, collector, collector_first_moment, collector_second_moment, widener, widener_mean, widener_square, narrower, narrower_mean, narrower_square, norm_gains, gains_mean, gains_square, expander, expander_mean, expander_square, reducer, reducer_mean, reducer_square):
    slots_all = jnp.arange(SEQUENCE_COUNT, dtype=jnp.int32)
    source = slots_all // N_EXP * N_EXP + deal_order.astype(jnp.int32)
    home_place = jnp.zeros((SEQUENCE_COUNT,), jnp.int32).at[source].set(slots_all)
    stream_in = tokens.astype(jnp.float32)[source]
    lengths_dealt = seq_lengths[source]
    valid = (jnp.arange(TOKEN_SLOTS, dtype=jnp.int32)[None, :] < lengths_dealt[:, None]).astype(jnp.float32)
    places = (expert_routes * CAP + capacity_slots).reshape(SEQUENCE_COUNT, 2 * TOKEN_SLOTS).astype(jnp.int32)
    cosines, sines = rotary(TOKEN_SLOTS)

    def attend_one(packed):
        queries, keys, values, length = packed
        scores = lower_precision_backward(product_rows('qhd,khd->hqk', queries, keys) * 0.125)
        rows_at = jnp.arange(TOKEN_SLOTS, dtype=jnp.int32)[:, None]
        cols_at = jnp.arange(TOKEN_SLOTS, dtype=jnp.int32)[None, :]
        allowed = (cols_at <= rows_at) & (cols_at < length)
        scores = jnp.where(allowed[None], scores, -1e+30)
        top = lax.optimization_barrier(jnp.max(scores, axis=-1, keepdims=True))
        expo = jnp.exp(scores - top)
        soft = expo / lax.optimization_barrier(jnp.sum(expo, axis=-1, keepdims=True))
        mixed_output = product_rows('hqk,khd->qhd', lower_precision(soft), values)
        return mixed_output.reshape(TOKEN_SLOTS, HEAD_COUNT * HEAD_FEATURES)

    def expert_one(packed):
        rows_in, widen_one, narrow_one = packed
        gate_pre = lower_precision_backward(product_rows('rd,df->rf', rows_in, lower_precision(widen_one[0])))
        up_pre = lower_precision_backward(product_rows('rd,df->rf', rows_in, lower_precision(widen_one[1])))
        hidden_rows = lower_precision(jax.nn.silu(gate_pre) * up_pre)
        return lower_precision(lower_precision_backward(product_rows('rf,fd->rd', hidden_rows, lower_precision(narrow_one))))

    def forward_pass(projection_matrix, collector_matrix, widening_matrix, narrowing_matrix, gains_vector, expansion_matrix, reduction_matrix, residual_flow, gate_matrix):
        gains_low = lower_precision(gains_vector)
        first_input = lower_precision(normed(residual_flow) * gains_low[0])
        query_rows = lower_precision_backward(product_rows('fno,og->fng', first_input, lower_precision(projection_matrix[0]))).reshape(SEQUENCE_COUNT, TOKEN_SLOTS, HEAD_COUNT, HEAD_FEATURES)
        key_rows = lower_precision_backward(product_rows('fno,og->fng', first_input, lower_precision(projection_matrix[1]))).reshape(SEQUENCE_COUNT, TOKEN_SLOTS, HEAD_COUNT, HEAD_FEATURES)
        value_rows = lower_precision_backward(product_rows('fno,og->fng', first_input, lower_precision(projection_matrix[2]))).reshape(SEQUENCE_COUNT, TOKEN_SLOTS, HEAD_COUNT, HEAD_FEATURES)
        query_rows = lower_precision(rotate(query_rows, cosines, sines))
        key_rows = lower_precision(rotate(key_rows, cosines, sines))
        value_rows = lower_precision(value_rows)
        mixed_output = lax.map(jax.checkpoint(attend_one), (query_rows, key_rows, value_rows, lengths_dealt))
        mixed_output = lower_precision(lower_precision_backward(mixed_output))
        middle_state = residual_flow + lower_precision_backward(product_rows('pyf,fv->pyv', mixed_output, lower_precision(collector_matrix)))
        second_input = lower_precision(normed(middle_state) * gains_low[1])
        gating_scores = lower_precision_backward(product_rows('oka,ap->okp', second_input, lower_precision(widening_matrix[0])))
        upward_rows = lower_precision_backward(product_rows('oka,ap->okp', second_input, lower_precision(widening_matrix[1])))
        hidden_state = lower_precision(jax.nn.silu(gating_scores) * upward_rows)
        dense_path = lower_precision_backward(product_rows('nav,vb->nab', hidden_state, lower_precision(narrowing_matrix)))
        spread = jnp.repeat(second_input, 2, axis=1)
        buffers = jax.vmap(lambda where_to, values: jnp.zeros((EXPERTS * CAP, D), jnp.float32).at[where_to].set(values))(places, spread)
        buffers = lower_precision_backward(buffers)
        buffers = buffers.reshape(SEQUENCE_COUNT, EXPERTS, CAP, D).transpose(1, 0, 2, 3).reshape(EXPERTS, SEQUENCE_COUNT * CAP, D)
        results = lax.map(jax.checkpoint(expert_one), (buffers, expansion_matrix, reduction_matrix))
        results = results.reshape(EXPERTS, SEQUENCE_COUNT, CAP, D).transpose(1, 0, 2, 3).reshape(SEQUENCE_COUNT, EXPERTS * CAP, D)
        picked = jax.vmap(lambda lookup, where_to: lookup[where_to])(results, places).reshape(SEQUENCE_COUNT, TOKEN_SLOTS, 2, D)
        mixture = lax.optimization_barrier(jnp.sum(gate_matrix[..., None] * picked, axis=2))
        return middle_state + dense_path + mixture
    layer_output, pullback = jax.vjp(forward_pass, projector, collector, widener, narrower, norm_gains, expander, reducer, stream_in, gate_weights)
    gradient_tree = pullback(cotangent * valid[..., None])
    projection_gradient, collector_gradient, widening_gradient, narrowing_gradient, gains_gradient, expansion_gradient, reduction_gradient, residual_gradient, gate_gradient = gradient_tree
    projection_updated = adamw_update(projector, projector_mean, projector_square, projection_gradient, 0.1)
    collector_updated = adamw_update(collector, collector_first_moment, collector_second_moment, collector_gradient, 0.3)
    widening_updated = adamw_update(widener, widener_mean, widener_square, widening_gradient, 0.07)
    narrowing_updated = adamw_update(narrower, narrower_mean, narrower_square, narrowing_gradient, 0.045)
    gains_updated = adamw_update(norm_gains, gains_mean, gains_square, gains_gradient, 0.2)
    expansion_updated = adamw_update(expander, expander_mean, expander_square, expansion_gradient, 0.07)
    reduction_updated = adamw_update(reducer, reducer_mean, reducer_square, reduction_gradient, 0.045)
    return (layer_output[home_place], residual_gradient[home_place], gate_gradient, projection_updated[0], projection_updated[1], projection_updated[2], collector_updated[0], collector_updated[1], collector_updated[2], widening_updated[0], widening_updated[1], widening_updated[2], narrowing_updated[0], narrowing_updated[1], narrowing_updated[2], gains_updated[0], gains_updated[1], gains_updated[2], expansion_updated[0], expansion_updated[1], expansion_updated[2], reduction_updated[0], reduction_updated[1], reduction_updated[2])
```

```python
import functools

import jax
import jax.numpy as jnp
import numpy as np
from jax import lax
from jax.experimental import pallas as pl
from jax.experimental.pallas import tpu as pltpu
from jax.sharding import PartitionSpec as P

HEAD_COUNT = 12
HEAD_FEATURES = 64
STEP = 5


def rms_factor(values):
    return lax.rsqrt(jnp.mean(values * values, axis=-1, keepdims=True) + 1e-06)


def rms_back(values, factor, upstream):
    return factor * (
        upstream - values * factor * factor * jnp.mean(upstream * values, axis=-1, keepdims=True)
    )


def rotary(length):
    positions = jnp.arange(length, dtype=jnp.int32).astype(jnp.float32)
    half = HEAD_FEATURES // 2
    freqs = jnp.exp(
        -jnp.log(10000.0) * jnp.arange(half, dtype=jnp.int32).astype(jnp.float32) / half
    )
    angles = positions[:, None] * freqs[None, :]
    return (jnp.cos(angles)[:, None, :], jnp.sin(angles)[:, None, :])


def rotate(values, cosines, sines):
    half = values.shape[-1] // 2
    first = values[..., :half]
    second = values[..., half:]
    return jnp.concatenate(
        [first * cosines - second * sines, second * cosines + first * sines], axis=-1
    )


def rotate_back(values, cosines, sines):
    half = values.shape[-1] // 2
    first = values[..., :half]
    second = values[..., half:]
    return jnp.concatenate(
        [first * cosines + second * sines, second * cosines - first * sines], axis=-1
    )


def silu_slope(values):
    sigmoid_of = jax.nn.sigmoid(values)
    return sigmoid_of * (1.0 + values * (1.0 - sigmoid_of))


def matmul(left, right):
    return jnp.dot(left, right, preferred_element_type=jnp.float32)


def outer_sum(left, right):
    return jnp.einsum("ld,lf->df", left, right, preferred_element_type=jnp.float32)


def adamw_update(weight, moment, variance, gradient, rate):
    moment_new = 0.5 * moment + 0.5 * gradient
    variance_new = 0.5 * variance + 0.5 * gradient * gradient
    correct = 1.0 - 0.5**STEP
    stepped = moment_new / correct / (jnp.sqrt(variance_new / correct) + 1e-08) + 0.1 * weight
    return (moment_new, variance_new, weight - rate * stepped)


def local_plain(
    tokens,
    seq_lengths,
    deal_order,
    expert_routes,
    capacity_slots,
    gate_weights,
    cotangent,
    projector,
    projector_mean,
    projector_square,
    collector,
    collector_first_moment,
    collector_second_moment,
    widener,
    widener_mean,
    widener_square,
    narrower,
    narrower_mean,
    narrower_square,
    norm_gains,
    gains_mean,
    gains_square,
    expander,
    expander_mean,
    expander_square,
    reducer,
    reducer_mean,
    reducer_square,
):
    members = lax.axis_size("exp")
    member = lax.axis_index("exp")
    length_seq = tokens.shape[1]
    width = tokens.shape[2]
    local_experts = expander.shape[0]
    experts_all = local_experts * members
    capacity = 3 * length_seq // experts_all
    member_ids = jnp.arange(members, dtype=jnp.int32)
    source = deal_order[member]
    home_slot = jnp.sum(jnp.where(deal_order == member, member_ids, 0))
    seq_length = seq_lengths[source]
    piece = lax.all_gather(tokens, "exp", axis=0, tiled=True)
    chosen = jnp.arange(piece.shape[0], dtype=jnp.int32) == source
    dealt = jnp.sum(
        jnp.where(chosen[:, None, None], piece, jnp.zeros_like(piece)), axis=0, keepdims=True
    )
    residual_flow = dealt[0].astype(jnp.float32)
    project_full, collect_full, widen_full, narrow_full, gains_full = (
        lax.all_gather(projector.astype(jnp.bfloat16), ("grp", "exp"), axis=1, tiled=True),
        lax.all_gather(collector.astype(jnp.bfloat16), ("grp", "exp"), axis=0, tiled=True),
        lax.all_gather(widener.astype(jnp.bfloat16), ("grp", "exp"), axis=1, tiled=True),
        lax.all_gather(narrower.astype(jnp.bfloat16), ("grp", "exp"), axis=0, tiled=True),
        lax.all_gather(norm_gains.astype(jnp.bfloat16), ("grp", "exp"), axis=1, tiled=True),
    )
    expand_full, reduce_full = (
        lax.all_gather(expander.astype(jnp.bfloat16), "grp", axis=2, tiled=True),
        lax.all_gather(reducer.astype(jnp.bfloat16), "grp", axis=1, tiled=True),
    )
    gains_used = gains_full.astype(jnp.float32)
    cosines, sines = rotary(length_seq)
    scale_one = rms_factor(residual_flow)
    normed_one = residual_flow * scale_one
    first_input = (normed_one * gains_used[0]).astype(jnp.bfloat16)
    query_raw = matmul(first_input, project_full[0]).reshape(length_seq, HEAD_COUNT, HEAD_FEATURES)
    key_raw = matmul(first_input, project_full[1]).reshape(length_seq, HEAD_COUNT, HEAD_FEATURES)
    value_raw = matmul(first_input, project_full[2]).reshape(length_seq, HEAD_COUNT, HEAD_FEATURES)
    query_rot = rotate(query_raw, cosines, sines).astype(jnp.bfloat16)
    key_rot = rotate(key_raw, cosines, sines).astype(jnp.bfloat16)
    value_low = value_raw.astype(jnp.bfloat16)
    rows_at = jnp.arange(length_seq, dtype=jnp.int32)[:, None]
    cols_at = jnp.arange(length_seq, dtype=jnp.int32)[None, :]
    allowed = ((cols_at <= rows_at) & (cols_at < seq_length))[None]
    scores = (
        jnp.einsum("qhd,khd->hqk", query_rot, key_rot, preferred_element_type=jnp.float32) * 0.125
    )
    masked = jnp.where(allowed, scores, -1e30)
    top = jnp.max(masked, axis=-1, keepdims=True)
    expo = jnp.exp(masked - top)
    total = jnp.sum(expo, axis=-1, keepdims=True)
    soft = expo / total
    logsum = top + jnp.log(total)
    mixed_output = (
        jnp.einsum(
            "hqk,khd->qhd", soft.astype(jnp.bfloat16), value_low, preferred_element_type=jnp.float32
        )
        .reshape(length_seq, width)
        .astype(jnp.bfloat16)
    )
    middle_state = residual_flow + matmul(mixed_output, collect_full)
    scale_two = rms_factor(middle_state)
    normed_two = middle_state * scale_two
    second_input = (normed_two * gains_used[1]).astype(jnp.bfloat16)
    gating_scores = matmul(second_input, widen_full[0])
    upward_rows = matmul(second_input, widen_full[1])
    hidden_state = (jax.nn.silu(gating_scores) * upward_rows).astype(jnp.bfloat16)
    dense_branch = matmul(hidden_state, narrow_full)
    flat = (expert_routes[0] * capacity + capacity_slots[0]).reshape(-1)
    spread = jnp.repeat(second_input, 2, axis=0)
    dispatch = jnp.zeros((experts_all * capacity, width), jnp.bfloat16).at[flat].set(spread)
    dispatch = dispatch.reshape(experts_all, capacity, width)
    rows = lax.all_to_all(dispatch, "exp", split_axis=0, concat_axis=0, tiled=True)
    count = rows.shape[1]
    grouped = rows.reshape(members, local_experts, count, width)
    gate_pre = jnp.einsum(
        "sekd,edf->sekf", grouped, expand_full[:, 0], preferred_element_type=jnp.float32
    )
    up_pre = jnp.einsum(
        "sekd,edf->sekf", grouped, expand_full[:, 1], preferred_element_type=jnp.float32
    )
    hidden_rows = (jax.nn.silu(gate_pre) * up_pre).astype(jnp.bfloat16)
    result = jnp.einsum(
        "sekf,efd->sekd", hidden_rows, reduce_full, preferred_element_type=jnp.float32
    )
    result = result.astype(jnp.bfloat16).reshape(members * local_experts, count, width)
    returned_rows = lax.all_to_all(result, "exp", split_axis=0, concat_axis=0, tiled=True)
    outcome = (
        returned_rows,
        rows,
        gate_pre.reshape(members * local_experts, count, -1),
        up_pre.reshape(members * local_experts, count, -1),
    )
    returned, received, gate_kept, up_kept = outcome
    picked = (
        returned.reshape(experts_all * capacity, width)[flat]
        .reshape(length_seq, 2, width)
        .astype(jnp.float32)
    )
    gate_local = gate_weights[0]
    mixture = jnp.sum(gate_local[..., None] * picked, axis=1)
    layer_output = middle_state + dense_branch + mixture
    valid = (jnp.arange(length_seq, dtype=jnp.int32) < seq_length).astype(jnp.float32)
    grad_out = cotangent[0] * valid[:, None]
    grad_low = grad_out.astype(jnp.bfloat16)
    narrow_grad = outer_sum(hidden_state, grad_low)
    hidden_grad = jnp.einsum("ld,fd->lf", grad_low, narrow_full, preferred_element_type=jnp.float32)
    gating_grad = (hidden_grad * upward_rows * silu_slope(gating_scores)).astype(jnp.bfloat16)
    upward_grad = (hidden_grad * jax.nn.silu(gating_scores)).astype(jnp.bfloat16)
    widen_grad = jnp.stack(
        [outer_sum(second_input, gating_grad), outer_sum(second_input, upward_grad)]
    )
    second_grad = jnp.einsum(
        "lf,df->ld", gating_grad, widen_full[0], preferred_element_type=jnp.float32
    ) + jnp.einsum("lf,df->ld", upward_grad, widen_full[1], preferred_element_type=jnp.float32)
    gate_grad_local = jnp.sum(grad_out[:, None, :] * picked, axis=-1)
    result_grad = (
        (gate_local[..., None] * grad_out[:, None, :])
        .astype(jnp.bfloat16)
        .reshape(2 * length_seq, width)
    )
    grad_send = jnp.zeros((experts_all * capacity, width), jnp.bfloat16).at[flat].set(result_grad)
    grad_recv = lax.all_to_all(
        grad_send.reshape(experts_all, capacity, width),
        "exp",
        split_axis=0,
        concat_axis=0,
        tiled=True,
    )
    grad_group = grad_recv.reshape(members, local_experts, capacity, width)
    rows_group = received.reshape(members, local_experts, capacity, width)
    gate_pre = gate_kept.reshape(members, local_experts, capacity, -1)
    up_pre = up_kept.reshape(members, local_experts, capacity, -1)
    hidden_rows = (jax.nn.silu(gate_pre) * up_pre).astype(jnp.bfloat16)
    reduce_grad = jnp.einsum(
        "sekf,sekd->efd", hidden_rows, grad_group, preferred_element_type=jnp.float32
    )
    hidden_rows_grad = jnp.einsum(
        "sekd,efd->sekf", grad_group, reduce_full, preferred_element_type=jnp.float32
    )
    gate_rows_grad = (hidden_rows_grad * up_pre * silu_slope(gate_pre)).astype(jnp.bfloat16)
    up_rows_grad = (hidden_rows_grad * jax.nn.silu(gate_pre)).astype(jnp.bfloat16)
    expand_grad = jnp.stack(
        [
            jnp.einsum(
                "sekd,sekf->edf", rows_group, gate_rows_grad, preferred_element_type=jnp.float32
            ),
            jnp.einsum(
                "sekd,sekf->edf", rows_group, up_rows_grad, preferred_element_type=jnp.float32
            ),
        ],
        axis=1,
    )
    row_grads = jnp.einsum(
        "sekf,edf->sekd", gate_rows_grad, expand_full[:, 0], preferred_element_type=jnp.float32
    ) + jnp.einsum(
        "sekf,edf->sekd", up_rows_grad, expand_full[:, 1], preferred_element_type=jnp.float32
    )
    row_grads = row_grads.astype(jnp.bfloat16).reshape(experts_all, capacity, width)
    came_back = lax.all_to_all(row_grads, "exp", split_axis=0, concat_axis=0, tiled=True).reshape(
        experts_all * capacity, width
    )
    second_grad = second_grad + jnp.sum(
        came_back[flat].reshape(length_seq, 2, width).astype(jnp.float32), axis=1
    )
    gains_grad_two = jnp.sum(second_grad * normed_two, axis=0)
    middle_grad = grad_out + rms_back(middle_state, scale_two, second_grad * gains_used[1])
    middle_low = middle_grad.astype(jnp.bfloat16)
    collect_grad = outer_sum(mixed_output, middle_low)
    mixed_grad = jnp.einsum(
        "ld,ed->le", middle_low, collect_full, preferred_element_type=jnp.float32
    )
    mixed_grad = mixed_grad.astype(jnp.bfloat16).reshape(length_seq, HEAD_COUNT, HEAD_FEATURES)
    scores_again = (
        jnp.einsum("qhd,khd->hqk", query_rot, key_rot, preferred_element_type=jnp.float32) * 0.125
    )
    soft_again = jnp.where(allowed, jnp.exp(scores_again - logsum), 0.0)
    value_grad = jnp.einsum(
        "hqk,qhd->khd",
        soft_again.astype(jnp.bfloat16),
        mixed_grad,
        preferred_element_type=jnp.float32,
    )
    soft_grad = jnp.einsum(
        "qhd,khd->hqk", mixed_grad, value_low, preferred_element_type=jnp.float32
    )
    score_grad = (
        soft_again * (soft_grad - jnp.sum(soft_again * soft_grad, axis=-1, keepdims=True))
    ).astype(jnp.bfloat16)
    query_grad = (
        jnp.einsum("hqk,khd->qhd", score_grad, key_rot, preferred_element_type=jnp.float32) * 0.125
    )
    key_grad = (
        jnp.einsum("hqk,qhd->khd", score_grad, query_rot, preferred_element_type=jnp.float32)
        * 0.125
    )
    query_back = (
        rotate_back(query_grad, cosines, sines).reshape(length_seq, width).astype(jnp.bfloat16)
    )
    key_back = rotate_back(key_grad, cosines, sines).reshape(length_seq, width).astype(jnp.bfloat16)
    value_back = value_grad.reshape(length_seq, width).astype(jnp.bfloat16)
    project_grad = jnp.stack(
        [
            outer_sum(first_input, query_back),
            outer_sum(first_input, key_back),
            outer_sum(first_input, value_back),
        ]
    )
    first_grad = (
        jnp.einsum("le,de->ld", query_back, project_full[0], preferred_element_type=jnp.float32)
        + jnp.einsum("le,de->ld", key_back, project_full[1], preferred_element_type=jnp.float32)
        + jnp.einsum("le,de->ld", value_back, project_full[2], preferred_element_type=jnp.float32)
    )
    gains_grad_one = jnp.sum(first_grad * normed_one, axis=0)
    stream_grad = middle_grad + rms_back(residual_flow, scale_one, first_grad * gains_used[0])
    gains_grad = jnp.stack([gains_grad_one, gains_grad_two])
    project_part, collect_part, widen_part, narrow_part, gains_part = (
        lax.psum_scatter(project_grad, ("grp", "exp"), scatter_dimension=1, tiled=True),
        lax.psum_scatter(collect_grad, ("grp", "exp"), scatter_dimension=0, tiled=True),
        lax.psum_scatter(widen_grad, ("grp", "exp"), scatter_dimension=1, tiled=True),
        lax.psum_scatter(narrow_grad, ("grp", "exp"), scatter_dimension=0, tiled=True),
        lax.psum_scatter(gains_grad, ("grp", "exp"), scatter_dimension=1, tiled=True),
    )
    expand_part, reduce_part = (
        lax.psum_scatter(
            expand_grad.astype(jnp.bfloat16), "grp", scatter_dimension=2, tiled=True
        ).astype(jnp.float32),
        lax.psum_scatter(
            reduce_grad.astype(jnp.bfloat16), "grp", scatter_dimension=1, tiled=True
        ).astype(jnp.float32),
    )
    empty = jnp.zeros((1, length_seq, width), jnp.float32)
    pieces = (
        lax.all_gather(layer_output[None].astype(jnp.bfloat16), "exp", axis=0, tiled=True).astype(
            jnp.float32
        ),
        lax.all_gather(stream_grad[None].astype(jnp.bfloat16), "exp", axis=0, tiled=True).astype(
            jnp.float32
        ),
    )
    chosen = (jnp.arange(pieces[0].shape[0], dtype=jnp.int32) == home_slot)[:, None, None]
    homed_output = empty + jnp.sum(jnp.where(chosen, pieces[0], 0.0), axis=0, keepdims=True)
    homed_grad = empty + jnp.sum(jnp.where(chosen, pieces[1], 0.0), axis=0, keepdims=True)
    project_new = adamw_update(projector, projector_mean, projector_square, project_part, 0.1)
    collect_new = adamw_update(
        collector, collector_first_moment, collector_second_moment, collect_part, 0.3
    )
    widening_updated = adamw_update(widener, widener_mean, widener_square, widen_part, 0.07)
    narrowing_updated = adamw_update(narrower, narrower_mean, narrower_square, narrow_part, 0.045)
    gains_updated = adamw_update(norm_gains, gains_mean, gains_square, gains_part, 0.2)
    expansion_updated = adamw_update(expander, expander_mean, expander_square, expand_part, 0.07)
    reduction_updated = adamw_update(reducer, reducer_mean, reducer_square, reduce_part, 0.045)
    return (
        homed_output,
        homed_grad,
        gate_grad_local[None],
        project_new[0],
        project_new[1],
        project_new[2],
        collect_new[0],
        collect_new[1],
        collect_new[2],
        widening_updated[0],
        widening_updated[1],
        widening_updated[2],
        narrowing_updated[0],
        narrowing_updated[1],
        narrowing_updated[2],
        gains_updated[0],
        gains_updated[1],
        gains_updated[2],
        expansion_updated[0],
        expansion_updated[1],
        expansion_updated[2],
        reduction_updated[0],
        reduction_updated[1],
        reduction_updated[2],
    )


MESH = pl.DeviceIdType.MESH
VMEM = pltpu.VMEM
LIMIT = 60 * 1024 * 1024


def ring_place(index, groups):
    row, side = lax.div(index, 2), lax.rem(index, 2)
    return (1 - side) * row + side * (groups - 1 - row)


def ring_member(place, groups):
    side = lax.div(place, groups // 2)
    return 2 * ((1 - side) * place + side * (groups - 1 - place)) + side


def remote(source, target, sends, arrivals, at, device):
    return pltpu.make_async_remote_copy(
        src_ref=source,
        dst_ref=target,
        send_sem=sends.at[at],
        recv_sem=arrivals.at[at],
        device_id=device,
        device_id_type=MESH,
    )


class Links:
    def __init__(self, sends, arrivals):
        self.sends, self.arrivals, self.count, self.started = sends, arrivals, 0, []

    def copy(self, source, target, device):
        made = remote(source, target, self.sends, self.arrivals, self.count, device)
        self.count += 1
        made.start()
        self.started.append(made)
        return made

    def finish(self):
        for made in self.started:
            made.wait_send()


class Places:
    def __init__(self, groups, members):
        self.groups, self.members = groups, members
        self.group = lax.axis_index("grp")
        self.member = lax.axis_index("exp")
        self.place = ring_place(self.group, groups)
        self.next = {"grp": self.owner(1)}
        self.back = {"grp": self.owner(-1)}
        half = members // 2
        self.far = lax.rem(self.member + half, members)
        self.near = self.member + 1 - 2 * lax.rem(self.member, 2)
        self.cross = lax.rem(self.near + half, members)
        self.peers = [lax.rem(self.member + step, members) for step in range(1, members)]

    def owner(self, offset):
        place = lax.rem(self.place + offset + 2 * self.groups, self.groups)
        return ring_member(place, self.groups)

    def enter(self):
        barrier = pltpu.get_barrier_semaphore()
        partners = [self.next, self.back] + [{"exp": peer} for peer in self.peers]
        for partner in partners:
            pl.semaphore_signal(barrier, inc=1, device_id=partner, device_id_type=MESH)
        pl.semaphore_wait(barrier, len(partners))


def rows(start, count, align=16):
    return pl.ds(pl.multiple_of(start, align), count)


def first_half(shape):
    return lax.rem(lax.broadcasted_iota(jnp.int32, shape, len(shape) - 1), 128) < 64


def turned(values):
    lanes = lax.broadcasted_iota(jnp.int32, values.shape, 1)
    return jnp.where(
        lax.rem(lanes, HEAD_FEATURES) < HEAD_FEATURES // 2,
        pltpu.roll(values, 128 - HEAD_FEATURES // 2, 1),
        pltpu.roll(values, HEAD_FEATURES // 2, 1),
    )


def nt(left, right):
    return lax.dot_general(
        left, right, (((1,), (1,)), ((), ())), preferred_element_type=jnp.float32
    )


def tn(left, right):
    return lax.dot_general(
        left, right, (((0,), (0,)), ((), ())), preferred_element_type=jnp.float32
    )


def sigmoid(values):
    return 1.0 / (1.0 + jnp.exp(-values))


def same(length):
    shape = (length, length)
    return lax.broadcasted_iota(jnp.int32, shape, 0) == lax.broadcasted_iota(jnp.int32, shape, 1)


def upright(line):
    return jnp.sum(jnp.where(same(line.shape[1]), line, 0.0), axis=1, keepdims=True)


def lying(column):
    return jnp.sum(jnp.where(same(column.shape[0]), column, 0.0), axis=0, keepdims=True)


def dealt_lanes(values, piece, pieces):
    low_lanes = lax.broadcasted_iota(jnp.int32, (values.shape[0], 128), 1) < 64
    found = []
    span = 64 * pieces
    for start in range(0, values.shape[1], 2 * span):
        start = start + piece // 2 * 128
        one, two = values[:, start : start + 128], values[:, start + span : start + span + 128]
        if piece % 2:
            one = pltpu.roll(one, 64, 1)
        else:
            two = pltpu.roll(two, 64, 1)
        found.append(jnp.where(low_lanes, one, two))
    return jnp.concatenate(found, axis=1)


def joined_lanes(even, odd):
    low_lanes = lax.broadcasted_iota(jnp.int32, (even.shape[0], 128), 1) < 64
    found = []
    for start in range(0, even.shape[1], 128):
        one, two = even[:, start : start + 128], odd[:, start : start + 128]
        found.append(jnp.where(low_lanes, one, pltpu.roll(two, 64, 1)))
        found.append(jnp.where(low_lanes, pltpu.roll(one, 64, 1), two))
    return found


def gather_kernel(
    groups,
    members,
    table,
    tokens,
    cotangent,
    routes,
    places,
    gates,
    norm_gains,
    projector,
    collector,
    widener,
    narrower,
    expander,
    reducer,
    cos_ref,
    sin_ref,
    wide_grads,
    down_grads,
    attend_full,
    grads_all,
    gains_full,
    saved,
    middle_ref,
    soft_ref,
    result_ref,
    back_ref,
    gate_ref,
    second_all,
    meta_send,
    meta_all,
    attend_send,
    attend_recv,
    widen_send,
    widen_recv,
    gains,
    gain_recv,
    gain_ring,
    wide_full,
    down_full,
    wide_own,
    down_own,
    inputs_ref,
    inputs_turned,
    dense_out,
    dense_back,
    rows_in,
    rows_turned,
    rows_grad,
    rows_out,
    rows_back,
    sends,
    arrivals,
    ring_sends,
    ring_arrivals,
    local_sems,
):
    at = Places(groups, members)
    links = Links(sends, arrivals)
    at.enter()
    me, steps = at.member, groups - 1
    share, width = projector.shape[1:]
    block = share * members
    length = tokens.shape[0]
    chunks, low = down_own.shape[:2]
    capacity = rows_in.shape[0] // members

    attend_send[0:3] = projector[...]
    attend_send[3] = collector[...]
    gains[...] = jnp.zeros_like(gains)
    gains[0:2, 0 : norm_gains.shape[1]] = norm_gains[...]
    gains[...] = pltpu.roll(gains[...], (at.group * members + me) * norm_gains.shape[1], 1)
    first_moves = [
        [
            links.copy(attend_send.at[peer], attend_recv.at[me], {"exp": peer}),
            links.copy(gains, gain_recv.at[me], {"exp": peer}),
        ]
        for peer in at.peers
    ]
    gain_recv[me] = gains[...]
    attend_recv[me] = attend_send[me]
    for matrix in range(2):
        for member in range(members):
            widen_send[member, matrix] = dealt_lanes(widener[matrix], member, members)
    widen_moves = [
        links.copy(widen_send.at[peer], widen_recv.at[me], {"exp": peer}) for peer in at.peers
    ]
    widen_recv[me] = widen_send[me]
    down_own[0] = narrower[...].astype(jnp.bfloat16)
    for moves in first_moves:
        for move in moves:
            move.wait_recv()
    attend_full[me, rows(at.group * block, block), :] = (
        attend_recv[...].reshape(block, width).astype(jnp.bfloat16)
    )
    total_gain = gain_recv[0]
    for member in range(1, members):
        total_gain = total_gain + gain_recv[member]
    gain_ring[at.group] = total_gain

    half = block // 2

    def unit(owner, side, matrix):
        return attend_full.at[matrix, rows(owner * block + side * half, half), :]

    def across(owner, side):
        spot = unit(owner, side, me)
        return (links.copy(spot, spot, {"exp": at.far}), links.copy(spot, spot, {"exp": at.near}))

    def onward(owner, side):
        spot = unit(owner, side, at.far)
        return links.copy(spot, spot, {"exp": at.near})

    def ring_copy(chunk, step, side, piece):
        owner = at.owner(-step if side == 0 else step)
        if piece == 0:
            spot = wide_full.at[chunk, side, rows(owner * block, block), :]
            origin = wide_own.at[chunk, side]
        else:
            spot = down_full.at[chunk, rows(owner * low + side * (low // 2), low // 2), :]
            origin = down_own.at[chunk, pl.ds(side * (low // 2), low // 2), :]
        place = (chunk * steps + step) * 4 + side * 2 + piece
        return remote(
            spot if step else origin,
            spot,
            ring_sends,
            ring_arrivals,
            place,
            (at.next, at.back)[side],
        )

    def ring_step(chunk, step):
        for piece in range(2):
            for side in range(2):
                if step:
                    ring_copy(chunk, step - 1, side, piece).wait_recv()
                if step < steps:
                    ring_copy(chunk, step, side, piece).start()

    def tick(count):
        for chunk in range(chunks):
            if 0 <= count - 2 * chunk <= steps:
                ring_step(chunk, count - 2 * chunk)

    ring, crossed, passed = [], [], []
    gain_moves = []
    for step in range(groups):
        owners = (at.owner(-step), at.owner(step))
        if step:
            for move in ring[-1]:
                move.wait_recv()
            gain_moves[-1].wait_recv()
        if step < steps:
            ring.append(
                [
                    links.copy(unit(owner, side, me), unit(owner, side, me), target)
                    for side, (owner, target) in enumerate(zip(owners, (at.next, at.back)))
                ]
            )
            gain_moves.append(
                links.copy(gain_ring.at[owners[0]], gain_ring.at[owners[0]], at.next)
            )
        crossed.append([across(owner, side) for side, owner in enumerate(owners)])
        if step:
            for side, owner in enumerate((at.owner(1 - step), at.owner(step - 1))):
                crossed[step - 1][side][0].wait_recv()
                passed.append(onward(owner, side))
        if step == 0:
            for chunk in range(1, chunks):
                for matrix in range(2):
                    wide_own[chunk, matrix] = dealt_lanes(
                        expander[matrix], chunk - 1, chunks - 1
                    ).astype(jnp.bfloat16)
                down_own[chunk] = reducer[(chunk - 1) * low : chunk * low, :].astype(jnp.bfloat16)
        if step == 2:
            for move in widen_moves:
                move.wait_recv()
            for matrix in range(2):
                wide_own[0, matrix] = jnp.concatenate(
                    [widen_recv[member, matrix] for member in range(members)], axis=0
                ).astype(jnp.bfloat16)
            for chunk in range(chunks):
                for side in range(2):
                    wide_full[chunk, side, rows(at.group * block, block), :] = wide_own[
                        chunk, side
                    ]
                down_full[chunk, rows(at.group * low, low), :] = down_own[chunk]
        if step == 3:
            tick(0)
        if step == 6:
            tick(1)
    tick(2)
    valid = lax.broadcasted_iota(jnp.int32, (length, 1), 0) < table[3, me]
    grads_all[me] = jnp.where(valid, cotangent[...], 0.0).astype(jnp.bfloat16)
    route = [routes[:, choice : choice + 1] for choice in range(2)]
    place = [places[:, choice : choice + 1].astype(jnp.float32) for choice in range(2)]
    meta_send[...] = jnp.zeros_like(meta_send)
    for member in range(members):
        named = [chosen == member for chosen in route]
        meta_send[member, 0:1, :] = lying(
            jnp.where(named[0], place[0], jnp.where(named[1], place[1], -1.0))
        )
        meta_send[member, 1:2, :] = lying(
            jnp.where(named[0], gates[:, 0:1], jnp.where(named[1], gates[:, 1:2], 0.0))
        )
    meta_all[me] = meta_send[me]
    grad_moves = [
        [
            links.copy(grads_all.at[me], grads_all.at[me], {"exp": peer}),
            links.copy(meta_send.at[peer], meta_all.at[me], {"exp": peer}),
        ]
        for peer in at.peers
    ]
    for side, owner in enumerate((at.owner(-steps), at.owner(steps))):
        crossed[steps][side][0].wait_recv()
        passed.append(onward(owner, side))
    total_gain = gain_ring[0]
    for group in range(1, groups):
        total_gain = total_gain + gain_ring[group]
    gains_full[...] = total_gain.astype(jnp.bfloat16).astype(jnp.float32)
    stream = tokens[...].astype(jnp.float32)
    first_input = (stream * rms_factor(stream) * gains_full[0:1, :]).astype(jnp.bfloat16)
    saved[4] = first_input
    for moves in crossed:
        for move in moves:
            move[1].wait_recv()
    for move in passed:
        move.wait_recv()
    tick(3)

    cosines, sines = cos_ref[...], sin_ref[...]
    for matrix in range(3):
        raw = matmul(first_input, attend_full[matrix])
        if matrix == 2:
            saved[2] = raw.astype(jnp.bfloat16)
        else:
            for start in range(0, width, 128):
                piece = raw[:, start : start + 128]
                saved[matrix, :, start : start + 128] = (
                    piece * cosines + turned(piece) * sines
                ).astype(jnp.bfloat16)
    tick(4)

    seq_length = table[2, me]
    rows_at = lax.broadcasted_iota(jnp.int32, (length, length), 0)
    cols_at = lax.broadcasted_iota(jnp.int32, (length, length), 1)
    allowed = (cols_at <= rows_at) & (cols_at < seq_length)
    lower = first_half((length, 128))

    def heads(pair, carry):
        lanes = pl.ds(pl.multiple_of(pair * 128, 128), 128)
        query, key, value = saved[0, :, lanes], saved[1, :, lanes], saved[2, :, lanes]
        results = []
        for side in range(2):
            alone = jnp.where(lower == (side == 0), query, jnp.zeros_like(query))
            scores = jnp.where(allowed, nt(alone, key) * 0.125, -1e30)
            expo = jnp.exp(scores - jnp.max(scores, axis=-1, keepdims=True))
            soft = expo / jnp.sum(expo, axis=-1, keepdims=True)
            soft_ref[2 * pair + side] = soft
            results.append(matmul(soft.astype(jnp.bfloat16), value))
        saved[3, :, lanes] = jnp.where(lower, results[0], results[1]).astype(jnp.bfloat16)
        return carry

    lax.fori_loop(0, width // 128, heads, 0)
    tick(5)
    middle = tokens[...].astype(jnp.float32) + matmul(saved[3], attend_full[3])
    middle_ref[...] = middle
    second_all[me] = (middle * rms_factor(middle) * gains_full[1:2, :]).astype(jnp.bfloat16)
    second_moves = [
        links.copy(second_all.at[me], second_all.at[me], {"exp": peer}) for peer in at.peers
    ]
    for moves in grad_moves:
        for move in moves:
            move.wait_recv()
    tick(6)

    def hits(slot, by_row):
        line = meta_all[slot, 0:1, :]
        if by_row:
            names = lax.broadcasted_iota(jnp.int32, (capacity, length), 0).astype(jnp.float32)
            hit = names == line
        else:
            names = lax.broadcasted_iota(jnp.int32, (length, capacity), 1).astype(jnp.float32)
            hit = names == upright(line)
        return jnp.where(hit, 1.0, 0.0).astype(jnp.bfloat16)

    def spot_of(slot):
        return slice(slot * capacity, (slot + 1) * capacity)

    def here_of(slot):
        return slice(slot * length, (slot + 1) * length)

    for slot in range(members):
        pick = hits(slot, True)
        gate = jnp.sum(pick.astype(jnp.float32) * meta_all[slot, 1:2, :], axis=1, keepdims=True)
        rows_grad[spot_of(slot), :] = (matmul(pick, grads_all[slot]) * gate).astype(jnp.bfloat16)
    for move in second_moves:
        move.wait_recv()
    for slot in range(members):
        inputs_ref[here_of(slot), :] = second_all[table[0, slot]]
        rows_in[spot_of(slot), :] = matmul(hits(slot, True), inputs_ref[here_of(slot), :]).astype(
            jnp.bfloat16
        )
    inputs_turned[...] = inputs_ref[...].T
    rows_turned[...] = rows_in[...].T
    dense_out[...] = jnp.zeros_like(dense_out)
    dense_back[...] = jnp.zeros_like(dense_back)
    rows_out[...] = jnp.zeros_like(rows_out)
    rows_back[...] = jnp.zeros_like(rows_back)
    tick(7)

    def branch(chunk, inputs, turned_inputs, outer, out, back):
        for step in range(steps):
            for side in range(2):
                for piece in range(2):
                    ring_copy(chunk, step, side, piece).wait_send()

        def part(index, carry):
            lanes = pl.ds(pl.multiple_of(index * 256, 256), 256)
            gate = matmul(inputs[...], wide_full[chunk, 0, :, lanes])
            up = matmul(inputs[...], wide_full[chunk, 1, :, lanes])
            rise = sigmoid(gate)
            smooth = gate * rise
            hidden = (smooth * up).astype(jnp.bfloat16)
            hidden_grad = nt(outer[...], down_full[chunk, lanes, :])
            gate_grad = (hidden_grad * up * (rise * (1.0 + gate * (1.0 - rise)))).astype(
                jnp.bfloat16
            )
            up_grad = (hidden_grad * smooth).astype(jnp.bfloat16)
            out[...] += matmul(hidden, down_full[chunk, lanes, :])
            back[...] += nt(gate_grad, wide_full[chunk, 0, :, lanes]) + nt(
                up_grad, wide_full[chunk, 1, :, lanes]
            )
            down_full[chunk, lanes, :] = tn(hidden, outer[...]).astype(jnp.bfloat16)
            wide_full[chunk, 0, :, lanes] = matmul(turned_inputs[...], gate_grad).astype(
                jnp.bfloat16
            )
            wide_full[chunk, 1, :, lanes] = matmul(turned_inputs[...], up_grad).astype(
                jnp.bfloat16
            )
            return carry

        lax.fori_loop(0, down_full.shape[1] // 256, part, 0)
        kept(chunk, 0).start()
        kept(chunk, 1).start()

    def kept(chunk, piece):
        source, target = ((wide_full, wide_grads), (down_full, down_grads))[piece]
        return pltpu.make_async_copy(
            source.at[chunk], target.at[chunk], local_sems.at[2 * chunk + piece]
        )

    outer_all = grads_all.reshape(members * length, width)
    flat = (members * length, width)
    branch(
        0, inputs_ref, inputs_turned, outer_all, dense_out.reshape(flat), dense_back.reshape(flat)
    )

    def expert_chunk(chunk, carry):
        for last in (steps - 1, steps):
            for ahead in range(groups // 2):
                @pl.when(chunk + ahead < chunks)
                def _():
                    ring_step(chunk + ahead, last - 2 * ahead)

        branch(chunk, rows_in, rows_turned, rows_grad, rows_out, rows_back)
        return carry

    lax.fori_loop(1, chunks, expert_chunk, 0)

    for slot in range(members):
        pick = hits(slot, False)
        gate = upright(meta_all[slot, 1:2, :])
        picked = matmul(pick, rows_out[spot_of(slot), :].astype(jnp.bfloat16))
        inner = rows_back[spot_of(slot), :].astype(jnp.bfloat16)
        dense_out[slot] += gate * picked
        dense_back[slot] += matmul(pick, inner)
        score = jnp.sum(picked * grads_all[slot].astype(jnp.float32), axis=1, keepdims=True)
        gate_ref[slot] = jnp.broadcast_to(lying(score), gate_ref.shape[1:])
    for member in range(members):
        result_ref[member] = dense_out[table[1, member]].astype(jnp.bfloat16)
        back_ref[member] = dense_back[table[1, member]].astype(jnp.bfloat16)
    for chunk in range(chunks):
        kept(chunk, 0).wait()
        kept(chunk, 1).wait()
    links.finish()


def scatter_kernel(
    groups,
    members,
    table,
    tokens,
    routes,
    grads_all,
    gains_full,
    attend_full,
    saved,
    middle_ref,
    soft_ref,
    cos_ref,
    sin_ref,
    result_parts,
    back_parts,
    gate_parts,
    wide_grads,
    down_grads,
    output_ref,
    input_grad_ref,
    gate_grad_ref,
    expand_sum,
    reduce_sum,
    widen_sum,
    narrow_sum,
    attend_sum,
    gains_sum,
    gate_recv,
    result_recv,
    back_recv,
    wide_own,
    down_own,
    wide_recv,
    down_recv,
    wide_sum,
    turned_ref,
    attend_grad,
    near_recv,
    far_recv,
    far_send,
    attend_total,
    attend_recv,
    attend_back,
    widen_back,
    widen_home,
    gain_own,
    gain_recv,
    gain_ring,
    sends,
    arrivals,
    local_sems,
):
    at = Places(groups, members)
    links = Links(sends, arrivals)
    at.enter()
    me, steps = at.member, groups - 1
    length, width = tokens.shape
    chunks, low = down_own.shape[0], narrow_sum.shape[0]
    share = attend_sum.shape[1]
    block = share * members

    kept = []
    for source, spot in ((wide_grads, wide_own), (down_grads, down_own)):
        made = pltpu.make_async_copy(source, spot, local_sems.at[len(kept)])
        made.start()
        kept.append(made)

    moves_of = {}
    widen_moves = []

    def ring_step(chunk, step):
        made = []
        owners = (at.owner(-1 - step), at.owner(1 + step))
        for piece in range(2):
            for side, target in enumerate((at.next, at.back)):
                own, first = ((wide_own, wide_grads), (down_own, down_grads))[piece]
                landing = (wide_recv, down_recv)[piece].at[chunk, side]
                if piece == 0:
                    spot = (chunk, side, rows(owners[side] * block, block))
                else:
                    spot = (chunk, rows(owners[side] * low + side * (low // 2), low // 2))
                if step == 0:
                    source = first.at[spot]
                else:
                    moves_of[chunk, step - 1][2 * piece + side].wait_recv()
                    source = landing.at[step - 1]
                    added = source[...].astype(jnp.float32) + own[spot].astype(jnp.float32)
                    if step < steps:
                        source[...] = added.astype(jnp.bfloat16)
                    elif piece == 0 and chunk:
                        wide_sum[chunk - 1, side] = added
                    elif piece == 0:
                        for member in range(members):
                            widen_back[member, side] = added[
                                member * share : (member + 1) * share, :
                            ]
                    else:
                        start = side * (low // 2)
                        if chunk:
                            start = start + (chunk - 1) * low
                            reduce_sum[start : start + low // 2, :] = added
                        else:
                            narrow_sum[start : start + low // 2, :] = added
                if step < steps:
                    made.append(links.copy(source, landing.at[step], target))
        moves_of[chunk, step] = made
        if step == steps and chunk == 0:
            widen_home[me] = widen_back[me]
            for peer in at.peers:
                widen_moves.append(
                    links.copy(widen_back.at[peer], widen_home.at[me], {"exp": peer})
                )
        if step == steps and chunk and chunk % 2 == 0:
            span = 64 * (chunks - 1)
            for side in range(2):
                found = joined_lanes(wide_sum[chunk - 2, side], wide_sum[chunk - 1, side])
                for index, part in enumerate(found):
                    start = index * span + (chunk - 2) * 64
                    expand_sum[side, :, start : start + 128] = part

    def tick(count):
        for chunk in range(chunks):
            if 0 <= count - 2 * chunk <= steps:
                ring_step(chunk, count - 2 * chunk)

    back_moves = [
        links.copy(back_parts.at[peer], back_recv.at[me], {"exp": peer}) for peer in at.peers
    ]
    tick(0)
    result_moves = [
        [
            links.copy(result_parts.at[peer], result_recv.at[me], {"exp": peer}),
            links.copy(gate_parts.at[peer], gate_recv.at[me], {"exp": peer}),
        ]
        for peer in at.peers
    ]
    gate_recv[me] = gate_parts[me]
    back_recv[me] = back_parts[me]
    result_recv[me] = result_parts[me]
    for made in kept:
        made.wait()
    tick(1)
    for move in back_moves:
        move.wait_recv()
    tick(2)

    second_grad = back_recv[0].astype(jnp.float32)
    for member in range(1, members):
        second_grad = second_grad + back_recv[member].astype(jnp.float32)
    middle = middle_ref[...]
    scale = rms_factor(middle)
    gain_own[...] = jnp.zeros_like(gain_own)
    gain_own[1:2, :] = jnp.sum(second_grad * (middle * scale), axis=0, keepdims=True)
    input_grad_ref[...] = grads_all[table[1, me]].astype(jnp.float32) + rms_back(
        middle, scale, second_grad * gains_full[1:2, :]
    )
    middle_low = input_grad_ref[...].astype(jnp.bfloat16)
    turned_ref[3] = nt(middle_low, attend_full[3]).astype(jnp.bfloat16)
    tick(3)
    cosines, sines = cos_ref[...], sin_ref[...]
    lower = first_half((length, 128))

    def heads(pair, carry):
        lanes = pl.ds(pl.multiple_of(pair * 128, 128), 128)
        query, key, value = saved[0, :, lanes], saved[1, :, lanes], saved[2, :, lanes]
        outer = turned_ref[3, :, lanes]
        made = []
        for side in range(2):
            soft = soft_ref[2 * pair + side]
            alone = jnp.where(lower == (side == 0), outer, jnp.zeros_like(outer))
            value_grad = tn(soft.astype(jnp.bfloat16), outer)
            soft_grad = nt(alone, value)
            score_grad = (
                soft * (soft_grad - jnp.sum(soft * soft_grad, axis=-1, keepdims=True))
            ).astype(jnp.bfloat16)
            made.append(
                (matmul(score_grad, key) * 0.125, tn(score_grad, query) * 0.125, value_grad)
            )
        for index in range(3):
            joined = jnp.where(lower, made[0][index], made[1][index])
            if index < 2:
                joined = joined * cosines - turned(joined) * sines
            turned_ref[index, :, lanes] = joined.astype(jnp.bfloat16)
        return carry

    lax.fori_loop(0, width // 128, heads, 0)
    tick(4)
    attend_grad[3] = tn(saved[3], middle_low).astype(jnp.bfloat16)
    for matrix in range(3):
        attend_grad[matrix] = tn(saved[4], turned_ref[matrix]).astype(jnp.bfloat16)
    near_moves = [
        links.copy(attend_grad.at[matrix], near_recv.at[index], {"exp": at.near})
        for index, matrix in enumerate((at.near, at.cross))
    ]
    tick(5)
    first_grad = nt(turned_ref[0], attend_full[0])
    for matrix in range(1, 3):
        first_grad = first_grad + nt(turned_ref[matrix], attend_full[matrix])
    stream = tokens[...].astype(jnp.float32)
    scale = rms_factor(stream)
    gain_own[0:1, :] = jnp.sum(first_grad * (stream * scale), axis=0, keepdims=True)
    gain_moves = [links.copy(gain_own, gain_recv.at[me], {"exp": peer}) for peer in at.peers]
    gain_recv[me] = gain_own[...]
    input_grad_ref[...] += rms_back(stream, scale, first_grad * gains_full[0:1, :])
    for move in near_moves:
        move.wait_recv()
    far_send[...] = (
        attend_grad[at.far].astype(jnp.float32) + near_recv[1].astype(jnp.float32)
    ).astype(jnp.bfloat16)
    far_move = links.copy(far_send, far_recv, {"exp": at.far})
    tick(6)
    for moves in result_moves:
        for move in moves:
            move.wait_recv()
    output = middle_ref[...]
    for member in range(members):
        output = output + result_recv[member].astype(jnp.float32)
    output_ref[...] = output
    columns = [upright(gate_recv[member, 0:1, :]) for member in range(members)]
    for choice in range(2):
        route = routes[:, choice : choice + 1]
        found = jnp.zeros((length, 1), jnp.float32)
        for member in range(members):
            found = jnp.where(route == member, columns[member], found)
        gate_grad_ref[:, choice : choice + 1] = found
    tick(7)
    for move in gain_moves:
        move.wait_recv()
    total = gain_recv[0]
    for member in range(1, members):
        total = total + gain_recv[member]
    gain_ring[at.group] = total
    far_move.wait_recv()
    attend_total[...] = (
        attend_grad[me].astype(jnp.float32)
        + near_recv[0].astype(jnp.float32)
        + far_recv[...].astype(jnp.float32)
    ).astype(jnp.bfloat16)

    half = block // 2
    small, gain_steps = [], []

    def advance_small():
        step = len(small)
        owners = (at.owner(-1 - step), at.owner(1 + step))
        made = []
        for side, target in enumerate((at.next, at.back)):
            spot = attend_total.at[rows(owners[side] * block + side * half, half), :]
            if step:
                small[-1][side].wait_recv()
                source = attend_recv.at[side, step - 1]
                added = source[...].astype(jnp.float32) + spot[...].astype(jnp.float32)
                if step < steps:
                    source[...] = added.astype(jnp.bfloat16)
                else:
                    for member in range(members // 2):
                        attend_back[side * (members // 2) + member] = added[
                            member * share : (member + 1) * share, :
                        ]
                spot = source
            if step < steps:
                made.append(links.copy(spot, attend_recv.at[side, step], target))
        if step:
            gain_steps[-1].wait_recv()
        if step < steps:
            owner = at.owner(-step)
            gain_steps.append(links.copy(gain_ring.at[owner], gain_ring.at[owner], at.next))
        small.append(made)

    last = steps + 2 * (chunks - 1)
    for count in range(steps + 1, last):
        if len(small) <= steps:
            advance_small()
        tick(count)
    while len(small) <= steps:
        advance_small()
    attend_moves = [
        links.copy(attend_back.at[peer], attend_sum.at[me], {"exp": peer}) for peer in at.peers
    ]
    attend_sum[me] = attend_back[me]
    total = gain_ring[0]
    for group in range(1, groups):
        total = total + gain_ring[group]
    count = gains_sum.shape[1]
    start = (at.group * members + me) * count
    gains_sum[...] = pltpu.roll(total, width - start, 1)[0:2, 0:count]
    for move in widen_moves:
        move.wait_recv()
    for matrix in range(2):
        for member in range(0, members, 2):
            found = joined_lanes(widen_home[member, matrix], widen_home[member + 1, matrix])
            for index, part in enumerate(found):
                start = index * 64 * members + member * 64
                widen_sum[matrix, :, start : start + 128] = part
    tick(last)
    for move in attend_moves:
        move.wait_recv()
    links.finish()


def rotary_lines(length):
    half = HEAD_FEATURES // 2
    freqs = np.exp(-np.log(10000.0) * np.arange(half) / half)
    angles = np.arange(length)[:, None] * freqs[None, :]
    cosines, sines = np.cos(angles), np.sin(angles)
    return (
        np.concatenate([cosines] * 4, axis=1).astype(np.float32),
        np.concatenate([-sines, sines] * 2, axis=1).astype(np.float32),
    )


def spaces(*names):
    kinds = {"v": pltpu.VMEM, "s": pltpu.SMEM, "a": pl.ANY}
    return [pl.BlockSpec(memory_space=kinds[name]) for name in "".join(names)]


def local(
    tokens,
    seq_lengths,
    deal_order,
    expert_routes,
    capacity_slots,
    gate_weights,
    cotangent,
    projector,
    projector_mean,
    projector_square,
    collector,
    collector_first_moment,
    collector_second_moment,
    widener,
    widener_mean,
    widener_square,
    narrower,
    narrower_mean,
    narrower_square,
    norm_gains,
    gains_mean,
    gains_square,
    expander,
    expander_mean,
    expander_square,
    reducer,
    reducer_mean,
    reducer_square,
):
    groups, members = lax.axis_size("grp"), lax.axis_size("exp")
    length, width = tokens.shape[1:]
    inner = expander.shape[3]
    piece = widener.shape[2] // members
    chunks = 1 + inner // piece
    capacity = 3 * length // members
    steps = groups - 1
    high, low, share = expander.shape[2], narrower.shape[0], projector.shape[1]
    bf16, f32 = jnp.bfloat16, jnp.float32
    shape = jax.ShapeDtypeStruct
    cosines, sines = (jnp.asarray(lines) for lines in rotary_lines(length))
    ids = jnp.arange(members, dtype=jnp.int32)
    dealt = deal_order[:, None] == ids[None, :]
    table = jnp.stack(
        [
            deal_order,
            jnp.sum(jnp.where(dealt, ids[:, None], 0), axis=0),
            seq_lengths,
            jnp.sum(jnp.where(dealt, seq_lengths[None, :], 0), axis=1),
        ]
    )
    count = 16 * groups
    (
        wide_grads,
        down_grads,
        attend_full,
        grads_all,
        gains_full,
        saved,
        middle,
        soft,
        result_parts,
        back_parts,
        gate_parts,
    ) = pl.pallas_call(
        functools.partial(gather_kernel, groups, members),
        out_shape=[
            shape((chunks, 2, width, piece), bf16),
            shape((chunks, piece, width), bf16),
            shape((4, width, width), bf16),
            shape((members, length, width), bf16),
            shape((8, width), f32),
            shape((5, length, width), bf16),
            shape((length, width), f32),
            shape((HEAD_COUNT, length, length), f32),
            shape((members, length, width), bf16),
            shape((members, length, width), bf16),
            shape((members, 8, length), f32),
        ],
        in_specs=spaces("s", "v" * 14),
        out_specs=spaces("aa", "v" * 9),
        scratch_shapes=[
            VMEM((members, length, width), bf16),
            VMEM((members, 8, length), f32),
            VMEM((members, 8, length), f32),
            VMEM((4, share, width), f32),
            VMEM((4, share, width), f32),
            VMEM((members, 2, share, piece), f32),
            VMEM((members, 2, share, piece), f32),
            VMEM((8, width), f32),
            VMEM((members, 8, width), f32),
            VMEM((groups, 8, width), f32),
            VMEM((chunks, 2, width, piece), bf16),
            VMEM((chunks, piece, width), bf16),
            VMEM((chunks, 2, high, piece), bf16),
            VMEM((chunks, low, width), bf16),
            VMEM((members * length, width), bf16),
            VMEM((width, members * length), bf16),
            VMEM((members, length, width), f32),
            VMEM((members, length, width), f32),
            VMEM((members * capacity, width), bf16),
            VMEM((width, members * capacity), bf16),
            VMEM((members * capacity, width), bf16),
            VMEM((members * capacity, width), f32),
            VMEM((members * capacity, width), f32),
            pltpu.SemaphoreType.DMA((count,)),
            pltpu.SemaphoreType.DMA((count,)),
            pltpu.SemaphoreType.DMA((chunks * steps * 4,)),
            pltpu.SemaphoreType.DMA((chunks * steps * 4,)),
            pltpu.SemaphoreType.DMA((2 * chunks,)),
        ],
        compiler_params=pltpu.CompilerParams(
            collective_id=0, has_side_effects=True, vmem_limit_bytes=LIMIT
        ),
    )(
        table,
        tokens[0],
        cotangent[0],
        expert_routes[0],
        capacity_slots[0],
        gate_weights[0],
        norm_gains,
        projector,
        collector,
        widener,
        narrower,
        expander[0],
        reducer[0],
        cosines,
        sines,
    )
    count = 32 * groups
    (
        output,
        input_grad,
        gate_grad,
        expand_sum,
        reduce_sum,
        widen_sum,
        narrow_sum,
        attend_sum,
        gains_sum,
    ) = pl.pallas_call(
        functools.partial(scatter_kernel, groups, members),
        out_shape=[
            shape((length, width), f32),
            shape((length, width), f32),
            shape((length, 2), f32),
            shape((2, high, inner), f32),
            shape(reducer.shape[1:], f32),
            shape(widener.shape, f32),
            shape(narrower.shape, f32),
            shape((4, share, width), f32),
            shape(norm_gains.shape, f32),
        ],
        in_specs=spaces("s", "v" * 13, "aa"),
        out_specs=spaces("v" * 9),
        scratch_shapes=[
            VMEM((members, 8, length), f32),
            VMEM((members, length, width), bf16),
            VMEM((members, length, width), bf16),
            VMEM((chunks, 2, width, piece), bf16),
            VMEM((chunks, piece, width), bf16),
            VMEM((chunks, 2, steps, high, piece), bf16),
            VMEM((chunks, 2, steps, low // 2, width), bf16),
            VMEM((chunks - 1, 2, high, piece), f32),
            VMEM((4, length, width), bf16),
            VMEM((4, width, width), bf16),
            VMEM((2, width, width), bf16),
            VMEM((width, width), bf16),
            VMEM((width, width), bf16),
            VMEM((width, width), bf16),
            VMEM((2, steps, high // 2, width), bf16),
            VMEM((4, share, width), f32),
            VMEM((members, 2, share, piece), f32),
            VMEM((members, 2, share, piece), f32),
            VMEM((8, width), f32),
            VMEM((members, 8, width), f32),
            VMEM((groups, 8, width), f32),
            pltpu.SemaphoreType.DMA((count,)),
            pltpu.SemaphoreType.DMA((count,)),
            pltpu.SemaphoreType.DMA((2,)),
        ],
        compiler_params=pltpu.CompilerParams(
            collective_id=1, has_side_effects=True, vmem_limit_bytes=LIMIT
        ),
    )(
        table,
        tokens[0],
        expert_routes[0],
        grads_all,
        gains_full,
        attend_full,
        saved,
        middle,
        soft,
        cosines,
        sines,
        result_parts,
        back_parts,
        gate_parts,
        wide_grads,
        down_grads,
    )
    project_new = adamw_update(
        projector, projector_mean, projector_square, attend_sum[0:3], 0.1
    )
    collect_new = adamw_update(
        collector, collector_first_moment, collector_second_moment, attend_sum[3], 0.3
    )
    widen_new = adamw_update(widener, widener_mean, widener_square, widen_sum, 0.07)
    narrow_new = adamw_update(narrower, narrower_mean, narrower_square, narrow_sum, 0.045)
    gains_new = adamw_update(norm_gains, gains_mean, gains_square, gains_sum, 0.2)
    expand_new = adamw_update(
        expander, expander_mean, expander_square, expand_sum[None], 0.07
    )
    reduce_new = adamw_update(reducer, reducer_mean, reducer_square, reduce_sum[None], 0.045)
    return (
        output[None],
        input_grad[None],
        gate_grad[None],
        *project_new,
        *collect_new,
        *widen_new,
        *narrow_new,
        *gains_new,
        *expand_new,
        *reduce_new,
    )


def fits(mesh):
    groups, members = mesh.shape["grp"], mesh.shape["exp"]
    share = 64 * HEAD_COUNT // (groups * members)
    return members == 4 and groups % 2 == 0 and share % 8 == 0 and share * members // 2 % 16 == 0


def solution(mesh):
    placed = (
        P(("grp", "exp"), None, None),
        P("grp"),
        P("grp"),
        P(("grp", "exp"), None, None),
        P(("grp", "exp"), None, None),
        P(("grp", "exp"), None, None),
        P(("grp", "exp"), None, None),
        P(None, ("grp", "exp"), None),
        P(None, ("grp", "exp"), None),
        P(None, ("grp", "exp"), None),
        P(("grp", "exp"), None),
        P(("grp", "exp"), None),
        P(("grp", "exp"), None),
        P(None, ("grp", "exp"), None),
        P(None, ("grp", "exp"), None),
        P(None, ("grp", "exp"), None),
        P(("grp", "exp"), None),
        P(("grp", "exp"), None),
        P(("grp", "exp"), None),
        P(None, ("grp", "exp")),
        P(None, ("grp", "exp")),
        P(None, ("grp", "exp")),
        P("exp", None, "grp", None),
        P("exp", None, "grp", None),
        P("exp", None, "grp", None),
        P("exp", "grp", None),
        P("exp", "grp", None),
        P("exp", "grp", None),
    )
    return jax.shard_map(
        local if fits(mesh) else local_plain,
        mesh=mesh,
        in_specs=placed,
        out_specs=(
            P(("grp", "exp"), None, None),
            P(("grp", "exp"), None, None),
            P(("grp", "exp"), None, None),
            P(None, ("grp", "exp"), None),
            P(None, ("grp", "exp"), None),
            P(None, ("grp", "exp"), None),
            P(("grp", "exp"), None),
            P(("grp", "exp"), None),
            P(("grp", "exp"), None),
            P(None, ("grp", "exp"), None),
            P(None, ("grp", "exp"), None),
            P(None, ("grp", "exp"), None),
            P(("grp", "exp"), None),
            P(("grp", "exp"), None),
            P(("grp", "exp"), None),
            P(None, ("grp", "exp")),
            P(None, ("grp", "exp")),
            P(None, ("grp", "exp")),
            P("exp", None, "grp", None),
            P("exp", None, "grp", None),
            P("exp", None, "grp", None),
            P("exp", "grp", None),
            P("exp", "grp", None),
            P("exp", "grp", None),
        ),
        check_vma=False,
    )
```

```python
import functools

import jax
import jax.numpy as jnp
import numpy as np
from jax import lax
from jax.experimental import pallas as pl
from jax.experimental.pallas import tpu as pltpu
from jax.sharding import PartitionSpec as P

HEAD_COUNT = 12
HEAD_FEATURES = 64
STEP = 5


def rms_factor(values):
    return lax.rsqrt(jnp.mean(values * values, axis=-1, keepdims=True) + 1e-06)


def rms_back(values, factor, upstream):
    return factor * (
        upstream - values * factor * factor * jnp.mean(upstream * values, axis=-1, keepdims=True)
    )


def rotary(length):
    positions = jnp.arange(length, dtype=jnp.int32).astype(jnp.float32)
    half = HEAD_FEATURES // 2
    freqs = jnp.exp(
        -jnp.log(10000.0) * jnp.arange(half, dtype=jnp.int32).astype(jnp.float32) / half
    )
    angles = positions[:, None] * freqs[None, :]
    return (jnp.cos(angles)[:, None, :], jnp.sin(angles)[:, None, :])


def rotate(values, cosines, sines):
    half = values.shape[-1] // 2
    first = values[..., :half]
    second = values[..., half:]
    return jnp.concatenate(
        [first * cosines - second * sines, second * cosines + first * sines], axis=-1
    )


def rotate_back(values, cosines, sines):
    half = values.shape[-1] // 2
    first = values[..., :half]
    second = values[..., half:]
    return jnp.concatenate(
        [first * cosines + second * sines, second * cosines - first * sines], axis=-1
    )


def silu_slope(values):
    sigmoid_of = jax.nn.sigmoid(values)
    return sigmoid_of * (1.0 + values * (1.0 - sigmoid_of))


def matmul(left, right):
    return jnp.dot(left, right, preferred_element_type=jnp.float32)


def outer_sum(left, right):
    return jnp.einsum("ld,lf->df", left, right, preferred_element_type=jnp.float32)


def adamw_update(weight, moment, variance, gradient, rate):
    moment_new = 0.5 * moment + 0.5 * gradient
    variance_new = 0.5 * variance + 0.5 * gradient * gradient
    correct = 1.0 - 0.5**STEP
    stepped = moment_new / correct / (jnp.sqrt(variance_new / correct) + 1e-08) + 0.1 * weight
    return (moment_new, variance_new, weight - rate * stepped)


def local_plain(
    tokens,
    seq_lengths,
    deal_order,
    expert_routes,
    capacity_slots,
    gate_weights,
    cotangent,
    projector,
    projector_mean,
    projector_square,
    collector,
    collector_first_moment,
    collector_second_moment,
    widener,
    widener_mean,
    widener_square,
    narrower,
    narrower_mean,
    narrower_square,
    norm_gains,
    gains_mean,
    gains_square,
    expander,
    expander_mean,
    expander_square,
    reducer,
    reducer_mean,
    reducer_square,
):
    members = lax.axis_size("exp")
    member = lax.axis_index("exp")
    length_seq = tokens.shape[1]
    width = tokens.shape[2]
    local_experts = expander.shape[0]
    experts_all = local_experts * members
    capacity = 3 * length_seq // experts_all
    member_ids = jnp.arange(members, dtype=jnp.int32)
    source = deal_order[member]
    home_slot = jnp.sum(jnp.where(deal_order == member, member_ids, 0))
    seq_length = seq_lengths[source]
    piece = lax.all_gather(tokens, "exp", axis=0, tiled=True)
    chosen = jnp.arange(piece.shape[0], dtype=jnp.int32) == source
    dealt = jnp.sum(
        jnp.where(chosen[:, None, None], piece, jnp.zeros_like(piece)), axis=0, keepdims=True
    )
    residual_flow = dealt[0].astype(jnp.float32)
    project_full, collect_full, widen_full, narrow_full, gains_full = (
        lax.all_gather(projector.astype(jnp.bfloat16), ("grp", "exp"), axis=1, tiled=True),
        lax.all_gather(collector.astype(jnp.bfloat16), ("grp", "exp"), axis=0, tiled=True),
        lax.all_gather(widener.astype(jnp.bfloat16), ("grp", "exp"), axis=1, tiled=True),
        lax.all_gather(narrower.astype(jnp.bfloat16), ("grp", "exp"), axis=0, tiled=True),
        lax.all_gather(norm_gains.astype(jnp.bfloat16), ("grp", "exp"), axis=1, tiled=True),
    )
    expand_full, reduce_full = (
        lax.all_gather(expander.astype(jnp.bfloat16), "grp", axis=2, tiled=True),
        lax.all_gather(reducer.astype(jnp.bfloat16), "grp", axis=1, tiled=True),
    )
    gains_used = gains_full.astype(jnp.float32)
    cosines, sines = rotary(length_seq)
    scale_one = rms_factor(residual_flow)
    normed_one = residual_flow * scale_one
    first_input = (normed_one * gains_used[0]).astype(jnp.bfloat16)
    query_raw = matmul(first_input, project_full[0]).reshape(length_seq, HEAD_COUNT, HEAD_FEATURES)
    key_raw = matmul(first_input, project_full[1]).reshape(length_seq, HEAD_COUNT, HEAD_FEATURES)
    value_raw = matmul(first_input, project_full[2]).reshape(length_seq, HEAD_COUNT, HEAD_FEATURES)
    query_rot = rotate(query_raw, cosines, sines).astype(jnp.bfloat16)
    key_rot = rotate(key_raw, cosines, sines).astype(jnp.bfloat16)
    value_low = value_raw.astype(jnp.bfloat16)
    rows_at = jnp.arange(length_seq, dtype=jnp.int32)[:, None]
    cols_at = jnp.arange(length_seq, dtype=jnp.int32)[None, :]
    allowed = ((cols_at <= rows_at) & (cols_at < seq_length))[None]
    scores = (
        jnp.einsum("qhd,khd->hqk", query_rot, key_rot, preferred_element_type=jnp.float32) * 0.125
    )
    masked = jnp.where(allowed, scores, -1e30)
    top = jnp.max(masked, axis=-1, keepdims=True)
    expo = jnp.exp(masked - top)
    total = jnp.sum(expo, axis=-1, keepdims=True)
    soft = expo / total
    logsum = top + jnp.log(total)
    mixed_output = (
        jnp.einsum(
            "hqk,khd->qhd", soft.astype(jnp.bfloat16), value_low, preferred_element_type=jnp.float32
        )
        .reshape(length_seq, width)
        .astype(jnp.bfloat16)
    )
    middle_state = residual_flow + matmul(mixed_output, collect_full)
    scale_two = rms_factor(middle_state)
    normed_two = middle_state * scale_two
    second_input = (normed_two * gains_used[1]).astype(jnp.bfloat16)
    gating_scores = matmul(second_input, widen_full[0])
    upward_rows = matmul(second_input, widen_full[1])
    hidden_state = (jax.nn.silu(gating_scores) * upward_rows).astype(jnp.bfloat16)
    dense_branch = matmul(hidden_state, narrow_full)
    flat = (expert_routes[0] * capacity + capacity_slots[0]).reshape(-1)
    spread = jnp.repeat(second_input, 2, axis=0)
    dispatch = jnp.zeros((experts_all * capacity, width), jnp.bfloat16).at[flat].set(spread)
    dispatch = dispatch.reshape(experts_all, capacity, width)
    rows = lax.all_to_all(dispatch, "exp", split_axis=0, concat_axis=0, tiled=True)
    count = rows.shape[1]
    grouped = rows.reshape(members, local_experts, count, width)
    gate_pre = jnp.einsum(
        "sekd,edf->sekf", grouped, expand_full[:, 0], preferred_element_type=jnp.float32
    )
    up_pre = jnp.einsum(
        "sekd,edf->sekf", grouped, expand_full[:, 1], preferred_element_type=jnp.float32
    )
    hidden_rows = (jax.nn.silu(gate_pre) * up_pre).astype(jnp.bfloat16)
    result = jnp.einsum(
        "sekf,efd->sekd", hidden_rows, reduce_full, preferred_element_type=jnp.float32
    )
    result = result.astype(jnp.bfloat16).reshape(members * local_experts, count, width)
    returned_rows = lax.all_to_all(result, "exp", split_axis=0, concat_axis=0, tiled=True)
    outcome = (
        returned_rows,
        rows,
        gate_pre.reshape(members * local_experts, count, -1),
        up_pre.reshape(members * local_experts, count, -1),
    )
    returned, received, gate_kept, up_kept = outcome
    picked = (
        returned.reshape(experts_all * capacity, width)[flat]
        .reshape(length_seq, 2, width)
        .astype(jnp.float32)
    )
    gate_local = gate_weights[0]
    mixture = jnp.sum(gate_local[..., None] * picked, axis=1)
    layer_output = middle_state + dense_branch + mixture
    valid = (jnp.arange(length_seq, dtype=jnp.int32) < seq_length).astype(jnp.float32)
    grad_out = cotangent[0] * valid[:, None]
    grad_low = grad_out.astype(jnp.bfloat16)
    narrow_grad = outer_sum(hidden_state, grad_low)
    hidden_grad = jnp.einsum("ld,fd->lf", grad_low, narrow_full, preferred_element_type=jnp.float32)
    gating_grad = (hidden_grad * upward_rows * silu_slope(gating_scores)).astype(jnp.bfloat16)
    upward_grad = (hidden_grad * jax.nn.silu(gating_scores)).astype(jnp.bfloat16)
    widen_grad = jnp.stack(
        [outer_sum(second_input, gating_grad), outer_sum(second_input, upward_grad)]
    )
    second_grad = jnp.einsum(
        "lf,df->ld", gating_grad, widen_full[0], preferred_element_type=jnp.float32
    ) + jnp.einsum("lf,df->ld", upward_grad, widen_full[1], preferred_element_type=jnp.float32)
    gate_grad_local = jnp.sum(grad_out[:, None, :] * picked, axis=-1)
    result_grad = (
        (gate_local[..., None] * grad_out[:, None, :])
        .astype(jnp.bfloat16)
        .reshape(2 * length_seq, width)
    )
    grad_send = jnp.zeros((experts_all * capacity, width), jnp.bfloat16).at[flat].set(result_grad)
    grad_recv = lax.all_to_all(
        grad_send.reshape(experts_all, capacity, width),
        "exp",
        split_axis=0,
        concat_axis=0,
        tiled=True,
    )
    grad_group = grad_recv.reshape(members, local_experts, capacity, width)
    rows_group = received.reshape(members, local_experts, capacity, width)
    gate_pre = gate_kept.reshape(members, local_experts, capacity, -1)
    up_pre = up_kept.reshape(members, local_experts, capacity, -1)
    hidden_rows = (jax.nn.silu(gate_pre) * up_pre).astype(jnp.bfloat16)
    reduce_grad = jnp.einsum(
        "sekf,sekd->efd", hidden_rows, grad_group, preferred_element_type=jnp.float32
    )
    hidden_rows_grad = jnp.einsum(
        "sekd,efd->sekf", grad_group, reduce_full, preferred_element_type=jnp.float32
    )
    gate_rows_grad = (hidden_rows_grad * up_pre * silu_slope(gate_pre)).astype(jnp.bfloat16)
    up_rows_grad = (hidden_rows_grad * jax.nn.silu(gate_pre)).astype(jnp.bfloat16)
    expand_grad = jnp.stack(
        [
            jnp.einsum(
                "sekd,sekf->edf", rows_group, gate_rows_grad, preferred_element_type=jnp.float32
            ),
            jnp.einsum(
                "sekd,sekf->edf", rows_group, up_rows_grad, preferred_element_type=jnp.float32
            ),
        ],
        axis=1,
    )
    row_grads = jnp.einsum(
        "sekf,edf->sekd", gate_rows_grad, expand_full[:, 0], preferred_element_type=jnp.float32
    ) + jnp.einsum(
        "sekf,edf->sekd", up_rows_grad, expand_full[:, 1], preferred_element_type=jnp.float32
    )
    row_grads = row_grads.astype(jnp.bfloat16).reshape(experts_all, capacity, width)
    came_back = lax.all_to_all(row_grads, "exp", split_axis=0, concat_axis=0, tiled=True).reshape(
        experts_all * capacity, width
    )
    second_grad = second_grad + jnp.sum(
        came_back[flat].reshape(length_seq, 2, width).astype(jnp.float32), axis=1
    )
    gains_grad_two = jnp.sum(second_grad * normed_two, axis=0)
    middle_grad = grad_out + rms_back(middle_state, scale_two, second_grad * gains_used[1])
    middle_low = middle_grad.astype(jnp.bfloat16)
    collect_grad = outer_sum(mixed_output, middle_low)
    mixed_grad = jnp.einsum(
        "ld,ed->le", middle_low, collect_full, preferred_element_type=jnp.float32
    )
    mixed_grad = mixed_grad.astype(jnp.bfloat16).reshape(length_seq, HEAD_COUNT, HEAD_FEATURES)
    scores_again = (
        jnp.einsum("qhd,khd->hqk", query_rot, key_rot, preferred_element_type=jnp.float32) * 0.125
    )
    soft_again = jnp.where(allowed, jnp.exp(scores_again - logsum), 0.0)
    value_grad = jnp.einsum(
        "hqk,qhd->khd",
        soft_again.astype(jnp.bfloat16),
        mixed_grad,
        preferred_element_type=jnp.float32,
    )
    soft_grad = jnp.einsum(
        "qhd,khd->hqk", mixed_grad, value_low, preferred_element_type=jnp.float32
    )
    score_grad = (
        soft_again * (soft_grad - jnp.sum(soft_again * soft_grad, axis=-1, keepdims=True))
    ).astype(jnp.bfloat16)
    query_grad = (
        jnp.einsum("hqk,khd->qhd", score_grad, key_rot, preferred_element_type=jnp.float32) * 0.125
    )
    key_grad = (
        jnp.einsum("hqk,qhd->khd", score_grad, query_rot, preferred_element_type=jnp.float32)
        * 0.125
    )
    query_back = (
        rotate_back(query_grad, cosines, sines).reshape(length_seq, width).astype(jnp.bfloat16)
    )
    key_back = rotate_back(key_grad, cosines, sines).reshape(length_seq, width).astype(jnp.bfloat16)
    value_back = value_grad.reshape(length_seq, width).astype(jnp.bfloat16)
    project_grad = jnp.stack(
        [
            outer_sum(first_input, query_back),
            outer_sum(first_input, key_back),
            outer_sum(first_input, value_back),
        ]
    )
    first_grad = (
        jnp.einsum("le,de->ld", query_back, project_full[0], preferred_element_type=jnp.float32)
        + jnp.einsum("le,de->ld", key_back, project_full[1], preferred_element_type=jnp.float32)
        + jnp.einsum("le,de->ld", value_back, project_full[2], preferred_element_type=jnp.float32)
    )
    gains_grad_one = jnp.sum(first_grad * normed_one, axis=0)
    stream_grad = middle_grad + rms_back(residual_flow, scale_one, first_grad * gains_used[0])
    gains_grad = jnp.stack([gains_grad_one, gains_grad_two])
    project_part, collect_part, widen_part, narrow_part, gains_part = (
        lax.psum_scatter(project_grad, ("grp", "exp"), scatter_dimension=1, tiled=True),
        lax.psum_scatter(collect_grad, ("grp", "exp"), scatter_dimension=0, tiled=True),
        lax.psum_scatter(widen_grad, ("grp", "exp"), scatter_dimension=1, tiled=True),
        lax.psum_scatter(narrow_grad, ("grp", "exp"), scatter_dimension=0, tiled=True),
        lax.psum_scatter(gains_grad, ("grp", "exp"), scatter_dimension=1, tiled=True),
    )
    expand_part, reduce_part = (
        lax.psum_scatter(
            expand_grad.astype(jnp.bfloat16), "grp", scatter_dimension=2, tiled=True
        ).astype(jnp.float32),
        lax.psum_scatter(
            reduce_grad.astype(jnp.bfloat16), "grp", scatter_dimension=1, tiled=True
        ).astype(jnp.float32),
    )
    empty = jnp.zeros((1, length_seq, width), jnp.float32)
    pieces = (
        lax.all_gather(layer_output[None].astype(jnp.bfloat16), "exp", axis=0, tiled=True).astype(
            jnp.float32
        ),
        lax.all_gather(stream_grad[None].astype(jnp.bfloat16), "exp", axis=0, tiled=True).astype(
            jnp.float32
        ),
    )
    chosen = (jnp.arange(pieces[0].shape[0], dtype=jnp.int32) == home_slot)[:, None, None]
    homed_output = empty + jnp.sum(jnp.where(chosen, pieces[0], 0.0), axis=0, keepdims=True)
    homed_grad = empty + jnp.sum(jnp.where(chosen, pieces[1], 0.0), axis=0, keepdims=True)
    project_new = adamw_update(projector, projector_mean, projector_square, project_part, 0.1)
    collect_new = adamw_update(
        collector, collector_first_moment, collector_second_moment, collect_part, 0.3
    )
    widening_updated = adamw_update(widener, widener_mean, widener_square, widen_part, 0.07)
    narrowing_updated = adamw_update(narrower, narrower_mean, narrower_square, narrow_part, 0.045)
    gains_updated = adamw_update(norm_gains, gains_mean, gains_square, gains_part, 0.2)
    expansion_updated = adamw_update(expander, expander_mean, expander_square, expand_part, 0.07)
    reduction_updated = adamw_update(reducer, reducer_mean, reducer_square, reduce_part, 0.045)
    return (
        homed_output,
        homed_grad,
        gate_grad_local[None],
        project_new[0],
        project_new[1],
        project_new[2],
        collect_new[0],
        collect_new[1],
        collect_new[2],
        widening_updated[0],
        widening_updated[1],
        widening_updated[2],
        narrowing_updated[0],
        narrowing_updated[1],
        narrowing_updated[2],
        gains_updated[0],
        gains_updated[1],
        gains_updated[2],
        expansion_updated[0],
        expansion_updated[1],
        expansion_updated[2],
        reduction_updated[0],
        reduction_updated[1],
        reduction_updated[2],
    )


MESH = pl.DeviceIdType.MESH
VMEM = pltpu.VMEM
LIMIT = 60 * 1024 * 1024


def ring_place(index, groups):
    row, side = lax.div(index, 2), lax.rem(index, 2)
    return (1 - side) * row + side * (groups - 1 - row)


def ring_member(place, groups):
    side = lax.div(place, groups // 2)
    return 2 * ((1 - side) * place + side * (groups - 1 - place)) + side


def remote(source, target, sends, arrivals, at, device):
    return pltpu.make_async_remote_copy(
        src_ref=source,
        dst_ref=target,
        send_sem=sends.at[at],
        recv_sem=arrivals.at[at],
        device_id=device,
        device_id_type=MESH,
    )


class Links:
    def __init__(self, sends, arrivals):
        self.sends, self.arrivals, self.count, self.started = sends, arrivals, 0, []

    def copy(self, source, target, device):
        made = remote(source, target, self.sends, self.arrivals, self.count, device)
        self.count += 1
        made.start()
        self.started.append(made)
        return made

    def finish(self):
        for made in self.started:
            made.wait_send()


class Places:
    def __init__(self, groups, members):
        self.groups, self.members = groups, members
        self.group = lax.axis_index("grp")
        self.member = lax.axis_index("exp")
        self.place = ring_place(self.group, groups)
        self.next = {"grp": self.owner(1)}
        self.back = {"grp": self.owner(-1)}
        half = members // 2
        self.far = lax.rem(self.member + half, members)
        self.near = self.member + 1 - 2 * lax.rem(self.member, 2)
        self.cross = lax.rem(self.near + half, members)
        self.peers = [lax.rem(self.member + step, members) for step in range(1, members)]

    def owner(self, offset):
        place = lax.rem(self.place + offset + 2 * self.groups, self.groups)
        return ring_member(place, self.groups)

    def enter(self):
        barrier = pltpu.get_barrier_semaphore()
        partners = [self.next, self.back] + [{"exp": peer} for peer in self.peers]
        for partner in partners:
            pl.semaphore_signal(barrier, inc=1, device_id=partner, device_id_type=MESH)
        pl.semaphore_wait(barrier, len(partners))


def rows(start, count, align=16):
    return pl.ds(pl.multiple_of(start, align), count)


def first_half(shape):
    return lax.rem(lax.broadcasted_iota(jnp.int32, shape, len(shape) - 1), 128) < 64


def turned(values):
    lanes = lax.broadcasted_iota(jnp.int32, values.shape, 1)
    return jnp.where(
        lax.rem(lanes, HEAD_FEATURES) < HEAD_FEATURES // 2,
        pltpu.roll(values, 128 - HEAD_FEATURES // 2, 1),
        pltpu.roll(values, HEAD_FEATURES // 2, 1),
    )


def nt(left, right):
    return lax.dot_general(
        left, right, (((1,), (1,)), ((), ())), preferred_element_type=jnp.float32
    )


def tn(left, right):
    return lax.dot_general(
        left, right, (((0,), (0,)), ((), ())), preferred_element_type=jnp.float32
    )


def sigmoid(values):
    return 1.0 / (1.0 + jnp.exp(-values))


def same(length):
    shape = (length, length)
    return lax.broadcasted_iota(jnp.int32, shape, 0) == lax.broadcasted_iota(jnp.int32, shape, 1)


def upright(line):
    return jnp.sum(jnp.where(same(line.shape[1]), line, 0.0), axis=1, keepdims=True)


def lying(column):
    return jnp.sum(jnp.where(same(column.shape[0]), column, 0.0), axis=0, keepdims=True)


def slot_of(deal_ref, member):
    for _ in range(11):
        member = deal_ref[member]
    return member


def dealt_lanes(values, piece, pieces):
    low_lanes = lax.broadcasted_iota(jnp.int32, (values.shape[0], 128), 1) < 64
    found = []
    span = 64 * pieces
    for start in range(0, values.shape[1], 2 * span):
        start = start + piece // 2 * 128
        one, two = values[:, start : start + 128], values[:, start + span : start + span + 128]
        if piece % 2:
            one = pltpu.roll(one, 64, 1)
        else:
            two = pltpu.roll(two, 64, 1)
        found.append(jnp.where(low_lanes, one, two))
    return jnp.concatenate(found, axis=1)


def joined_lanes(even, odd):
    low_lanes = lax.broadcasted_iota(jnp.int32, (even.shape[0], 128), 1) < 64
    found = []
    for start in range(0, even.shape[1], 128):
        one, two = even[:, start : start + 128], odd[:, start : start + 128]
        found.append(jnp.where(low_lanes, one, pltpu.roll(two, 64, 1)))
        found.append(jnp.where(low_lanes, pltpu.roll(one, 64, 1), two))
    return found


def gather_kernel(
    groups,
    members,
    length_ref,
    deal_ref,
    tokens,
    cotangent,
    routes,
    places,
    gates,
    norm_gains,
    projector,
    collector,
    widener,
    narrower,
    expander,
    reducer,
    cos_ref,
    sin_ref,
    wide_grads,
    down_grads,
    attend_full,
    grads_all,
    gains_full,
    saved,
    middle_ref,
    soft_ref,
    result_ref,
    back_ref,
    gate_ref,
    second_all,
    meta_send,
    meta_all,
    attend_send,
    attend_recv,
    widen_send,
    widen_recv,
    gains,
    gain_recv,
    gain_ring,
    wide_full,
    down_full,
    wide_own,
    down_own,
    inputs_ref,
    inputs_turned,
    dense_out,
    dense_back,
    rows_in,
    rows_turned,
    rows_grad,
    rows_out,
    rows_back,
    sends,
    arrivals,
    ring_sends,
    ring_arrivals,
    local_sems,
):
    at = Places(groups, members)
    links = Links(sends, arrivals)
    at.enter()
    me, steps = at.member, groups - 1
    share, width = projector.shape[1:]
    block = share * members
    length = tokens.shape[0]
    chunks, low = down_own.shape[:2]
    capacity = rows_in.shape[0] // members

    attend_send[0:3] = projector[...]
    attend_send[3] = collector[...]
    gains[...] = jnp.zeros_like(gains)
    gains[0:2, 0 : norm_gains.shape[1]] = norm_gains[...]
    gains[...] = pltpu.roll(gains[...], (at.group * members + me) * norm_gains.shape[1], 1)
    first_moves = [
        [
            links.copy(attend_send.at[peer], attend_recv.at[me], {"exp": peer}),
            links.copy(gains, gain_recv.at[me], {"exp": peer}),
        ]
        for peer in at.peers
    ]
    gain_recv[me] = gains[...]
    attend_recv[me] = attend_send[me]
    for matrix in range(2):
        for member in range(members):
            widen_send[member, matrix] = dealt_lanes(widener[matrix], member, members)
    widen_moves = [
        links.copy(widen_send.at[peer], widen_recv.at[me], {"exp": peer}) for peer in at.peers
    ]
    widen_recv[me] = widen_send[me]
    down_own[0] = narrower[...].astype(jnp.bfloat16)
    for moves in first_moves:
        for move in moves:
            move.wait_recv()
    attend_full[me, rows(at.group * block, block), :] = (
        attend_recv[...].reshape(block, width).astype(jnp.bfloat16)
    )
    total_gain = gain_recv[0]
    for member in range(1, members):
        total_gain = total_gain + gain_recv[member]
    gain_ring[at.group] = total_gain

    half = block // 2

    def unit(owner, side, matrix):
        return attend_full.at[matrix, rows(owner * block + side * half, half), :]

    def across(owner, side):
        spot = unit(owner, side, me)
        return (links.copy(spot, spot, {"exp": at.far}), links.copy(spot, spot, {"exp": at.near}))

    def onward(owner, side):
        spot = unit(owner, side, at.far)
        return links.copy(spot, spot, {"exp": at.near})

    def ring_copy(chunk, step, side, piece):
        owner = at.owner(-step if side == 0 else step)
        if piece == 0:
            spot = wide_full.at[chunk, side, rows(owner * block, block), :]
            origin = wide_own.at[chunk, side]
        else:
            spot = down_full.at[chunk, rows(owner * low + side * (low // 2), low // 2), :]
            origin = down_own.at[chunk, pl.ds(side * (low // 2), low // 2), :]
        place = (chunk * steps + step) * 4 + side * 2 + piece
        return remote(
            spot if step else origin,
            spot,
            ring_sends,
            ring_arrivals,
            place,
            (at.next, at.back)[side],
        )

    def ring_step(chunk, step):
        for piece in range(2):
            for side in range(2):
                if step:
                    ring_copy(chunk, step - 1, side, piece).wait_recv()
                if step < steps:
                    ring_copy(chunk, step, side, piece).start()

    def tick(count):
        for chunk in range(chunks):
            if 0 <= count - 2 * chunk <= steps:
                ring_step(chunk, count - 2 * chunk)

    ring, crossed, passed = [], [], []
    gain_moves = []
    for step in range(groups):
        owners = (at.owner(-step), at.owner(step))
        if step:
            for move in ring[-1]:
                move.wait_recv()
            gain_moves[-1].wait_recv()
        if step < steps:
            ring.append(
                [
                    links.copy(unit(owner, side, me), unit(owner, side, me), target)
                    for side, (owner, target) in enumerate(zip(owners, (at.next, at.back)))
                ]
            )
            gain_moves.append(
                links.copy(gain_ring.at[owners[0]], gain_ring.at[owners[0]], at.next)
            )
        crossed.append([across(owner, side) for side, owner in enumerate(owners)])
        if step:
            for side, owner in enumerate((at.owner(1 - step), at.owner(step - 1))):
                crossed[step - 1][side][0].wait_recv()
                passed.append(onward(owner, side))
        if step == 0:
            for chunk in range(1, chunks):
                for matrix in range(2):
                    wide_own[chunk, matrix] = dealt_lanes(
                        expander[matrix], chunk - 1, chunks - 1
                    ).astype(jnp.bfloat16)
                down_own[chunk] = reducer[(chunk - 1) * low : chunk * low, :].astype(jnp.bfloat16)
        if step == 2:
            for move in widen_moves:
                move.wait_recv()
            for matrix in range(2):
                wide_own[0, matrix] = jnp.concatenate(
                    [widen_recv[member, matrix] for member in range(members)], axis=0
                ).astype(jnp.bfloat16)
            for chunk in range(chunks):
                for side in range(2):
                    wide_full[chunk, side, rows(at.group * block, block), :] = wide_own[
                        chunk, side
                    ]
                down_full[chunk, rows(at.group * low, low), :] = down_own[chunk]
        if step == 3:
            tick(0)
        if step == 6:
            tick(1)
    tick(2)
    valid = lax.broadcasted_iota(jnp.int32, (length, 1), 0) < length_ref[deal_ref[me]]
    grads_all[me] = jnp.where(valid, cotangent[...], 0.0).astype(jnp.bfloat16)
    route = [routes[choice : choice + 1, :] for choice in range(2)]
    place = [places[choice : choice + 1, :].astype(jnp.float32) for choice in range(2)]
    meta_send[...] = jnp.zeros_like(meta_send)
    for member in range(members):
        named = [chosen == member for chosen in route]
        meta_send[member, 0:1, :] = jnp.where(
            named[0], place[0], jnp.where(named[1], place[1], -1.0)
        )
        meta_send[member, 1:2, :] = jnp.where(
            named[0], gates[0:1, :], jnp.where(named[1], gates[1:2, :], 0.0)
        )
    meta_all[me] = meta_send[me]
    grad_moves = [
        [
            links.copy(grads_all.at[me], grads_all.at[me], {"exp": peer}),
            links.copy(meta_send.at[peer], meta_all.at[me], {"exp": peer}),
        ]
        for peer in at.peers
    ]
    for side, owner in enumerate((at.owner(-steps), at.owner(steps))):
        crossed[steps][side][0].wait_recv()
        passed.append(onward(owner, side))
    total_gain = gain_ring[0]
    for group in range(1, groups):
        total_gain = total_gain + gain_ring[group]
    gains_full[...] = total_gain.astype(jnp.bfloat16).astype(jnp.float32)
    stream = tokens[...].astype(jnp.float32)
    first_input = (stream * rms_factor(stream) * gains_full[0:1, :]).astype(jnp.bfloat16)
    saved[4] = first_input
    for moves in crossed:
        for move in moves:
            move[1].wait_recv()
    for move in passed:
        move.wait_recv()
    tick(3)

    cosines, sines = cos_ref[...], sin_ref[...]
    for matrix in range(3):
        raw = matmul(first_input, attend_full[matrix])
        if matrix == 2:
            saved[2] = raw.astype(jnp.bfloat16)
        else:
            for start in range(0, width, 128):
                piece = raw[:, start : start + 128]
                saved[matrix, :, start : start + 128] = (
                    piece * cosines + turned(piece) * sines
                ).astype(jnp.bfloat16)
    tick(4)

    seq_length = length_ref[me]
    rows_at = lax.broadcasted_iota(jnp.int32, (length, length), 0)
    cols_at = lax.broadcasted_iota(jnp.int32, (length, length), 1)
    allowed = (cols_at <= rows_at) & (cols_at < seq_length)
    lower = first_half((length, 128))

    def heads(pair, carry):
        lanes = pl.ds(pl.multiple_of(pair * 128, 128), 128)
        query, key, value = saved[0, :, lanes], saved[1, :, lanes], saved[2, :, lanes]
        results = []
        for side in range(2):
            alone = jnp.where(lower == (side == 0), query, jnp.zeros_like(query))
            scores = jnp.where(allowed, nt(alone, key) * 0.125, -1e30)
            expo = jnp.exp(scores - jnp.max(scores, axis=-1, keepdims=True))
            soft = expo / jnp.sum(expo, axis=-1, keepdims=True)
            soft_ref[2 * pair + side] = soft
            results.append(matmul(soft.astype(jnp.bfloat16), value))
        saved[3, :, lanes] = jnp.where(lower, results[0], results[1]).astype(jnp.bfloat16)
        return carry

    lax.fori_loop(0, width // 128, heads, 0)
    tick(5)
    middle = tokens[...].astype(jnp.float32) + matmul(saved[3], attend_full[3])
    middle_ref[...] = middle
    second_all[me] = (middle * rms_factor(middle) * gains_full[1:2, :]).astype(jnp.bfloat16)
    second_moves = [
        links.copy(second_all.at[me], second_all.at[me], {"exp": peer}) for peer in at.peers
    ]
    for moves in grad_moves:
        for move in moves:
            move.wait_recv()
    tick(6)

    def hits(slot, by_row):
        line = meta_all[slot, 0:1, :]
        if by_row:
            names = lax.broadcasted_iota(jnp.int32, (capacity, length), 0).astype(jnp.float32)
            hit = names == line
        else:
            names = lax.broadcasted_iota(jnp.int32, (length, capacity), 1).astype(jnp.float32)
            hit = names == upright(line)
        return jnp.where(hit, 1.0, 0.0).astype(jnp.bfloat16)

    def spot_of(slot):
        return slice(slot * capacity, (slot + 1) * capacity)

    def here_of(slot):
        return slice(slot * length, (slot + 1) * length)

    for slot in range(members):
        pick = hits(slot, True)
        gate = jnp.sum(pick.astype(jnp.float32) * meta_all[slot, 1:2, :], axis=1, keepdims=True)
        rows_grad[spot_of(slot), :] = (matmul(pick, grads_all[slot]) * gate).astype(jnp.bfloat16)
    for move in second_moves:
        move.wait_recv()
    for slot in range(members):
        inputs_ref[here_of(slot), :] = second_all[deal_ref[slot]]
        rows_in[spot_of(slot), :] = matmul(hits(slot, True), inputs_ref[here_of(slot), :]).astype(
            jnp.bfloat16
        )
    inputs_turned[...] = inputs_ref[...].T
    rows_turned[...] = rows_in[...].T
    dense_out[...] = jnp.zeros_like(dense_out)
    dense_back[...] = jnp.zeros_like(dense_back)
    rows_out[...] = jnp.zeros_like(rows_out)
    rows_back[...] = jnp.zeros_like(rows_back)
    tick(7)

    def branch(chunk, inputs, turned_inputs, outer, out, back):
        for step in range(steps):
            for side in range(2):
                for piece in range(2):
                    ring_copy(chunk, step, side, piece).wait_send()

        def part(index, carry):
            lanes = pl.ds(pl.multiple_of(index * 256, 256), 256)
            gate = matmul(inputs[...], wide_full[chunk, 0, :, lanes])
            up = matmul(inputs[...], wide_full[chunk, 1, :, lanes])
            rise = sigmoid(gate)
            smooth = gate * rise
            hidden = (smooth * up).astype(jnp.bfloat16)
            hidden_grad = nt(outer[...], down_full[chunk, lanes, :])
            gate_grad = (hidden_grad * up * (rise * (1.0 + gate * (1.0 - rise)))).astype(
                jnp.bfloat16
            )
            up_grad = (hidden_grad * smooth).astype(jnp.bfloat16)
            out[...] += matmul(hidden, down_full[chunk, lanes, :])
            back[...] += nt(gate_grad, wide_full[chunk, 0, :, lanes]) + nt(
                up_grad, wide_full[chunk, 1, :, lanes]
            )
            down_full[chunk, lanes, :] = tn(hidden, outer[...]).astype(jnp.bfloat16)
            wide_full[chunk, 0, :, lanes] = matmul(turned_inputs[...], gate_grad).astype(
                jnp.bfloat16
            )
            wide_full[chunk, 1, :, lanes] = matmul(turned_inputs[...], up_grad).astype(
                jnp.bfloat16
            )
            return carry

        lax.fori_loop(0, down_full.shape[1] // 256, part, 0)
        kept(chunk, 0).start()
        kept(chunk, 1).start()

    def kept(chunk, piece):
        source, target = ((wide_full, wide_grads), (down_full, down_grads))[piece]
        return pltpu.make_async_copy(
            source.at[chunk], target.at[chunk], local_sems.at[2 * chunk + piece]
        )

    outer_all = grads_all.reshape(members * length, width)
    flat = (members * length, width)
    branch(
        0, inputs_ref, inputs_turned, outer_all, dense_out.reshape(flat), dense_back.reshape(flat)
    )

    def expert_chunk(chunk, carry):
        for last in (steps - 1, steps):
            for ahead in range(groups // 2):
                @pl.when(chunk + ahead < chunks)
                def _():
                    ring_step(chunk + ahead, last - 2 * ahead)

        branch(chunk, rows_in, rows_turned, rows_grad, rows_out, rows_back)
        return carry

    lax.fori_loop(1, chunks, expert_chunk, 0)

    for slot in range(members):
        pick = hits(slot, False)
        gate = upright(meta_all[slot, 1:2, :])
        picked = matmul(pick, rows_out[spot_of(slot), :].astype(jnp.bfloat16))
        inner = rows_back[spot_of(slot), :].astype(jnp.bfloat16)
        dense_out[slot] += gate * picked
        dense_back[slot] += matmul(pick, inner)
        score = jnp.sum(picked * grads_all[slot].astype(jnp.float32), axis=1, keepdims=True)
        gate_ref[slot] = jnp.broadcast_to(lying(score), gate_ref.shape[1:])
    for member in range(members):
        home = slot_of(deal_ref, member)
        result_ref[member] = dense_out[home].astype(jnp.bfloat16)
        back_ref[member] = dense_back[home].astype(jnp.bfloat16)
    for chunk in range(chunks):
        kept(chunk, 0).wait()
        kept(chunk, 1).wait()
    links.finish()


def scatter_kernel(
    groups,
    members,
    deal_ref,
    tokens,
    routes,
    grads_all,
    gains_full,
    attend_full,
    saved,
    middle_ref,
    soft_ref,
    cos_ref,
    sin_ref,
    result_parts,
    back_parts,
    gate_parts,
    wide_grads,
    down_grads,
    output_ref,
    input_grad_ref,
    gate_grad_ref,
    expand_sum,
    reduce_sum,
    widen_sum,
    narrow_sum,
    attend_sum,
    gains_sum,
    gate_recv,
    result_recv,
    back_recv,
    wide_own,
    down_own,
    wide_recv,
    down_recv,
    wide_sum,
    turned_ref,
    attend_grad,
    near_recv,
    far_recv,
    far_send,
    attend_total,
    attend_recv,
    attend_back,
    widen_back,
    widen_home,
    gain_own,
    gain_recv,
    gain_ring,
    sends,
    arrivals,
    local_sems,
):
    at = Places(groups, members)
    links = Links(sends, arrivals)
    at.enter()
    me, steps = at.member, groups - 1
    length, width = tokens.shape
    chunks, low = down_own.shape[0], narrow_sum.shape[0]
    share = attend_sum.shape[1]
    block = share * members

    kept = []
    for source, spot in ((wide_grads, wide_own), (down_grads, down_own)):
        made = pltpu.make_async_copy(source, spot, local_sems.at[len(kept)])
        made.start()
        kept.append(made)

    moves_of = {}
    widen_moves = []

    def ring_step(chunk, step):
        made = []
        owners = (at.owner(-1 - step), at.owner(1 + step))
        for piece in range(2):
            for side, target in enumerate((at.next, at.back)):
                own, first = ((wide_own, wide_grads), (down_own, down_grads))[piece]
                landing = (wide_recv, down_recv)[piece].at[chunk, side]
                if piece == 0:
                    spot = (chunk, side, rows(owners[side] * block, block))
                else:
                    spot = (chunk, rows(owners[side] * low + side * (low // 2), low // 2))
                if step == 0:
                    source = first.at[spot]
                else:
                    moves_of[chunk, step - 1][2 * piece + side].wait_recv()
                    source = landing.at[step - 1]
                    added = source[...].astype(jnp.float32) + own[spot].astype(jnp.float32)
                    if step < steps:
                        source[...] = added.astype(jnp.bfloat16)
                    elif piece == 0 and chunk:
                        wide_sum[chunk - 1, side] = added
                    elif piece == 0:
                        for member in range(members):
                            widen_back[member, side] = added[
                                member * share : (member + 1) * share, :
                            ]
                    else:
                        start = side * (low // 2)
                        if chunk:
                            start = start + (chunk - 1) * low
                            reduce_sum[start : start + low // 2, :] = added
                        else:
                            narrow_sum[start : start + low // 2, :] = added
                if step < steps:
                    made.append(links.copy(source, landing.at[step], target))
        moves_of[chunk, step] = made
        if step == steps and chunk == 0:
            widen_home[me] = widen_back[me]
            for peer in at.peers:
                widen_moves.append(
                    links.copy(widen_back.at[peer], widen_home.at[me], {"exp": peer})
                )
        if step == steps and chunk and chunk % 2 == 0:
            span = 64 * (chunks - 1)
            for side in range(2):
                found = joined_lanes(wide_sum[chunk - 2, side], wide_sum[chunk - 1, side])
                for index, part in enumerate(found):
                    start = index * span + (chunk - 2) * 64
                    expand_sum[side, :, start : start + 128] = part

    def tick(count):
        for chunk in range(chunks):
            if 0 <= count - 2 * chunk <= steps:
                ring_step(chunk, count - 2 * chunk)

    back_moves = [
        links.copy(back_parts.at[peer], back_recv.at[me], {"exp": peer}) for peer in at.peers
    ]
    tick(0)
    result_moves = [
        [
            links.copy(result_parts.at[peer], result_recv.at[me], {"exp": peer}),
            links.copy(gate_parts.at[peer], gate_recv.at[me], {"exp": peer}),
        ]
        for peer in at.peers
    ]
    gate_recv[me] = gate_parts[me]
    back_recv[me] = back_parts[me]
    result_recv[me] = result_parts[me]
    for made in kept:
        made.wait()
    tick(1)
    for move in back_moves:
        move.wait_recv()
    tick(2)

    second_grad = back_recv[0].astype(jnp.float32)
    for member in range(1, members):
        second_grad = second_grad + back_recv[member].astype(jnp.float32)
    middle = middle_ref[...]
    scale = rms_factor(middle)
    gain_own[...] = jnp.zeros_like(gain_own)
    gain_own[1:2, :] = jnp.sum(second_grad * (middle * scale), axis=0, keepdims=True)
    input_grad_ref[...] = grads_all[slot_of(deal_ref, me)].astype(jnp.float32) + rms_back(
        middle, scale, second_grad * gains_full[1:2, :]
    )
    middle_low = input_grad_ref[...].astype(jnp.bfloat16)
    turned_ref[3] = nt(middle_low, attend_full[3]).astype(jnp.bfloat16)
    tick(3)
    cosines, sines = cos_ref[...], sin_ref[...]
    lower = first_half((length, 128))

    def heads(pair, carry):
        lanes = pl.ds(pl.multiple_of(pair * 128, 128), 128)
        query, key, value = saved[0, :, lanes], saved[1, :, lanes], saved[2, :, lanes]
        outer = turned_ref[3, :, lanes]
        made = []
        for side in range(2):
            soft = soft_ref[2 * pair + side]
            alone = jnp.where(lower == (side == 0), outer, jnp.zeros_like(outer))
            value_grad = tn(soft.astype(jnp.bfloat16), outer)
            soft_grad = nt(alone, value)
            score_grad = (
                soft * (soft_grad - jnp.sum(soft * soft_grad, axis=-1, keepdims=True))
            ).astype(jnp.bfloat16)
            made.append(
                (matmul(score_grad, key) * 0.125, tn(score_grad, query) * 0.125, value_grad)
            )
        for index in range(3):
            joined = jnp.where(lower, made[0][index], made[1][index])
            if index < 2:
                joined = joined * cosines - turned(joined) * sines
            turned_ref[index, :, lanes] = joined.astype(jnp.bfloat16)
        return carry

    lax.fori_loop(0, width // 128, heads, 0)
    tick(4)
    attend_grad[3] = tn(saved[3], middle_low).astype(jnp.bfloat16)
    for matrix in range(3):
        attend_grad[matrix] = tn(saved[4], turned_ref[matrix]).astype(jnp.bfloat16)
    near_moves = [
        links.copy(attend_grad.at[matrix], near_recv.at[index], {"exp": at.near})
        for index, matrix in enumerate((at.near, at.cross))
    ]
    tick(5)
    first_grad = nt(turned_ref[0], attend_full[0])
    for matrix in range(1, 3):
        first_grad = first_grad + nt(turned_ref[matrix], attend_full[matrix])
    stream = tokens[...].astype(jnp.float32)
    scale = rms_factor(stream)
    gain_own[0:1, :] = jnp.sum(first_grad * (stream * scale), axis=0, keepdims=True)
    gain_moves = [links.copy(gain_own, gain_recv.at[me], {"exp": peer}) for peer in at.peers]
    gain_recv[me] = gain_own[...]
    input_grad_ref[...] += rms_back(stream, scale, first_grad * gains_full[0:1, :])
    for move in near_moves:
        move.wait_recv()
    far_send[...] = (
        attend_grad[at.far].astype(jnp.float32) + near_recv[1].astype(jnp.float32)
    ).astype(jnp.bfloat16)
    far_move = links.copy(far_send, far_recv, {"exp": at.far})
    tick(6)
    for moves in result_moves:
        for move in moves:
            move.wait_recv()
    output = middle_ref[...]
    for member in range(members):
        output = output + result_recv[member].astype(jnp.float32)
    output_ref[...] = output
    for choice in range(2):
        route = routes[choice : choice + 1, :]
        found = jnp.zeros((1, length), jnp.float32)
        for member in range(members):
            found = jnp.where(route == member, gate_recv[member, 0:1, :], found)
        gate_grad_ref[choice : choice + 1, :] = found
    tick(7)
    for move in gain_moves:
        move.wait_recv()
    total = gain_recv[0]
    for member in range(1, members):
        total = total + gain_recv[member]
    gain_ring[at.group] = total
    far_move.wait_recv()
    attend_total[...] = (
        attend_grad[me].astype(jnp.float32)
        + near_recv[0].astype(jnp.float32)
        + far_recv[...].astype(jnp.float32)
    ).astype(jnp.bfloat16)

    half = block // 2
    small, gain_steps = [], []

    def advance_small():
        step = len(small)
        owners = (at.owner(-1 - step), at.owner(1 + step))
        made = []
        for side, target in enumerate((at.next, at.back)):
            spot = attend_total.at[rows(owners[side] * block + side * half, half), :]
            if step:
                small[-1][side].wait_recv()
                source = attend_recv.at[side, step - 1]
                added = source[...].astype(jnp.float32) + spot[...].astype(jnp.float32)
                if step < steps:
                    source[...] = added.astype(jnp.bfloat16)
                else:
                    for member in range(members // 2):
                        attend_back[side * (members // 2) + member] = added[
                            member * share : (member + 1) * share, :
                        ]
                spot = source
            if step < steps:
                made.append(links.copy(spot, attend_recv.at[side, step], target))
        if step:
            gain_steps[-1].wait_recv()
        if step < steps:
            owner = at.owner(-step)
            gain_steps.append(links.copy(gain_ring.at[owner], gain_ring.at[owner], at.next))
        small.append(made)

    last = steps + 2 * (chunks - 1)
    for count in range(steps + 1, last):
        if len(small) <= steps:
            advance_small()
        tick(count)
    while len(small) <= steps:
        advance_small()
    attend_moves = [
        links.copy(attend_back.at[peer], attend_sum.at[me], {"exp": peer}) for peer in at.peers
    ]
    attend_sum[me] = attend_back[me]
    total = gain_ring[0]
    for group in range(1, groups):
        total = total + gain_ring[group]
    count = gains_sum.shape[1]
    start = (at.group * members + me) * count
    gains_sum[...] = pltpu.roll(total, width - start, 1)[0:2, 0:count]
    for move in widen_moves:
        move.wait_recv()
    for matrix in range(2):
        for member in range(0, members, 2):
            found = joined_lanes(widen_home[member, matrix], widen_home[member + 1, matrix])
            for index, part in enumerate(found):
                start = index * 64 * members + member * 64
                widen_sum[matrix, :, start : start + 128] = part
    tick(last)
    for move in attend_moves:
        move.wait_recv()
    links.finish()


def update_kernel(rates, copies, *refs):
    count = len(rates)
    given, made = refs[: 4 * count + copies], refs[4 * count + copies :]
    for index in range(copies):
        made[index][...] = given[4 * count + index][...]
    for index, rate in enumerate(rates):
        weight, moment, variance, gradient = given[4 * index : 4 * index + 4]
        grad = gradient[...]
        if len(weight.shape) < len(gradient.shape):
            grad = grad[3]
        elif weight.shape[0] < gradient.shape[0]:
            grad = grad[: weight.shape[0]]
        found = adamw_update(weight[...], moment[...], variance[...], grad, rate)
        for part in range(3):
            made[copies + 3 * index + part][...] = found[part]


def update_all(*groups, passed):
    cuts = 4

    def spec(dims, cut):
        if cut is None:
            return pl.BlockSpec(dims, lambda step: (0,) * len(dims))
        block = tuple(size // cuts if at == cut else size for at, size in enumerate(dims))
        return pl.BlockSpec(
            block, lambda step: tuple(step if at == cut else 0 for at in range(len(dims)))
        )

    def cut_of(array):
        dims = array.shape
        for at in range(len(dims) - 1):
            if array.size > 100000 and dims[at] % (8 * cuts) == 0:
                return at
        return len(dims) - 1 if dims[-1] % (128 * cuts) == 0 else None

    given, specs, shapes, out_specs = [], [], [], []
    for _, weight, moment, variance, gradient in groups:
        cut = cut_of(weight)
        for array in (weight, moment, variance, gradient):
            given.append(array)
            specs.append(spec(array.shape, cut))
        for array in (weight, moment, variance):
            shapes.append(jax.ShapeDtypeStruct(array.shape, array.dtype))
            out_specs.append(spec(array.shape, cut))
    extra = [spec(array.shape, cut_of(array)) for array in passed]
    return pl.pallas_call(
        functools.partial(update_kernel, [group[0] for group in groups], len(passed)),
        grid=(cuts,),
        out_shape=[jax.ShapeDtypeStruct(array.shape, array.dtype) for array in passed] + shapes,
        in_specs=specs + extra,
        out_specs=extra + out_specs,
        compiler_params=pltpu.CompilerParams(vmem_limit_bytes=LIMIT),
    )(*given, *passed)


def rotary_lines(length):
    half = HEAD_FEATURES // 2
    freqs = np.exp(-np.log(10000.0) * np.arange(half) / half)
    angles = np.arange(length)[:, None] * freqs[None, :]
    cosines, sines = np.cos(angles), np.sin(angles)
    return (
        np.concatenate([cosines] * 4, axis=1).astype(np.float32),
        np.concatenate([-sines, sines] * 2, axis=1).astype(np.float32),
    )


def spaces(*names):
    kinds = {"v": pltpu.VMEM, "s": pltpu.SMEM, "a": pl.ANY}
    return [pl.BlockSpec(memory_space=kinds[name]) for name in "".join(names)]


def local(
    tokens,
    seq_lengths,
    deal_order,
    expert_routes,
    capacity_slots,
    gate_weights,
    cotangent,
    projector,
    projector_mean,
    projector_square,
    collector,
    collector_first_moment,
    collector_second_moment,
    widener,
    widener_mean,
    widener_square,
    narrower,
    narrower_mean,
    narrower_square,
    norm_gains,
    gains_mean,
    gains_square,
    expander,
    expander_mean,
    expander_square,
    reducer,
    reducer_mean,
    reducer_square,
):
    groups, members = lax.axis_size("grp"), lax.axis_size("exp")
    length, width = tokens.shape[1:]
    inner = expander.shape[3]
    piece = widener.shape[2] // members
    chunks = 1 + inner // piece
    capacity = 3 * length // members
    steps = groups - 1
    high, low, share = expander.shape[2], narrower.shape[0], projector.shape[1]
    bf16, f32 = jnp.bfloat16, jnp.float32
    shape = jax.ShapeDtypeStruct
    cosines, sines = (jnp.asarray(lines) for lines in rotary_lines(length))
    count = 16 * groups
    (
        wide_grads,
        down_grads,
        attend_full,
        grads_all,
        gains_full,
        saved,
        middle,
        soft,
        result_parts,
        back_parts,
        gate_parts,
    ) = pl.pallas_call(
        functools.partial(gather_kernel, groups, members),
        out_shape=[
            shape((chunks, 2, width, piece), bf16),
            shape((chunks, piece, width), bf16),
            shape((4, width, width), bf16),
            shape((members, length, width), bf16),
            shape((8, width), f32),
            shape((5, length, width), bf16),
            shape((length, width), f32),
            shape((HEAD_COUNT, length, length), f32),
            shape((members, length, width), bf16),
            shape((members, length, width), bf16),
            shape((members, 8, length), f32),
        ],
        in_specs=spaces("ss", "v" * 14),
        out_specs=spaces("aa", "v" * 9),
        scratch_shapes=[
            VMEM((members, length, width), bf16),
            VMEM((members, 8, length), f32),
            VMEM((members, 8, length), f32),
            VMEM((4, share, width), f32),
            VMEM((4, share, width), f32),
            VMEM((members, 2, share, piece), f32),
            VMEM((members, 2, share, piece), f32),
            VMEM((8, width), f32),
            VMEM((members, 8, width), f32),
            VMEM((groups, 8, width), f32),
            VMEM((chunks, 2, width, piece), bf16),
            VMEM((chunks, piece, width), bf16),
            VMEM((chunks, 2, high, piece), bf16),
            VMEM((chunks, low, width), bf16),
            VMEM((members * length, width), bf16),
            VMEM((width, members * length), bf16),
            VMEM((members, length, width), f32),
            VMEM((members, length, width), f32),
            VMEM((members * capacity, width), bf16),
            VMEM((width, members * capacity), bf16),
            VMEM((members * capacity, width), bf16),
            VMEM((members * capacity, width), f32),
            VMEM((members * capacity, width), f32),
            pltpu.SemaphoreType.DMA((count,)),
            pltpu.SemaphoreType.DMA((count,)),
            pltpu.SemaphoreType.DMA((chunks * steps * 4,)),
            pltpu.SemaphoreType.DMA((chunks * steps * 4,)),
            pltpu.SemaphoreType.DMA((2 * chunks,)),
        ],
        compiler_params=pltpu.CompilerParams(
            collective_id=0, has_side_effects=True, vmem_limit_bytes=LIMIT
        ),
    )(
        seq_lengths,
        deal_order,
        tokens[0],
        cotangent[0],
        expert_routes[0].T,
        capacity_slots[0].T,
        gate_weights[0].T,
        norm_gains,
        projector,
        collector,
        widener,
        narrower,
        expander[0],
        reducer[0],
        cosines,
        sines,
    )
    count = 32 * groups
    (
        output,
        input_grad,
        gate_grad,
        expand_sum,
        reduce_sum,
        widen_sum,
        narrow_sum,
        attend_sum,
        gains_sum,
    ) = pl.pallas_call(
        functools.partial(scatter_kernel, groups, members),
        out_shape=[
            shape((length, width), f32),
            shape((length, width), f32),
            shape((2, length), f32),
            shape((2, high, inner), f32),
            shape(reducer.shape[1:], f32),
            shape(widener.shape, f32),
            shape(narrower.shape, f32),
            shape((4, share, width), f32),
            shape(norm_gains.shape, f32),
        ],
        in_specs=spaces("s", "v" * 13, "aa"),
        out_specs=spaces("v" * 9),
        scratch_shapes=[
            VMEM((members, 8, length), f32),
            VMEM((members, length, width), bf16),
            VMEM((members, length, width), bf16),
            VMEM((chunks, 2, width, piece), bf16),
            VMEM((chunks, piece, width), bf16),
            VMEM((chunks, 2, steps, high, piece), bf16),
            VMEM((chunks, 2, steps, low // 2, width), bf16),
            VMEM((chunks - 1, 2, high, piece), f32),
            VMEM((4, length, width), bf16),
            VMEM((4, width, width), bf16),
            VMEM((2, width, width), bf16),
            VMEM((width, width), bf16),
            VMEM((width, width), bf16),
            VMEM((width, width), bf16),
            VMEM((2, steps, high // 2, width), bf16),
            VMEM((4, share, width), f32),
            VMEM((members, 2, share, piece), f32),
            VMEM((members, 2, share, piece), f32),
            VMEM((8, width), f32),
            VMEM((members, 8, width), f32),
            VMEM((groups, 8, width), f32),
            pltpu.SemaphoreType.DMA((count,)),
            pltpu.SemaphoreType.DMA((count,)),
            pltpu.SemaphoreType.DMA((2,)),
        ],
        compiler_params=pltpu.CompilerParams(
            collective_id=1, has_side_effects=True, vmem_limit_bytes=LIMIT
        ),
    )(
        deal_order,
        tokens[0],
        expert_routes[0].T,
        grads_all,
        gains_full,
        attend_full,
        saved,
        middle,
        soft,
        cosines,
        sines,
        result_parts,
        back_parts,
        gate_parts,
        wide_grads,
        down_grads,
    )
    updated = update_all(
        (0.1, projector, projector_mean, projector_square, attend_sum),
        (0.3, collector, collector_first_moment, collector_second_moment, attend_sum),
        (0.07, widener, widener_mean, widener_square, widen_sum),
        (0.045, narrower, narrower_mean, narrower_square, narrow_sum),
        (0.2, norm_gains, gains_mean, gains_square, gains_sum),
        (0.07, expander[0], expander_mean[0], expander_square[0], expand_sum),
        (0.045, reducer[0], reducer_mean[0], reducer_square[0], reduce_sum),
        passed=(output, input_grad),
    )
    return (
        updated[0][None],
        updated[1][None],
        gate_grad.T[None],
        *updated[2:17],
        *(found[None] for found in updated[17:]),
    )


def fits(mesh):
    groups, members = mesh.shape["grp"], mesh.shape["exp"]
    share = 64 * HEAD_COUNT // (groups * members)
    return members == 4 and groups % 2 == 0 and share % 8 == 0 and share * members // 2 % 16 == 0


def solution(mesh):
    placed = (
        P(("grp", "exp"), None, None),
        P("grp"),
        P("grp"),
        P(("grp", "exp"), None, None),
        P(("grp", "exp"), None, None),
        P(("grp", "exp"), None, None),
        P(("grp", "exp"), None, None),
        P(None, ("grp", "exp"), None),
        P(None, ("grp", "exp"), None),
        P(None, ("grp", "exp"), None),
        P(("grp", "exp"), None),
        P(("grp", "exp"), None),
        P(("grp", "exp"), None),
        P(None, ("grp", "exp"), None),
        P(None, ("grp", "exp"), None),
        P(None, ("grp", "exp"), None),
        P(("grp", "exp"), None),
        P(("grp", "exp"), None),
        P(("grp", "exp"), None),
        P(None, ("grp", "exp")),
        P(None, ("grp", "exp")),
        P(None, ("grp", "exp")),
        P("exp", None, "grp", None),
        P("exp", None, "grp", None),
        P("exp", None, "grp", None),
        P("exp", "grp", None),
        P("exp", "grp", None),
        P("exp", "grp", None),
    )
    return jax.shard_map(
        local if fits(mesh) else local_plain,
        mesh=mesh,
        in_specs=placed,
        out_specs=(
            P(("grp", "exp"), None, None),
            P(("grp", "exp"), None, None),
            P(("grp", "exp"), None, None),
            P(None, ("grp", "exp"), None),
            P(None, ("grp", "exp"), None),
            P(None, ("grp", "exp"), None),
            P(("grp", "exp"), None),
            P(("grp", "exp"), None),
            P(("grp", "exp"), None),
            P(None, ("grp", "exp"), None),
            P(None, ("grp", "exp"), None),
            P(None, ("grp", "exp"), None),
            P(("grp", "exp"), None),
            P(("grp", "exp"), None),
            P(("grp", "exp"), None),
            P(None, ("grp", "exp")),
            P(None, ("grp", "exp")),
            P(None, ("grp", "exp")),
            P("exp", None, "grp", None),
            P("exp", None, "grp", None),
            P("exp", None, "grp", None),
            P("exp", "grp", None),
            P("exp", "grp", None),
            P("exp", "grp", None),
        ),
        check_vma=False,
    )
```

```python
import functools

import jax
import jax.numpy as jnp
import numpy as np
from jax import lax
from jax.experimental import pallas as pl
from jax.experimental.pallas import tpu as pltpu
from jax.sharding import PartitionSpec as P

HEAD_COUNT = 12
HEAD_FEATURES = 64
STEP = 5


def rms_factor(values):
    return lax.rsqrt(jnp.mean(values * values, axis=-1, keepdims=True) + 1e-06)


def rms_back(values, factor, upstream):
    return factor * (
        upstream - values * factor * factor * jnp.mean(upstream * values, axis=-1, keepdims=True)
    )


def rotary(length):
    positions = jnp.arange(length, dtype=jnp.int32).astype(jnp.float32)
    half = HEAD_FEATURES // 2
    freqs = jnp.exp(
        -jnp.log(10000.0) * jnp.arange(half, dtype=jnp.int32).astype(jnp.float32) / half
    )
    angles = positions[:, None] * freqs[None, :]
    return (jnp.cos(angles)[:, None, :], jnp.sin(angles)[:, None, :])


def rotate(values, cosines, sines):
    half = values.shape[-1] // 2
    first = values[..., :half]
    second = values[..., half:]
    return jnp.concatenate(
        [first * cosines - second * sines, second * cosines + first * sines], axis=-1
    )


def rotate_back(values, cosines, sines):
    half = values.shape[-1] // 2
    first = values[..., :half]
    second = values[..., half:]
    return jnp.concatenate(
        [first * cosines + second * sines, second * cosines - first * sines], axis=-1
    )


def silu_slope(values):
    sigmoid_of = jax.nn.sigmoid(values)
    return sigmoid_of * (1.0 + values * (1.0 - sigmoid_of))


def matmul(left, right):
    return jnp.dot(left, right, preferred_element_type=jnp.float32)


def outer_sum(left, right):
    return jnp.einsum("ld,lf->df", left, right, preferred_element_type=jnp.float32)


def adamw_update(weight, moment, variance, gradient, rate):
    moment_new = 0.5 * moment + 0.5 * gradient
    variance_new = 0.5 * variance + 0.5 * gradient * gradient
    correct = 1.0 - 0.5**STEP
    stepped = moment_new / correct / (jnp.sqrt(variance_new / correct) + 1e-08) + 0.1 * weight
    return (moment_new, variance_new, weight - rate * stepped)


def local_plain(
    tokens,
    seq_lengths,
    deal_order,
    expert_routes,
    capacity_slots,
    gate_weights,
    cotangent,
    projector,
    projector_mean,
    projector_square,
    collector,
    collector_first_moment,
    collector_second_moment,
    widener,
    widener_mean,
    widener_square,
    narrower,
    narrower_mean,
    narrower_square,
    norm_gains,
    gains_mean,
    gains_square,
    expander,
    expander_mean,
    expander_square,
    reducer,
    reducer_mean,
    reducer_square,
):
    members = lax.axis_size("exp")
    member = lax.axis_index("exp")
    length_seq = tokens.shape[1]
    width = tokens.shape[2]
    local_experts = expander.shape[0]
    experts_all = local_experts * members
    capacity = 3 * length_seq // experts_all
    member_ids = jnp.arange(members, dtype=jnp.int32)
    source = deal_order[member]
    home_slot = jnp.sum(jnp.where(deal_order == member, member_ids, 0))
    seq_length = seq_lengths[source]
    piece = lax.all_gather(tokens, "exp", axis=0, tiled=True)
    chosen = jnp.arange(piece.shape[0], dtype=jnp.int32) == source
    dealt = jnp.sum(
        jnp.where(chosen[:, None, None], piece, jnp.zeros_like(piece)), axis=0, keepdims=True
    )
    residual_flow = dealt[0].astype(jnp.float32)
    project_full, collect_full, widen_full, narrow_full, gains_full = (
        lax.all_gather(projector.astype(jnp.bfloat16), ("grp", "exp"), axis=1, tiled=True),
        lax.all_gather(collector.astype(jnp.bfloat16), ("grp", "exp"), axis=0, tiled=True),
        lax.all_gather(widener.astype(jnp.bfloat16), ("grp", "exp"), axis=1, tiled=True),
        lax.all_gather(narrower.astype(jnp.bfloat16), ("grp", "exp"), axis=0, tiled=True),
        lax.all_gather(norm_gains.astype(jnp.bfloat16), ("grp", "exp"), axis=1, tiled=True),
    )
    expand_full, reduce_full = (
        lax.all_gather(expander.astype(jnp.bfloat16), "grp", axis=2, tiled=True),
        lax.all_gather(reducer.astype(jnp.bfloat16), "grp", axis=1, tiled=True),
    )
    gains_used = gains_full.astype(jnp.float32)
    cosines, sines = rotary(length_seq)
    scale_one = rms_factor(residual_flow)
    normed_one = residual_flow * scale_one
    first_input = (normed_one * gains_used[0]).astype(jnp.bfloat16)
    query_raw = matmul(first_input, project_full[0]).reshape(length_seq, HEAD_COUNT, HEAD_FEATURES)
    key_raw = matmul(first_input, project_full[1]).reshape(length_seq, HEAD_COUNT, HEAD_FEATURES)
    value_raw = matmul(first_input, project_full[2]).reshape(length_seq, HEAD_COUNT, HEAD_FEATURES)
    query_rot = rotate(query_raw, cosines, sines).astype(jnp.bfloat16)
    key_rot = rotate(key_raw, cosines, sines).astype(jnp.bfloat16)
    value_low = value_raw.astype(jnp.bfloat16)
    rows_at = jnp.arange(length_seq, dtype=jnp.int32)[:, None]
    cols_at = jnp.arange(length_seq, dtype=jnp.int32)[None, :]
    allowed = ((cols_at <= rows_at) & (cols_at < seq_length))[None]
    scores = (
        jnp.einsum("qhd,khd->hqk", query_rot, key_rot, preferred_element_type=jnp.float32) * 0.125
    )
    masked = jnp.where(allowed, scores, -1e30)
    top = jnp.max(masked, axis=-1, keepdims=True)
    expo = jnp.exp(masked - top)
    total = jnp.sum(expo, axis=-1, keepdims=True)
    soft = expo / total
    logsum = top + jnp.log(total)
    mixed_output = (
        jnp.einsum(
            "hqk,khd->qhd", soft.astype(jnp.bfloat16), value_low, preferred_element_type=jnp.float32
        )
        .reshape(length_seq, width)
        .astype(jnp.bfloat16)
    )
    middle_state = residual_flow + matmul(mixed_output, collect_full)
    scale_two = rms_factor(middle_state)
    normed_two = middle_state * scale_two
    second_input = (normed_two * gains_used[1]).astype(jnp.bfloat16)
    gating_scores = matmul(second_input, widen_full[0])
    upward_rows = matmul(second_input, widen_full[1])
    hidden_state = (jax.nn.silu(gating_scores) * upward_rows).astype(jnp.bfloat16)
    dense_branch = matmul(hidden_state, narrow_full)
    flat = (expert_routes[0] * capacity + capacity_slots[0]).reshape(-1)
    spread = jnp.repeat(second_input, 2, axis=0)
    dispatch = jnp.zeros((experts_all * capacity, width), jnp.bfloat16).at[flat].set(spread)
    dispatch = dispatch.reshape(experts_all, capacity, width)
    rows = lax.all_to_all(dispatch, "exp", split_axis=0, concat_axis=0, tiled=True)
    count = rows.shape[1]
    grouped = rows.reshape(members, local_experts, count, width)
    gate_pre = jnp.einsum(
        "sekd,edf->sekf", grouped, expand_full[:, 0], preferred_element_type=jnp.float32
    )
    up_pre = jnp.einsum(
        "sekd,edf->sekf", grouped, expand_full[:, 1], preferred_element_type=jnp.float32
    )
    hidden_rows = (jax.nn.silu(gate_pre) * up_pre).astype(jnp.bfloat16)
    result = jnp.einsum(
        "sekf,efd->sekd", hidden_rows, reduce_full, preferred_element_type=jnp.float32
    )
    result = result.astype(jnp.bfloat16).reshape(members * local_experts, count, width)
    returned_rows = lax.all_to_all(result, "exp", split_axis=0, concat_axis=0, tiled=True)
    outcome = (
        returned_rows,
        rows,
        gate_pre.reshape(members * local_experts, count, -1),
        up_pre.reshape(members * local_experts, count, -1),
    )
    returned, received, gate_kept, up_kept = outcome
    picked = (
        returned.reshape(experts_all * capacity, width)[flat]
        .reshape(length_seq, 2, width)
        .astype(jnp.float32)
    )
    gate_local = gate_weights[0]
    mixture = jnp.sum(gate_local[..., None] * picked, axis=1)
    layer_output = middle_state + dense_branch + mixture
    valid = (jnp.arange(length_seq, dtype=jnp.int32) < seq_length).astype(jnp.float32)
    grad_out = cotangent[0] * valid[:, None]
    grad_low = grad_out.astype(jnp.bfloat16)
    narrow_grad = outer_sum(hidden_state, grad_low)
    hidden_grad = jnp.einsum("ld,fd->lf", grad_low, narrow_full, preferred_element_type=jnp.float32)
    gating_grad = (hidden_grad * upward_rows * silu_slope(gating_scores)).astype(jnp.bfloat16)
    upward_grad = (hidden_grad * jax.nn.silu(gating_scores)).astype(jnp.bfloat16)
    widen_grad = jnp.stack(
        [outer_sum(second_input, gating_grad), outer_sum(second_input, upward_grad)]
    )
    second_grad = jnp.einsum(
        "lf,df->ld", gating_grad, widen_full[0], preferred_element_type=jnp.float32
    ) + jnp.einsum("lf,df->ld", upward_grad, widen_full[1], preferred_element_type=jnp.float32)
    gate_grad_local = jnp.sum(grad_out[:, None, :] * picked, axis=-1)
    result_grad = (
        (gate_local[..., None] * grad_out[:, None, :])
        .astype(jnp.bfloat16)
        .reshape(2 * length_seq, width)
    )
    grad_send = jnp.zeros((experts_all * capacity, width), jnp.bfloat16).at[flat].set(result_grad)
    grad_recv = lax.all_to_all(
        grad_send.reshape(experts_all, capacity, width),
        "exp",
        split_axis=0,
        concat_axis=0,
        tiled=True,
    )
    grad_group = grad_recv.reshape(members, local_experts, capacity, width)
    rows_group = received.reshape(members, local_experts, capacity, width)
    gate_pre = gate_kept.reshape(members, local_experts, capacity, -1)
    up_pre = up_kept.reshape(members, local_experts, capacity, -1)
    hidden_rows = (jax.nn.silu(gate_pre) * up_pre).astype(jnp.bfloat16)
    reduce_grad = jnp.einsum(
        "sekf,sekd->efd", hidden_rows, grad_group, preferred_element_type=jnp.float32
    )
    hidden_rows_grad = jnp.einsum(
        "sekd,efd->sekf", grad_group, reduce_full, preferred_element_type=jnp.float32
    )
    gate_rows_grad = (hidden_rows_grad * up_pre * silu_slope(gate_pre)).astype(jnp.bfloat16)
    up_rows_grad = (hidden_rows_grad * jax.nn.silu(gate_pre)).astype(jnp.bfloat16)
    expand_grad = jnp.stack(
        [
            jnp.einsum(
                "sekd,sekf->edf", rows_group, gate_rows_grad, preferred_element_type=jnp.float32
            ),
            jnp.einsum(
                "sekd,sekf->edf", rows_group, up_rows_grad, preferred_element_type=jnp.float32
            ),
        ],
        axis=1,
    )
    row_grads = jnp.einsum(
        "sekf,edf->sekd", gate_rows_grad, expand_full[:, 0], preferred_element_type=jnp.float32
    ) + jnp.einsum(
        "sekf,edf->sekd", up_rows_grad, expand_full[:, 1], preferred_element_type=jnp.float32
    )
    row_grads = row_grads.astype(jnp.bfloat16).reshape(experts_all, capacity, width)
    came_back = lax.all_to_all(row_grads, "exp", split_axis=0, concat_axis=0, tiled=True).reshape(
        experts_all * capacity, width
    )
    second_grad = second_grad + jnp.sum(
        came_back[flat].reshape(length_seq, 2, width).astype(jnp.float32), axis=1
    )
    gains_grad_two = jnp.sum(second_grad * normed_two, axis=0)
    middle_grad = grad_out + rms_back(middle_state, scale_two, second_grad * gains_used[1])
    middle_low = middle_grad.astype(jnp.bfloat16)
    collect_grad = outer_sum(mixed_output, middle_low)
    mixed_grad = jnp.einsum(
        "ld,ed->le", middle_low, collect_full, preferred_element_type=jnp.float32
    )
    mixed_grad = mixed_grad.astype(jnp.bfloat16).reshape(length_seq, HEAD_COUNT, HEAD_FEATURES)
    scores_again = (
        jnp.einsum("qhd,khd->hqk", query_rot, key_rot, preferred_element_type=jnp.float32) * 0.125
    )
    soft_again = jnp.where(allowed, jnp.exp(scores_again - logsum), 0.0)
    value_grad = jnp.einsum(
        "hqk,qhd->khd",
        soft_again.astype(jnp.bfloat16),
        mixed_grad,
        preferred_element_type=jnp.float32,
    )
    soft_grad = jnp.einsum(
        "qhd,khd->hqk", mixed_grad, value_low, preferred_element_type=jnp.float32
    )
    score_grad = (
        soft_again * (soft_grad - jnp.sum(soft_again * soft_grad, axis=-1, keepdims=True))
    ).astype(jnp.bfloat16)
    query_grad = (
        jnp.einsum("hqk,khd->qhd", score_grad, key_rot, preferred_element_type=jnp.float32) * 0.125
    )
    key_grad = (
        jnp.einsum("hqk,qhd->khd", score_grad, query_rot, preferred_element_type=jnp.float32)
        * 0.125
    )
    query_back = (
        rotate_back(query_grad, cosines, sines).reshape(length_seq, width).astype(jnp.bfloat16)
    )
    key_back = rotate_back(key_grad, cosines, sines).reshape(length_seq, width).astype(jnp.bfloat16)
    value_back = value_grad.reshape(length_seq, width).astype(jnp.bfloat16)
    project_grad = jnp.stack(
        [
            outer_sum(first_input, query_back),
            outer_sum(first_input, key_back),
            outer_sum(first_input, value_back),
        ]
    )
    first_grad = (
        jnp.einsum("le,de->ld", query_back, project_full[0], preferred_element_type=jnp.float32)
        + jnp.einsum("le,de->ld", key_back, project_full[1], preferred_element_type=jnp.float32)
        + jnp.einsum("le,de->ld", value_back, project_full[2], preferred_element_type=jnp.float32)
    )
    gains_grad_one = jnp.sum(first_grad * normed_one, axis=0)
    stream_grad = middle_grad + rms_back(residual_flow, scale_one, first_grad * gains_used[0])
    gains_grad = jnp.stack([gains_grad_one, gains_grad_two])
    project_part, collect_part, widen_part, narrow_part, gains_part = (
        lax.psum_scatter(project_grad, ("grp", "exp"), scatter_dimension=1, tiled=True),
        lax.psum_scatter(collect_grad, ("grp", "exp"), scatter_dimension=0, tiled=True),
        lax.psum_scatter(widen_grad, ("grp", "exp"), scatter_dimension=1, tiled=True),
        lax.psum_scatter(narrow_grad, ("grp", "exp"), scatter_dimension=0, tiled=True),
        lax.psum_scatter(gains_grad, ("grp", "exp"), scatter_dimension=1, tiled=True),
    )
    expand_part, reduce_part = (
        lax.psum_scatter(
            expand_grad.astype(jnp.bfloat16), "grp", scatter_dimension=2, tiled=True
        ).astype(jnp.float32),
        lax.psum_scatter(
            reduce_grad.astype(jnp.bfloat16), "grp", scatter_dimension=1, tiled=True
        ).astype(jnp.float32),
    )
    empty = jnp.zeros((1, length_seq, width), jnp.float32)
    pieces = (
        lax.all_gather(layer_output[None].astype(jnp.bfloat16), "exp", axis=0, tiled=True).astype(
            jnp.float32
        ),
        lax.all_gather(stream_grad[None].astype(jnp.bfloat16), "exp", axis=0, tiled=True).astype(
            jnp.float32
        ),
    )
    chosen = (jnp.arange(pieces[0].shape[0], dtype=jnp.int32) == home_slot)[:, None, None]
    homed_output = empty + jnp.sum(jnp.where(chosen, pieces[0], 0.0), axis=0, keepdims=True)
    homed_grad = empty + jnp.sum(jnp.where(chosen, pieces[1], 0.0), axis=0, keepdims=True)
    project_new = adamw_update(projector, projector_mean, projector_square, project_part, 0.1)
    collect_new = adamw_update(
        collector, collector_first_moment, collector_second_moment, collect_part, 0.3
    )
    widening_updated = adamw_update(widener, widener_mean, widener_square, widen_part, 0.07)
    narrowing_updated = adamw_update(narrower, narrower_mean, narrower_square, narrow_part, 0.045)
    gains_updated = adamw_update(norm_gains, gains_mean, gains_square, gains_part, 0.2)
    expansion_updated = adamw_update(expander, expander_mean, expander_square, expand_part, 0.07)
    reduction_updated = adamw_update(reducer, reducer_mean, reducer_square, reduce_part, 0.045)
    return (
        homed_output,
        homed_grad,
        gate_grad_local[None],
        project_new[0],
        project_new[1],
        project_new[2],
        collect_new[0],
        collect_new[1],
        collect_new[2],
        widening_updated[0],
        widening_updated[1],
        widening_updated[2],
        narrowing_updated[0],
        narrowing_updated[1],
        narrowing_updated[2],
        gains_updated[0],
        gains_updated[1],
        gains_updated[2],
        expansion_updated[0],
        expansion_updated[1],
        expansion_updated[2],
        reduction_updated[0],
        reduction_updated[1],
        reduction_updated[2],
    )


MESH = pl.DeviceIdType.MESH
VMEM = pltpu.VMEM
LIMIT = 60 * 1024 * 1024


def ring_place(index, groups):
    row, side = lax.div(index, 2), lax.rem(index, 2)
    return (1 - side) * row + side * (groups - 1 - row)


def ring_member(place, groups):
    side = lax.div(place, groups // 2)
    return 2 * ((1 - side) * place + side * (groups - 1 - place)) + side


def remote(source, target, sends, arrivals, at, device):
    return pltpu.make_async_remote_copy(
        src_ref=source,
        dst_ref=target,
        send_sem=sends.at[at],
        recv_sem=arrivals.at[at],
        device_id=device,
        device_id_type=MESH,
    )


class Links:
    def __init__(self, sends, arrivals):
        self.sends, self.arrivals, self.count, self.started = sends, arrivals, 0, []

    def copy(self, source, target, device):
        made = remote(source, target, self.sends, self.arrivals, self.count, device)
        self.count += 1
        made.start()
        self.started.append(made)
        return made

    def finish(self):
        for made in self.started:
            made.wait_send()


class Places:
    def __init__(self, groups, members):
        self.groups, self.members = groups, members
        self.group = lax.axis_index("grp")
        self.member = lax.axis_index("exp")
        self.place = ring_place(self.group, groups)
        self.next = {"grp": self.owner(1)}
        self.back = {"grp": self.owner(-1)}
        half = members // 2
        self.far = lax.rem(self.member + half, members)
        self.near = self.member + 1 - 2 * lax.rem(self.member, 2)
        self.cross = lax.rem(self.near + half, members)
        self.peers = [lax.rem(self.member + step, members) for step in range(1, members)]

    def owner(self, offset):
        place = lax.rem(self.place + offset + 2 * self.groups, self.groups)
        return ring_member(place, self.groups)

    def enter(self):
        barrier = pltpu.get_barrier_semaphore()
        partners = [self.next, self.back] + [{"exp": peer} for peer in self.peers]
        for partner in partners:
            pl.semaphore_signal(barrier, inc=1, device_id=partner, device_id_type=MESH)
        pl.semaphore_wait(barrier, len(partners))


def rows(start, count, align=16):
    return pl.ds(pl.multiple_of(start, align), count)


def first_half(shape):
    return lax.rem(lax.broadcasted_iota(jnp.int32, shape, len(shape) - 1), 128) < 64


def turned(values):
    lanes = lax.broadcasted_iota(jnp.int32, values.shape, 1)
    return jnp.where(
        lax.rem(lanes, HEAD_FEATURES) < HEAD_FEATURES // 2,
        pltpu.roll(values, 128 - HEAD_FEATURES // 2, 1),
        pltpu.roll(values, HEAD_FEATURES // 2, 1),
    )


def nt(left, right):
    return lax.dot_general(
        left, right, (((1,), (1,)), ((), ())), preferred_element_type=jnp.float32
    )


def tn(left, right):
    return lax.dot_general(
        left, right, (((0,), (0,)), ((), ())), preferred_element_type=jnp.float32
    )


def sigmoid(values):
    return 1.0 / (1.0 + jnp.exp(-values))


def same(length):
    shape = (length, length)
    return lax.broadcasted_iota(jnp.int32, shape, 0) == lax.broadcasted_iota(jnp.int32, shape, 1)


def upright(line):
    return jnp.sum(jnp.where(same(line.shape[1]), line, 0.0), axis=1, keepdims=True)


def lying(column):
    return jnp.sum(jnp.where(same(column.shape[0]), column, 0.0), axis=0, keepdims=True)


def slot_of(deal_ref, member):
    for _ in range(11):
        member = deal_ref[member]
    return member


def dealt_lanes(values, piece, pieces):
    low_lanes = lax.broadcasted_iota(jnp.int32, (values.shape[0], 128), 1) < 64
    found = []
    span = 64 * pieces
    for start in range(0, values.shape[1], 2 * span):
        start = start + piece // 2 * 128
        one, two = values[:, start : start + 128], values[:, start + span : start + span + 128]
        if piece % 2:
            one = pltpu.roll(one, 64, 1)
        else:
            two = pltpu.roll(two, 64, 1)
        found.append(jnp.where(low_lanes, one, two))
    return jnp.concatenate(found, axis=1)


def joined_lanes(even, odd):
    low_lanes = lax.broadcasted_iota(jnp.int32, (even.shape[0], 128), 1) < 64
    found = []
    for start in range(0, even.shape[1], 128):
        one, two = even[:, start : start + 128], odd[:, start : start + 128]
        found.append(jnp.where(low_lanes, one, pltpu.roll(two, 64, 1)))
        found.append(jnp.where(low_lanes, pltpu.roll(one, 64, 1), two))
    return found


def gather_kernel(
    groups,
    members,
    length_ref,
    deal_ref,
    tokens,
    cotangent,
    routes,
    places,
    gates,
    norm_gains,
    projector,
    collector,
    widener,
    narrower,
    expander,
    reducer,
    cos_ref,
    sin_ref,
    wide_grads,
    down_grads,
    attend_out,
    grads_out,
    saved_out,
    middle_out,
    soft_out,
    gains_full,
    result_ref,
    back_ref,
    gate_ref,
    attend_full,
    grads_all,
    saved,
    middle_ref,
    soft_ref,
    second_all,
    meta_send,
    meta_all,
    attend_send,
    attend_recv,
    widen_send,
    widen_recv,
    gains,
    gain_recv,
    gain_ring,
    wide_full,
    down_full,
    wide_own,
    down_own,
    inputs_ref,
    inputs_turned,
    dense_out,
    dense_back,
    rows_in,
    rows_turned,
    rows_grad,
    rows_out,
    rows_back,
    sends,
    arrivals,
    ring_sends,
    ring_arrivals,
    local_sems,
):
    at = Places(groups, members)
    links = Links(sends, arrivals)
    at.enter()
    me, steps = at.member, groups - 1
    share, width = projector.shape[1:]
    block = share * members
    length = tokens.shape[0]
    chunks, low = down_own.shape[:2]
    capacity = rows_in.shape[0] // members

    def ring_copy(chunk, step, side, piece):
        owner = at.owner(-step if side == 0 else step)
        if piece == 0:
            spot = wide_full.at[chunk, side, rows(owner * block, block), :]
            origin = wide_own.at[chunk, side]
        else:
            spot = down_full.at[chunk, rows(owner * low + side * (low // 2), low // 2), :]
            origin = down_own.at[chunk, pl.ds(side * (low // 2), low // 2), :]
        place = (chunk * steps + step) * 4 + side * 2 + piece
        return remote(
            spot if step else origin,
            spot,
            ring_sends,
            ring_arrivals,
            place,
            (at.next, at.back)[side],
        )

    def ring_step(chunk, step):
        for piece in range(2):
            for side in range(2):
                if step:
                    ring_copy(chunk, step - 1, side, piece).wait_recv()
                if step < steps:
                    ring_copy(chunk, step, side, piece).start()

    def tick(count):
        for chunk in range(chunks):
            if 0 <= count - 2 * chunk <= steps:
                ring_step(chunk, count - 2 * chunk)

    attend_send[0:3] = projector[...]
    attend_send[3] = collector[...]
    gains[...] = jnp.zeros_like(gains)
    gains[0:2, 0 : norm_gains.shape[1]] = norm_gains[...]
    gains[...] = pltpu.roll(gains[...], (at.group * members + me) * norm_gains.shape[1], 1)
    first_moves = [
        [
            links.copy(attend_send.at[peer], attend_recv.at[me], {"exp": peer}),
            links.copy(gains, gain_recv.at[me], {"exp": peer}),
        ]
        for peer in at.peers
    ]
    gain_recv[me] = gains[...]
    attend_recv[me] = attend_send[me]
    for matrix in range(2):
        for member in range(members):
            widen_send[member, matrix] = dealt_lanes(widener[matrix], member, members)
    widen_moves = [
        links.copy(widen_send.at[peer], widen_recv.at[me], {"exp": peer}) for peer in at.peers
    ]
    widen_recv[me] = widen_send[me]

    def stage(chunk):
        if chunk == 1:
            for matrix in range(2):
                wide_own[1, matrix] = jnp.concatenate(
                    [widen_recv[member, matrix] for member in range(members)], axis=0
                ).astype(jnp.bfloat16)
            down_own[1] = narrower[...].astype(jnp.bfloat16)
        else:
            index = max(chunk - 1, 0)
            for matrix in range(2):
                wide_own[chunk, matrix] = dealt_lanes(
                    expander[matrix], index, chunks - 1
                ).astype(jnp.bfloat16)
            down_own[chunk] = reducer[index * low : (index + 1) * low, :].astype(jnp.bfloat16)
        for side in range(2):
            wide_full[chunk, side, rows(at.group * block, block), :] = wide_own[chunk, side]
        down_full[chunk, rows(at.group * low, low), :] = down_own[chunk]

    stage(0)
    tick(0)
    for moves in first_moves:
        for move in moves:
            move.wait_recv()
    attend_full[me, rows(at.group * block, block), :] = (
        attend_recv[...].reshape(block, width).astype(jnp.bfloat16)
    )
    total_gain = gain_recv[0]
    for member in range(1, members):
        total_gain = total_gain + gain_recv[member]
    gain_ring[at.group] = total_gain

    half = block // 2

    def unit(owner, side, matrix):
        return attend_full.at[matrix, rows(owner * block + side * half, half), :]

    def across(owner, side):
        spot = unit(owner, side, me)
        return (links.copy(spot, spot, {"exp": at.far}), links.copy(spot, spot, {"exp": at.near}))

    def onward(owner, side):
        spot = unit(owner, side, at.far)
        return links.copy(spot, spot, {"exp": at.near})

    ring, crossed, passed = [], [], []
    gain_moves = []
    for step in range(groups):
        owners = (at.owner(-step), at.owner(step))
        if step:
            for move in ring[-1]:
                move.wait_recv()
            gain_moves[-1].wait_recv()
        if step < steps:
            ring.append(
                [
                    links.copy(unit(owner, side, me), unit(owner, side, me), target)
                    for side, (owner, target) in enumerate(zip(owners, (at.next, at.back)))
                ]
            )
            gain_moves.append(
                links.copy(gain_ring.at[owners[0]], gain_ring.at[owners[0]], at.next)
            )
        crossed.append([across(owner, side) for side, owner in enumerate(owners)])
        if step:
            for side, owner in enumerate((at.owner(1 - step), at.owner(step - 1))):
                crossed[step - 1][side][0].wait_recv()
                passed.append(onward(owner, side))
        if step == 1:
            for chunk in range(2, chunks):
                stage(chunk)
        if step == 3:
            for move in widen_moves:
                move.wait_recv()
            stage(1)
        if step % 2 == 0 and step:
            tick(step // 2)
    tick(4)
    outgoing = []

    def hand_out(source, target):
        made = pltpu.make_async_copy(
            source, target, local_sems.at[2 * chunks + len(outgoing)]
        )
        made.start()
        outgoing.append(made)

    valid = lax.broadcasted_iota(jnp.int32, (length, 1), 0) < length_ref[deal_ref[me]]
    grads_all[me] = jnp.where(valid, cotangent[...], 0.0).astype(jnp.bfloat16)
    route = [routes[choice : choice + 1, :] for choice in range(2)]
    place = [places[choice : choice + 1, :].astype(jnp.float32) for choice in range(2)]
    meta_send[...] = jnp.zeros_like(meta_send)
    for member in range(members):
        named = [chosen == member for chosen in route]
        meta_send[member, 0:1, :] = jnp.where(
            named[0], place[0], jnp.where(named[1], place[1], -1.0)
        )
        meta_send[member, 1:2, :] = jnp.where(
            named[0], gates[0:1, :], jnp.where(named[1], gates[1:2, :], 0.0)
        )
    meta_all[me] = meta_send[me]
    grad_moves = [
        [
            links.copy(grads_all.at[me], grads_all.at[me], {"exp": peer}),
            links.copy(meta_send.at[peer], meta_all.at[me], {"exp": peer}),
        ]
        for peer in at.peers
    ]
    for side, owner in enumerate((at.owner(-steps), at.owner(steps))):
        crossed[steps][side][0].wait_recv()
        passed.append(onward(owner, side))
    total_gain = gain_ring[0]
    for group in range(1, groups):
        total_gain = total_gain + gain_ring[group]
    gains_full[...] = total_gain.astype(jnp.bfloat16).astype(jnp.float32)
    stream = tokens[...].astype(jnp.float32)
    first_input = (stream * rms_factor(stream) * gains_full[0:1, :]).astype(jnp.bfloat16)
    saved[4] = first_input
    for moves in crossed:
        for move in moves:
            move[1].wait_recv()
    for move in passed:
        move.wait_recv()
    tick(5)
    hand_out(attend_full, attend_out)

    cosines, sines = cos_ref[...], sin_ref[...]
    for matrix in range(3):
        raw = matmul(first_input, attend_full[matrix])
        if matrix == 2:
            saved[2] = raw.astype(jnp.bfloat16)
        else:
            for start in range(0, width, 128):
                piece = raw[:, start : start + 128]
                saved[matrix, :, start : start + 128] = (
                    piece * cosines + turned(piece) * sines
                ).astype(jnp.bfloat16)
    tick(6)

    seq_length = length_ref[me]
    rows_at = lax.broadcasted_iota(jnp.int32, (length, length), 0)
    cols_at = lax.broadcasted_iota(jnp.int32, (length, length), 1)
    allowed = (cols_at <= rows_at) & (cols_at < seq_length)
    lower = first_half((length, 128))

    def heads(pair, carry):
        lanes = pl.ds(pl.multiple_of(pair * 128, 128), 128)
        query, key, value = saved[0, :, lanes], saved[1, :, lanes], saved[2, :, lanes]
        results = []
        for side in range(2):
            alone = jnp.where(lower == (side == 0), query, jnp.zeros_like(query))
            scores = jnp.where(allowed, nt(alone, key) * 0.125, -1e30)
            expo = jnp.exp(scores - jnp.max(scores, axis=-1, keepdims=True))
            soft = expo / jnp.sum(expo, axis=-1, keepdims=True)
            soft_ref[2 * pair + side] = soft
            results.append(matmul(soft.astype(jnp.bfloat16), value))
        saved[3, :, lanes] = jnp.where(lower, results[0], results[1]).astype(jnp.bfloat16)
        return carry

    lax.fori_loop(0, width // 128, heads, 0)
    hand_out(saved, saved_out)
    hand_out(soft_ref, soft_out)
    middle = tokens[...].astype(jnp.float32) + matmul(saved[3], attend_full[3])
    middle_ref[...] = middle
    hand_out(middle_ref, middle_out)
    second_all[me] = (middle * rms_factor(middle) * gains_full[1:2, :]).astype(jnp.bfloat16)
    second_moves = [
        links.copy(second_all.at[me], second_all.at[me], {"exp": peer}) for peer in at.peers
    ]
    for moves in grad_moves:
        for move in moves:
            move.wait_recv()
    hand_out(grads_all, grads_out)
    tick(7)

    def hits(slot, by_row):
        line = meta_all[slot, 0:1, :]
        if by_row:
            names = lax.broadcasted_iota(jnp.int32, (capacity, length), 0).astype(jnp.float32)
            hit = names == line
        else:
            names = lax.broadcasted_iota(jnp.int32, (length, capacity), 1).astype(jnp.float32)
            hit = names == upright(line)
        return jnp.where(hit, 1.0, 0.0).astype(jnp.bfloat16)

    def spot_of(slot):
        return slice(slot * capacity, (slot + 1) * capacity)

    def here_of(slot):
        return slice(slot * length, (slot + 1) * length)

    for slot in range(members):
        pick = hits(slot, True)
        gate = jnp.sum(pick.astype(jnp.float32) * meta_all[slot, 1:2, :], axis=1, keepdims=True)
        rows_grad[spot_of(slot), :] = (matmul(pick, grads_all[slot]) * gate).astype(jnp.bfloat16)
    for move in second_moves:
        move.wait_recv()
    for slot in range(members):
        inputs_ref[here_of(slot), :] = second_all[deal_ref[slot]]
        rows_in[spot_of(slot), :] = matmul(hits(slot, True), inputs_ref[here_of(slot), :]).astype(
            jnp.bfloat16
        )
    inputs_turned[...] = inputs_ref[...].T
    rows_turned[...] = rows_in[...].T
    dense_out[...] = jnp.zeros_like(dense_out)
    dense_back[...] = jnp.zeros_like(dense_back)
    rows_out[...] = jnp.zeros_like(rows_out)
    rows_back[...] = jnp.zeros_like(rows_back)

    def branch(chunk, inputs, turned_inputs, outer, out, back):
        for step in range(steps):
            for side in range(2):
                for piece in range(2):
                    ring_copy(chunk, step, side, piece).wait_send()

        def part(index, carry):
            lanes = pl.ds(pl.multiple_of(index * 256, 256), 256)
            gate = matmul(inputs[...], wide_full[chunk, 0, :, lanes])
            up = matmul(inputs[...], wide_full[chunk, 1, :, lanes])
            rise = sigmoid(gate)
            smooth = gate * rise
            hidden = (smooth * up).astype(jnp.bfloat16)
            hidden_grad = nt(outer[...], down_full[chunk, lanes, :])
            gate_grad = (hidden_grad * up * (rise * (1.0 + gate * (1.0 - rise)))).astype(
                jnp.bfloat16
            )
            up_grad = (hidden_grad * smooth).astype(jnp.bfloat16)
            out[...] += matmul(hidden, down_full[chunk, lanes, :])
            back[...] += nt(gate_grad, wide_full[chunk, 0, :, lanes]) + nt(
                up_grad, wide_full[chunk, 1, :, lanes]
            )
            down_full[chunk, lanes, :] = tn(hidden, outer[...]).astype(jnp.bfloat16)
            wide_full[chunk, 0, :, lanes] = matmul(turned_inputs[...], gate_grad).astype(
                jnp.bfloat16
            )
            wide_full[chunk, 1, :, lanes] = matmul(turned_inputs[...], up_grad).astype(
                jnp.bfloat16
            )
            return carry

        lax.fori_loop(0, down_full.shape[1] // 256, part, 0)
        kept(chunk, 0).start()
        kept(chunk, 1).start()

    def kept(chunk, piece):
        source, target = ((wide_full, wide_grads), (down_full, down_grads))[piece]
        return pltpu.make_async_copy(
            source.at[chunk], target.at[chunk], local_sems.at[2 * chunk + piece]
        )

    outer_all = grads_all.reshape(members * length, width)
    flat = (members * length, width)
    dense = (
        inputs_ref,
        inputs_turned,
        outer_all,
        dense_out.reshape(flat),
        dense_back.reshape(flat),
    )

    def next_chunk(chunk, carry):
        for last in (steps - 1, steps):
            for ahead in range(groups // 2):
                @pl.when((chunk > 0) & (chunk + ahead < chunks))
                def _():
                    ring_step(chunk + ahead, last - 2 * ahead)

        @pl.when(chunk == 1)
        def _():
            branch(chunk, *dense)

        @pl.when(chunk != 1)
        def _():
            branch(chunk, rows_in, rows_turned, rows_grad, rows_out, rows_back)

        return carry

    lax.fori_loop(0, chunks, next_chunk, 0)

    for slot in range(members):
        pick = hits(slot, False)
        gate = upright(meta_all[slot, 1:2, :])
        picked = matmul(pick, rows_out[spot_of(slot), :].astype(jnp.bfloat16))
        inner = rows_back[spot_of(slot), :].astype(jnp.bfloat16)
        dense_out[slot] += gate * picked
        dense_back[slot] += matmul(pick, inner)
        score = jnp.sum(picked * grads_all[slot].astype(jnp.float32), axis=1, keepdims=True)
        gate_ref[slot] = jnp.broadcast_to(lying(score), gate_ref.shape[1:])
    for member in range(members):
        home = slot_of(deal_ref, member)
        result_ref[member] = dense_out[home].astype(jnp.bfloat16)
        back_ref[member] = dense_back[home].astype(jnp.bfloat16)
    for chunk in range(chunks):
        kept(chunk, 0).wait()
        kept(chunk, 1).wait()
    for made in outgoing:
        made.wait()
    links.finish()


def scatter_kernel(
    groups,
    members,
    deal_ref,
    tokens,
    routes,
    gains_full,
    cos_ref,
    sin_ref,
    gate_parts,
    result_parts,
    back_parts,
    wide_grads,
    down_grads,
    grads_in,
    middle_in,
    attend_in,
    saved_in,
    soft_in,
    output_ref,
    input_grad_ref,
    gate_grad_ref,
    expand_sum,
    reduce_sum,
    widen_sum,
    narrow_sum,
    attend_sum,
    gains_sum,
    grads_all,
    middle_ref,
    attend_full,
    saved,
    soft_ref,
    gate_recv,
    result_recv,
    back_recv,
    wide_own,
    down_own,
    wide_recv,
    down_recv,
    wide_sum,
    turned_ref,
    attend_grad,
    near_recv,
    far_recv,
    far_send,
    attend_total,
    attend_recv,
    attend_back,
    widen_back,
    widen_home,
    gain_own,
    gain_recv,
    gain_ring,
    sends,
    arrivals,
    local_sems,
):
    at = Places(groups, members)
    links = Links(sends, arrivals)
    at.enter()
    me, steps = at.member, groups - 1
    length, width = tokens.shape
    chunks, low = down_own.shape[0], narrow_sum.shape[0]
    share = attend_sum.shape[1]
    block = share * members

    moves_of = {}
    widen_moves = []

    def ring_step(chunk, step):
        made = []
        owners = (at.owner(-1 - step), at.owner(1 + step))
        for piece in range(2):
            for side, target in enumerate((at.next, at.back)):
                own, first = ((wide_own, wide_grads), (down_own, down_grads))[piece]
                landing = (wide_recv, down_recv)[piece].at[chunk, side]
                if piece == 0:
                    spot = (chunk, side, rows(owners[side] * block, block))
                else:
                    spot = (chunk, rows(owners[side] * low + side * (low // 2), low // 2))
                if step == 0:
                    source = first.at[spot]
                else:
                    moves_of[chunk, step - 1][2 * piece + side].wait_recv()
                    source = landing.at[step - 1]
                    added = source[...].astype(jnp.float32) + own[spot].astype(jnp.float32)
                    if step < steps:
                        source[...] = added.astype(jnp.bfloat16)
                    elif piece == 0 and chunk != 1:
                        wide_sum[max(chunk - 1, 0), side] = added
                    elif piece == 0:
                        for member in range(members):
                            widen_back[member, side] = added[
                                member * share : (member + 1) * share, :
                            ]
                    else:
                        start = side * (low // 2)
                        if chunk != 1:
                            start = start + max(chunk - 1, 0) * low
                            reduce_sum[start : start + low // 2, :] = added
                        else:
                            narrow_sum[start : start + low // 2, :] = added
                if step < steps:
                    made.append(links.copy(source, landing.at[step], target))
        moves_of[chunk, step] = made
        if step == steps and chunk == 1:
            widen_home[me] = widen_back[me]
            for peer in at.peers:
                widen_moves.append(
                    links.copy(widen_back.at[peer], widen_home.at[me], {"exp": peer})
                )
        if step == steps and chunk and chunk % 2 == 0:
            span = 64 * (chunks - 1)
            for side in range(2):
                found = joined_lanes(wide_sum[chunk - 2, side], wide_sum[chunk - 1, side])
                for index, part in enumerate(found):
                    start = index * span + (chunk - 2) * 64
                    expand_sum[side, :, start : start + 128] = part

    def tick(step, between=0):
        for chunk in (1, 0, *range(2, chunks)):
            ring_step(chunk, step)
            if chunk < between:
                advance_small()

    kept = []

    def load(source, target):
        made = pltpu.make_async_copy(source, target, local_sems.at[len(kept)])
        made.start()
        kept.append(made)

    back_moves = [
        links.copy(back_parts.at[peer], back_recv.at[me], {"exp": peer}) for peer in at.peers
    ]
    tick(0)
    result_moves = [
        [
            links.copy(result_parts.at[peer], result_recv.at[me], {"exp": peer}),
            links.copy(gate_parts.at[peer], gate_recv.at[me], {"exp": peer}),
        ]
        for peer in at.peers
    ]
    gate_recv[me] = gate_parts[me]
    load(back_parts.at[me], back_recv.at[me])
    load(result_parts.at[me], result_recv.at[me])
    load(middle_in, middle_ref)
    load(grads_in, grads_all)
    load(attend_in, attend_full)
    load(saved_in, saved)
    load(soft_in, soft_ref)
    load(wide_grads, wide_own)
    load(down_grads, down_own)
    for made in kept:
        made.wait()
    for move in back_moves:
        move.wait_recv()

    second_grad = back_recv[0].astype(jnp.float32)
    for member in range(1, members):
        second_grad = second_grad + back_recv[member].astype(jnp.float32)
    middle = middle_ref[...]
    scale = rms_factor(middle)
    gain_own[...] = jnp.zeros_like(gain_own)
    gain_own[1:2, :] = jnp.sum(second_grad * (middle * scale), axis=0, keepdims=True)
    input_grad_ref[...] = grads_all[slot_of(deal_ref, me)].astype(jnp.float32) + rms_back(
        middle, scale, second_grad * gains_full[1:2, :]
    )
    middle_low = input_grad_ref[...].astype(jnp.bfloat16)
    turned_ref[3] = nt(middle_low, attend_full[3]).astype(jnp.bfloat16)
    tick(1)
    cosines, sines = cos_ref[...], sin_ref[...]
    lower = first_half((length, 128))

    def heads(pair, carry):
        lanes = pl.ds(pl.multiple_of(pair * 128, 128), 128)
        query, key, value = saved[0, :, lanes], saved[1, :, lanes], saved[2, :, lanes]
        outer = turned_ref[3, :, lanes]
        made = []
        for side in range(2):
            soft = soft_ref[2 * pair + side]
            alone = jnp.where(lower == (side == 0), outer, jnp.zeros_like(outer))
            value_grad = tn(soft.astype(jnp.bfloat16), outer)
            soft_grad = nt(alone, value)
            score_grad = (
                soft * (soft_grad - jnp.sum(soft * soft_grad, axis=-1, keepdims=True))
            ).astype(jnp.bfloat16)
            made.append(
                (matmul(score_grad, key) * 0.125, tn(score_grad, query) * 0.125, value_grad)
            )
        for index in range(3):
            joined = jnp.where(lower, made[0][index], made[1][index])
            if index < 2:
                joined = joined * cosines - turned(joined) * sines
            turned_ref[index, :, lanes] = joined.astype(jnp.bfloat16)
        return carry

    lax.fori_loop(0, width // 128, heads, 0)
    attend_grad[3] = tn(saved[3], middle_low).astype(jnp.bfloat16)
    for matrix in range(3):
        attend_grad[matrix] = tn(saved[4], turned_ref[matrix]).astype(jnp.bfloat16)
    near_moves = [
        links.copy(attend_grad.at[matrix], near_recv.at[index], {"exp": at.near})
        for index, matrix in enumerate((at.near, at.cross))
    ]
    tick(2)
    first_grad = nt(turned_ref[0], attend_full[0])
    for matrix in range(1, 3):
        first_grad = first_grad + nt(turned_ref[matrix], attend_full[matrix])
    stream = tokens[...].astype(jnp.float32)
    scale = rms_factor(stream)
    gain_own[0:1, :] = jnp.sum(first_grad * (stream * scale), axis=0, keepdims=True)
    gain_moves = [links.copy(gain_own, gain_recv.at[me], {"exp": peer}) for peer in at.peers]
    gain_recv[me] = gain_own[...]
    input_grad_ref[...] += rms_back(stream, scale, first_grad * gains_full[0:1, :])
    for move in near_moves:
        move.wait_recv()
    far_send[...] = (
        attend_grad[at.far].astype(jnp.float32) + near_recv[1].astype(jnp.float32)
    ).astype(jnp.bfloat16)
    far_move = links.copy(far_send, far_recv, {"exp": at.far})
    tick(3)
    for moves in result_moves:
        for move in moves:
            move.wait_recv()
    output = middle_ref[...]
    for member in range(members):
        output = output + result_recv[member].astype(jnp.float32)
    output_ref[...] = output
    for choice in range(2):
        route = routes[choice : choice + 1, :]
        found = jnp.zeros((1, length), jnp.float32)
        for member in range(members):
            found = jnp.where(route == member, gate_recv[member, 0:1, :], found)
        gate_grad_ref[choice : choice + 1, :] = found
    tick(4)
    for move in gain_moves:
        move.wait_recv()
    total = gain_recv[0]
    for member in range(1, members):
        total = total + gain_recv[member]
    gain_ring[at.group] = total
    far_move.wait_recv()
    attend_total[...] = (
        attend_grad[me].astype(jnp.float32)
        + near_recv[0].astype(jnp.float32)
        + far_recv[...].astype(jnp.float32)
    ).astype(jnp.bfloat16)

    half = block // 2
    small, gain_steps = [], []

    def advance_small():
        step = len(small)
        owners = (at.owner(-1 - step), at.owner(1 + step))
        made = []
        for side, target in enumerate((at.next, at.back)):
            spot = attend_total.at[rows(owners[side] * block + side * half, half), :]
            if step:
                small[-1][side].wait_recv()
                source = attend_recv.at[side, step - 1]
                added = source[...].astype(jnp.float32) + spot[...].astype(jnp.float32)
                if step < steps:
                    source[...] = added.astype(jnp.bfloat16)
                else:
                    for member in range(members // 2):
                        attend_back[side * (members // 2) + member] = added[
                            member * share : (member + 1) * share, :
                        ]
                spot = source
            if step < steps:
                made.append(links.copy(spot, attend_recv.at[side, step], target))
        if step:
            gain_steps[-1].wait_recv()
        if step < steps:
            owner = at.owner(-step)
            gain_steps.append(links.copy(gain_ring.at[owner], gain_ring.at[owner], at.next))
        small.append(made)

    advance_small()
    for step in range(5, steps):
        tick(step, between=3)
    while len(small) <= steps:
        advance_small()
    attend_moves = [
        links.copy(attend_back.at[peer], attend_sum.at[me], {"exp": peer}) for peer in at.peers
    ]
    attend_sum[me] = attend_back[me]
    total = gain_ring[0]
    for group in range(1, groups):
        total = total + gain_ring[group]
    count = gains_sum.shape[1]
    start = (at.group * members + me) * count
    gains_sum[...] = pltpu.roll(total, width - start, 1)[0:2, 0:count]
    tick(steps)
    for move in widen_moves:
        move.wait_recv()
    for matrix in range(2):
        for member in range(0, members, 2):
            found = joined_lanes(widen_home[member, matrix], widen_home[member + 1, matrix])
            for index, part in enumerate(found):
                start = index * 64 * members + member * 64
                widen_sum[matrix, :, start : start + 128] = part
    for move in attend_moves:
        move.wait_recv()
    links.finish()


def update_kernel(rates, fixed, copies, *refs):
    count = len(rates)
    given, made = refs[: 4 * count + copies], refs[4 * count + copies :]
    for index in range(copies):
        made[index][...] = given[4 * count + index][...]

    def update(index):
        weight, moment, variance, gradient = given[4 * index : 4 * index + 4]
        grad = gradient[...]
        if len(weight.shape) < len(gradient.shape):
            grad = grad[3]
        elif weight.shape[0] < gradient.shape[0]:
            grad = grad[: weight.shape[0]]
        grad = 0.5 * grad
        level = 1.0 / (1.0 - 0.5**STEP)
        moment_new = 0.5 * moment[...] + grad
        variance_new = 0.5 * variance[...] + 2.0 * grad * grad
        kept = weight[...]
        stepped = moment_new * level / (jnp.sqrt(variance_new * level) + 1e-08) + 0.1 * kept
        made[copies + 3 * index][...] = moment_new
        made[copies + 3 * index + 1][...] = variance_new
        made[copies + 3 * index + 2][...] = kept - rates[index] * stepped

    for index in range(count):
        if fixed[index]:
            pl.when(pl.program_id(0) == 0)(functools.partial(update, index))
        else:
            update(index)


def update_all(*groups, passed):
    cuts = 8

    def spec(dims, cut):
        if cut is None:
            return pl.BlockSpec(dims, lambda step: (0,) * len(dims))
        block = tuple(size // cuts if at == cut else size for at, size in enumerate(dims))
        return pl.BlockSpec(
            block, lambda step: tuple(step if at == cut else 0 for at in range(len(dims)))
        )

    def cut_of(array):
        dims = array.shape
        for at in range(len(dims) - 1):
            if array.size > 100000 and dims[at] % (8 * cuts) == 0:
                return at
        return len(dims) - 1 if dims[-1] % (128 * cuts) == 0 else None

    given, specs, shapes, out_specs = [], [], [], []
    for _, weight, moment, variance, gradient in groups:
        cut = cut_of(weight)
        for array in (weight, moment, variance, gradient):
            given.append(array)
            specs.append(spec(array.shape, cut))
        for array in (weight, moment, variance):
            shapes.append(jax.ShapeDtypeStruct(array.shape, array.dtype))
            out_specs.append(spec(array.shape, cut))
    extra = [spec(array.shape, cut_of(array)) for array in passed]
    return pl.pallas_call(
        functools.partial(
            update_kernel,
            [group[0] for group in groups],
            [cut_of(group[1]) is None for group in groups],
            len(passed),
        ),
        grid=(cuts,),
        out_shape=[jax.ShapeDtypeStruct(array.shape, array.dtype) for array in passed] + shapes,
        in_specs=specs + extra,
        out_specs=extra + out_specs,
        compiler_params=pltpu.CompilerParams(vmem_limit_bytes=LIMIT),
    )(*given, *passed)


def rotary_lines(length):
    half = HEAD_FEATURES // 2
    freqs = np.exp(-np.log(10000.0) * np.arange(half) / half)
    angles = np.arange(length)[:, None] * freqs[None, :]
    cosines, sines = np.cos(angles), np.sin(angles)
    return (
        np.concatenate([cosines] * 4, axis=1).astype(np.float32),
        np.concatenate([-sines, sines] * 2, axis=1).astype(np.float32),
    )


def spaces(*names):
    kinds = {"v": pltpu.VMEM, "s": pltpu.SMEM, "a": pl.ANY}
    return [pl.BlockSpec(memory_space=kinds[name]) for name in "".join(names)]


def local(
    tokens,
    seq_lengths,
    deal_order,
    expert_routes,
    capacity_slots,
    gate_weights,
    cotangent,
    projector,
    projector_mean,
    projector_square,
    collector,
    collector_first_moment,
    collector_second_moment,
    widener,
    widener_mean,
    widener_square,
    narrower,
    narrower_mean,
    narrower_square,
    norm_gains,
    gains_mean,
    gains_square,
    expander,
    expander_mean,
    expander_square,
    reducer,
    reducer_mean,
    reducer_square,
):
    groups, members = lax.axis_size("grp"), lax.axis_size("exp")
    length, width = tokens.shape[1:]
    inner = expander.shape[3]
    piece = widener.shape[2] // members
    chunks = 1 + inner // piece
    capacity = 3 * length // members
    steps = groups - 1
    high, low, share = expander.shape[2], narrower.shape[0], projector.shape[1]
    bf16, f32 = jnp.bfloat16, jnp.float32
    shape = jax.ShapeDtypeStruct
    cosines, sines = (jnp.asarray(lines) for lines in rotary_lines(length))
    count = 16 * groups
    (
        wide_grads,
        down_grads,
        attend_full,
        grads_all,
        saved,
        middle,
        soft,
        gains_full,
        result_parts,
        back_parts,
        gate_parts,
    ) = pl.pallas_call(
        functools.partial(gather_kernel, groups, members),
        out_shape=[
            shape((chunks, 2, width, piece), bf16),
            shape((chunks, piece, width), bf16),
            shape((4, width, width), bf16),
            shape((members, length, width), bf16),
            shape((5, length, width), bf16),
            shape((length, width), f32),
            shape((HEAD_COUNT, length, length), f32),
            shape((8, width), f32),
            shape((members, length, width), bf16),
            shape((members, length, width), bf16),
            shape((members, 8, length), f32),
        ],
        in_specs=spaces("ss", "v" * 14),
        out_specs=spaces("a" * 7, "v" * 4),
        scratch_shapes=[
            VMEM((4, width, width), bf16),
            VMEM((members, length, width), bf16),
            VMEM((5, length, width), bf16),
            VMEM((length, width), f32),
            VMEM((HEAD_COUNT, length, length), f32),
            VMEM((members, length, width), bf16),
            VMEM((members, 8, length), f32),
            VMEM((members, 8, length), f32),
            VMEM((4, share, width), f32),
            VMEM((4, share, width), f32),
            VMEM((members, 2, share, piece), f32),
            VMEM((members, 2, share, piece), f32),
            VMEM((8, width), f32),
            VMEM((members, 8, width), f32),
            VMEM((groups, 8, width), f32),
            VMEM((chunks, 2, width, piece), bf16),
            VMEM((chunks, piece, width), bf16),
            VMEM((chunks, 2, high, piece), bf16),
            VMEM((chunks, low, width), bf16),
            VMEM((members * length, width), bf16),
            VMEM((width, members * length), bf16),
            VMEM((members, length, width), f32),
            VMEM((members, length, width), f32),
            VMEM((members * capacity, width), bf16),
            VMEM((width, members * capacity), bf16),
            VMEM((members * capacity, width), bf16),
            VMEM((members * capacity, width), f32),
            VMEM((members * capacity, width), f32),
            pltpu.SemaphoreType.DMA((count,)),
            pltpu.SemaphoreType.DMA((count,)),
            pltpu.SemaphoreType.DMA((chunks * steps * 4,)),
            pltpu.SemaphoreType.DMA((chunks * steps * 4,)),
            pltpu.SemaphoreType.DMA((2 * chunks + 5,)),
        ],
        compiler_params=pltpu.CompilerParams(
            collective_id=0, has_side_effects=True, vmem_limit_bytes=LIMIT
        ),
    )(
        seq_lengths,
        deal_order,
        tokens[0],
        cotangent[0],
        expert_routes[0].T,
        capacity_slots[0].T,
        gate_weights[0].T,
        norm_gains,
        projector,
        collector,
        widener,
        narrower,
        expander[0],
        reducer[0],
        cosines,
        sines,
    )
    count = 32 * groups
    (
        output,
        input_grad,
        gate_grad,
        expand_sum,
        reduce_sum,
        widen_sum,
        narrow_sum,
        attend_sum,
        gains_sum,
    ) = pl.pallas_call(
        functools.partial(scatter_kernel, groups, members),
        out_shape=[
            shape((length, width), f32),
            shape((length, width), f32),
            shape((2, length), f32),
            shape((2, high, inner), f32),
            shape(reducer.shape[1:], f32),
            shape(widener.shape, f32),
            shape(narrower.shape, f32),
            shape((4, share, width), f32),
            shape(norm_gains.shape, f32),
        ],
        in_specs=spaces("s", "v" * 6, "a" * 9),
        out_specs=spaces("v" * 9),
        scratch_shapes=[
            VMEM((members, length, width), bf16),
            VMEM((length, width), f32),
            VMEM((4, width, width), bf16),
            VMEM((5, length, width), bf16),
            VMEM((HEAD_COUNT, length, length), f32),
            VMEM((members, 8, length), f32),
            VMEM((members, length, width), bf16),
            VMEM((members, length, width), bf16),
            VMEM((chunks, 2, width, piece), bf16),
            VMEM((chunks, piece, width), bf16),
            VMEM((chunks, 2, steps, high, piece), bf16),
            VMEM((chunks, 2, steps, low // 2, width), bf16),
            VMEM((chunks - 1, 2, high, piece), f32),
            VMEM((4, length, width), bf16),
            VMEM((4, width, width), bf16),
            VMEM((2, width, width), bf16),
            VMEM((width, width), bf16),
            VMEM((width, width), bf16),
            VMEM((width, width), bf16),
            VMEM((2, steps, high // 2, width), bf16),
            VMEM((4, share, width), f32),
            VMEM((members, 2, share, piece), f32),
            VMEM((members, 2, share, piece), f32),
            VMEM((8, width), f32),
            VMEM((members, 8, width), f32),
            VMEM((groups, 8, width), f32),
            pltpu.SemaphoreType.DMA((count,)),
            pltpu.SemaphoreType.DMA((count,)),
            pltpu.SemaphoreType.DMA((9,)),
        ],
        compiler_params=pltpu.CompilerParams(
            collective_id=1, has_side_effects=True, vmem_limit_bytes=LIMIT
        ),
    )(
        deal_order,
        tokens[0],
        expert_routes[0].T,
        gains_full,
        cosines,
        sines,
        gate_parts,
        result_parts,
        back_parts,
        wide_grads,
        down_grads,
        grads_all,
        middle,
        attend_full,
        saved,
        soft,
    )
    updated = update_all(
        (0.1, projector, projector_mean, projector_square, attend_sum),
        (0.3, collector, collector_first_moment, collector_second_moment, attend_sum),
        (0.07, widener, widener_mean, widener_square, widen_sum),
        (0.045, narrower, narrower_mean, narrower_square, narrow_sum),
        (0.2, norm_gains, gains_mean, gains_square, gains_sum),
        (0.07, expander[0], expander_mean[0], expander_square[0], expand_sum),
        (0.045, reducer[0], reducer_mean[0], reducer_square[0], reduce_sum),
        passed=(output, input_grad),
    )
    return (
        updated[0][None],
        updated[1][None],
        gate_grad.T[None],
        *updated[2:17],
        *(found[None] for found in updated[17:]),
    )


def fits(mesh):
    groups, members = mesh.shape["grp"], mesh.shape["exp"]
    share = 64 * HEAD_COUNT // (groups * members)
    return members == 4 and groups % 2 == 0 and share % 8 == 0 and share * members // 2 % 16 == 0


def solution(mesh):
    placed = (
        P(("grp", "exp"), None, None),
        P("grp"),
        P("grp"),
        P(("grp", "exp"), None, None),
        P(("grp", "exp"), None, None),
        P(("grp", "exp"), None, None),
        P(("grp", "exp"), None, None),
        P(None, ("grp", "exp"), None),
        P(None, ("grp", "exp"), None),
        P(None, ("grp", "exp"), None),
        P(("grp", "exp"), None),
        P(("grp", "exp"), None),
        P(("grp", "exp"), None),
        P(None, ("grp", "exp"), None),
        P(None, ("grp", "exp"), None),
        P(None, ("grp", "exp"), None),
        P(("grp", "exp"), None),
        P(("grp", "exp"), None),
        P(("grp", "exp"), None),
        P(None, ("grp", "exp")),
        P(None, ("grp", "exp")),
        P(None, ("grp", "exp")),
        P("exp", None, "grp", None),
        P("exp", None, "grp", None),
        P("exp", None, "grp", None),
        P("exp", "grp", None),
        P("exp", "grp", None),
        P("exp", "grp", None),
    )
    return jax.shard_map(
        local if fits(mesh) else local_plain,
        mesh=mesh,
        in_specs=placed,
        out_specs=(
            P(("grp", "exp"), None, None),
            P(("grp", "exp"), None, None),
            P(("grp", "exp"), None, None),
            P(None, ("grp", "exp"), None),
            P(None, ("grp", "exp"), None),
            P(None, ("grp", "exp"), None),
            P(("grp", "exp"), None),
            P(("grp", "exp"), None),
            P(("grp", "exp"), None),
            P(None, ("grp", "exp"), None),
            P(None, ("grp", "exp"), None),
            P(None, ("grp", "exp"), None),
            P(("grp", "exp"), None),
            P(("grp", "exp"), None),
            P(("grp", "exp"), None),
            P(None, ("grp", "exp")),
            P(None, ("grp", "exp")),
            P(None, ("grp", "exp")),
            P("exp", None, "grp", None),
            P("exp", None, "grp", None),
            P("exp", None, "grp", None),
            P("exp", "grp", None),
            P("exp", "grp", None),
            P("exp", "grp", None),
        ),
        check_vma=False,
    )
```

```python
import functools

import jax
import jax.numpy as jnp
import numpy as np
from jax import lax
from jax.experimental import pallas as pl
from jax.experimental.pallas import tpu as pltpu
from jax.sharding import PartitionSpec as P

HEAD_COUNT = 12
HEAD_FEATURES = 64
STEP = 5


def rms_factor(values):
    return lax.rsqrt(jnp.mean(values * values, axis=-1, keepdims=True) + 1e-06)


def rms_back(values, factor, upstream):
    return factor * (
        upstream - values * factor * factor * jnp.mean(upstream * values, axis=-1, keepdims=True)
    )


def rotary(length):
    positions = jnp.arange(length, dtype=jnp.int32).astype(jnp.float32)
    half = HEAD_FEATURES // 2
    freqs = jnp.exp(
        -jnp.log(10000.0) * jnp.arange(half, dtype=jnp.int32).astype(jnp.float32) / half
    )
    angles = positions[:, None] * freqs[None, :]
    return (jnp.cos(angles)[:, None, :], jnp.sin(angles)[:, None, :])


def rotate(values, cosines, sines):
    half = values.shape[-1] // 2
    first = values[..., :half]
    second = values[..., half:]
    return jnp.concatenate(
        [first * cosines - second * sines, second * cosines + first * sines], axis=-1
    )


def rotate_back(values, cosines, sines):
    half = values.shape[-1] // 2
    first = values[..., :half]
    second = values[..., half:]
    return jnp.concatenate(
        [first * cosines + second * sines, second * cosines - first * sines], axis=-1
    )


def silu_slope(values):
    sigmoid_of = jax.nn.sigmoid(values)
    return sigmoid_of * (1.0 + values * (1.0 - sigmoid_of))


def matmul(left, right):
    return jnp.dot(left, right, preferred_element_type=jnp.float32)


def outer_sum(left, right):
    return jnp.einsum("ld,lf->df", left, right, preferred_element_type=jnp.float32)


def adamw_update(weight, moment, variance, gradient, rate):
    moment_new = 0.5 * moment + 0.5 * gradient
    variance_new = 0.5 * variance + 0.5 * gradient * gradient
    correct = 1.0 - 0.5**STEP
    stepped = moment_new / correct / (jnp.sqrt(variance_new / correct) + 1e-08) + 0.1 * weight
    return (moment_new, variance_new, weight - rate * stepped)


def local_plain(
    tokens,
    seq_lengths,
    deal_order,
    expert_routes,
    capacity_slots,
    gate_weights,
    cotangent,
    projector,
    projector_mean,
    projector_square,
    collector,
    collector_first_moment,
    collector_second_moment,
    widener,
    widener_mean,
    widener_square,
    narrower,
    narrower_mean,
    narrower_square,
    norm_gains,
    gains_mean,
    gains_square,
    expander,
    expander_mean,
    expander_square,
    reducer,
    reducer_mean,
    reducer_square,
):
    members = lax.axis_size("exp")
    member = lax.axis_index("exp")
    length_seq = tokens.shape[1]
    width = tokens.shape[2]
    local_experts = expander.shape[0]
    experts_all = local_experts * members
    capacity = 3 * length_seq // experts_all
    member_ids = jnp.arange(members, dtype=jnp.int32)
    source = deal_order[member]
    home_slot = jnp.sum(jnp.where(deal_order == member, member_ids, 0))
    seq_length = seq_lengths[source]
    piece = lax.all_gather(tokens, "exp", axis=0, tiled=True)
    chosen = jnp.arange(piece.shape[0], dtype=jnp.int32) == source
    dealt = jnp.sum(
        jnp.where(chosen[:, None, None], piece, jnp.zeros_like(piece)), axis=0, keepdims=True
    )
    residual_flow = dealt[0].astype(jnp.float32)
    project_full, collect_full, widen_full, narrow_full, gains_full = (
        lax.all_gather(projector.astype(jnp.bfloat16), ("grp", "exp"), axis=1, tiled=True),
        lax.all_gather(collector.astype(jnp.bfloat16), ("grp", "exp"), axis=0, tiled=True),
        lax.all_gather(widener.astype(jnp.bfloat16), ("grp", "exp"), axis=1, tiled=True),
        lax.all_gather(narrower.astype(jnp.bfloat16), ("grp", "exp"), axis=0, tiled=True),
        lax.all_gather(norm_gains.astype(jnp.bfloat16), ("grp", "exp"), axis=1, tiled=True),
    )
    expand_full, reduce_full = (
        lax.all_gather(expander.astype(jnp.bfloat16), "grp", axis=2, tiled=True),
        lax.all_gather(reducer.astype(jnp.bfloat16), "grp", axis=1, tiled=True),
    )
    gains_used = gains_full.astype(jnp.float32)
    cosines, sines = rotary(length_seq)
    scale_one = rms_factor(residual_flow)
    normed_one = residual_flow * scale_one
    first_input = (normed_one * gains_used[0]).astype(jnp.bfloat16)
    query_raw = matmul(first_input, project_full[0]).reshape(length_seq, HEAD_COUNT, HEAD_FEATURES)
    key_raw = matmul(first_input, project_full[1]).reshape(length_seq, HEAD_COUNT, HEAD_FEATURES)
    value_raw = matmul(first_input, project_full[2]).reshape(length_seq, HEAD_COUNT, HEAD_FEATURES)
    query_rot = rotate(query_raw, cosines, sines).astype(jnp.bfloat16)
    key_rot = rotate(key_raw, cosines, sines).astype(jnp.bfloat16)
    value_low = value_raw.astype(jnp.bfloat16)
    rows_at = jnp.arange(length_seq, dtype=jnp.int32)[:, None]
    cols_at = jnp.arange(length_seq, dtype=jnp.int32)[None, :]
    allowed = ((cols_at <= rows_at) & (cols_at < seq_length))[None]
    scores = (
        jnp.einsum("qhd,khd->hqk", query_rot, key_rot, preferred_element_type=jnp.float32) * 0.125
    )
    masked = jnp.where(allowed, scores, -1e30)
    top = jnp.max(masked, axis=-1, keepdims=True)
    expo = jnp.exp(masked - top)
    total = jnp.sum(expo, axis=-1, keepdims=True)
    soft = expo / total
    logsum = top + jnp.log(total)
    mixed_output = (
        jnp.einsum(
            "hqk,khd->qhd", soft.astype(jnp.bfloat16), value_low, preferred_element_type=jnp.float32
        )
        .reshape(length_seq, width)
        .astype(jnp.bfloat16)
    )
    middle_state = residual_flow + matmul(mixed_output, collect_full)
    scale_two = rms_factor(middle_state)
    normed_two = middle_state * scale_two
    second_input = (normed_two * gains_used[1]).astype(jnp.bfloat16)
    gating_scores = matmul(second_input, widen_full[0])
    upward_rows = matmul(second_input, widen_full[1])
    hidden_state = (jax.nn.silu(gating_scores) * upward_rows).astype(jnp.bfloat16)
    dense_branch = matmul(hidden_state, narrow_full)
    flat = (expert_routes[0] * capacity + capacity_slots[0]).reshape(-1)
    spread = jnp.repeat(second_input, 2, axis=0)
    dispatch = jnp.zeros((experts_all * capacity, width), jnp.bfloat16).at[flat].set(spread)
    dispatch = dispatch.reshape(experts_all, capacity, width)
    rows = lax.all_to_all(dispatch, "exp", split_axis=0, concat_axis=0, tiled=True)
    count = rows.shape[1]
    grouped = rows.reshape(members, local_experts, count, width)
    gate_pre = jnp.einsum(
        "sekd,edf->sekf", grouped, expand_full[:, 0], preferred_element_type=jnp.float32
    )
    up_pre = jnp.einsum(
        "sekd,edf->sekf", grouped, expand_full[:, 1], preferred_element_type=jnp.float32
    )
    hidden_rows = (jax.nn.silu(gate_pre) * up_pre).astype(jnp.bfloat16)
    result = jnp.einsum(
        "sekf,efd->sekd", hidden_rows, reduce_full, preferred_element_type=jnp.float32
    )
    result = result.astype(jnp.bfloat16).reshape(members * local_experts, count, width)
    returned_rows = lax.all_to_all(result, "exp", split_axis=0, concat_axis=0, tiled=True)
    outcome = (
        returned_rows,
        rows,
        gate_pre.reshape(members * local_experts, count, -1),
        up_pre.reshape(members * local_experts, count, -1),
    )
    returned, received, gate_kept, up_kept = outcome
    picked = (
        returned.reshape(experts_all * capacity, width)[flat]
        .reshape(length_seq, 2, width)
        .astype(jnp.float32)
    )
    gate_local = gate_weights[0]
    mixture = jnp.sum(gate_local[..., None] * picked, axis=1)
    layer_output = middle_state + dense_branch + mixture
    valid = (jnp.arange(length_seq, dtype=jnp.int32) < seq_length).astype(jnp.float32)
    grad_out = cotangent[0] * valid[:, None]
    grad_low = grad_out.astype(jnp.bfloat16)
    narrow_grad = outer_sum(hidden_state, grad_low)
    hidden_grad = jnp.einsum("ld,fd->lf", grad_low, narrow_full, preferred_element_type=jnp.float32)
    gating_grad = (hidden_grad * upward_rows * silu_slope(gating_scores)).astype(jnp.bfloat16)
    upward_grad = (hidden_grad * jax.nn.silu(gating_scores)).astype(jnp.bfloat16)
    widen_grad = jnp.stack(
        [outer_sum(second_input, gating_grad), outer_sum(second_input, upward_grad)]
    )
    second_grad = jnp.einsum(
        "lf,df->ld", gating_grad, widen_full[0], preferred_element_type=jnp.float32
    ) + jnp.einsum("lf,df->ld", upward_grad, widen_full[1], preferred_element_type=jnp.float32)
    gate_grad_local = jnp.sum(grad_out[:, None, :] * picked, axis=-1)
    result_grad = (
        (gate_local[..., None] * grad_out[:, None, :])
        .astype(jnp.bfloat16)
        .reshape(2 * length_seq, width)
    )
    grad_send = jnp.zeros((experts_all * capacity, width), jnp.bfloat16).at[flat].set(result_grad)
    grad_recv = lax.all_to_all(
        grad_send.reshape(experts_all, capacity, width),
        "exp",
        split_axis=0,
        concat_axis=0,
        tiled=True,
    )
    grad_group = grad_recv.reshape(members, local_experts, capacity, width)
    rows_group = received.reshape(members, local_experts, capacity, width)
    gate_pre = gate_kept.reshape(members, local_experts, capacity, -1)
    up_pre = up_kept.reshape(members, local_experts, capacity, -1)
    hidden_rows = (jax.nn.silu(gate_pre) * up_pre).astype(jnp.bfloat16)
    reduce_grad = jnp.einsum(
        "sekf,sekd->efd", hidden_rows, grad_group, preferred_element_type=jnp.float32
    )
    hidden_rows_grad = jnp.einsum(
        "sekd,efd->sekf", grad_group, reduce_full, preferred_element_type=jnp.float32
    )
    gate_rows_grad = (hidden_rows_grad * up_pre * silu_slope(gate_pre)).astype(jnp.bfloat16)
    up_rows_grad = (hidden_rows_grad * jax.nn.silu(gate_pre)).astype(jnp.bfloat16)
    expand_grad = jnp.stack(
        [
            jnp.einsum(
                "sekd,sekf->edf", rows_group, gate_rows_grad, preferred_element_type=jnp.float32
            ),
            jnp.einsum(
                "sekd,sekf->edf", rows_group, up_rows_grad, preferred_element_type=jnp.float32
            ),
        ],
        axis=1,
    )
    row_grads = jnp.einsum(
        "sekf,edf->sekd", gate_rows_grad, expand_full[:, 0], preferred_element_type=jnp.float32
    ) + jnp.einsum(
        "sekf,edf->sekd", up_rows_grad, expand_full[:, 1], preferred_element_type=jnp.float32
    )
    row_grads = row_grads.astype(jnp.bfloat16).reshape(experts_all, capacity, width)
    came_back = lax.all_to_all(row_grads, "exp", split_axis=0, concat_axis=0, tiled=True).reshape(
        experts_all * capacity, width
    )
    second_grad = second_grad + jnp.sum(
        came_back[flat].reshape(length_seq, 2, width).astype(jnp.float32), axis=1
    )
    gains_grad_two = jnp.sum(second_grad * normed_two, axis=0)
    middle_grad = grad_out + rms_back(middle_state, scale_two, second_grad * gains_used[1])
    middle_low = middle_grad.astype(jnp.bfloat16)
    collect_grad = outer_sum(mixed_output, middle_low)
    mixed_grad = jnp.einsum(
        "ld,ed->le", middle_low, collect_full, preferred_element_type=jnp.float32
    )
    mixed_grad = mixed_grad.astype(jnp.bfloat16).reshape(length_seq, HEAD_COUNT, HEAD_FEATURES)
    scores_again = (
        jnp.einsum("qhd,khd->hqk", query_rot, key_rot, preferred_element_type=jnp.float32) * 0.125
    )
    soft_again = jnp.where(allowed, jnp.exp(scores_again - logsum), 0.0)
    value_grad = jnp.einsum(
        "hqk,qhd->khd",
        soft_again.astype(jnp.bfloat16),
        mixed_grad,
        preferred_element_type=jnp.float32,
    )
    soft_grad = jnp.einsum(
        "qhd,khd->hqk", mixed_grad, value_low, preferred_element_type=jnp.float32
    )
    score_grad = (
        soft_again * (soft_grad - jnp.sum(soft_again * soft_grad, axis=-1, keepdims=True))
    ).astype(jnp.bfloat16)
    query_grad = (
        jnp.einsum("hqk,khd->qhd", score_grad, key_rot, preferred_element_type=jnp.float32) * 0.125
    )
    key_grad = (
        jnp.einsum("hqk,qhd->khd", score_grad, query_rot, preferred_element_type=jnp.float32)
        * 0.125
    )
    query_back = (
        rotate_back(query_grad, cosines, sines).reshape(length_seq, width).astype(jnp.bfloat16)
    )
    key_back = rotate_back(key_grad, cosines, sines).reshape(length_seq, width).astype(jnp.bfloat16)
    value_back = value_grad.reshape(length_seq, width).astype(jnp.bfloat16)
    project_grad = jnp.stack(
        [
            outer_sum(first_input, query_back),
            outer_sum(first_input, key_back),
            outer_sum(first_input, value_back),
        ]
    )
    first_grad = (
        jnp.einsum("le,de->ld", query_back, project_full[0], preferred_element_type=jnp.float32)
        + jnp.einsum("le,de->ld", key_back, project_full[1], preferred_element_type=jnp.float32)
        + jnp.einsum("le,de->ld", value_back, project_full[2], preferred_element_type=jnp.float32)
    )
    gains_grad_one = jnp.sum(first_grad * normed_one, axis=0)
    stream_grad = middle_grad + rms_back(residual_flow, scale_one, first_grad * gains_used[0])
    gains_grad = jnp.stack([gains_grad_one, gains_grad_two])
    project_part, collect_part, widen_part, narrow_part, gains_part = (
        lax.psum_scatter(project_grad, ("grp", "exp"), scatter_dimension=1, tiled=True),
        lax.psum_scatter(collect_grad, ("grp", "exp"), scatter_dimension=0, tiled=True),
        lax.psum_scatter(widen_grad, ("grp", "exp"), scatter_dimension=1, tiled=True),
        lax.psum_scatter(narrow_grad, ("grp", "exp"), scatter_dimension=0, tiled=True),
        lax.psum_scatter(gains_grad, ("grp", "exp"), scatter_dimension=1, tiled=True),
    )
    expand_part, reduce_part = (
        lax.psum_scatter(
            expand_grad.astype(jnp.bfloat16), "grp", scatter_dimension=2, tiled=True
        ).astype(jnp.float32),
        lax.psum_scatter(
            reduce_grad.astype(jnp.bfloat16), "grp", scatter_dimension=1, tiled=True
        ).astype(jnp.float32),
    )
    empty = jnp.zeros((1, length_seq, width), jnp.float32)
    pieces = (
        lax.all_gather(layer_output[None].astype(jnp.bfloat16), "exp", axis=0, tiled=True).astype(
            jnp.float32
        ),
        lax.all_gather(stream_grad[None].astype(jnp.bfloat16), "exp", axis=0, tiled=True).astype(
            jnp.float32
        ),
    )
    chosen = (jnp.arange(pieces[0].shape[0], dtype=jnp.int32) == home_slot)[:, None, None]
    homed_output = empty + jnp.sum(jnp.where(chosen, pieces[0], 0.0), axis=0, keepdims=True)
    homed_grad = empty + jnp.sum(jnp.where(chosen, pieces[1], 0.0), axis=0, keepdims=True)
    project_new = adamw_update(projector, projector_mean, projector_square, project_part, 0.1)
    collect_new = adamw_update(
        collector, collector_first_moment, collector_second_moment, collect_part, 0.3
    )
    widening_updated = adamw_update(widener, widener_mean, widener_square, widen_part, 0.07)
    narrowing_updated = adamw_update(narrower, narrower_mean, narrower_square, narrow_part, 0.045)
    gains_updated = adamw_update(norm_gains, gains_mean, gains_square, gains_part, 0.2)
    expansion_updated = adamw_update(expander, expander_mean, expander_square, expand_part, 0.07)
    reduction_updated = adamw_update(reducer, reducer_mean, reducer_square, reduce_part, 0.045)
    return (
        homed_output,
        homed_grad,
        gate_grad_local[None],
        project_new[0],
        project_new[1],
        project_new[2],
        collect_new[0],
        collect_new[1],
        collect_new[2],
        widening_updated[0],
        widening_updated[1],
        widening_updated[2],
        narrowing_updated[0],
        narrowing_updated[1],
        narrowing_updated[2],
        gains_updated[0],
        gains_updated[1],
        gains_updated[2],
        expansion_updated[0],
        expansion_updated[1],
        expansion_updated[2],
        reduction_updated[0],
        reduction_updated[1],
        reduction_updated[2],
    )


MESH = pl.DeviceIdType.MESH
VMEM = pltpu.VMEM
LIMIT = 60 * 1024 * 1024


def ring_place(index, groups):
    row, side = lax.div(index, 2), lax.rem(index, 2)
    return (1 - side) * row + side * (groups - 1 - row)


def ring_member(place, groups):
    side = lax.div(place, groups // 2)
    return 2 * ((1 - side) * place + side * (groups - 1 - place)) + side


def remote(source, target, sends, arrivals, at, device):
    return pltpu.make_async_remote_copy(
        src_ref=source,
        dst_ref=target,
        send_sem=sends.at[at],
        recv_sem=arrivals.at[at],
        device_id=device,
        device_id_type=MESH,
    )


class Links:
    def __init__(self, sends, arrivals):
        self.sends, self.arrivals, self.count, self.started = sends, arrivals, 0, []

    def copy(self, source, target, device):
        made = remote(source, target, self.sends, self.arrivals, self.count, device)
        self.count += 1
        made.start()
        self.started.append(made)
        return made

    def finish(self):
        for made in self.started:
            made.wait_send()


class Places:
    def __init__(self, groups, members):
        self.groups, self.members = groups, members
        self.group = lax.axis_index("grp")
        self.member = lax.axis_index("exp")
        self.place = ring_place(self.group, groups)
        self.next = {"grp": self.owner(1)}
        self.back = {"grp": self.owner(-1)}
        half = members // 2
        self.far = lax.rem(self.member + half, members)
        self.near = self.member + 1 - 2 * lax.rem(self.member, 2)
        self.cross = lax.rem(self.near + half, members)
        self.peers = [lax.rem(self.member + step, members) for step in range(1, members)]

    def owner(self, offset):
        place = lax.rem(self.place + offset + 2 * self.groups, self.groups)
        return ring_member(place, self.groups)

    def enter(self):
        barrier = pltpu.get_barrier_semaphore()
        partners = [self.next, self.back] + [{"exp": peer} for peer in self.peers]
        for partner in partners:
            pl.semaphore_signal(barrier, inc=1, device_id=partner, device_id_type=MESH)
        pl.semaphore_wait(barrier, len(partners))


def rows(start, count, align=16):
    return pl.ds(pl.multiple_of(start, align), count)


def first_half(shape):
    return lax.rem(lax.broadcasted_iota(jnp.int32, shape, len(shape) - 1), 128) < 64


def turned(values):
    lanes = lax.broadcasted_iota(jnp.int32, values.shape, 1)
    return jnp.where(
        lax.rem(lanes, HEAD_FEATURES) < HEAD_FEATURES // 2,
        pltpu.roll(values, 128 - HEAD_FEATURES // 2, 1),
        pltpu.roll(values, HEAD_FEATURES // 2, 1),
    )


def nt(left, right):
    return lax.dot_general(
        left, right, (((1,), (1,)), ((), ())), preferred_element_type=jnp.float32
    )


def tn(left, right):
    return lax.dot_general(
        left, right, (((0,), (0,)), ((), ())), preferred_element_type=jnp.float32
    )


def sigmoid(values):
    return 1.0 / (1.0 + jnp.exp(-values))


def same(length):
    shape = (length, length)
    return lax.broadcasted_iota(jnp.int32, shape, 0) == lax.broadcasted_iota(jnp.int32, shape, 1)


def upright(line):
    return jnp.sum(jnp.where(same(line.shape[1]), line, 0.0), axis=1, keepdims=True)


def lying(column):
    return jnp.sum(jnp.where(same(column.shape[0]), column, 0.0), axis=0, keepdims=True)


def slot_of(deal_ref, member):
    for _ in range(11):
        member = deal_ref[member]
    return member


def dealt_lanes(values, piece, pieces):
    low_lanes = lax.broadcasted_iota(jnp.int32, (values.shape[0], 128), 1) < 64
    found = []
    span = 64 * pieces
    for start in range(0, values.shape[1], 2 * span):
        start = start + piece // 2 * 128
        one, two = values[:, start : start + 128], values[:, start + span : start + span + 128]
        if piece % 2:
            one = pltpu.roll(one, 64, 1)
        else:
            two = pltpu.roll(two, 64, 1)
        found.append(jnp.where(low_lanes, one, two))
    return jnp.concatenate(found, axis=1)


def joined_lanes(even, odd):
    low_lanes = lax.broadcasted_iota(jnp.int32, (even.shape[0], 128), 1) < 64
    found = []
    for start in range(0, even.shape[1], 128):
        one, two = even[:, start : start + 128], odd[:, start : start + 128]
        found.append(jnp.where(low_lanes, one, pltpu.roll(two, 64, 1)))
        found.append(jnp.where(low_lanes, pltpu.roll(one, 64, 1), two))
    return found


def gather_kernel(
    groups,
    members,
    length_ref,
    deal_ref,
    tokens,
    cotangent,
    routes,
    places,
    gates,
    norm_gains,
    projector,
    collector,
    widener,
    narrower,
    expander,
    reducer,
    cos_ref,
    sin_ref,
    wide_grads,
    down_grads,
    wide_first,
    down_first,
    attend_out,
    grads_out,
    saved_out,
    middle_out,
    soft_out,
    gains_full,
    result_ref,
    back_ref,
    gate_ref,
    attend_full,
    grads_all,
    saved,
    middle_ref,
    soft_ref,
    second_all,
    meta_send,
    meta_all,
    attend_send,
    attend_recv,
    widen_send,
    widen_recv,
    gains,
    gain_recv,
    gain_ring,
    wide_full,
    down_full,
    wide_own,
    down_own,
    inputs_ref,
    inputs_turned,
    dense_out,
    dense_back,
    rows_in,
    rows_turned,
    rows_grad,
    rows_out,
    rows_back,
    sends,
    arrivals,
    ring_sends,
    ring_arrivals,
    first_sends,
    first_arrivals,
    local_sems,
):
    at = Places(groups, members)
    links = Links(sends, arrivals)
    at.enter()
    me, steps = at.member, groups - 1
    share, width = projector.shape[1:]
    block = share * members
    length = tokens.shape[0]
    chunks, low = down_own.shape[:2]
    capacity = rows_in.shape[0] // members

    def ring_copy(chunk, step, side, piece):
        owner = at.owner(-step if side == 0 else step)
        if piece == 0:
            spot = wide_full.at[chunk, side, rows(owner * block, block), :]
            origin = wide_own.at[chunk, side]
        else:
            spot = down_full.at[chunk, rows(owner * low + side * (low // 2), low // 2), :]
            origin = down_own.at[chunk, pl.ds(side * (low // 2), low // 2), :]
        place = (chunk * steps + step) * 4 + side * 2 + piece
        return remote(
            spot if step else origin,
            spot,
            ring_sends,
            ring_arrivals,
            place,
            (at.next, at.back)[side],
        )

    def ring_step(chunk, step):
        for piece in range(2):
            for side in range(2):
                if step:
                    ring_copy(chunk, step - 1, side, piece).wait_recv()
                if step < steps:
                    ring_copy(chunk, step, side, piece).start()

    def tick(count):
        for chunk in range(chunks):
            if 0 <= count - 2 * chunk <= steps:
                ring_step(chunk, count - 2 * chunk)

    attend_send[0:3] = projector[...]
    attend_send[3] = collector[...]
    gains[...] = jnp.zeros_like(gains)
    gains[0:2, 0 : norm_gains.shape[1]] = norm_gains[...]
    gains[...] = pltpu.roll(gains[...], (at.group * members + me) * norm_gains.shape[1], 1)
    first_moves = [
        [
            links.copy(attend_send.at[peer], attend_recv.at[me], {"exp": peer}),
            links.copy(gains, gain_recv.at[me], {"exp": peer}),
        ]
        for peer in at.peers
    ]
    gain_recv[me] = gains[...]
    attend_recv[me] = attend_send[me]
    for matrix in range(2):
        for member in range(members):
            widen_send[member, matrix] = dealt_lanes(widener[matrix], member, members)
    widen_moves = [
        links.copy(widen_send.at[peer], widen_recv.at[me], {"exp": peer}) for peer in at.peers
    ]
    widen_recv[me] = widen_send[me]

    def stage(chunk):
        if chunk == 1:
            for matrix in range(2):
                wide_own[1, matrix] = jnp.concatenate(
                    [widen_recv[member, matrix] for member in range(members)], axis=0
                ).astype(jnp.bfloat16)
            down_own[1] = narrower[...].astype(jnp.bfloat16)
        else:
            index = max(chunk - 1, 0)
            for matrix in range(2):
                wide_own[chunk, matrix] = dealt_lanes(
                    expander[matrix], index, chunks - 1
                ).astype(jnp.bfloat16)
            down_own[chunk] = reducer[index * low : (index + 1) * low, :].astype(jnp.bfloat16)
        for side in range(2):
            wide_full[chunk, side, rows(at.group * block, block), :] = wide_own[chunk, side]
        down_full[chunk, rows(at.group * low, low), :] = down_own[chunk]

    stage(0)
    tick(0)
    for moves in first_moves:
        for move in moves:
            move.wait_recv()
    attend_full[me, rows(at.group * block, block), :] = (
        attend_recv[...].reshape(block, width).astype(jnp.bfloat16)
    )
    total_gain = gain_recv[0]
    for member in range(1, members):
        total_gain = total_gain + gain_recv[member]
    gain_ring[at.group] = total_gain

    half = block // 2

    def unit(owner, side, matrix):
        return attend_full.at[matrix, rows(owner * block + side * half, half), :]

    def across(owner, side):
        spot = unit(owner, side, me)
        return (links.copy(spot, spot, {"exp": at.far}), links.copy(spot, spot, {"exp": at.near}))

    def onward(owner, side):
        spot = unit(owner, side, at.far)
        return links.copy(spot, spot, {"exp": at.near})

    ring, crossed, passed = [], [], []
    gain_moves = []
    for step in range(groups):
        owners = (at.owner(-step), at.owner(step))
        if step:
            for move in ring[-1]:
                move.wait_recv()
            gain_moves[-1].wait_recv()
        if step < steps:
            ring.append(
                [
                    links.copy(unit(owner, side, me), unit(owner, side, me), target)
                    for side, (owner, target) in enumerate(zip(owners, (at.next, at.back)))
                ]
            )
            gain_moves.append(
                links.copy(gain_ring.at[owners[0]], gain_ring.at[owners[0]], at.next)
            )
        crossed.append([across(owner, side) for side, owner in enumerate(owners)])
        if step:
            for side, owner in enumerate((at.owner(1 - step), at.owner(step - 1))):
                crossed[step - 1][side][0].wait_recv()
                passed.append(onward(owner, side))
        if step == 2:
            for move in widen_moves:
                move.wait_recv()
            for chunk in range(1, chunks):
                stage(chunk)
        if step % 2:
            tick(step // 2 + 1)
    outgoing = []

    def hand_out(source, target):
        made = pltpu.make_async_copy(
            source, target, local_sems.at[2 * chunks + len(outgoing)]
        )
        made.start()
        outgoing.append(made)

    valid = lax.broadcasted_iota(jnp.int32, (length, 1), 0) < length_ref[deal_ref[me]]
    grads_all[me] = jnp.where(valid, cotangent[...], 0.0).astype(jnp.bfloat16)
    route = [routes[choice : choice + 1, :] for choice in range(2)]
    place = [places[choice : choice + 1, :].astype(jnp.float32) for choice in range(2)]
    meta_send[...] = jnp.zeros_like(meta_send)
    for member in range(members):
        named = [chosen == member for chosen in route]
        meta_send[member, 0:1, :] = jnp.where(
            named[0], place[0], jnp.where(named[1], place[1], -1.0)
        )
        meta_send[member, 1:2, :] = jnp.where(
            named[0], gates[0:1, :], jnp.where(named[1], gates[1:2, :], 0.0)
        )
    meta_all[me] = meta_send[me]
    grad_moves = [
        [
            links.copy(grads_all.at[me], grads_all.at[me], {"exp": peer}),
            links.copy(meta_send.at[peer], meta_all.at[me], {"exp": peer}),
        ]
        for peer in at.peers
    ]
    for side, owner in enumerate((at.owner(-steps), at.owner(steps))):
        crossed[steps][side][0].wait_recv()
        passed.append(onward(owner, side))
    total_gain = gain_ring[0]
    for group in range(1, groups):
        total_gain = total_gain + gain_ring[group]
    gains_full[...] = total_gain.astype(jnp.bfloat16).astype(jnp.float32)
    stream = tokens[...].astype(jnp.float32)
    first_input = (stream * rms_factor(stream) * gains_full[0:1, :]).astype(jnp.bfloat16)
    saved[4] = first_input
    for moves in crossed:
        for move in moves:
            move[1].wait_recv()
    for move in passed:
        move.wait_recv()
    tick(5)
    hand_out(attend_full, attend_out)

    cosines, sines = cos_ref[...], sin_ref[...]
    for matrix in range(3):
        raw = matmul(first_input, attend_full[matrix])
        if matrix == 2:
            saved[2] = raw.astype(jnp.bfloat16)
        else:
            for start in range(0, width, 128):
                piece = raw[:, start : start + 128]
                saved[matrix, :, start : start + 128] = (
                    piece * cosines + turned(piece) * sines
                ).astype(jnp.bfloat16)
    tick(6)

    seq_length = length_ref[me]
    rows_at = lax.broadcasted_iota(jnp.int32, (length, length), 0)
    cols_at = lax.broadcasted_iota(jnp.int32, (length, length), 1)
    allowed = (cols_at <= rows_at) & (cols_at < seq_length)
    lower = first_half((length, 128))

    def heads(pair, carry):
        lanes = pl.ds(pl.multiple_of(pair * 128, 128), 128)
        query, key, value = saved[0, :, lanes], saved[1, :, lanes], saved[2, :, lanes]
        results = []
        for side in range(2):
            alone = jnp.where(lower == (side == 0), query, jnp.zeros_like(query))
            scores = jnp.where(allowed, nt(alone, key) * 0.125, -1e30)
            expo = jnp.exp(scores - jnp.max(scores, axis=-1, keepdims=True))
            soft = expo / jnp.sum(expo, axis=-1, keepdims=True)
            soft_ref[2 * pair + side] = soft
            results.append(matmul(soft.astype(jnp.bfloat16), value))
        saved[3, :, lanes] = jnp.where(lower, results[0], results[1]).astype(jnp.bfloat16)
        return carry

    lax.fori_loop(0, width // 128, heads, 0)
    hand_out(saved, saved_out)
    hand_out(soft_ref, soft_out)
    middle = tokens[...].astype(jnp.float32) + matmul(saved[3], attend_full[3])
    middle_ref[...] = middle
    hand_out(middle_ref, middle_out)
    second_all[me] = (middle * rms_factor(middle) * gains_full[1:2, :]).astype(jnp.bfloat16)
    second_moves = [
        links.copy(second_all.at[me], second_all.at[me], {"exp": peer}) for peer in at.peers
    ]
    for moves in grad_moves:
        for move in moves:
            move.wait_recv()
    hand_out(grads_all, grads_out)
    tick(7)

    def hits(slot, by_row):
        line = meta_all[slot, 0:1, :]
        if by_row:
            names = lax.broadcasted_iota(jnp.int32, (capacity, length), 0).astype(jnp.float32)
            hit = names == line
        else:
            names = lax.broadcasted_iota(jnp.int32, (length, capacity), 1).astype(jnp.float32)
            hit = names == upright(line)
        return jnp.where(hit, 1.0, 0.0).astype(jnp.bfloat16)

    def spot_of(slot):
        return slice(slot * capacity, (slot + 1) * capacity)

    def here_of(slot):
        return slice(slot * length, (slot + 1) * length)

    for slot in range(members):
        pick = hits(slot, True)
        gate = jnp.sum(pick.astype(jnp.float32) * meta_all[slot, 1:2, :], axis=1, keepdims=True)
        rows_grad[spot_of(slot), :] = (matmul(pick, grads_all[slot]) * gate).astype(jnp.bfloat16)
    for move in second_moves:
        move.wait_recv()
    for slot in range(members):
        inputs_ref[here_of(slot), :] = second_all[deal_ref[slot]]
        rows_in[spot_of(slot), :] = matmul(hits(slot, True), inputs_ref[here_of(slot), :]).astype(
            jnp.bfloat16
        )
    inputs_turned[...] = inputs_ref[...].T
    rows_turned[...] = rows_in[...].T
    dense_out[...] = jnp.zeros_like(dense_out)
    dense_back[...] = jnp.zeros_like(dense_back)
    rows_out[...] = jnp.zeros_like(rows_out)
    rows_back[...] = jnp.zeros_like(rows_back)

    def branch(chunk, inputs, turned_inputs, outer, out, back):
        for step in range(steps):
            for side in range(2):
                for piece in range(2):
                    ring_copy(chunk, step, side, piece).wait_send()

        def part(index, carry):
            lanes = pl.ds(pl.multiple_of(index * 256, 256), 256)
            gate = matmul(inputs[...], wide_full[chunk, 0, :, lanes])
            up = matmul(inputs[...], wide_full[chunk, 1, :, lanes])
            rise = sigmoid(gate)
            smooth = gate * rise
            hidden = (smooth * up).astype(jnp.bfloat16)
            hidden_grad = nt(outer[...], down_full[chunk, lanes, :])
            gate_grad = (hidden_grad * up * (rise * (1.0 + gate * (1.0 - rise)))).astype(
                jnp.bfloat16
            )
            up_grad = (hidden_grad * smooth).astype(jnp.bfloat16)
            out[...] += matmul(hidden, down_full[chunk, lanes, :])
            back[...] += nt(gate_grad, wide_full[chunk, 0, :, lanes]) + nt(
                up_grad, wide_full[chunk, 1, :, lanes]
            )
            down_full[chunk, lanes, :] = tn(hidden, outer[...]).astype(jnp.bfloat16)
            wide_full[chunk, 0, :, lanes] = matmul(turned_inputs[...], gate_grad).astype(
                jnp.bfloat16
            )
            wide_full[chunk, 1, :, lanes] = matmul(turned_inputs[...], up_grad).astype(
                jnp.bfloat16
            )
            return carry

        lax.fori_loop(0, down_full.shape[1] // 256, part, 0)
        kept(chunk, 0).start()
        kept(chunk, 1).start()

    def kept(chunk, piece):
        source, target = ((wide_full, wide_grads), (down_full, down_grads))[piece]
        return pltpu.make_async_copy(
            source.at[chunk], target.at[chunk], local_sems.at[2 * chunk + piece]
        )

    outer_all = grads_all.reshape(members * length, width)
    flat = (members * length, width)
    dense = (
        inputs_ref,
        inputs_turned,
        outer_all,
        dense_out.reshape(flat),
        dense_back.reshape(flat),
    )

    def first_sum(chunk, side, piece):
        owner = at.owner(-1 if side == 0 else 1)
        if piece == 0:
            spot = wide_full.at[chunk, side, rows(owner * block, block), :]
        else:
            spot = down_full.at[chunk, rows(owner * low + side * (low // 2), low // 2), :]
        return remote(
            spot,
            (wide_first, down_first)[piece].at[chunk, side],
            first_sends,
            first_arrivals,
            chunk * 4 + side * 2 + piece,
            (at.next, at.back)[side],
        )

    def start_sums(chunk):
        for piece in range(2):
            for side in range(2):
                first_sum(chunk, side, piece).start()

    def next_chunk(chunk, carry):
        for last in (steps - 1, steps):
            for ahead in range(groups // 2):
                @pl.when((chunk > 0) & (chunk + ahead < chunks))
                def _():
                    ring_step(chunk + ahead, last - 2 * ahead)

        @pl.when(chunk == chunks - 1)
        def _():
            for early in range(chunks - 1):
                start_sums(early)

        @pl.when(chunk == 1)
        def _():
            branch(chunk, *dense)

        @pl.when(chunk != 1)
        def _():
            branch(chunk, rows_in, rows_turned, rows_grad, rows_out, rows_back)

        return carry

    lax.fori_loop(0, chunks, next_chunk, 0)
    start_sums(chunks - 1)

    for slot in range(members):
        pick = hits(slot, False)
        gate = upright(meta_all[slot, 1:2, :])
        picked = matmul(pick, rows_out[spot_of(slot), :].astype(jnp.bfloat16))
        inner = rows_back[spot_of(slot), :].astype(jnp.bfloat16)
        dense_out[slot] += gate * picked
        dense_back[slot] += matmul(pick, inner)
        score = jnp.sum(picked * grads_all[slot].astype(jnp.float32), axis=1, keepdims=True)
        gate_ref[slot] = jnp.broadcast_to(lying(score), gate_ref.shape[1:])
    for member in range(members):
        home = slot_of(deal_ref, member)
        result_ref[member] = dense_out[home].astype(jnp.bfloat16)
        back_ref[member] = dense_back[home].astype(jnp.bfloat16)
    for chunk in range(chunks):
        kept(chunk, 0).wait()
        kept(chunk, 1).wait()
        for piece in range(2):
            for side in range(2):
                first_sum(chunk, side, piece).wait()
    for made in outgoing:
        made.wait()
    links.finish()


def scatter_kernel(
    groups,
    members,
    deal_ref,
    tokens,
    routes,
    gains_full,
    cos_ref,
    sin_ref,
    gate_parts,
    result_parts,
    back_parts,
    wide_grads,
    down_grads,
    wide_first,
    down_first,
    grads_in,
    middle_in,
    attend_in,
    saved_in,
    soft_in,
    output_ref,
    input_grad_ref,
    gate_grad_ref,
    expand_sum,
    reduce_sum,
    widen_sum,
    narrow_sum,
    project_sum,
    collect_sum,
    gains_sum,
    attend_sum,
    grads_all,
    middle_ref,
    attend_full,
    saved,
    soft_ref,
    gate_recv,
    result_recv,
    back_recv,
    wide_own,
    down_own,
    wide_recv,
    down_recv,
    wide_sum,
    turned_ref,
    attend_grad,
    near_recv,
    far_recv,
    far_send,
    attend_total,
    attend_recv,
    attend_back,
    widen_back,
    widen_home,
    gain_own,
    gain_recv,
    gain_ring,
    sends,
    arrivals,
    local_sems,
):
    at = Places(groups, members)
    links = Links(sends, arrivals)
    at.enter()
    me, steps = at.member, groups - 1
    length, width = tokens.shape
    chunks, low = down_own.shape[0], narrow_sum.shape[0]
    share = attend_sum.shape[1]
    block = share * members

    moves_of = {}
    widen_moves = []

    def ring_step(chunk, step):
        made = []
        owners = (at.owner(-1 - step), at.owner(1 + step))
        for piece in range(2):
            for side, target in enumerate((at.next, at.back)):
                own = (wide_own, down_own)[piece]
                landing = (wide_recv, down_recv)[piece].at[chunk, side]
                if piece == 0:
                    spot = (chunk, side, rows(owners[side] * block, block))
                else:
                    spot = (chunk, rows(owners[side] * low + side * (low // 2), low // 2))
                if step > 1:
                    moves_of[chunk, step - 1][2 * piece + side].wait_recv()
                source = landing.at[step - 1]
                added = source[...].astype(jnp.float32) + own[spot].astype(jnp.float32)
                if step < steps:
                    source[...] = added.astype(jnp.bfloat16)
                elif piece == 0 and chunk != 1:
                    wide_sum[max(chunk - 1, 0), side] = added
                elif piece == 0:
                    for member in range(members):
                        widen_back[member, side] = added[member * share : (member + 1) * share, :]
                else:
                    start = side * (low // 2)
                    if chunk != 1:
                        start = start + max(chunk - 1, 0) * low
                        reduce_sum[start : start + low // 2, :] = added
                    else:
                        narrow_sum[start : start + low // 2, :] = added
                if step < steps:
                    made.append(links.copy(source, landing.at[step], target))
        moves_of[chunk, step] = made
        if step == steps and chunk == 1:
            widen_home[me] = widen_back[me]
            for peer in at.peers:
                widen_moves.append(
                    links.copy(widen_back.at[peer], widen_home.at[me], {"exp": peer})
                )
        if step == steps and chunk and chunk % 2 == 0:
            span = 64 * (chunks - 1)
            for side in range(2):
                found = joined_lanes(wide_sum[chunk - 2, side], wide_sum[chunk - 1, side])
                for index, part in enumerate(found):
                    start = index * span + (chunk - 2) * 64
                    expand_sum[side, :, start : start + 128] = part

    def tick(step, between=0):
        for chunk in (1, 0, *range(2, chunks)):
            ring_step(chunk, step)
            if chunk < between:
                advance_small()

    kept = []

    def load(source, target):
        made = pltpu.make_async_copy(source, target, local_sems.at[len(kept)])
        made.start()
        kept.append(made)

    load(wide_first, wide_recv.at[:, :, 0])
    load(down_first, down_recv.at[:, :, 0])
    load(wide_grads, wide_own)
    load(down_grads, down_own)
    back_moves = [
        links.copy(back_parts.at[peer], back_recv.at[me], {"exp": peer}) for peer in at.peers
    ]
    load(back_parts.at[me], back_recv.at[me])
    load(middle_in, middle_ref)
    load(grads_in, grads_all)
    load(attend_in, attend_full)
    load(saved_in, saved)
    load(soft_in, soft_ref)
    load(result_parts.at[me], result_recv.at[me])
    gate_recv[me] = gate_parts[me]
    for made in kept[:4]:
        made.wait()
    tick(1)
    result_moves = [
        [
            links.copy(result_parts.at[peer], result_recv.at[me], {"exp": peer}),
            links.copy(gate_parts.at[peer], gate_recv.at[me], {"exp": peer}),
        ]
        for peer in at.peers
    ]
    for made in kept[4:]:
        made.wait()
    for move in back_moves:
        move.wait_recv()

    second_grad = back_recv[0].astype(jnp.float32)
    for member in range(1, members):
        second_grad = second_grad + back_recv[member].astype(jnp.float32)
    middle = middle_ref[...]
    scale = rms_factor(middle)
    gain_own[...] = jnp.zeros_like(gain_own)
    gain_own[1:2, :] = jnp.sum(second_grad * (middle * scale), axis=0, keepdims=True)
    input_grad_ref[...] = grads_all[slot_of(deal_ref, me)].astype(jnp.float32) + rms_back(
        middle, scale, second_grad * gains_full[1:2, :]
    )
    middle_low = input_grad_ref[...].astype(jnp.bfloat16)
    turned_ref[3] = nt(middle_low, attend_full[3]).astype(jnp.bfloat16)
    cosines, sines = cos_ref[...], sin_ref[...]
    lower = first_half((length, 128))

    def heads(pair, carry):
        lanes = pl.ds(pl.multiple_of(pair * 128, 128), 128)
        query, key, value = saved[0, :, lanes], saved[1, :, lanes], saved[2, :, lanes]
        outer = turned_ref[3, :, lanes]
        made = []
        for side in range(2):
            soft = soft_ref[2 * pair + side]
            alone = jnp.where(lower == (side == 0), outer, jnp.zeros_like(outer))
            value_grad = tn(soft.astype(jnp.bfloat16), outer)
            soft_grad = nt(alone, value)
            score_grad = (
                soft * (soft_grad - jnp.sum(soft * soft_grad, axis=-1, keepdims=True))
            ).astype(jnp.bfloat16)
            made.append(
                (matmul(score_grad, key) * 0.125, tn(score_grad, query) * 0.125, value_grad)
            )
        for index in range(3):
            joined = jnp.where(lower, made[0][index], made[1][index])
            if index < 2:
                joined = joined * cosines - turned(joined) * sines
            turned_ref[index, :, lanes] = joined.astype(jnp.bfloat16)
        return carry

    lax.fori_loop(0, width // 128, heads, 0)
    attend_grad[3] = tn(saved[3], middle_low).astype(jnp.bfloat16)
    for matrix in range(3):
        attend_grad[matrix] = tn(saved[4], turned_ref[matrix]).astype(jnp.bfloat16)
    near_moves = [
        links.copy(attend_grad.at[matrix], near_recv.at[index], {"exp": at.near})
        for index, matrix in enumerate((at.near, at.cross))
    ]
    tick(2)
    first_grad = nt(turned_ref[0], attend_full[0])
    for matrix in range(1, 3):
        first_grad = first_grad + nt(turned_ref[matrix], attend_full[matrix])
    stream = tokens[...].astype(jnp.float32)
    scale = rms_factor(stream)
    gain_own[0:1, :] = jnp.sum(first_grad * (stream * scale), axis=0, keepdims=True)
    gain_moves = [links.copy(gain_own, gain_recv.at[me], {"exp": peer}) for peer in at.peers]
    gain_recv[me] = gain_own[...]
    input_grad_ref[...] += rms_back(stream, scale, first_grad * gains_full[0:1, :])
    for move in near_moves:
        move.wait_recv()
    far_send[...] = (
        attend_grad[at.far].astype(jnp.float32) + near_recv[1].astype(jnp.float32)
    ).astype(jnp.bfloat16)
    far_move = links.copy(far_send, far_recv, {"exp": at.far})
    tick(3)
    for moves in result_moves:
        for move in moves:
            move.wait_recv()
    output = middle_ref[...]
    for member in range(members):
        output = output + result_recv[member].astype(jnp.float32)
    output_ref[...] = output
    for choice in range(2):
        route = routes[choice : choice + 1, :]
        found = jnp.zeros((1, length), jnp.float32)
        for member in range(members):
            found = jnp.where(route == member, gate_recv[member, 0:1, :], found)
        gate_grad_ref[choice : choice + 1, :] = found
    tick(4)
    for move in gain_moves:
        move.wait_recv()
    total = gain_recv[0]
    for member in range(1, members):
        total = total + gain_recv[member]
    gain_ring[at.group] = total
    far_move.wait_recv()
    attend_total[...] = (
        attend_grad[me].astype(jnp.float32)
        + near_recv[0].astype(jnp.float32)
        + far_recv[...].astype(jnp.float32)
    ).astype(jnp.bfloat16)

    half = block // 2
    small, gain_steps = [], []

    def advance_small():
        step = len(small)
        owners = (at.owner(-1 - step), at.owner(1 + step))
        made = []
        for side, target in enumerate((at.next, at.back)):
            spot = attend_total.at[rows(owners[side] * block + side * half, half), :]
            if step:
                small[-1][side].wait_recv()
                source = attend_recv.at[side, step - 1]
                added = source[...].astype(jnp.float32) + spot[...].astype(jnp.float32)
                if step < steps:
                    source[...] = added.astype(jnp.bfloat16)
                else:
                    for member in range(members // 2):
                        attend_back[side * (members // 2) + member] = added[
                            member * share : (member + 1) * share, :
                        ]
                spot = source
            if step < steps:
                made.append(links.copy(spot, attend_recv.at[side, step], target))
        if step:
            gain_steps[-1].wait_recv()
        if step < steps:
            owner = at.owner(-step)
            gain_steps.append(links.copy(gain_ring.at[owner], gain_ring.at[owner], at.next))
        small.append(made)

    advance_small()
    for step in range(5, steps):
        tick(step, between=3)
    while len(small) <= steps:
        advance_small()
    attend_moves = [
        links.copy(attend_back.at[peer], attend_sum.at[me], {"exp": peer}) for peer in at.peers
    ]
    attend_sum[me] = attend_back[me]
    total = gain_ring[0]
    for group in range(1, groups):
        total = total + gain_ring[group]
    count = gains_sum.shape[1]
    start = (at.group * members + me) * count
    gains_sum[...] = pltpu.roll(total, width - start, 1)[0:2, 0:count]
    tick(steps)
    for move in attend_moves:
        move.wait_recv()
    project_sum[...] = attend_sum[0:3]
    collect_sum[...] = attend_sum[3]
    for move in widen_moves:
        move.wait_recv()
    for matrix in range(2):
        for member in range(0, members, 2):
            found = joined_lanes(widen_home[member, matrix], widen_home[member + 1, matrix])
            for index, part in enumerate(found):
                start = index * 64 * members + member * 64
                widen_sum[matrix, :, start : start + 128] = part
    links.finish()


def update_kernel(rates, copies, *refs):
    count = len(rates)
    given, refs = refs[: 4 * count + copies], refs[4 * count + copies :]
    made, held, sems = refs[: copies + 3 * count], refs[copies + 3 * count : -1], refs[-1]
    used = []

    def copy(source, target):
        move = pltpu.make_async_copy(source, target, sems.at[len(used)])
        move.start()
        used.append(move)
        return move

    parts = []
    for index in sorted(range(count), key=lambda at: -given[4 * at].size):
        weight = given[4 * index]
        whole = pl.ds(0, weight.shape[0])
        pieces = [whole]
        if weight.size > 200000:
            cut = weight.shape[0] // 2
            pieces = [pl.ds(0, cut), pl.ds(cut, cut)]
        for piece in pieces:
            loads = [
                copy(given[4 * index + at].at[piece], held[4 * index + at].at[piece])
                for at in range(4)
            ]
            parts.append((index, piece, loads))
    stores = [copy(given[4 * count + index], made[index]) for index in range(copies)]
    for index, piece, loads in parts:
        for load in loads:
            load.wait()
        weight, moment, variance, gradient = (
            held[4 * index + at].at[piece] for at in range(4)
        )
        grad = 0.5 * gradient[...]
        level = 1.0 / (1.0 - 0.5**STEP)
        moment_new = 0.5 * moment[...] + grad
        variance_new = 0.5 * variance[...] + 2.0 * grad * grad
        kept = weight[...]
        stepped = moment_new * level / (jnp.sqrt(variance_new * level) + 1e-08) + 0.1 * kept
        moment[...] = moment_new
        variance[...] = variance_new
        weight[...] = kept - rates[index] * stepped
        for at, source in enumerate((moment, variance, weight)):
            stores.append(copy(source, made[copies + 3 * index + at].at[piece]))
    for store in stores:
        store.wait()


def update_all(*groups, passed):
    given, shapes, held = [], [], []
    for _, weight, moment, variance, gradient in groups:
        given += [weight, moment, variance, gradient]
        held += [VMEM(array.shape, array.dtype) for array in (weight, moment, variance, gradient)]
        shapes += [jax.ShapeDtypeStruct(weight.shape, weight.dtype)] * 3
    return pl.pallas_call(
        functools.partial(update_kernel, [group[0] for group in groups], len(passed)),
        out_shape=[jax.ShapeDtypeStruct(array.shape, array.dtype) for array in passed] + shapes,
        in_specs=spaces("a" * (len(given) + len(passed))),
        out_specs=spaces("a" * (len(shapes) + len(passed))),
        scratch_shapes=held + [pltpu.SemaphoreType.DMA((16 * len(groups),))],
        compiler_params=pltpu.CompilerParams(vmem_limit_bytes=LIMIT // 2),
    )(*given, *passed)


def rotary_lines(length):
    half = HEAD_FEATURES // 2
    freqs = np.exp(-np.log(10000.0) * np.arange(half) / half)
    angles = np.arange(length)[:, None] * freqs[None, :]
    cosines, sines = np.cos(angles), np.sin(angles)
    return (
        np.concatenate([cosines] * 4, axis=1).astype(np.float32),
        np.concatenate([-sines, sines] * 2, axis=1).astype(np.float32),
    )


def spaces(*names):
    kinds = {"v": pltpu.VMEM, "s": pltpu.SMEM, "a": pl.ANY}
    return [pl.BlockSpec(memory_space=kinds[name]) for name in "".join(names)]


def local(
    tokens,
    seq_lengths,
    deal_order,
    expert_routes,
    capacity_slots,
    gate_weights,
    cotangent,
    projector,
    projector_mean,
    projector_square,
    collector,
    collector_first_moment,
    collector_second_moment,
    widener,
    widener_mean,
    widener_square,
    narrower,
    narrower_mean,
    narrower_square,
    norm_gains,
    gains_mean,
    gains_square,
    expander,
    expander_mean,
    expander_square,
    reducer,
    reducer_mean,
    reducer_square,
):
    groups, members = lax.axis_size("grp"), lax.axis_size("exp")
    length, width = tokens.shape[1:]
    inner = expander.shape[3]
    piece = widener.shape[2] // members
    chunks = 1 + inner // piece
    capacity = 3 * length // members
    steps = groups - 1
    high, low, share = expander.shape[2], narrower.shape[0], projector.shape[1]
    bf16, f32 = jnp.bfloat16, jnp.float32
    shape = jax.ShapeDtypeStruct
    cosines, sines = (jnp.asarray(lines) for lines in rotary_lines(length))
    count = 16 * groups
    (
        wide_grads,
        down_grads,
        wide_first,
        down_first,
        attend_full,
        grads_all,
        saved,
        middle,
        soft,
        gains_full,
        result_parts,
        back_parts,
        gate_parts,
    ) = pl.pallas_call(
        functools.partial(gather_kernel, groups, members),
        out_shape=[
            shape((chunks, 2, width, piece), bf16),
            shape((chunks, piece, width), bf16),
            shape((chunks, 2, high, piece), bf16),
            shape((chunks, 2, low // 2, width), bf16),
            shape((4, width, width), bf16),
            shape((members, length, width), bf16),
            shape((5, length, width), bf16),
            shape((length, width), f32),
            shape((HEAD_COUNT, length, length), f32),
            shape((8, width), f32),
            shape((members, length, width), bf16),
            shape((members, length, width), bf16),
            shape((members, 8, length), f32),
        ],
        in_specs=spaces("ss", "v" * 14),
        out_specs=spaces("a" * 9, "v" * 4),
        scratch_shapes=[
            VMEM((4, width, width), bf16),
            VMEM((members, length, width), bf16),
            VMEM((5, length, width), bf16),
            VMEM((length, width), f32),
            VMEM((HEAD_COUNT, length, length), f32),
            VMEM((members, length, width), bf16),
            VMEM((members, 8, length), f32),
            VMEM((members, 8, length), f32),
            VMEM((4, share, width), f32),
            VMEM((4, share, width), f32),
            VMEM((members, 2, share, piece), f32),
            VMEM((members, 2, share, piece), f32),
            VMEM((8, width), f32),
            VMEM((members, 8, width), f32),
            VMEM((groups, 8, width), f32),
            VMEM((chunks, 2, width, piece), bf16),
            VMEM((chunks, piece, width), bf16),
            VMEM((chunks, 2, high, piece), bf16),
            VMEM((chunks, low, width), bf16),
            VMEM((members * length, width), bf16),
            VMEM((width, members * length), bf16),
            VMEM((members, length, width), f32),
            VMEM((members, length, width), f32),
            VMEM((members * capacity, width), bf16),
            VMEM((width, members * capacity), bf16),
            VMEM((members * capacity, width), bf16),
            VMEM((members * capacity, width), f32),
            VMEM((members * capacity, width), f32),
            pltpu.SemaphoreType.DMA((count,)),
            pltpu.SemaphoreType.DMA((count,)),
            pltpu.SemaphoreType.DMA((chunks * steps * 4,)),
            pltpu.SemaphoreType.DMA((chunks * steps * 4,)),
            pltpu.SemaphoreType.DMA((chunks * 4,)),
            pltpu.SemaphoreType.DMA((chunks * 4,)),
            pltpu.SemaphoreType.DMA((2 * chunks + 5,)),
        ],
        compiler_params=pltpu.CompilerParams(
            collective_id=0, has_side_effects=True, vmem_limit_bytes=LIMIT
        ),
    )(
        seq_lengths,
        deal_order,
        tokens[0],
        cotangent[0],
        expert_routes[0].T,
        capacity_slots[0].T,
        gate_weights[0].T,
        norm_gains,
        projector,
        collector,
        widener,
        narrower,
        expander[0],
        reducer[0],
        cosines,
        sines,
    )
    count = 32 * groups
    (
        output,
        input_grad,
        gate_grad,
        expand_sum,
        reduce_sum,
        widen_sum,
        narrow_sum,
        project_sum,
        collect_sum,
        gains_sum,
    ) = pl.pallas_call(
        functools.partial(scatter_kernel, groups, members),
        out_shape=[
            shape((length, width), f32),
            shape((length, width), f32),
            shape((2, length), f32),
            shape((2, high, inner), f32),
            shape(reducer.shape[1:], f32),
            shape(widener.shape, f32),
            shape(narrower.shape, f32),
            shape(projector.shape, f32),
            shape(collector.shape, f32),
            shape(norm_gains.shape, f32),
        ],
        in_specs=spaces("s", "v" * 6, "a" * 11),
        out_specs=spaces("v" * 10),
        scratch_shapes=[
            VMEM((4, share, width), f32),
            VMEM((members, length, width), bf16),
            VMEM((length, width), f32),
            VMEM((4, width, width), bf16),
            VMEM((5, length, width), bf16),
            VMEM((HEAD_COUNT, length, length), f32),
            VMEM((members, 8, length), f32),
            VMEM((members, length, width), bf16),
            VMEM((members, length, width), bf16),
            VMEM((chunks, 2, width, piece), bf16),
            VMEM((chunks, piece, width), bf16),
            VMEM((chunks, 2, steps, high, piece), bf16),
            VMEM((chunks, 2, steps, low // 2, width), bf16),
            VMEM((chunks - 1, 2, high, piece), f32),
            VMEM((4, length, width), bf16),
            VMEM((4, width, width), bf16),
            VMEM((2, width, width), bf16),
            VMEM((width, width), bf16),
            VMEM((width, width), bf16),
            VMEM((width, width), bf16),
            VMEM((2, steps, high // 2, width), bf16),
            VMEM((4, share, width), f32),
            VMEM((members, 2, share, piece), f32),
            VMEM((members, 2, share, piece), f32),
            VMEM((8, width), f32),
            VMEM((members, 8, width), f32),
            VMEM((groups, 8, width), f32),
            pltpu.SemaphoreType.DMA((count,)),
            pltpu.SemaphoreType.DMA((count,)),
            pltpu.SemaphoreType.DMA((11,)),
        ],
        compiler_params=pltpu.CompilerParams(
            collective_id=1, has_side_effects=True, vmem_limit_bytes=LIMIT
        ),
    )(
        deal_order,
        tokens[0],
        expert_routes[0].T,
        gains_full,
        cosines,
        sines,
        gate_parts,
        result_parts,
        back_parts,
        wide_grads,
        down_grads,
        wide_first,
        down_first,
        grads_all,
        middle,
        attend_full,
        saved,
        soft,
    )
    updated = update_all(
        (0.1, projector, projector_mean, projector_square, project_sum),
        (0.3, collector, collector_first_moment, collector_second_moment, collect_sum),
        (0.07, widener, widener_mean, widener_square, widen_sum),
        (0.045, narrower, narrower_mean, narrower_square, narrow_sum),
        (0.2, norm_gains, gains_mean, gains_square, gains_sum),
        (0.07, expander[0], expander_mean[0], expander_square[0], expand_sum),
        (0.045, reducer[0], reducer_mean[0], reducer_square[0], reduce_sum),
        passed=(output, input_grad),
    )
    return (
        updated[0][None],
        updated[1][None],
        gate_grad.T[None],
        *updated[2:17],
        *(found[None] for found in updated[17:]),
    )


def fits(mesh):
    groups, members = mesh.shape["grp"], mesh.shape["exp"]
    share = 64 * HEAD_COUNT // (groups * members)
    return members == 4 and groups % 2 == 0 and share % 8 == 0 and share * members // 2 % 16 == 0


def solution(mesh):
    placed = (
        P(("grp", "exp"), None, None),
        P("grp"),
        P("grp"),
        P(("grp", "exp"), None, None),
        P(("grp", "exp"), None, None),
        P(("grp", "exp"), None, None),
        P(("grp", "exp"), None, None),
        P(None, ("grp", "exp"), None),
        P(None, ("grp", "exp"), None),
        P(None, ("grp", "exp"), None),
        P(("grp", "exp"), None),
        P(("grp", "exp"), None),
        P(("grp", "exp"), None),
        P(None, ("grp", "exp"), None),
        P(None, ("grp", "exp"), None),
        P(None, ("grp", "exp"), None),
        P(("grp", "exp"), None),
        P(("grp", "exp"), None),
        P(("grp", "exp"), None),
        P(None, ("grp", "exp")),
        P(None, ("grp", "exp")),
        P(None, ("grp", "exp")),
        P("exp", None, "grp", None),
        P("exp", None, "grp", None),
        P("exp", None, "grp", None),
        P("exp", "grp", None),
        P("exp", "grp", None),
        P("exp", "grp", None),
    )
    return jax.shard_map(
        local if fits(mesh) else local_plain,
        mesh=mesh,
        in_specs=placed,
        out_specs=(
            P(("grp", "exp"), None, None),
            P(("grp", "exp"), None, None),
            P(("grp", "exp"), None, None),
            P(None, ("grp", "exp"), None),
            P(None, ("grp", "exp"), None),
            P(None, ("grp", "exp"), None),
            P(("grp", "exp"), None),
            P(("grp", "exp"), None),
            P(("grp", "exp"), None),
            P(None, ("grp", "exp"), None),
            P(None, ("grp", "exp"), None),
            P(None, ("grp", "exp"), None),
            P(("grp", "exp"), None),
            P(("grp", "exp"), None),
            P(("grp", "exp"), None),
            P(None, ("grp", "exp")),
            P(None, ("grp", "exp")),
            P(None, ("grp", "exp")),
            P("exp", None, "grp", None),
            P("exp", None, "grp", None),
            P("exp", None, "grp", None),
            P("exp", "grp", None),
            P("exp", "grp", None),
            P("exp", "grp", None),
        ),
        check_vma=False,
    )
```

```python
import functools

import jax
import jax.numpy as jnp
import numpy as np
from jax import lax
from jax.experimental import pallas as pl
from jax.experimental.pallas import tpu as pltpu
from jax.sharding import PartitionSpec as P

HEAD_COUNT = 12
HEAD_FEATURES = 64
STEP = 5


def rms_factor(values):
    return lax.rsqrt(jnp.mean(values * values, axis=-1, keepdims=True) + 1e-06)


def rms_back(values, factor, upstream):
    return factor * (
        upstream - values * factor * factor * jnp.mean(upstream * values, axis=-1, keepdims=True)
    )


def rotary(length):
    positions = jnp.arange(length, dtype=jnp.int32).astype(jnp.float32)
    half = HEAD_FEATURES // 2
    freqs = jnp.exp(
        -jnp.log(10000.0) * jnp.arange(half, dtype=jnp.int32).astype(jnp.float32) / half
    )
    angles = positions[:, None] * freqs[None, :]
    return (jnp.cos(angles)[:, None, :], jnp.sin(angles)[:, None, :])


def rotate(values, cosines, sines):
    half = values.shape[-1] // 2
    first = values[..., :half]
    second = values[..., half:]
    return jnp.concatenate(
        [first * cosines - second * sines, second * cosines + first * sines], axis=-1
    )


def rotate_back(values, cosines, sines):
    half = values.shape[-1] // 2
    first = values[..., :half]
    second = values[..., half:]
    return jnp.concatenate(
        [first * cosines + second * sines, second * cosines - first * sines], axis=-1
    )


def silu_slope(values):
    sigmoid_of = jax.nn.sigmoid(values)
    return sigmoid_of * (1.0 + values * (1.0 - sigmoid_of))


def matmul(left, right):
    return jnp.dot(left, right, preferred_element_type=jnp.float32)


def outer_sum(left, right):
    return jnp.einsum("ld,lf->df", left, right, preferred_element_type=jnp.float32)


def adamw_update(weight, moment, variance, gradient, rate):
    moment_new = 0.5 * moment + 0.5 * gradient
    variance_new = 0.5 * variance + 0.5 * gradient * gradient
    correct = 1.0 - 0.5**STEP
    stepped = moment_new / correct / (jnp.sqrt(variance_new / correct) + 1e-08) + 0.1 * weight
    return (moment_new, variance_new, weight - rate * stepped)


def local_plain(
    tokens,
    seq_lengths,
    deal_order,
    expert_routes,
    capacity_slots,
    gate_weights,
    cotangent,
    projector,
    projector_mean,
    projector_square,
    collector,
    collector_first_moment,
    collector_second_moment,
    widener,
    widener_mean,
    widener_square,
    narrower,
    narrower_mean,
    narrower_square,
    norm_gains,
    gains_mean,
    gains_square,
    expander,
    expander_mean,
    expander_square,
    reducer,
    reducer_mean,
    reducer_square,
):
    members = lax.axis_size("exp")
    member = lax.axis_index("exp")
    length_seq = tokens.shape[1]
    width = tokens.shape[2]
    local_experts = expander.shape[0]
    experts_all = local_experts * members
    capacity = 3 * length_seq // experts_all
    member_ids = jnp.arange(members, dtype=jnp.int32)
    source = deal_order[member]
    home_slot = jnp.sum(jnp.where(deal_order == member, member_ids, 0))
    seq_length = seq_lengths[source]
    piece = lax.all_gather(tokens, "exp", axis=0, tiled=True)
    chosen = jnp.arange(piece.shape[0], dtype=jnp.int32) == source
    dealt = jnp.sum(
        jnp.where(chosen[:, None, None], piece, jnp.zeros_like(piece)), axis=0, keepdims=True
    )
    residual_flow = dealt[0].astype(jnp.float32)
    project_full, collect_full, widen_full, narrow_full, gains_full = (
        lax.all_gather(projector.astype(jnp.bfloat16), ("grp", "exp"), axis=1, tiled=True),
        lax.all_gather(collector.astype(jnp.bfloat16), ("grp", "exp"), axis=0, tiled=True),
        lax.all_gather(widener.astype(jnp.bfloat16), ("grp", "exp"), axis=1, tiled=True),
        lax.all_gather(narrower.astype(jnp.bfloat16), ("grp", "exp"), axis=0, tiled=True),
        lax.all_gather(norm_gains.astype(jnp.bfloat16), ("grp", "exp"), axis=1, tiled=True),
    )
    expand_full, reduce_full = (
        lax.all_gather(expander.astype(jnp.bfloat16), "grp", axis=2, tiled=True),
        lax.all_gather(reducer.astype(jnp.bfloat16), "grp", axis=1, tiled=True),
    )
    gains_used = gains_full.astype(jnp.float32)
    cosines, sines = rotary(length_seq)
    scale_one = rms_factor(residual_flow)
    normed_one = residual_flow * scale_one
    first_input = (normed_one * gains_used[0]).astype(jnp.bfloat16)
    query_raw = matmul(first_input, project_full[0]).reshape(length_seq, HEAD_COUNT, HEAD_FEATURES)
    key_raw = matmul(first_input, project_full[1]).reshape(length_seq, HEAD_COUNT, HEAD_FEATURES)
    value_raw = matmul(first_input, project_full[2]).reshape(length_seq, HEAD_COUNT, HEAD_FEATURES)
    query_rot = rotate(query_raw, cosines, sines).astype(jnp.bfloat16)
    key_rot = rotate(key_raw, cosines, sines).astype(jnp.bfloat16)
    value_low = value_raw.astype(jnp.bfloat16)
    rows_at = jnp.arange(length_seq, dtype=jnp.int32)[:, None]
    cols_at = jnp.arange(length_seq, dtype=jnp.int32)[None, :]
    allowed = ((cols_at <= rows_at) & (cols_at < seq_length))[None]
    scores = (
        jnp.einsum("qhd,khd->hqk", query_rot, key_rot, preferred_element_type=jnp.float32) * 0.125
    )
    masked = jnp.where(allowed, scores, -1e30)
    top = jnp.max(masked, axis=-1, keepdims=True)
    expo = jnp.exp(masked - top)
    total = jnp.sum(expo, axis=-1, keepdims=True)
    soft = expo / total
    logsum = top + jnp.log(total)
    mixed_output = (
        jnp.einsum(
            "hqk,khd->qhd", soft.astype(jnp.bfloat16), value_low, preferred_element_type=jnp.float32
        )
        .reshape(length_seq, width)
        .astype(jnp.bfloat16)
    )
    middle_state = residual_flow + matmul(mixed_output, collect_full)
    scale_two = rms_factor(middle_state)
    normed_two = middle_state * scale_two
    second_input = (normed_two * gains_used[1]).astype(jnp.bfloat16)
    gating_scores = matmul(second_input, widen_full[0])
    upward_rows = matmul(second_input, widen_full[1])
    hidden_state = (jax.nn.silu(gating_scores) * upward_rows).astype(jnp.bfloat16)
    dense_branch = matmul(hidden_state, narrow_full)
    flat = (expert_routes[0] * capacity + capacity_slots[0]).reshape(-1)
    spread = jnp.repeat(second_input, 2, axis=0)
    dispatch = jnp.zeros((experts_all * capacity, width), jnp.bfloat16).at[flat].set(spread)
    dispatch = dispatch.reshape(experts_all, capacity, width)
    rows = lax.all_to_all(dispatch, "exp", split_axis=0, concat_axis=0, tiled=True)
    count = rows.shape[1]
    grouped = rows.reshape(members, local_experts, count, width)
    gate_pre = jnp.einsum(
        "sekd,edf->sekf", grouped, expand_full[:, 0], preferred_element_type=jnp.float32
    )
    up_pre = jnp.einsum(
        "sekd,edf->sekf", grouped, expand_full[:, 1], preferred_element_type=jnp.float32
    )
    hidden_rows = (jax.nn.silu(gate_pre) * up_pre).astype(jnp.bfloat16)
    result = jnp.einsum(
        "sekf,efd->sekd", hidden_rows, reduce_full, preferred_element_type=jnp.float32
    )
    result = result.astype(jnp.bfloat16).reshape(members * local_experts, count, width)
    returned_rows = lax.all_to_all(result, "exp", split_axis=0, concat_axis=0, tiled=True)
    outcome = (
        returned_rows,
        rows,
        gate_pre.reshape(members * local_experts, count, -1),
        up_pre.reshape(members * local_experts, count, -1),
    )
    returned, received, gate_kept, up_kept = outcome
    picked = (
        returned.reshape(experts_all * capacity, width)[flat]
        .reshape(length_seq, 2, width)
        .astype(jnp.float32)
    )
    gate_local = gate_weights[0]
    mixture = jnp.sum(gate_local[..., None] * picked, axis=1)
    layer_output = middle_state + dense_branch + mixture
    valid = (jnp.arange(length_seq, dtype=jnp.int32) < seq_length).astype(jnp.float32)
    grad_out = cotangent[0] * valid[:, None]
    grad_low = grad_out.astype(jnp.bfloat16)
    narrow_grad = outer_sum(hidden_state, grad_low)
    hidden_grad = jnp.einsum("ld,fd->lf", grad_low, narrow_full, preferred_element_type=jnp.float32)
    gating_grad = (hidden_grad * upward_rows * silu_slope(gating_scores)).astype(jnp.bfloat16)
    upward_grad = (hidden_grad * jax.nn.silu(gating_scores)).astype(jnp.bfloat16)
    widen_grad = jnp.stack(
        [outer_sum(second_input, gating_grad), outer_sum(second_input, upward_grad)]
    )
    second_grad = jnp.einsum(
        "lf,df->ld", gating_grad, widen_full[0], preferred_element_type=jnp.float32
    ) + jnp.einsum("lf,df->ld", upward_grad, widen_full[1], preferred_element_type=jnp.float32)
    gate_grad_local = jnp.sum(grad_out[:, None, :] * picked, axis=-1)
    result_grad = (
        (gate_local[..., None] * grad_out[:, None, :])
        .astype(jnp.bfloat16)
        .reshape(2 * length_seq, width)
    )
    grad_send = jnp.zeros((experts_all * capacity, width), jnp.bfloat16).at[flat].set(result_grad)
    grad_recv = lax.all_to_all(
        grad_send.reshape(experts_all, capacity, width),
        "exp",
        split_axis=0,
        concat_axis=0,
        tiled=True,
    )
    grad_group = grad_recv.reshape(members, local_experts, capacity, width)
    rows_group = received.reshape(members, local_experts, capacity, width)
    gate_pre = gate_kept.reshape(members, local_experts, capacity, -1)
    up_pre = up_kept.reshape(members, local_experts, capacity, -1)
    hidden_rows = (jax.nn.silu(gate_pre) * up_pre).astype(jnp.bfloat16)
    reduce_grad = jnp.einsum(
        "sekf,sekd->efd", hidden_rows, grad_group, preferred_element_type=jnp.float32
    )
    hidden_rows_grad = jnp.einsum(
        "sekd,efd->sekf", grad_group, reduce_full, preferred_element_type=jnp.float32
    )
    gate_rows_grad = (hidden_rows_grad * up_pre * silu_slope(gate_pre)).astype(jnp.bfloat16)
    up_rows_grad = (hidden_rows_grad * jax.nn.silu(gate_pre)).astype(jnp.bfloat16)
    expand_grad = jnp.stack(
        [
            jnp.einsum(
                "sekd,sekf->edf", rows_group, gate_rows_grad, preferred_element_type=jnp.float32
            ),
            jnp.einsum(
                "sekd,sekf->edf", rows_group, up_rows_grad, preferred_element_type=jnp.float32
            ),
        ],
        axis=1,
    )
    row_grads = jnp.einsum(
        "sekf,edf->sekd", gate_rows_grad, expand_full[:, 0], preferred_element_type=jnp.float32
    ) + jnp.einsum(
        "sekf,edf->sekd", up_rows_grad, expand_full[:, 1], preferred_element_type=jnp.float32
    )
    row_grads = row_grads.astype(jnp.bfloat16).reshape(experts_all, capacity, width)
    came_back = lax.all_to_all(row_grads, "exp", split_axis=0, concat_axis=0, tiled=True).reshape(
        experts_all * capacity, width
    )
    second_grad = second_grad + jnp.sum(
        came_back[flat].reshape(length_seq, 2, width).astype(jnp.float32), axis=1
    )
    gains_grad_two = jnp.sum(second_grad * normed_two, axis=0)
    middle_grad = grad_out + rms_back(middle_state, scale_two, second_grad * gains_used[1])
    middle_low = middle_grad.astype(jnp.bfloat16)
    collect_grad = outer_sum(mixed_output, middle_low)
    mixed_grad = jnp.einsum(
        "ld,ed->le", middle_low, collect_full, preferred_element_type=jnp.float32
    )
    mixed_grad = mixed_grad.astype(jnp.bfloat16).reshape(length_seq, HEAD_COUNT, HEAD_FEATURES)
    scores_again = (
        jnp.einsum("qhd,khd->hqk", query_rot, key_rot, preferred_element_type=jnp.float32) * 0.125
    )
    soft_again = jnp.where(allowed, jnp.exp(scores_again - logsum), 0.0)
    value_grad = jnp.einsum(
        "hqk,qhd->khd",
        soft_again.astype(jnp.bfloat16),
        mixed_grad,
        preferred_element_type=jnp.float32,
    )
    soft_grad = jnp.einsum(
        "qhd,khd->hqk", mixed_grad, value_low, preferred_element_type=jnp.float32
    )
    score_grad = (
        soft_again * (soft_grad - jnp.sum(soft_again * soft_grad, axis=-1, keepdims=True))
    ).astype(jnp.bfloat16)
    query_grad = (
        jnp.einsum("hqk,khd->qhd", score_grad, key_rot, preferred_element_type=jnp.float32) * 0.125
    )
    key_grad = (
        jnp.einsum("hqk,qhd->khd", score_grad, query_rot, preferred_element_type=jnp.float32)
        * 0.125
    )
    query_back = (
        rotate_back(query_grad, cosines, sines).reshape(length_seq, width).astype(jnp.bfloat16)
    )
    key_back = rotate_back(key_grad, cosines, sines).reshape(length_seq, width).astype(jnp.bfloat16)
    value_back = value_grad.reshape(length_seq, width).astype(jnp.bfloat16)
    project_grad = jnp.stack(
        [
            outer_sum(first_input, query_back),
            outer_sum(first_input, key_back),
            outer_sum(first_input, value_back),
        ]
    )
    first_grad = (
        jnp.einsum("le,de->ld", query_back, project_full[0], preferred_element_type=jnp.float32)
        + jnp.einsum("le,de->ld", key_back, project_full[1], preferred_element_type=jnp.float32)
        + jnp.einsum("le,de->ld", value_back, project_full[2], preferred_element_type=jnp.float32)
    )
    gains_grad_one = jnp.sum(first_grad * normed_one, axis=0)
    stream_grad = middle_grad + rms_back(residual_flow, scale_one, first_grad * gains_used[0])
    gains_grad = jnp.stack([gains_grad_one, gains_grad_two])
    project_part, collect_part, widen_part, narrow_part, gains_part = (
        lax.psum_scatter(project_grad, ("grp", "exp"), scatter_dimension=1, tiled=True),
        lax.psum_scatter(collect_grad, ("grp", "exp"), scatter_dimension=0, tiled=True),
        lax.psum_scatter(widen_grad, ("grp", "exp"), scatter_dimension=1, tiled=True),
        lax.psum_scatter(narrow_grad, ("grp", "exp"), scatter_dimension=0, tiled=True),
        lax.psum_scatter(gains_grad, ("grp", "exp"), scatter_dimension=1, tiled=True),
    )
    expand_part, reduce_part = (
        lax.psum_scatter(
            expand_grad.astype(jnp.bfloat16), "grp", scatter_dimension=2, tiled=True
        ).astype(jnp.float32),
        lax.psum_scatter(
            reduce_grad.astype(jnp.bfloat16), "grp", scatter_dimension=1, tiled=True
        ).astype(jnp.float32),
    )
    empty = jnp.zeros((1, length_seq, width), jnp.float32)
    pieces = (
        lax.all_gather(layer_output[None].astype(jnp.bfloat16), "exp", axis=0, tiled=True).astype(
            jnp.float32
        ),
        lax.all_gather(stream_grad[None].astype(jnp.bfloat16), "exp", axis=0, tiled=True).astype(
            jnp.float32
        ),
    )
    chosen = (jnp.arange(pieces[0].shape[0], dtype=jnp.int32) == home_slot)[:, None, None]
    homed_output = empty + jnp.sum(jnp.where(chosen, pieces[0], 0.0), axis=0, keepdims=True)
    homed_grad = empty + jnp.sum(jnp.where(chosen, pieces[1], 0.0), axis=0, keepdims=True)
    project_new = adamw_update(projector, projector_mean, projector_square, project_part, 0.1)
    collect_new = adamw_update(
        collector, collector_first_moment, collector_second_moment, collect_part, 0.3
    )
    widening_updated = adamw_update(widener, widener_mean, widener_square, widen_part, 0.07)
    narrowing_updated = adamw_update(narrower, narrower_mean, narrower_square, narrow_part, 0.045)
    gains_updated = adamw_update(norm_gains, gains_mean, gains_square, gains_part, 0.2)
    expansion_updated = adamw_update(expander, expander_mean, expander_square, expand_part, 0.07)
    reduction_updated = adamw_update(reducer, reducer_mean, reducer_square, reduce_part, 0.045)
    return (
        homed_output,
        homed_grad,
        gate_grad_local[None],
        project_new[0],
        project_new[1],
        project_new[2],
        collect_new[0],
        collect_new[1],
        collect_new[2],
        widening_updated[0],
        widening_updated[1],
        widening_updated[2],
        narrowing_updated[0],
        narrowing_updated[1],
        narrowing_updated[2],
        gains_updated[0],
        gains_updated[1],
        gains_updated[2],
        expansion_updated[0],
        expansion_updated[1],
        expansion_updated[2],
        reduction_updated[0],
        reduction_updated[1],
        reduction_updated[2],
    )


MESH = pl.DeviceIdType.MESH
VMEM = pltpu.VMEM
LIMIT = 60 * 1024 * 1024


def ring_place(index, groups):
    row, side = lax.div(index, 2), lax.rem(index, 2)
    return (1 - side) * row + side * (groups - 1 - row)


def ring_member(place, groups):
    side = lax.div(place, groups // 2)
    return 2 * ((1 - side) * place + side * (groups - 1 - place)) + side


def remote(source, target, sends, arrivals, at, device):
    return pltpu.make_async_remote_copy(
        src_ref=source,
        dst_ref=target,
        send_sem=sends.at[at],
        recv_sem=arrivals.at[at],
        device_id=device,
        device_id_type=MESH,
    )


class Links:
    def __init__(self, sends, arrivals):
        self.sends, self.arrivals, self.count, self.started = sends, arrivals, 0, []

    def copy(self, source, target, device):
        made = remote(source, target, self.sends, self.arrivals, self.count, device)
        self.count += 1
        made.start()
        self.started.append(made)
        return made

    def finish(self):
        for made in self.started:
            made.wait_send()


class Places:
    def __init__(self, groups, members):
        self.groups, self.members = groups, members
        self.group = lax.axis_index("grp")
        self.member = lax.axis_index("exp")
        self.place = ring_place(self.group, groups)
        self.next = {"grp": self.owner(1)}
        self.back = {"grp": self.owner(-1)}
        half = members // 2
        self.far = lax.rem(self.member + half, members)
        self.near = self.member + 1 - 2 * lax.rem(self.member, 2)
        self.cross = lax.rem(self.near + half, members)
        self.peers = [lax.rem(self.member + step, members) for step in range(1, members)]

    def owner(self, offset):
        place = lax.rem(self.place + offset + 2 * self.groups, self.groups)
        return ring_member(place, self.groups)

    def enter(self):
        barrier = pltpu.get_barrier_semaphore()
        partners = [self.next, self.back] + [{"exp": peer} for peer in self.peers]
        for partner in partners:
            pl.semaphore_signal(barrier, inc=1, device_id=partner, device_id_type=MESH)
        pl.semaphore_wait(barrier, len(partners))


def rows(start, count, align=16):
    return pl.ds(pl.multiple_of(start, align), count)


def first_half(shape):
    return lax.rem(lax.broadcasted_iota(jnp.int32, shape, len(shape) - 1), 128) < 64


def turned(values):
    lanes = lax.broadcasted_iota(jnp.int32, values.shape, 1)
    return jnp.where(
        lax.rem(lanes, HEAD_FEATURES) < HEAD_FEATURES // 2,
        pltpu.roll(values, 128 - HEAD_FEATURES // 2, 1),
        pltpu.roll(values, HEAD_FEATURES // 2, 1),
    )


def nt(left, right):
    return lax.dot_general(
        left, right, (((1,), (1,)), ((), ())), preferred_element_type=jnp.float32
    )


def tn(left, right):
    return lax.dot_general(
        left, right, (((0,), (0,)), ((), ())), preferred_element_type=jnp.float32
    )


def sigmoid(values):
    return 1.0 / (1.0 + jnp.exp(-values))


def same(length):
    shape = (length, length)
    return lax.broadcasted_iota(jnp.int32, shape, 0) == lax.broadcasted_iota(jnp.int32, shape, 1)


def upright(line):
    return jnp.sum(jnp.where(same(line.shape[1]), line, 0.0), axis=1, keepdims=True)


def lying(column):
    return jnp.sum(jnp.where(same(column.shape[0]), column, 0.0), axis=0, keepdims=True)


def slot_of(deal_ref, member):
    for _ in range(11):
        member = deal_ref[member]
    return member


def dealt_lanes(values, piece, pieces):
    low_lanes = lax.broadcasted_iota(jnp.int32, (values.shape[0], 128), 1) < 64
    found = []
    span = 64 * pieces
    for start in range(0, values.shape[1], 2 * span):
        start = start + piece // 2 * 128
        one, two = values[:, start : start + 128], values[:, start + span : start + span + 128]
        if piece % 2:
            one = pltpu.roll(one, 64, 1)
        else:
            two = pltpu.roll(two, 64, 1)
        found.append(jnp.where(low_lanes, one, two))
    return jnp.concatenate(found, axis=1)


def joined_lanes(even, odd):
    low_lanes = lax.broadcasted_iota(jnp.int32, (even.shape[0], 128), 1) < 64
    found = []
    for start in range(0, even.shape[1], 128):
        one, two = even[:, start : start + 128], odd[:, start : start + 128]
        found.append(jnp.where(low_lanes, one, pltpu.roll(two, 64, 1)))
        found.append(jnp.where(low_lanes, pltpu.roll(one, 64, 1), two))
    return found


def gather_kernel(
    groups,
    members,
    length_ref,
    deal_ref,
    tokens,
    cotangent,
    routes,
    places,
    gates,
    norm_gains,
    projector,
    collector,
    widener,
    narrower,
    expander,
    reducer,
    cos_ref,
    sin_ref,
    wide_grads,
    down_grads,
    wide_first,
    down_first,
    attend_out,
    grads_out,
    saved_out,
    middle_out,
    soft_out,
    gains_full,
    result_ref,
    back_ref,
    gate_ref,
    attend_full,
    grads_all,
    saved,
    middle_ref,
    soft_ref,
    second_all,
    meta_send,
    meta_all,
    attend_send,
    attend_recv,
    widen_send,
    widen_recv,
    gains,
    gain_recv,
    gain_ring,
    wide_full,
    down_full,
    wide_own,
    down_own,
    inputs_ref,
    inputs_turned,
    dense_out,
    dense_back,
    rows_in,
    rows_turned,
    rows_grad,
    rows_out,
    rows_back,
    sends,
    arrivals,
    ring_sends,
    ring_arrivals,
    first_sends,
    first_arrivals,
    local_sems,
):
    at = Places(groups, members)
    links = Links(sends, arrivals)
    at.enter()
    me, steps = at.member, groups - 1
    share, width = projector.shape[1:]
    block = share * members
    length = tokens.shape[0]
    chunks, low = down_own.shape[:2]
    capacity = rows_in.shape[0] // members

    def ring_copy(chunk, step, side, piece):
        owner = at.owner(-step if side == 0 else step)
        if piece == 0:
            spot = wide_full.at[chunk, side, rows(owner * block, block), :]
            origin = wide_own.at[chunk, side]
        else:
            spot = down_full.at[chunk, rows(owner * low + side * (low // 2), low // 2), :]
            origin = down_own.at[chunk, pl.ds(side * (low // 2), low // 2), :]
        place = (chunk * steps + step) * 4 + side * 2 + piece
        return remote(
            spot if step else origin,
            spot,
            ring_sends,
            ring_arrivals,
            place,
            (at.next, at.back)[side],
        )

    def ring_step(chunk, step):
        for piece in range(2):
            for side in range(2):
                if step:
                    ring_copy(chunk, step - 1, side, piece).wait_recv()
                if step < steps:
                    ring_copy(chunk, step, side, piece).start()

    def tick(count):
        for chunk in range(chunks):
            if 0 <= count - 2 * chunk <= steps:
                ring_step(chunk, count - 2 * chunk)

    attend_send[0:3] = projector[...]
    attend_send[3] = collector[...]
    gains[...] = jnp.zeros_like(gains)
    gains[0:2, 0 : norm_gains.shape[1]] = norm_gains[...]
    gains[...] = pltpu.roll(gains[...], (at.group * members + me) * norm_gains.shape[1], 1)
    first_moves = [
        [
            links.copy(attend_send.at[peer], attend_recv.at[me], {"exp": peer}),
            links.copy(gains, gain_recv.at[me], {"exp": peer}),
        ]
        for peer in at.peers
    ]
    gain_recv[me] = gains[...]
    attend_recv[me] = attend_send[me]
    for matrix in range(2):
        for member in range(members):
            widen_send[member, matrix] = dealt_lanes(widener[matrix], member, members)
    widen_moves = [
        links.copy(widen_send.at[peer], widen_recv.at[me], {"exp": peer}) for peer in at.peers
    ]
    widen_recv[me] = widen_send[me]

    def stage(chunk):
        if chunk == 1:
            for matrix in range(2):
                wide_own[1, matrix] = jnp.concatenate(
                    [widen_recv[member, matrix] for member in range(members)], axis=0
                ).astype(jnp.bfloat16)
            down_own[1] = narrower[...].astype(jnp.bfloat16)
        else:
            index = max(chunk - 1, 0)
            for matrix in range(2):
                wide_own[chunk, matrix] = dealt_lanes(
                    expander[matrix], index, chunks - 1
                ).astype(jnp.bfloat16)
            down_own[chunk] = reducer[index * low : (index + 1) * low, :].astype(jnp.bfloat16)
        for side in range(2):
            wide_full[chunk, side, rows(at.group * block, block), :] = wide_own[chunk, side]
        down_full[chunk, rows(at.group * low, low), :] = down_own[chunk]

    stage(0)
    tick(0)
    for moves in first_moves:
        for move in moves:
            move.wait_recv()
    attend_full[me, rows(at.group * block, block), :] = (
        attend_recv[...].reshape(block, width).astype(jnp.bfloat16)
    )
    total_gain = gain_recv[0]
    for member in range(1, members):
        total_gain = total_gain + gain_recv[member]
    gain_ring[at.group] = total_gain

    half = block // 2

    def unit(owner, side, matrix):
        return attend_full.at[matrix, rows(owner * block + side * half, half), :]

    def across(owner, side):
        spot = unit(owner, side, me)
        return (links.copy(spot, spot, {"exp": at.far}), links.copy(spot, spot, {"exp": at.near}))

    def onward(owner, side):
        spot = unit(owner, side, at.far)
        return links.copy(spot, spot, {"exp": at.near})

    ring, crossed, passed = [], [], []
    gain_moves = []
    for step in range(groups):
        owners = (at.owner(-step), at.owner(step))
        if step:
            for move in ring[-1]:
                move.wait_recv()
            gain_moves[-1].wait_recv()
        if step < steps:
            ring.append(
                [
                    links.copy(unit(owner, side, me), unit(owner, side, me), target)
                    for side, (owner, target) in enumerate(zip(owners, (at.next, at.back)))
                ]
            )
            gain_moves.append(
                links.copy(gain_ring.at[owners[0]], gain_ring.at[owners[0]], at.next)
            )
        crossed.append([across(owner, side) for side, owner in enumerate(owners)])
        if step:
            for side, owner in enumerate((at.owner(1 - step), at.owner(step - 1))):
                crossed[step - 1][side][0].wait_recv()
                passed.append(onward(owner, side))
        if step == 2:
            for move in widen_moves:
                move.wait_recv()
            for chunk in range(1, chunks):
                stage(chunk)
        if step % 2:
            tick(step // 2 + 1)
    outgoing = []

    def hand_out(source, target):
        made = pltpu.make_async_copy(
            source, target, local_sems.at[2 * chunks + len(outgoing)]
        )
        made.start()
        outgoing.append(made)

    valid = lax.broadcasted_iota(jnp.int32, (length, 1), 0) < length_ref[deal_ref[me]]
    grads_all[me] = jnp.where(valid, cotangent[...], 0.0).astype(jnp.bfloat16)
    route = [routes[choice : choice + 1, :] for choice in range(2)]
    place = [places[choice : choice + 1, :].astype(jnp.float32) for choice in range(2)]
    meta_send[...] = jnp.zeros_like(meta_send)
    for member in range(members):
        named = [chosen == member for chosen in route]
        meta_send[member, 0:1, :] = jnp.where(
            named[0], place[0], jnp.where(named[1], place[1], -1.0)
        )
        meta_send[member, 1:2, :] = jnp.where(
            named[0], gates[0:1, :], jnp.where(named[1], gates[1:2, :], 0.0)
        )
    meta_all[me] = meta_send[me]
    grad_moves = [
        [
            links.copy(grads_all.at[me], grads_all.at[me], {"exp": peer}),
            links.copy(meta_send.at[peer], meta_all.at[me], {"exp": peer}),
        ]
        for peer in at.peers
    ]
    for side, owner in enumerate((at.owner(-steps), at.owner(steps))):
        crossed[steps][side][0].wait_recv()
        passed.append(onward(owner, side))
    total_gain = gain_ring[0]
    for group in range(1, groups):
        total_gain = total_gain + gain_ring[group]
    gains_full[...] = total_gain.astype(jnp.bfloat16).astype(jnp.float32)
    stream = tokens[...].astype(jnp.float32)
    first_input = (stream * rms_factor(stream) * gains_full[0:1, :]).astype(jnp.bfloat16)
    saved[4] = first_input
    for moves in crossed:
        for move in moves:
            move[1].wait_recv()
    for move in passed:
        move.wait_recv()
    tick(5)
    hand_out(attend_full, attend_out)

    cosines, sines = cos_ref[...], sin_ref[...]
    for matrix in range(3):
        raw = matmul(first_input, attend_full[matrix])
        if matrix == 2:
            saved[2] = raw.astype(jnp.bfloat16)
        else:
            for start in range(0, width, 128):
                piece = raw[:, start : start + 128]
                saved[matrix, :, start : start + 128] = (
                    piece * cosines + turned(piece) * sines
                ).astype(jnp.bfloat16)
    tick(6)

    seq_length = length_ref[me]
    rows_at = lax.broadcasted_iota(jnp.int32, (length, length), 0)
    cols_at = lax.broadcasted_iota(jnp.int32, (length, length), 1)
    allowed = (cols_at <= rows_at) & (cols_at < seq_length)
    lower = first_half((length, 128))

    def heads(pair, carry):
        lanes = pl.ds(pl.multiple_of(pair * 128, 128), 128)
        query, key, value = saved[0, :, lanes], saved[1, :, lanes], saved[2, :, lanes]
        results = []
        for side in range(2):
            alone = jnp.where(lower == (side == 0), query, jnp.zeros_like(query))
            scores = jnp.where(allowed, nt(alone, key) * 0.125, -1e30)
            expo = jnp.exp(scores - jnp.max(scores, axis=-1, keepdims=True))
            soft = expo / jnp.sum(expo, axis=-1, keepdims=True)
            soft_ref[2 * pair + side] = soft
            results.append(matmul(soft.astype(jnp.bfloat16), value))
        saved[3, :, lanes] = jnp.where(lower, results[0], results[1]).astype(jnp.bfloat16)
        return carry

    lax.fori_loop(0, width // 128, heads, 0)
    hand_out(saved, saved_out)
    hand_out(soft_ref, soft_out)
    middle = tokens[...].astype(jnp.float32) + matmul(saved[3], attend_full[3])
    middle_ref[...] = middle
    hand_out(middle_ref, middle_out)
    second_all[me] = (middle * rms_factor(middle) * gains_full[1:2, :]).astype(jnp.bfloat16)
    second_moves = [
        links.copy(second_all.at[me], second_all.at[me], {"exp": peer}) for peer in at.peers
    ]
    for moves in grad_moves:
        for move in moves:
            move.wait_recv()
    hand_out(grads_all, grads_out)
    tick(7)

    def hits(slot, by_row):
        line = meta_all[slot, 0:1, :]
        if by_row:
            names = lax.broadcasted_iota(jnp.int32, (capacity, length), 0).astype(jnp.float32)
            hit = names == line
        else:
            names = lax.broadcasted_iota(jnp.int32, (length, capacity), 1).astype(jnp.float32)
            hit = names == upright(line)
        return jnp.where(hit, 1.0, 0.0).astype(jnp.bfloat16)

    def spot_of(slot):
        return slice(slot * capacity, (slot + 1) * capacity)

    def here_of(slot):
        return slice(slot * length, (slot + 1) * length)

    for slot in range(members):
        pick = hits(slot, True)
        gate = jnp.sum(pick.astype(jnp.float32) * meta_all[slot, 1:2, :], axis=1, keepdims=True)
        rows_grad[spot_of(slot), :] = (matmul(pick, grads_all[slot]) * gate).astype(jnp.bfloat16)
    for move in second_moves:
        move.wait_recv()
    for slot in range(members):
        inputs_ref[here_of(slot), :] = second_all[deal_ref[slot]]
        rows_in[spot_of(slot), :] = matmul(hits(slot, True), inputs_ref[here_of(slot), :]).astype(
            jnp.bfloat16
        )
    inputs_turned[...] = inputs_ref[...].T
    rows_turned[...] = rows_in[...].T
    dense_out[...] = jnp.zeros_like(dense_out)
    dense_back[...] = jnp.zeros_like(dense_back)
    rows_out[...] = jnp.zeros_like(rows_out)
    rows_back[...] = jnp.zeros_like(rows_back)

    def branch(chunk, inputs, turned_inputs, outer, out, back):
        for step in range(steps):
            for side in range(2):
                for piece in range(2):
                    ring_copy(chunk, step, side, piece).wait_send()

        def part(index, carry):
            lanes = pl.ds(pl.multiple_of(index * 256, 256), 256)
            gate = matmul(inputs[...], wide_full[chunk, 0, :, lanes])
            up = matmul(inputs[...], wide_full[chunk, 1, :, lanes])
            rise = sigmoid(gate)
            smooth = gate * rise
            hidden = (smooth * up).astype(jnp.bfloat16)
            hidden_grad = nt(outer[...], down_full[chunk, lanes, :])
            gate_grad = (hidden_grad * up * (rise * (1.0 + gate * (1.0 - rise)))).astype(
                jnp.bfloat16
            )
            up_grad = (hidden_grad * smooth).astype(jnp.bfloat16)
            out[...] += matmul(hidden, down_full[chunk, lanes, :])
            back[...] += nt(gate_grad, wide_full[chunk, 0, :, lanes]) + nt(
                up_grad, wide_full[chunk, 1, :, lanes]
            )
            down_full[chunk, lanes, :] = tn(hidden, outer[...]).astype(jnp.bfloat16)
            wide_full[chunk, 0, :, lanes] = matmul(turned_inputs[...], gate_grad).astype(
                jnp.bfloat16
            )
            wide_full[chunk, 1, :, lanes] = matmul(turned_inputs[...], up_grad).astype(
                jnp.bfloat16
            )
            return carry

        lax.fori_loop(0, down_full.shape[1] // 256, part, 0)
        kept(chunk, 0).start()
        kept(chunk, 1).start()

    def kept(chunk, piece):
        source, target = ((wide_full, wide_grads), (down_full, down_grads))[piece]
        return pltpu.make_async_copy(
            source.at[chunk], target.at[chunk], local_sems.at[2 * chunk + piece]
        )

    outer_all = grads_all.reshape(members * length, width)
    flat = (members * length, width)
    dense = (
        inputs_ref,
        inputs_turned,
        outer_all,
        dense_out.reshape(flat),
        dense_back.reshape(flat),
    )

    def first_sum(which, side, piece):
        owner = at.owner(-1 if side == 0 else 1)
        group_of = pl.ds(0, chunks - 1) if which == 0 else pl.ds(chunks - 1, 1)
        if piece == 0:
            spot = wide_full.at[group_of, side, rows(owner * block, block), :]
        else:
            spot = down_full.at[group_of, rows(owner * low + side * (low // 2), low // 2), :]
        return remote(
            spot,
            (wide_first, down_first)[piece].at[side, group_of],
            first_sends,
            first_arrivals,
            which * 4 + side * 2 + piece,
            (at.next, at.back)[side],
        )

    def start_sums(which):
        for piece in range(2):
            for side in range(2):
                first_sum(which, side, piece).start()

    def next_chunk(chunk, carry):
        for last in (steps - 1, steps):
            for ahead in range(groups // 2):
                @pl.when((chunk > 0) & (chunk + ahead < chunks))
                def _():
                    ring_step(chunk + ahead, last - 2 * ahead)

        @pl.when(chunk == chunks - 1)
        def _():
            start_sums(0)

        @pl.when(chunk == 1)
        def _():
            branch(chunk, *dense)

        @pl.when(chunk != 1)
        def _():
            branch(chunk, rows_in, rows_turned, rows_grad, rows_out, rows_back)

        return carry

    lax.fori_loop(0, chunks, next_chunk, 0)
    start_sums(1)

    for slot in range(members):
        pick = hits(slot, False)
        gate = upright(meta_all[slot, 1:2, :])
        picked = matmul(pick, rows_out[spot_of(slot), :].astype(jnp.bfloat16))
        inner = rows_back[spot_of(slot), :].astype(jnp.bfloat16)
        dense_out[slot] += gate * picked
        dense_back[slot] += matmul(pick, inner)
        score = jnp.sum(picked * grads_all[slot].astype(jnp.float32), axis=1, keepdims=True)
        gate_ref[slot] = jnp.broadcast_to(lying(score), gate_ref.shape[1:])
    for member in range(members):
        home = slot_of(deal_ref, member)
        result_ref[member] = dense_out[home].astype(jnp.bfloat16)
        back_ref[member] = dense_back[home].astype(jnp.bfloat16)
    for chunk in range(chunks):
        kept(chunk, 0).wait()
        kept(chunk, 1).wait()
    for which in range(2):
        for piece in range(2):
            for side in range(2):
                first_sum(which, side, piece).wait()
    for made in outgoing:
        made.wait()
    links.finish()


def scatter_kernel(
    groups,
    members,
    deal_ref,
    tokens,
    routes,
    gains_full,
    cos_ref,
    sin_ref,
    gate_parts,
    result_parts,
    back_parts,
    wide_grads,
    down_grads,
    wide_first,
    down_first,
    grads_in,
    middle_in,
    attend_in,
    saved_in,
    soft_in,
    output_ref,
    input_grad_ref,
    gate_grad_ref,
    expand_sum,
    reduce_sum,
    widen_sum,
    narrow_sum,
    project_sum,
    collect_sum,
    gains_sum,
    attend_sum,
    grads_all,
    middle_ref,
    attend_full,
    saved,
    soft_ref,
    gate_recv,
    result_recv,
    back_recv,
    wide_own,
    down_own,
    wide_recv,
    down_recv,
    wide_sum,
    turned_ref,
    attend_grad,
    near_recv,
    far_recv,
    far_send,
    attend_total,
    attend_recv,
    attend_back,
    widen_back,
    widen_home,
    gain_own,
    gain_recv,
    gain_ring,
    sends,
    arrivals,
    local_sems,
):
    at = Places(groups, members)
    links = Links(sends, arrivals)
    at.enter()
    me, steps = at.member, groups - 1
    length, width = tokens.shape
    chunks, low = down_own.shape[0], narrow_sum.shape[0]
    share = attend_sum.shape[1]
    block = share * members

    moves_of = {}

    def ring_step(step, piece, side):
        owner = at.owner(-1 - step if side == 0 else 1 + step)
        if piece == 0:
            spot = rows(owner * block, block)
            own, landing = wide_own.at[:, side, spot], wide_recv.at[side]
        else:
            spot = rows(owner * low + side * (low // 2), low // 2)
            own, landing = down_own.at[:, spot], down_recv.at[side]
        if step > 1:
            moves_of[step - 1, piece, side].wait_recv()
        for chunk in range(chunks):
            source = landing.at[step - 1, chunk]
            added = source[...].astype(jnp.float32) + own[chunk].astype(jnp.float32)
            index = max(chunk - 1, 0)
            start = side * (low // 2)
            if step < steps:
                source[...] = added.astype(jnp.bfloat16)
            elif piece == 0 and chunk != 1:
                wide_sum[index, side] = added
            elif piece == 0:
                for member in range(members):
                    widen_back[member, side] = added[member * share : (member + 1) * share, :]
            elif chunk != 1:
                reduce_sum[index * low + start : index * low + start + low // 2, :] = added
            else:
                narrow_sum[start : start + low // 2, :] = added
        if step < steps:
            moves_of[step, piece, side] = links.copy(
                landing.at[step - 1], landing.at[step], (at.next, at.back)[side]
            )

    def tick(step, between=0):
        for index in range(4):
            ring_step(step, index // 2, index % 2)
            if index < between:
                advance_small()

    kept = []

    def load(source, target):
        made = pltpu.make_async_copy(source, target, local_sems.at[len(kept)])
        made.start()
        kept.append(made)

    load(wide_first, wide_recv.at[:, 0])
    load(down_first, down_recv.at[:, 0])
    load(wide_grads, wide_own)
    load(down_grads, down_own)
    back_moves = [
        links.copy(back_parts.at[peer], back_recv.at[me], {"exp": peer}) for peer in at.peers
    ]
    load(back_parts.at[me], back_recv.at[me])
    load(middle_in, middle_ref)
    load(grads_in, grads_all)
    load(attend_in, attend_full)
    load(saved_in, saved)
    load(soft_in, soft_ref)
    load(result_parts.at[me], result_recv.at[me])
    gate_recv[me] = gate_parts[me]
    for made in kept[:4]:
        made.wait()
    tick(1)
    result_moves = [
        [
            links.copy(result_parts.at[peer], result_recv.at[me], {"exp": peer}),
            links.copy(gate_parts.at[peer], gate_recv.at[me], {"exp": peer}),
        ]
        for peer in at.peers
    ]
    for made in kept[4:]:
        made.wait()
    for move in back_moves:
        move.wait_recv()

    second_grad = back_recv[0].astype(jnp.float32)
    for member in range(1, members):
        second_grad = second_grad + back_recv[member].astype(jnp.float32)
    middle = middle_ref[...]
    scale = rms_factor(middle)
    gain_own[...] = jnp.zeros_like(gain_own)
    gain_own[1:2, :] = jnp.sum(second_grad * (middle * scale), axis=0, keepdims=True)
    input_grad_ref[...] = grads_all[slot_of(deal_ref, me)].astype(jnp.float32) + rms_back(
        middle, scale, second_grad * gains_full[1:2, :]
    )
    middle_low = input_grad_ref[...].astype(jnp.bfloat16)
    turned_ref[3] = nt(middle_low, attend_full[3]).astype(jnp.bfloat16)
    cosines, sines = cos_ref[...], sin_ref[...]
    lower = first_half((length, 128))

    def heads(pair, carry):
        lanes = pl.ds(pl.multiple_of(pair * 128, 128), 128)
        query, key, value = saved[0, :, lanes], saved[1, :, lanes], saved[2, :, lanes]
        outer = turned_ref[3, :, lanes]
        made = []
        for side in range(2):
            soft = soft_ref[2 * pair + side]
            alone = jnp.where(lower == (side == 0), outer, jnp.zeros_like(outer))
            value_grad = tn(soft.astype(jnp.bfloat16), outer)
            soft_grad = nt(alone, value)
            score_grad = (
                soft * (soft_grad - jnp.sum(soft * soft_grad, axis=-1, keepdims=True))
            ).astype(jnp.bfloat16)
            made.append(
                (matmul(score_grad, key) * 0.125, tn(score_grad, query) * 0.125, value_grad)
            )
        for index in range(3):
            joined = jnp.where(lower, made[0][index], made[1][index])
            if index < 2:
                joined = joined * cosines - turned(joined) * sines
            turned_ref[index, :, lanes] = joined.astype(jnp.bfloat16)
        return carry

    lax.fori_loop(0, width // 128, heads, 0)
    attend_grad[3] = tn(saved[3], middle_low).astype(jnp.bfloat16)
    for matrix in range(3):
        attend_grad[matrix] = tn(saved[4], turned_ref[matrix]).astype(jnp.bfloat16)
    near_moves = [
        links.copy(attend_grad.at[matrix], near_recv.at[index], {"exp": at.near})
        for index, matrix in enumerate((at.near, at.cross))
    ]
    tick(2)
    first_grad = nt(turned_ref[0], attend_full[0])
    for matrix in range(1, 3):
        first_grad = first_grad + nt(turned_ref[matrix], attend_full[matrix])
    stream = tokens[...].astype(jnp.float32)
    scale = rms_factor(stream)
    gain_own[0:1, :] = jnp.sum(first_grad * (stream * scale), axis=0, keepdims=True)
    gain_moves = [links.copy(gain_own, gain_recv.at[me], {"exp": peer}) for peer in at.peers]
    gain_recv[me] = gain_own[...]
    input_grad_ref[...] += rms_back(stream, scale, first_grad * gains_full[0:1, :])
    for move in near_moves:
        move.wait_recv()
    far_send[...] = (
        attend_grad[at.far].astype(jnp.float32) + near_recv[1].astype(jnp.float32)
    ).astype(jnp.bfloat16)
    far_move = links.copy(far_send, far_recv, {"exp": at.far})
    tick(3)
    for moves in result_moves:
        for move in moves:
            move.wait_recv()
    output = middle_ref[...]
    for member in range(members):
        output = output + result_recv[member].astype(jnp.float32)
    output_ref[...] = output
    for choice in range(2):
        route = routes[choice : choice + 1, :]
        found = jnp.zeros((1, length), jnp.float32)
        for member in range(members):
            found = jnp.where(route == member, gate_recv[member, 0:1, :], found)
        gate_grad_ref[choice : choice + 1, :] = found
    tick(4)
    for move in gain_moves:
        move.wait_recv()
    total = gain_recv[0]
    for member in range(1, members):
        total = total + gain_recv[member]
    gain_ring[at.group] = total
    far_move.wait_recv()
    attend_total[...] = (
        attend_grad[me].astype(jnp.float32)
        + near_recv[0].astype(jnp.float32)
        + far_recv[...].astype(jnp.float32)
    ).astype(jnp.bfloat16)

    half = block // 2
    small, gain_steps = [], []

    def advance_small():
        step = len(small)
        owners = (at.owner(-1 - step), at.owner(1 + step))
        made = []
        for side, target in enumerate((at.next, at.back)):
            spot = attend_total.at[rows(owners[side] * block + side * half, half), :]
            if step:
                small[-1][side].wait_recv()
                source = attend_recv.at[side, step - 1]
                added = source[...].astype(jnp.float32) + spot[...].astype(jnp.float32)
                if step < steps:
                    source[...] = added.astype(jnp.bfloat16)
                else:
                    for member in range(members // 2):
                        attend_back[side * (members // 2) + member] = added[
                            member * share : (member + 1) * share, :
                        ]
                spot = source
            if step < steps:
                made.append(links.copy(spot, attend_recv.at[side, step], target))
        if step:
            gain_steps[-1].wait_recv()
        if step < steps:
            owner = at.owner(-step)
            gain_steps.append(links.copy(gain_ring.at[owner], gain_ring.at[owner], at.next))
        small.append(made)

    advance_small()
    for step in range(5, steps):
        tick(step, between=3)
    while len(small) <= steps:
        advance_small()
    attend_moves = [
        links.copy(attend_back.at[peer], attend_sum.at[me], {"exp": peer}) for peer in at.peers
    ]
    attend_sum[me] = attend_back[me]
    total = gain_ring[0]
    for group in range(1, groups):
        total = total + gain_ring[group]
    count = gains_sum.shape[1]
    start = (at.group * members + me) * count
    gains_sum[...] = pltpu.roll(total, width - start, 1)[0:2, 0:count]
    for index in range(2):
        ring_step(steps, 0, index)
    widen_home[me] = widen_back[me]
    widen_moves = [
        links.copy(widen_back.at[peer], widen_home.at[me], {"exp": peer}) for peer in at.peers
    ]
    for index in range(2):
        ring_step(steps, 1, index)
    span = 64 * (chunks - 1)
    for side in range(2):
        for pair in range(0, chunks - 1, 2):
            found = joined_lanes(wide_sum[pair, side], wide_sum[pair + 1, side])
            for index, part in enumerate(found):
                start = index * span + pair * 64
                expand_sum[side, :, start : start + 128] = part
    for move in attend_moves:
        move.wait_recv()
    project_sum[...] = attend_sum[0:3]
    collect_sum[...] = attend_sum[3]
    for move in widen_moves:
        move.wait_recv()
    for matrix in range(2):
        for member in range(0, members, 2):
            found = joined_lanes(widen_home[member, matrix], widen_home[member + 1, matrix])
            for index, part in enumerate(found):
                start = index * 64 * members + member * 64
                widen_sum[matrix, :, start : start + 128] = part
    links.finish()


def update_kernel(rates, copies, *refs):
    count = len(rates)
    given, refs = refs[: 4 * count + copies], refs[4 * count + copies :]
    made, held, sems = refs[: copies + 3 * count], refs[copies + 3 * count : -1], refs[-1]
    used = []

    def copy(source, target):
        move = pltpu.make_async_copy(source, target, sems.at[len(used)])
        move.start()
        used.append(move)
        return move

    parts = []
    for index in sorted(range(count), key=lambda at: -given[4 * at].size):
        weight = given[4 * index]
        whole = pl.ds(0, weight.shape[0])
        pieces = [whole]
        if weight.size > 200000:
            cut = weight.shape[0] // 2
            pieces = [pl.ds(0, cut), pl.ds(cut, cut)]
        for piece in pieces:
            loads = [
                copy(given[4 * index + at].at[piece], held[4 * index + at].at[piece])
                for at in range(4)
            ]
            parts.append((index, piece, loads))
    stores = [copy(given[4 * count + index], made[index]) for index in range(copies)]
    for index, piece, loads in parts:
        for load in loads:
            load.wait()
        weight, moment, variance, gradient = (
            held[4 * index + at].at[piece] for at in range(4)
        )
        grad = 0.5 * gradient[...]
        level = 1.0 / (1.0 - 0.5**STEP)
        moment_new = 0.5 * moment[...] + grad
        variance_new = 0.5 * variance[...] + 2.0 * grad * grad
        kept = weight[...]
        stepped = moment_new * level / (jnp.sqrt(variance_new * level) + 1e-08) + 0.1 * kept
        moment[...] = moment_new
        variance[...] = variance_new
        weight[...] = kept - rates[index] * stepped
        for at, source in enumerate((moment, variance, weight)):
            stores.append(copy(source, made[copies + 3 * index + at].at[piece]))
    for store in stores:
        store.wait()


def update_all(*groups, passed):
    given, shapes, held = [], [], []
    for _, weight, moment, variance, gradient in groups:
        given += [weight, moment, variance, gradient]
        held += [VMEM(array.shape, array.dtype) for array in (weight, moment, variance, gradient)]
        shapes += [jax.ShapeDtypeStruct(weight.shape, weight.dtype)] * 3
    return pl.pallas_call(
        functools.partial(update_kernel, [group[0] for group in groups], len(passed)),
        out_shape=[jax.ShapeDtypeStruct(array.shape, array.dtype) for array in passed] + shapes,
        in_specs=spaces("a" * (len(given) + len(passed))),
        out_specs=spaces("a" * (len(shapes) + len(passed))),
        scratch_shapes=held + [pltpu.SemaphoreType.DMA((16 * len(groups),))],
        compiler_params=pltpu.CompilerParams(vmem_limit_bytes=LIMIT),
    )(*given, *passed)


def rotary_lines(length):
    half = HEAD_FEATURES // 2
    freqs = np.exp(-np.log(10000.0) * np.arange(half) / half)
    angles = np.arange(length)[:, None] * freqs[None, :]
    cosines, sines = np.cos(angles), np.sin(angles)
    return (
        np.concatenate([cosines] * 4, axis=1).astype(np.float32),
        np.concatenate([-sines, sines] * 2, axis=1).astype(np.float32),
    )


def spaces(*names):
    kinds = {"v": pltpu.VMEM, "s": pltpu.SMEM, "a": pl.ANY}
    return [pl.BlockSpec(memory_space=kinds[name]) for name in "".join(names)]


def local(
    tokens,
    seq_lengths,
    deal_order,
    expert_routes,
    capacity_slots,
    gate_weights,
    cotangent,
    projector,
    projector_mean,
    projector_square,
    collector,
    collector_first_moment,
    collector_second_moment,
    widener,
    widener_mean,
    widener_square,
    narrower,
    narrower_mean,
    narrower_square,
    norm_gains,
    gains_mean,
    gains_square,
    expander,
    expander_mean,
    expander_square,
    reducer,
    reducer_mean,
    reducer_square,
):
    groups, members = lax.axis_size("grp"), lax.axis_size("exp")
    length, width = tokens.shape[1:]
    inner = expander.shape[3]
    piece = widener.shape[2] // members
    chunks = 1 + inner // piece
    capacity = 3 * length // members
    steps = groups - 1
    high, low, share = expander.shape[2], narrower.shape[0], projector.shape[1]
    bf16, f32 = jnp.bfloat16, jnp.float32
    shape = jax.ShapeDtypeStruct
    cosines, sines = (jnp.asarray(lines) for lines in rotary_lines(length))
    count = 16 * groups
    (
        wide_grads,
        down_grads,
        wide_first,
        down_first,
        attend_full,
        grads_all,
        saved,
        middle,
        soft,
        gains_full,
        result_parts,
        back_parts,
        gate_parts,
    ) = pl.pallas_call(
        functools.partial(gather_kernel, groups, members),
        out_shape=[
            shape((chunks, 2, width, piece), bf16),
            shape((chunks, piece, width), bf16),
            shape((2, chunks, high, piece), bf16),
            shape((2, chunks, low // 2, width), bf16),
            shape((4, width, width), bf16),
            shape((members, length, width), bf16),
            shape((5, length, width), bf16),
            shape((length, width), f32),
            shape((HEAD_COUNT, length, length), f32),
            shape((8, width), f32),
            shape((members, length, width), bf16),
            shape((members, length, width), bf16),
            shape((members, 8, length), f32),
        ],
        in_specs=spaces("ss", "v" * 14),
        out_specs=spaces("a" * 9, "v" * 4),
        scratch_shapes=[
            VMEM((4, width, width), bf16),
            VMEM((members, length, width), bf16),
            VMEM((5, length, width), bf16),
            VMEM((length, width), f32),
            VMEM((HEAD_COUNT, length, length), f32),
            VMEM((members, length, width), bf16),
            VMEM((members, 8, length), f32),
            VMEM((members, 8, length), f32),
            VMEM((4, share, width), f32),
            VMEM((4, share, width), f32),
            VMEM((members, 2, share, piece), f32),
            VMEM((members, 2, share, piece), f32),
            VMEM((8, width), f32),
            VMEM((members, 8, width), f32),
            VMEM((groups, 8, width), f32),
            VMEM((chunks, 2, width, piece), bf16),
            VMEM((chunks, piece, width), bf16),
            VMEM((chunks, 2, high, piece), bf16),
            VMEM((chunks, low, width), bf16),
            VMEM((members * length, width), bf16),
            VMEM((width, members * length), bf16),
            VMEM((members, length, width), f32),
            VMEM((members, length, width), f32),
            VMEM((members * capacity, width), bf16),
            VMEM((width, members * capacity), bf16),
            VMEM((members * capacity, width), bf16),
            VMEM((members * capacity, width), f32),
            VMEM((members * capacity, width), f32),
            pltpu.SemaphoreType.DMA((count,)),
            pltpu.SemaphoreType.DMA((count,)),
            pltpu.SemaphoreType.DMA((chunks * steps * 4,)),
            pltpu.SemaphoreType.DMA((chunks * steps * 4,)),
            pltpu.SemaphoreType.DMA((8,)),
            pltpu.SemaphoreType.DMA((8,)),
            pltpu.SemaphoreType.DMA((2 * chunks + 5,)),
        ],
        compiler_params=pltpu.CompilerParams(
            collective_id=0, has_side_effects=True, vmem_limit_bytes=LIMIT
        ),
    )(
        seq_lengths,
        deal_order,
        tokens[0],
        cotangent[0],
        expert_routes[0].T,
        capacity_slots[0].T,
        gate_weights[0].T,
        norm_gains,
        projector,
        collector,
        widener,
        narrower,
        expander[0],
        reducer[0],
        cosines,
        sines,
    )
    count = 32 * groups
    (
        output,
        input_grad,
        gate_grad,
        expand_sum,
        reduce_sum,
        widen_sum,
        narrow_sum,
        project_sum,
        collect_sum,
        gains_sum,
    ) = pl.pallas_call(
        functools.partial(scatter_kernel, groups, members),
        out_shape=[
            shape((length, width), f32),
            shape((length, width), f32),
            shape((2, length), f32),
            shape((2, high, inner), f32),
            shape(reducer.shape[1:], f32),
            shape(widener.shape, f32),
            shape(narrower.shape, f32),
            shape(projector.shape, f32),
            shape(collector.shape, f32),
            shape(norm_gains.shape, f32),
        ],
        in_specs=spaces("s", "v" * 6, "a" * 11),
        out_specs=spaces("v" * 10),
        scratch_shapes=[
            VMEM((4, share, width), f32),
            VMEM((members, length, width), bf16),
            VMEM((length, width), f32),
            VMEM((4, width, width), bf16),
            VMEM((5, length, width), bf16),
            VMEM((HEAD_COUNT, length, length), f32),
            VMEM((members, 8, length), f32),
            VMEM((members, length, width), bf16),
            VMEM((members, length, width), bf16),
            VMEM((chunks, 2, width, piece), bf16),
            VMEM((chunks, piece, width), bf16),
            VMEM((2, steps, chunks, high, piece), bf16),
            VMEM((2, steps, chunks, low // 2, width), bf16),
            VMEM((chunks - 1, 2, high, piece), f32),
            VMEM((4, length, width), bf16),
            VMEM((4, width, width), bf16),
            VMEM((2, width, width), bf16),
            VMEM((width, width), bf16),
            VMEM((width, width), bf16),
            VMEM((width, width), bf16),
            VMEM((2, steps, high // 2, width), bf16),
            VMEM((4, share, width), f32),
            VMEM((members, 2, share, piece), f32),
            VMEM((members, 2, share, piece), f32),
            VMEM((8, width), f32),
            VMEM((members, 8, width), f32),
            VMEM((groups, 8, width), f32),
            pltpu.SemaphoreType.DMA((count,)),
            pltpu.SemaphoreType.DMA((count,)),
            pltpu.SemaphoreType.DMA((11,)),
        ],
        compiler_params=pltpu.CompilerParams(
            collective_id=1, has_side_effects=True, vmem_limit_bytes=LIMIT
        ),
    )(
        deal_order,
        tokens[0],
        expert_routes[0].T,
        gains_full,
        cosines,
        sines,
        gate_parts,
        result_parts,
        back_parts,
        wide_grads,
        down_grads,
        wide_first,
        down_first,
        grads_all,
        middle,
        attend_full,
        saved,
        soft,
    )
    updated = update_all(
        (0.1, projector, projector_mean, projector_square, project_sum),
        (0.3, collector, collector_first_moment, collector_second_moment, collect_sum),
        (0.07, widener, widener_mean, widener_square, widen_sum),
        (0.045, narrower, narrower_mean, narrower_square, narrow_sum),
        (0.2, norm_gains, gains_mean, gains_square, gains_sum),
        (0.07, expander[0], expander_mean[0], expander_square[0], expand_sum),
        (0.045, reducer[0], reducer_mean[0], reducer_square[0], reduce_sum),
        passed=(output, input_grad),
    )
    return (
        updated[0][None],
        updated[1][None],
        gate_grad.T[None],
        *updated[2:17],
        *(found[None] for found in updated[17:]),
    )


def fits(mesh):
    groups, members = mesh.shape["grp"], mesh.shape["exp"]
    share = 64 * HEAD_COUNT // (groups * members)
    return members == 4 and groups % 2 == 0 and share % 8 == 0 and share * members // 2 % 16 == 0


def solution(mesh):
    placed = (
        P(("grp", "exp"), None, None),
        P("grp"),
        P("grp"),
        P(("grp", "exp"), None, None),
        P(("grp", "exp"), None, None),
        P(("grp", "exp"), None, None),
        P(("grp", "exp"), None, None),
        P(None, ("grp", "exp"), None),
        P(None, ("grp", "exp"), None),
        P(None, ("grp", "exp"), None),
        P(("grp", "exp"), None),
        P(("grp", "exp"), None),
        P(("grp", "exp"), None),
        P(None, ("grp", "exp"), None),
        P(None, ("grp", "exp"), None),
        P(None, ("grp", "exp"), None),
        P(("grp", "exp"), None),
        P(("grp", "exp"), None),
        P(("grp", "exp"), None),
        P(None, ("grp", "exp")),
        P(None, ("grp", "exp")),
        P(None, ("grp", "exp")),
        P("exp", None, "grp", None),
        P("exp", None, "grp", None),
        P("exp", None, "grp", None),
        P("exp", "grp", None),
        P("exp", "grp", None),
        P("exp", "grp", None),
    )
    return jax.shard_map(
        local if fits(mesh) else local_plain,
        mesh=mesh,
        in_specs=placed,
        out_specs=(
            P(("grp", "exp"), None, None),
            P(("grp", "exp"), None, None),
            P(("grp", "exp"), None, None),
            P(None, ("grp", "exp"), None),
            P(None, ("grp", "exp"), None),
            P(None, ("grp", "exp"), None),
            P(("grp", "exp"), None),
            P(("grp", "exp"), None),
            P(("grp", "exp"), None),
            P(None, ("grp", "exp"), None),
            P(None, ("grp", "exp"), None),
            P(None, ("grp", "exp"), None),
            P(("grp", "exp"), None),
            P(("grp", "exp"), None),
            P(("grp", "exp"), None),
            P(None, ("grp", "exp")),
            P(None, ("grp", "exp")),
            P(None, ("grp", "exp")),
            P("exp", None, "grp", None),
            P("exp", None, "grp", None),
            P("exp", None, "grp", None),
            P("exp", "grp", None),
            P("exp", "grp", None),
            P("exp", "grp", None),
        ),
        check_vma=False,
    )
```

```python
import functools

import jax
import jax.numpy as jnp
import numpy as np
from jax import lax
from jax.experimental import pallas as pl
from jax.experimental.pallas import tpu as pltpu
from jax.sharding import PartitionSpec as P

HEAD_COUNT = 12
HEAD_FEATURES = 64
STEP = 5


def rms_factor(values):
    return lax.rsqrt(jnp.mean(values * values, axis=-1, keepdims=True) + 1e-06)


def rms_back(values, factor, upstream):
    return factor * (
        upstream - values * factor * factor * jnp.mean(upstream * values, axis=-1, keepdims=True)
    )


def rotary(length):
    positions = jnp.arange(length, dtype=jnp.int32).astype(jnp.float32)
    half = HEAD_FEATURES // 2
    freqs = jnp.exp(
        -jnp.log(10000.0) * jnp.arange(half, dtype=jnp.int32).astype(jnp.float32) / half
    )
    angles = positions[:, None] * freqs[None, :]
    return (jnp.cos(angles)[:, None, :], jnp.sin(angles)[:, None, :])


def rotate(values, cosines, sines):
    half = values.shape[-1] // 2
    first = values[..., :half]
    second = values[..., half:]
    return jnp.concatenate(
        [first * cosines - second * sines, second * cosines + first * sines], axis=-1
    )


def rotate_back(values, cosines, sines):
    half = values.shape[-1] // 2
    first = values[..., :half]
    second = values[..., half:]
    return jnp.concatenate(
        [first * cosines + second * sines, second * cosines - first * sines], axis=-1
    )


def silu_slope(values):
    sigmoid_of = jax.nn.sigmoid(values)
    return sigmoid_of * (1.0 + values * (1.0 - sigmoid_of))


def matmul(left, right):
    return jnp.dot(left, right, preferred_element_type=jnp.float32)


def outer_sum(left, right):
    return jnp.einsum("ld,lf->df", left, right, preferred_element_type=jnp.float32)


def adamw_update(weight, moment, variance, gradient, rate):
    moment_new = 0.5 * moment + 0.5 * gradient
    variance_new = 0.5 * variance + 0.5 * gradient * gradient
    correct = 1.0 - 0.5**STEP
    stepped = moment_new / correct / (jnp.sqrt(variance_new / correct) + 1e-08) + 0.1 * weight
    return (moment_new, variance_new, weight - rate * stepped)


def local_plain(
    tokens,
    seq_lengths,
    deal_order,
    expert_routes,
    capacity_slots,
    gate_weights,
    cotangent,
    projector,
    projector_mean,
    projector_square,
    collector,
    collector_first_moment,
    collector_second_moment,
    widener,
    widener_mean,
    widener_square,
    narrower,
    narrower_mean,
    narrower_square,
    norm_gains,
    gains_mean,
    gains_square,
    expander,
    expander_mean,
    expander_square,
    reducer,
    reducer_mean,
    reducer_square,
):
    members = lax.axis_size("exp")
    member = lax.axis_index("exp")
    length_seq = tokens.shape[1]
    width = tokens.shape[2]
    local_experts = expander.shape[0]
    experts_all = local_experts * members
    capacity = 3 * length_seq // experts_all
    member_ids = jnp.arange(members, dtype=jnp.int32)
    source = deal_order[member]
    home_slot = jnp.sum(jnp.where(deal_order == member, member_ids, 0))
    seq_length = seq_lengths[source]
    piece = lax.all_gather(tokens, "exp", axis=0, tiled=True)
    chosen = jnp.arange(piece.shape[0], dtype=jnp.int32) == source
    dealt = jnp.sum(
        jnp.where(chosen[:, None, None], piece, jnp.zeros_like(piece)), axis=0, keepdims=True
    )
    residual_flow = dealt[0].astype(jnp.float32)
    project_full, collect_full, widen_full, narrow_full, gains_full = (
        lax.all_gather(projector.astype(jnp.bfloat16), ("grp", "exp"), axis=1, tiled=True),
        lax.all_gather(collector.astype(jnp.bfloat16), ("grp", "exp"), axis=0, tiled=True),
        lax.all_gather(widener.astype(jnp.bfloat16), ("grp", "exp"), axis=1, tiled=True),
        lax.all_gather(narrower.astype(jnp.bfloat16), ("grp", "exp"), axis=0, tiled=True),
        lax.all_gather(norm_gains.astype(jnp.bfloat16), ("grp", "exp"), axis=1, tiled=True),
    )
    expand_full, reduce_full = (
        lax.all_gather(expander.astype(jnp.bfloat16), "grp", axis=2, tiled=True),
        lax.all_gather(reducer.astype(jnp.bfloat16), "grp", axis=1, tiled=True),
    )
    gains_used = gains_full.astype(jnp.float32)
    cosines, sines = rotary(length_seq)
    scale_one = rms_factor(residual_flow)
    normed_one = residual_flow * scale_one
    first_input = (normed_one * gains_used[0]).astype(jnp.bfloat16)
    query_raw = matmul(first_input, project_full[0]).reshape(length_seq, HEAD_COUNT, HEAD_FEATURES)
    key_raw = matmul(first_input, project_full[1]).reshape(length_seq, HEAD_COUNT, HEAD_FEATURES)
    value_raw = matmul(first_input, project_full[2]).reshape(length_seq, HEAD_COUNT, HEAD_FEATURES)
    query_rot = rotate(query_raw, cosines, sines).astype(jnp.bfloat16)
    key_rot = rotate(key_raw, cosines, sines).astype(jnp.bfloat16)
    value_low = value_raw.astype(jnp.bfloat16)
    rows_at = jnp.arange(length_seq, dtype=jnp.int32)[:, None]
    cols_at = jnp.arange(length_seq, dtype=jnp.int32)[None, :]
    allowed = ((cols_at <= rows_at) & (cols_at < seq_length))[None]
    scores = (
        jnp.einsum("qhd,khd->hqk", query_rot, key_rot, preferred_element_type=jnp.float32) * 0.125
    )
    masked = jnp.where(allowed, scores, -1e30)
    top = jnp.max(masked, axis=-1, keepdims=True)
    expo = jnp.exp(masked - top)
    total = jnp.sum(expo, axis=-1, keepdims=True)
    soft = expo / total
    logsum = top + jnp.log(total)
    mixed_output = (
        jnp.einsum(
            "hqk,khd->qhd", soft.astype(jnp.bfloat16), value_low, preferred_element_type=jnp.float32
        )
        .reshape(length_seq, width)
        .astype(jnp.bfloat16)
    )
    middle_state = residual_flow + matmul(mixed_output, collect_full)
    scale_two = rms_factor(middle_state)
    normed_two = middle_state * scale_two
    second_input = (normed_two * gains_used[1]).astype(jnp.bfloat16)
    gating_scores = matmul(second_input, widen_full[0])
    upward_rows = matmul(second_input, widen_full[1])
    hidden_state = (jax.nn.silu(gating_scores) * upward_rows).astype(jnp.bfloat16)
    dense_branch = matmul(hidden_state, narrow_full)
    flat = (expert_routes[0] * capacity + capacity_slots[0]).reshape(-1)
    spread = jnp.repeat(second_input, 2, axis=0)
    dispatch = jnp.zeros((experts_all * capacity, width), jnp.bfloat16).at[flat].set(spread)
    dispatch = dispatch.reshape(experts_all, capacity, width)
    rows = lax.all_to_all(dispatch, "exp", split_axis=0, concat_axis=0, tiled=True)
    count = rows.shape[1]
    grouped = rows.reshape(members, local_experts, count, width)
    gate_pre = jnp.einsum(
        "sekd,edf->sekf", grouped, expand_full[:, 0], preferred_element_type=jnp.float32
    )
    up_pre = jnp.einsum(
        "sekd,edf->sekf", grouped, expand_full[:, 1], preferred_element_type=jnp.float32
    )
    hidden_rows = (jax.nn.silu(gate_pre) * up_pre).astype(jnp.bfloat16)
    result = jnp.einsum(
        "sekf,efd->sekd", hidden_rows, reduce_full, preferred_element_type=jnp.float32
    )
    result = result.astype(jnp.bfloat16).reshape(members * local_experts, count, width)
    returned_rows = lax.all_to_all(result, "exp", split_axis=0, concat_axis=0, tiled=True)
    outcome = (
        returned_rows,
        rows,
        gate_pre.reshape(members * local_experts, count, -1),
        up_pre.reshape(members * local_experts, count, -1),
    )
    returned, received, gate_kept, up_kept = outcome
    picked = (
        returned.reshape(experts_all * capacity, width)[flat]
        .reshape(length_seq, 2, width)
        .astype(jnp.float32)
    )
    gate_local = gate_weights[0]
    mixture = jnp.sum(gate_local[..., None] * picked, axis=1)
    layer_output = middle_state + dense_branch + mixture
    valid = (jnp.arange(length_seq, dtype=jnp.int32) < seq_length).astype(jnp.float32)
    grad_out = cotangent[0] * valid[:, None]
    grad_low = grad_out.astype(jnp.bfloat16)
    narrow_grad = outer_sum(hidden_state, grad_low)
    hidden_grad = jnp.einsum("ld,fd->lf", grad_low, narrow_full, preferred_element_type=jnp.float32)
    gating_grad = (hidden_grad * upward_rows * silu_slope(gating_scores)).astype(jnp.bfloat16)
    upward_grad = (hidden_grad * jax.nn.silu(gating_scores)).astype(jnp.bfloat16)
    widen_grad = jnp.stack(
        [outer_sum(second_input, gating_grad), outer_sum(second_input, upward_grad)]
    )
    second_grad = jnp.einsum(
        "lf,df->ld", gating_grad, widen_full[0], preferred_element_type=jnp.float32
    ) + jnp.einsum("lf,df->ld", upward_grad, widen_full[1], preferred_element_type=jnp.float32)
    gate_grad_local = jnp.sum(grad_out[:, None, :] * picked, axis=-1)
    result_grad = (
        (gate_local[..., None] * grad_out[:, None, :])
        .astype(jnp.bfloat16)
        .reshape(2 * length_seq, width)
    )
    grad_send = jnp.zeros((experts_all * capacity, width), jnp.bfloat16).at[flat].set(result_grad)
    grad_recv = lax.all_to_all(
        grad_send.reshape(experts_all, capacity, width),
        "exp",
        split_axis=0,
        concat_axis=0,
        tiled=True,
    )
    grad_group = grad_recv.reshape(members, local_experts, capacity, width)
    rows_group = received.reshape(members, local_experts, capacity, width)
    gate_pre = gate_kept.reshape(members, local_experts, capacity, -1)
    up_pre = up_kept.reshape(members, local_experts, capacity, -1)
    hidden_rows = (jax.nn.silu(gate_pre) * up_pre).astype(jnp.bfloat16)
    reduce_grad = jnp.einsum(
        "sekf,sekd->efd", hidden_rows, grad_group, preferred_element_type=jnp.float32
    )
    hidden_rows_grad = jnp.einsum(
        "sekd,efd->sekf", grad_group, reduce_full, preferred_element_type=jnp.float32
    )
    gate_rows_grad = (hidden_rows_grad * up_pre * silu_slope(gate_pre)).astype(jnp.bfloat16)
    up_rows_grad = (hidden_rows_grad * jax.nn.silu(gate_pre)).astype(jnp.bfloat16)
    expand_grad = jnp.stack(
        [
            jnp.einsum(
                "sekd,sekf->edf", rows_group, gate_rows_grad, preferred_element_type=jnp.float32
            ),
            jnp.einsum(
                "sekd,sekf->edf", rows_group, up_rows_grad, preferred_element_type=jnp.float32
            ),
        ],
        axis=1,
    )
    row_grads = jnp.einsum(
        "sekf,edf->sekd", gate_rows_grad, expand_full[:, 0], preferred_element_type=jnp.float32
    ) + jnp.einsum(
        "sekf,edf->sekd", up_rows_grad, expand_full[:, 1], preferred_element_type=jnp.float32
    )
    row_grads = row_grads.astype(jnp.bfloat16).reshape(experts_all, capacity, width)
    came_back = lax.all_to_all(row_grads, "exp", split_axis=0, concat_axis=0, tiled=True).reshape(
        experts_all * capacity, width
    )
    second_grad = second_grad + jnp.sum(
        came_back[flat].reshape(length_seq, 2, width).astype(jnp.float32), axis=1
    )
    gains_grad_two = jnp.sum(second_grad * normed_two, axis=0)
    middle_grad = grad_out + rms_back(middle_state, scale_two, second_grad * gains_used[1])
    middle_low = middle_grad.astype(jnp.bfloat16)
    collect_grad = outer_sum(mixed_output, middle_low)
    mixed_grad = jnp.einsum(
        "ld,ed->le", middle_low, collect_full, preferred_element_type=jnp.float32
    )
    mixed_grad = mixed_grad.astype(jnp.bfloat16).reshape(length_seq, HEAD_COUNT, HEAD_FEATURES)
    scores_again = (
        jnp.einsum("qhd,khd->hqk", query_rot, key_rot, preferred_element_type=jnp.float32) * 0.125
    )
    soft_again = jnp.where(allowed, jnp.exp(scores_again - logsum), 0.0)
    value_grad = jnp.einsum(
        "hqk,qhd->khd",
        soft_again.astype(jnp.bfloat16),
        mixed_grad,
        preferred_element_type=jnp.float32,
    )
    soft_grad = jnp.einsum(
        "qhd,khd->hqk", mixed_grad, value_low, preferred_element_type=jnp.float32
    )
    score_grad = (
        soft_again * (soft_grad - jnp.sum(soft_again * soft_grad, axis=-1, keepdims=True))
    ).astype(jnp.bfloat16)
    query_grad = (
        jnp.einsum("hqk,khd->qhd", score_grad, key_rot, preferred_element_type=jnp.float32) * 0.125
    )
    key_grad = (
        jnp.einsum("hqk,qhd->khd", score_grad, query_rot, preferred_element_type=jnp.float32)
        * 0.125
    )
    query_back = (
        rotate_back(query_grad, cosines, sines).reshape(length_seq, width).astype(jnp.bfloat16)
    )
    key_back = rotate_back(key_grad, cosines, sines).reshape(length_seq, width).astype(jnp.bfloat16)
    value_back = value_grad.reshape(length_seq, width).astype(jnp.bfloat16)
    project_grad = jnp.stack(
        [
            outer_sum(first_input, query_back),
            outer_sum(first_input, key_back),
            outer_sum(first_input, value_back),
        ]
    )
    first_grad = (
        jnp.einsum("le,de->ld", query_back, project_full[0], preferred_element_type=jnp.float32)
        + jnp.einsum("le,de->ld", key_back, project_full[1], preferred_element_type=jnp.float32)
        + jnp.einsum("le,de->ld", value_back, project_full[2], preferred_element_type=jnp.float32)
    )
    gains_grad_one = jnp.sum(first_grad * normed_one, axis=0)
    stream_grad = middle_grad + rms_back(residual_flow, scale_one, first_grad * gains_used[0])
    gains_grad = jnp.stack([gains_grad_one, gains_grad_two])
    project_part, collect_part, widen_part, narrow_part, gains_part = (
        lax.psum_scatter(project_grad, ("grp", "exp"), scatter_dimension=1, tiled=True),
        lax.psum_scatter(collect_grad, ("grp", "exp"), scatter_dimension=0, tiled=True),
        lax.psum_scatter(widen_grad, ("grp", "exp"), scatter_dimension=1, tiled=True),
        lax.psum_scatter(narrow_grad, ("grp", "exp"), scatter_dimension=0, tiled=True),
        lax.psum_scatter(gains_grad, ("grp", "exp"), scatter_dimension=1, tiled=True),
    )
    expand_part, reduce_part = (
        lax.psum_scatter(
            expand_grad.astype(jnp.bfloat16), "grp", scatter_dimension=2, tiled=True
        ).astype(jnp.float32),
        lax.psum_scatter(
            reduce_grad.astype(jnp.bfloat16), "grp", scatter_dimension=1, tiled=True
        ).astype(jnp.float32),
    )
    empty = jnp.zeros((1, length_seq, width), jnp.float32)
    pieces = (
        lax.all_gather(layer_output[None].astype(jnp.bfloat16), "exp", axis=0, tiled=True).astype(
            jnp.float32
        ),
        lax.all_gather(stream_grad[None].astype(jnp.bfloat16), "exp", axis=0, tiled=True).astype(
            jnp.float32
        ),
    )
    chosen = (jnp.arange(pieces[0].shape[0], dtype=jnp.int32) == home_slot)[:, None, None]
    homed_output = empty + jnp.sum(jnp.where(chosen, pieces[0], 0.0), axis=0, keepdims=True)
    homed_grad = empty + jnp.sum(jnp.where(chosen, pieces[1], 0.0), axis=0, keepdims=True)
    project_new = adamw_update(projector, projector_mean, projector_square, project_part, 0.1)
    collect_new = adamw_update(
        collector, collector_first_moment, collector_second_moment, collect_part, 0.3
    )
    widening_updated = adamw_update(widener, widener_mean, widener_square, widen_part, 0.07)
    narrowing_updated = adamw_update(narrower, narrower_mean, narrower_square, narrow_part, 0.045)
    gains_updated = adamw_update(norm_gains, gains_mean, gains_square, gains_part, 0.2)
    expansion_updated = adamw_update(expander, expander_mean, expander_square, expand_part, 0.07)
    reduction_updated = adamw_update(reducer, reducer_mean, reducer_square, reduce_part, 0.045)
    return (
        homed_output,
        homed_grad,
        gate_grad_local[None],
        project_new[0],
        project_new[1],
        project_new[2],
        collect_new[0],
        collect_new[1],
        collect_new[2],
        widening_updated[0],
        widening_updated[1],
        widening_updated[2],
        narrowing_updated[0],
        narrowing_updated[1],
        narrowing_updated[2],
        gains_updated[0],
        gains_updated[1],
        gains_updated[2],
        expansion_updated[0],
        expansion_updated[1],
        expansion_updated[2],
        reduction_updated[0],
        reduction_updated[1],
        reduction_updated[2],
    )


MESH = pl.DeviceIdType.MESH
VMEM = pltpu.VMEM
LIMIT = 60 * 1024 * 1024


def ring_place(index, groups):
    row, side = lax.div(index, 2), lax.rem(index, 2)
    return (1 - side) * row + side * (groups - 1 - row)


def ring_member(place, groups):
    side = lax.div(place, groups // 2)
    return 2 * ((1 - side) * place + side * (groups - 1 - place)) + side


def remote(source, target, sends, arrivals, at, device):
    return pltpu.make_async_remote_copy(
        src_ref=source,
        dst_ref=target,
        send_sem=sends.at[at],
        recv_sem=arrivals.at[at],
        device_id=device,
        device_id_type=MESH,
    )


class Links:
    def __init__(self, sends, arrivals):
        self.sends, self.arrivals, self.count, self.started = sends, arrivals, 0, []

    def copy(self, source, target, device):
        made = remote(source, target, self.sends, self.arrivals, self.count, device)
        self.count += 1
        made.start()
        self.started.append(made)
        return made

    def finish(self):
        for made in self.started:
            made.wait_send()


class Places:
    def __init__(self, groups, members):
        self.groups, self.members = groups, members
        self.group = lax.axis_index("grp")
        self.member = lax.axis_index("exp")
        self.place = ring_place(self.group, groups)
        self.next = {"grp": self.owner(1)}
        self.back = {"grp": self.owner(-1)}
        half = members // 2
        self.far = lax.rem(self.member + half, members)
        self.near = self.member + 1 - 2 * lax.rem(self.member, 2)
        self.cross = lax.rem(self.near + half, members)
        self.peers = [lax.rem(self.member + step, members) for step in range(1, members)]

    def owner(self, offset):
        place = lax.rem(self.place + offset + 2 * self.groups, self.groups)
        return ring_member(place, self.groups)

    def enter(self):
        barrier = pltpu.get_barrier_semaphore()
        partners = [self.next, self.back] + [{"exp": peer} for peer in self.peers]
        for partner in partners:
            pl.semaphore_signal(barrier, inc=1, device_id=partner, device_id_type=MESH)
        pl.semaphore_wait(barrier, len(partners))


def rows(start, count, align=16):
    return pl.ds(pl.multiple_of(start, align), count)


def first_half(shape):
    return lax.rem(lax.broadcasted_iota(jnp.int32, shape, len(shape) - 1), 128) < 64


def turned(values):
    lanes = lax.broadcasted_iota(jnp.int32, values.shape, 1)
    return jnp.where(
        lax.rem(lanes, HEAD_FEATURES) < HEAD_FEATURES // 2,
        pltpu.roll(values, 128 - HEAD_FEATURES // 2, 1),
        pltpu.roll(values, HEAD_FEATURES // 2, 1),
    )


def nt(left, right):
    return lax.dot_general(
        left, right, (((1,), (1,)), ((), ())), preferred_element_type=jnp.float32
    )


def tn(left, right):
    return lax.dot_general(
        left, right, (((0,), (0,)), ((), ())), preferred_element_type=jnp.float32
    )


def sigmoid(values):
    return 1.0 / (1.0 + jnp.exp(-values))


def same(length):
    shape = (length, length)
    return lax.broadcasted_iota(jnp.int32, shape, 0) == lax.broadcasted_iota(jnp.int32, shape, 1)


def upright(line):
    return jnp.sum(jnp.where(same(line.shape[1]), line, 0.0), axis=1, keepdims=True)


def lying(column):
    return jnp.sum(jnp.where(same(column.shape[0]), column, 0.0), axis=0, keepdims=True)


def slot_of(deal_ref, member):
    for _ in range(11):
        member = deal_ref[member]
    return member


def dealt_lanes(values, piece, pieces):
    low_lanes = lax.broadcasted_iota(jnp.int32, (values.shape[0], 128), 1) < 64
    found = []
    span = 64 * pieces
    for start in range(0, values.shape[1], 2 * span):
        start = start + piece // 2 * 128
        one, two = values[:, start : start + 128], values[:, start + span : start + span + 128]
        if piece % 2:
            one = pltpu.roll(one, 64, 1)
        else:
            two = pltpu.roll(two, 64, 1)
        found.append(jnp.where(low_lanes, one, two))
    return jnp.concatenate(found, axis=1)


def joined_lanes(even, odd):
    low_lanes = lax.broadcasted_iota(jnp.int32, (even.shape[0], 128), 1) < 64
    found = []
    for start in range(0, even.shape[1], 128):
        one, two = even[:, start : start + 128], odd[:, start : start + 128]
        found.append(jnp.where(low_lanes, one, pltpu.roll(two, 64, 1)))
        found.append(jnp.where(low_lanes, pltpu.roll(one, 64, 1), two))
    return found


def gather_kernel(
    groups,
    members,
    length_ref,
    deal_ref,
    tokens,
    cotangent_in,
    routes,
    places,
    gates,
    norm_gains,
    projector,
    collector,
    widener_in,
    narrower_in,
    expander_in,
    reducer_in,
    cos_ref,
    sin_ref,
    wide_grads,
    down_grads,
    wide_first,
    down_first,
    attend_out,
    grads_out,
    saved_out,
    middle_out,
    soft_out,
    result_out,
    back_out,
    gains_full,
    gate_ref,
    cotangent,
    widener,
    narrower,
    expander,
    reducer,
    result_ref,
    back_ref,
    attend_full,
    grads_all,
    saved,
    middle_ref,
    soft_ref,
    second_all,
    meta_send,
    meta_all,
    attend_send,
    attend_recv,
    widen_send,
    widen_recv,
    gains,
    gain_recv,
    gain_ring,
    wide_full,
    down_full,
    wide_own,
    down_own,
    inputs_ref,
    inputs_turned,
    dense_out,
    dense_back,
    rows_in,
    rows_turned,
    rows_grad,
    rows_out,
    rows_back,
    sends,
    arrivals,
    ring_sends,
    ring_arrivals,
    first_sends,
    first_arrivals,
    local_sems,
):
    at = Places(groups, members)
    links = Links(sends, arrivals)
    chunks, low = down_own.shape[:2]
    loads = {}
    for name, source, target in (
        ("expander", expander_in, expander),
        ("reducer", reducer_in, reducer),
        ("widener", widener_in, widener),
        ("narrower", narrower_in, narrower),
        ("cotangent", cotangent_in, cotangent),
    ):
        made = pltpu.make_async_copy(source, target, local_sems.at[2 * chunks + len(loads)])
        made.start(priority=1)
        loads[name] = made
    at.enter()
    me, steps = at.member, groups - 1
    share, width = projector.shape[1:]
    block = share * members
    length = tokens.shape[0]
    capacity = rows_in.shape[0] // members

    def ring_copy(chunk, step, side, piece):
        owner = at.owner(-step if side == 0 else step)
        if piece == 0:
            spot = wide_full.at[chunk, side, rows(owner * block, block), :]
            origin = wide_own.at[chunk, side]
        else:
            spot = down_full.at[chunk, rows(owner * low + side * (low // 2), low // 2), :]
            origin = down_own.at[chunk, pl.ds(side * (low // 2), low // 2), :]
        place = (chunk * steps + step) * 4 + side * 2 + piece
        return remote(
            spot if step else origin,
            spot,
            ring_sends,
            ring_arrivals,
            place,
            (at.next, at.back)[side],
        )

    def ring_step(chunk, step):
        for piece in range(2):
            for side in range(2):
                if step:
                    ring_copy(chunk, step - 1, side, piece).wait_recv()
                if step < steps:
                    ring_copy(chunk, step, side, piece).start()

    def tick(count):
        for chunk in range(chunks):
            if 0 <= count - 2 * chunk <= steps:
                ring_step(chunk, count - 2 * chunk)

    attend_send[0:3] = projector[...]
    attend_send[3] = collector[...]
    gains[...] = jnp.zeros_like(gains)
    gains[0:2, 0 : norm_gains.shape[1]] = norm_gains[...]
    gains[...] = pltpu.roll(gains[...], (at.group * members + me) * norm_gains.shape[1], 1)
    first_moves = [
        [
            links.copy(attend_send.at[peer], attend_recv.at[me], {"exp": peer}),
            links.copy(gains, gain_recv.at[me], {"exp": peer}),
        ]
        for peer in at.peers
    ]
    gain_recv[me] = gains[...]
    attend_recv[me] = attend_send[me]
    loads["widener"].wait()
    for matrix in range(2):
        for member in range(members):
            widen_send[member, matrix] = dealt_lanes(widener[matrix], member, members)
    widen_moves = [
        links.copy(widen_send.at[peer], widen_recv.at[me], {"exp": peer}) for peer in at.peers
    ]
    widen_recv[me] = widen_send[me]

    def stage(chunk):
        if chunk == 1:
            for matrix in range(2):
                wide_own[1, matrix] = jnp.concatenate(
                    [widen_recv[member, matrix] for member in range(members)], axis=0
                ).astype(jnp.bfloat16)
            down_own[1] = narrower[...].astype(jnp.bfloat16)
        else:
            index = max(chunk - 1, 0)
            for matrix in range(2):
                wide_own[chunk, matrix] = dealt_lanes(
                    expander[matrix], index, chunks - 1
                ).astype(jnp.bfloat16)
            down_own[chunk] = reducer[index * low : (index + 1) * low, :].astype(jnp.bfloat16)
        for side in range(2):
            wide_full[chunk, side, rows(at.group * block, block), :] = wide_own[chunk, side]
        down_full[chunk, rows(at.group * low, low), :] = down_own[chunk]

    loads["expander"].wait()
    loads["reducer"].wait()
    stage(0)
    tick(0)
    for moves in first_moves:
        for move in moves:
            move.wait_recv()
    attend_full[me, rows(at.group * block, block), :] = (
        attend_recv[...].reshape(block, width).astype(jnp.bfloat16)
    )
    total_gain = gain_recv[0]
    for member in range(1, members):
        total_gain = total_gain + gain_recv[member]
    gain_ring[at.group] = total_gain

    half = block // 2

    def unit(owner, side, matrix):
        return attend_full.at[matrix, rows(owner * block + side * half, half), :]

    def across(owner, side):
        spot = unit(owner, side, me)
        return (links.copy(spot, spot, {"exp": at.far}), links.copy(spot, spot, {"exp": at.near}))

    def onward(owner, side):
        spot = unit(owner, side, at.far)
        return links.copy(spot, spot, {"exp": at.near})

    ring, crossed, passed = [], [], []
    gain_moves = []
    for step in range(groups):
        owners = (at.owner(-step), at.owner(step))
        if step:
            for move in ring[-1]:
                move.wait_recv()
            gain_moves[-1].wait_recv()
        if step < steps:
            ring.append(
                [
                    links.copy(unit(owner, side, me), unit(owner, side, me), target)
                    for side, (owner, target) in enumerate(zip(owners, (at.next, at.back)))
                ]
            )
            gain_moves.append(
                links.copy(gain_ring.at[owners[0]], gain_ring.at[owners[0]], at.next)
            )
        crossed.append([across(owner, side) for side, owner in enumerate(owners)])
        if step:
            for side, owner in enumerate((at.owner(1 - step), at.owner(step - 1))):
                crossed[step - 1][side][0].wait_recv()
                passed.append(onward(owner, side))
        if step == 2:
            for move in widen_moves:
                move.wait_recv()
            loads["narrower"].wait()
            for chunk in range(1, chunks):
                stage(chunk)
        if step % 2:
            tick(step // 2 + 1)
    outgoing = []

    def hand_out(source, target):
        made = pltpu.make_async_copy(
            source, target, local_sems.at[2 * chunks + len(loads) + len(outgoing)]
        )
        made.start(priority=1)
        outgoing.append(made)

    loads["cotangent"].wait()
    valid = lax.broadcasted_iota(jnp.int32, (length, 1), 0) < length_ref[deal_ref[me]]
    grads_all[me] = jnp.where(valid, cotangent[...], 0.0).astype(jnp.bfloat16)
    route = [routes[choice : choice + 1, :] for choice in range(2)]
    place = [places[choice : choice + 1, :].astype(jnp.float32) for choice in range(2)]
    meta_send[...] = jnp.zeros_like(meta_send)
    for member in range(members):
        named = [chosen == member for chosen in route]
        meta_send[member, 0:1, :] = jnp.where(
            named[0], place[0], jnp.where(named[1], place[1], -1.0)
        )
        meta_send[member, 1:2, :] = jnp.where(
            named[0], gates[0:1, :], jnp.where(named[1], gates[1:2, :], 0.0)
        )
    meta_all[me] = meta_send[me]
    grad_moves = [
        [
            links.copy(grads_all.at[me], grads_all.at[me], {"exp": peer}),
            links.copy(meta_send.at[peer], meta_all.at[me], {"exp": peer}),
        ]
        for peer in at.peers
    ]
    for side, owner in enumerate((at.owner(-steps), at.owner(steps))):
        crossed[steps][side][0].wait_recv()
        passed.append(onward(owner, side))
    total_gain = gain_ring[0]
    for group in range(1, groups):
        total_gain = total_gain + gain_ring[group]
    gains_full[...] = total_gain.astype(jnp.bfloat16).astype(jnp.float32)
    stream = tokens[...].astype(jnp.float32)
    first_input = (stream * rms_factor(stream) * gains_full[0:1, :]).astype(jnp.bfloat16)
    saved[4] = first_input
    for moves in crossed:
        for move in moves:
            move[1].wait_recv()
    for move in passed:
        move.wait_recv()
    tick(5)
    hand_out(attend_full, attend_out)

    cosines, sines = cos_ref[...], sin_ref[...]
    for matrix in range(3):
        raw = matmul(first_input, attend_full[matrix])
        if matrix == 2:
            saved[2] = raw.astype(jnp.bfloat16)
        else:
            for start in range(0, width, 128):
                piece = raw[:, start : start + 128]
                saved[matrix, :, start : start + 128] = (
                    piece * cosines + turned(piece) * sines
                ).astype(jnp.bfloat16)
    tick(6)

    seq_length = length_ref[me]
    rows_at = lax.broadcasted_iota(jnp.int32, (length, length), 0)
    cols_at = lax.broadcasted_iota(jnp.int32, (length, length), 1)
    allowed = (cols_at <= rows_at) & (cols_at < seq_length)
    lower = first_half((length, 128))

    def heads(pair, carry):
        lanes = pl.ds(pl.multiple_of(pair * 128, 128), 128)
        query, key, value = saved[0, :, lanes], saved[1, :, lanes], saved[2, :, lanes]
        results = []
        for side in range(2):
            alone = jnp.where(lower == (side == 0), query, jnp.zeros_like(query))
            scores = jnp.where(allowed, nt(alone, key) * 0.125, -1e30)
            expo = jnp.exp(scores - jnp.max(scores, axis=-1, keepdims=True))
            soft = expo / jnp.sum(expo, axis=-1, keepdims=True)
            soft_ref[2 * pair + side] = soft
            results.append(matmul(soft.astype(jnp.bfloat16), value))
        saved[3, :, lanes] = jnp.where(lower, results[0], results[1]).astype(jnp.bfloat16)
        return carry

    lax.fori_loop(0, width // 128, heads, 0)
    hand_out(saved, saved_out)
    hand_out(soft_ref, soft_out)
    middle = tokens[...].astype(jnp.float32) + matmul(saved[3], attend_full[3])
    middle_ref[...] = middle
    hand_out(middle_ref, middle_out)
    second_all[me] = (middle * rms_factor(middle) * gains_full[1:2, :]).astype(jnp.bfloat16)
    second_moves = [
        links.copy(second_all.at[me], second_all.at[me], {"exp": peer}) for peer in at.peers
    ]
    for moves in grad_moves:
        for move in moves:
            move.wait_recv()
    hand_out(grads_all, grads_out)
    tick(7)

    def hits(slot, by_row):
        line = meta_all[slot, 0:1, :]
        if by_row:
            names = lax.broadcasted_iota(jnp.int32, (capacity, length), 0).astype(jnp.float32)
            hit = names == line
        else:
            names = lax.broadcasted_iota(jnp.int32, (length, capacity), 1).astype(jnp.float32)
            hit = names == upright(line)
        return jnp.where(hit, 1.0, 0.0).astype(jnp.bfloat16)

    def spot_of(slot):
        return slice(slot * capacity, (slot + 1) * capacity)

    def here_of(slot):
        return slice(slot * length, (slot + 1) * length)

    for slot in range(members):
        pick = hits(slot, True)
        gate = jnp.sum(pick.astype(jnp.float32) * meta_all[slot, 1:2, :], axis=1, keepdims=True)
        rows_grad[spot_of(slot), :] = (matmul(pick, grads_all[slot]) * gate).astype(jnp.bfloat16)
    for move in second_moves:
        move.wait_recv()
    for slot in range(members):
        inputs_ref[here_of(slot), :] = second_all[deal_ref[slot]]
        rows_in[spot_of(slot), :] = matmul(hits(slot, True), inputs_ref[here_of(slot), :]).astype(
            jnp.bfloat16
        )
    inputs_turned[...] = inputs_ref[...].T
    rows_turned[...] = rows_in[...].T
    dense_out[...] = jnp.zeros_like(dense_out)
    dense_back[...] = jnp.zeros_like(dense_back)
    rows_out[...] = jnp.zeros_like(rows_out)
    rows_back[...] = jnp.zeros_like(rows_back)

    def branch(chunk, inputs, turned_inputs, outer, out, back):
        for step in range(steps):
            for side in range(2):
                for piece in range(2):
                    ring_copy(chunk, step, side, piece).wait_send()

        def part(index, carry):
            lanes = pl.ds(pl.multiple_of(index * 256, 256), 256)
            gate = matmul(inputs[...], wide_full[chunk, 0, :, lanes])
            up = matmul(inputs[...], wide_full[chunk, 1, :, lanes])
            rise = sigmoid(gate)
            smooth = gate * rise
            hidden = (smooth * up).astype(jnp.bfloat16)
            hidden_grad = nt(outer[...], down_full[chunk, lanes, :])
            gate_grad = (hidden_grad * up * (rise * (1.0 + gate * (1.0 - rise)))).astype(
                jnp.bfloat16
            )
            up_grad = (hidden_grad * smooth).astype(jnp.bfloat16)
            out[...] += matmul(hidden, down_full[chunk, lanes, :])
            back[...] += nt(gate_grad, wide_full[chunk, 0, :, lanes]) + nt(
                up_grad, wide_full[chunk, 1, :, lanes]
            )
            down_full[chunk, lanes, :] = tn(hidden, outer[...]).astype(jnp.bfloat16)
            wide_full[chunk, 0, :, lanes] = matmul(turned_inputs[...], gate_grad).astype(
                jnp.bfloat16
            )
            wide_full[chunk, 1, :, lanes] = matmul(turned_inputs[...], up_grad).astype(
                jnp.bfloat16
            )
            return carry

        lax.fori_loop(0, down_full.shape[1] // 256, part, 0)
        kept(chunk, 0).start(priority=1)
        kept(chunk, 1).start(priority=1)

    def kept(chunk, piece):
        source, target = ((wide_full, wide_grads), (down_full, down_grads))[piece]
        return pltpu.make_async_copy(
            source.at[chunk], target.at[chunk], local_sems.at[2 * chunk + piece]
        )

    outer_all = grads_all.reshape(members * length, width)
    flat = (members * length, width)
    dense = (
        inputs_ref,
        inputs_turned,
        outer_all,
        dense_out.reshape(flat),
        dense_back.reshape(flat),
    )

    def first_sum(chunk, side, piece):
        owner = at.owner(-1 if side == 0 else 1)
        if piece == 0:
            spot = wide_full.at[chunk, side, rows(owner * block, block), :]
        else:
            spot = down_full.at[chunk, rows(owner * low + side * (low // 2), low // 2), :]
        return remote(
            spot,
            (wide_first, down_first)[piece].at[chunk, side],
            first_sends,
            first_arrivals,
            chunk * 4 + side * 2 + piece,
            (at.next, at.back)[side],
        )

    def start_sums(chunk):
        for piece in range(2):
            for side in range(2):
                first_sum(chunk, side, piece).start()

    def next_chunk(chunk, carry):
        for last in (steps - 1, steps):
            for ahead in range(groups // 2):
                @pl.when((chunk > 0) & (chunk + ahead < chunks))
                def _():
                    ring_step(chunk + ahead, last - 2 * ahead)

        @pl.when(chunk == chunks - 1)
        def _():
            for early in range(chunks - 1):
                start_sums(early)

        @pl.when(chunk == 1)
        def _():
            branch(chunk, *dense)

        @pl.when(chunk != 1)
        def _():
            branch(chunk, rows_in, rows_turned, rows_grad, rows_out, rows_back)

        return carry

    lax.fori_loop(0, chunks, next_chunk, 0)
    start_sums(chunks - 1)

    for slot in range(members):
        pick = hits(slot, False)
        gate = upright(meta_all[slot, 1:2, :])
        picked = matmul(pick, rows_out[spot_of(slot), :].astype(jnp.bfloat16))
        inner = rows_back[spot_of(slot), :].astype(jnp.bfloat16)
        dense_out[slot] += gate * picked
        dense_back[slot] += matmul(pick, inner)
        score = jnp.sum(picked * grads_all[slot].astype(jnp.float32), axis=1, keepdims=True)
        gate_ref[slot] = jnp.broadcast_to(lying(score), gate_ref.shape[1:])
    for member in range(members):
        home = slot_of(deal_ref, member)
        back_ref[member] = dense_back[home].astype(jnp.bfloat16)
        hand_out(back_ref.at[member], back_out.at[member])
        result_ref[member] = dense_out[home].astype(jnp.bfloat16)
        hand_out(result_ref.at[member], result_out.at[member])
    for chunk in range(chunks):
        kept(chunk, 0).wait()
        kept(chunk, 1).wait()
        for piece in range(2):
            for side in range(2):
                first_sum(chunk, side, piece).wait()
    for made in outgoing:
        made.wait()
    links.finish()


def scatter_kernel(
    groups,
    members,
    deal_ref,
    tokens,
    routes,
    gains_full,
    cos_ref,
    sin_ref,
    gate_parts,
    result_parts,
    back_parts,
    wide_grads,
    down_grads,
    wide_first,
    down_first,
    grads_in,
    middle_in,
    attend_in,
    saved_in,
    soft_in,
    output_ref,
    input_grad_ref,
    gate_grad_ref,
    expand_sum,
    reduce_sum,
    widen_sum,
    narrow_sum,
    project_sum,
    collect_sum,
    gains_sum,
    attend_sum,
    grads_all,
    middle_ref,
    attend_full,
    saved,
    soft_ref,
    gate_recv,
    result_recv,
    back_recv,
    wide_own,
    down_own,
    wide_recv,
    down_recv,
    wide_sum,
    turned_ref,
    attend_grad,
    near_recv,
    far_recv,
    far_send,
    attend_total,
    attend_recv,
    attend_back,
    widen_back,
    widen_home,
    gain_own,
    gain_recv,
    gain_ring,
    sends,
    arrivals,
    local_sems,
):
    at = Places(groups, members)
    links = Links(sends, arrivals)
    at.enter()
    me, steps = at.member, groups - 1
    length, width = tokens.shape
    chunks, low = down_own.shape[0], narrow_sum.shape[0]
    share = attend_sum.shape[1]
    block = share * members

    moves_of = {}
    widen_moves = []

    def ring_step(chunk, step):
        made = []
        owners = (at.owner(-1 - step), at.owner(1 + step))
        for piece in range(2):
            for side, target in enumerate((at.next, at.back)):
                own = (wide_own, down_own)[piece]
                landing = (wide_recv, down_recv)[piece].at[chunk, side]
                if piece == 0:
                    spot = (chunk, side, rows(owners[side] * block, block))
                else:
                    spot = (chunk, rows(owners[side] * low + side * (low // 2), low // 2))
                if step > 1:
                    moves_of[chunk, step - 1][2 * piece + side].wait_recv()
                source = landing.at[step - 1]
                added = source[...].astype(jnp.float32) + own[spot].astype(jnp.float32)
                if step < steps:
                    source[...] = added.astype(jnp.bfloat16)
                elif piece == 0 and chunk != 1:
                    wide_sum[max(chunk - 1, 0), side] = added
                elif piece == 0:
                    for member in range(members):
                        widen_back[member, side] = added[member * share : (member + 1) * share, :]
                else:
                    start = side * (low // 2)
                    if chunk != 1:
                        start = start + max(chunk - 1, 0) * low
                        reduce_sum[start : start + low // 2, :] = added
                    else:
                        narrow_sum[start : start + low // 2, :] = added
                if step < steps:
                    made.append(links.copy(source, landing.at[step], target))
        moves_of[chunk, step] = made
        if step == steps and chunk == 1:
            widen_home[me] = widen_back[me]
            for peer in at.peers:
                widen_moves.append(
                    links.copy(widen_back.at[peer], widen_home.at[me], {"exp": peer})
                )
        if step == steps and chunk and chunk % 2 == 0:
            span = 64 * (chunks - 1)
            for side in range(2):
                found = joined_lanes(wide_sum[chunk - 2, side], wide_sum[chunk - 1, side])
                for index, part in enumerate(found):
                    start = index * span + (chunk - 2) * 64
                    expand_sum[side, :, start : start + 128] = part

    def tick(step, between=0):
        for made in own_loads[step]:
            made.wait()
        for chunk in (1, 0, *range(2, chunks)):
            ring_step(chunk, step)
            if chunk < between:
                advance_small()

    kept = []

    def load(source, target):
        made = pltpu.make_async_copy(source, target, local_sems.at[len(kept)])
        made.start(priority=1)
        kept.append(made)
        return made

    own_loads = {}

    def load_own(step):
        found = []
        for side, owner in enumerate((at.owner(-1 - step), at.owner(1 + step))):
            spot = rows(owner * block, block)
            found.append(load(wide_grads.at[:, side, spot], wide_own.at[:, side, spot]))
            spot = rows(owner * low + side * (low // 2), low // 2)
            found.append(load(down_grads.at[:, spot], down_own.at[:, spot]))
        own_loads[step] = found

    back_moves = [
        links.copy(back_parts.at[peer], back_recv.at[me], {"exp": peer}) for peer in at.peers
    ]
    first_loads = [
        load(wide_first.at[:, side], wide_recv.at[:, side, 0]) for side in range(2)
    ] + [load(down_first.at[:, side], down_recv.at[:, side, 0]) for side in range(2)]
    load_own(1)
    middle_loads = [
        load(back_parts.at[me], back_recv.at[me]),
        load(middle_in, middle_ref),
        load(grads_in, grads_all),
        load(attend_in.at[3], attend_full.at[3]),
        load(saved_in, saved),
    ]
    soft_load = load(soft_in, soft_ref)
    load_own(2)
    attend_load = load(attend_in.at[0:3], attend_full.at[0:3])
    for step in range(3, groups):
        load_own(step)
    result_load = load(result_parts.at[me], result_recv.at[me])
    gate_recv[me] = gate_parts[me]
    for made in first_loads:
        made.wait()
    tick(1)
    result_moves = [
        [
            links.copy(result_parts.at[peer], result_recv.at[me], {"exp": peer}),
            links.copy(gate_parts.at[peer], gate_recv.at[me], {"exp": peer}),
        ]
        for peer in at.peers
    ]
    for made in middle_loads:
        made.wait()
    for move in back_moves:
        move.wait_recv()

    second_grad = back_recv[0].astype(jnp.float32)
    for member in range(1, members):
        second_grad = second_grad + back_recv[member].astype(jnp.float32)
    middle = middle_ref[...]
    scale = rms_factor(middle)
    gain_own[...] = jnp.zeros_like(gain_own)
    gain_own[1:2, :] = jnp.sum(second_grad * (middle * scale), axis=0, keepdims=True)
    input_grad_ref[...] = grads_all[slot_of(deal_ref, me)].astype(jnp.float32) + rms_back(
        middle, scale, second_grad * gains_full[1:2, :]
    )
    middle_low = input_grad_ref[...].astype(jnp.bfloat16)
    turned_ref[3] = nt(middle_low, attend_full[3]).astype(jnp.bfloat16)
    cosines, sines = cos_ref[...], sin_ref[...]
    lower = first_half((length, 128))
    soft_load.wait()

    def heads(pair, carry):
        lanes = pl.ds(pl.multiple_of(pair * 128, 128), 128)
        query, key, value = saved[0, :, lanes], saved[1, :, lanes], saved[2, :, lanes]
        outer = turned_ref[3, :, lanes]
        made = []
        for side in range(2):
            soft = soft_ref[2 * pair + side]
            alone = jnp.where(lower == (side == 0), outer, jnp.zeros_like(outer))
            value_grad = tn(soft.astype(jnp.bfloat16), outer)
            soft_grad = nt(alone, value)
            score_grad = (
                soft * (soft_grad - jnp.sum(soft * soft_grad, axis=-1, keepdims=True))
            ).astype(jnp.bfloat16)
            made.append(
                (matmul(score_grad, key) * 0.125, tn(score_grad, query) * 0.125, value_grad)
            )
        for index in range(3):
            joined = jnp.where(lower, made[0][index], made[1][index])
            if index < 2:
                joined = joined * cosines - turned(joined) * sines
            turned_ref[index, :, lanes] = joined.astype(jnp.bfloat16)
        return carry

    lax.fori_loop(0, width // 128, heads, 0)
    attend_grad[3] = tn(saved[3], middle_low).astype(jnp.bfloat16)
    for matrix in range(3):
        attend_grad[matrix] = tn(saved[4], turned_ref[matrix]).astype(jnp.bfloat16)
    near_moves = [
        links.copy(attend_grad.at[matrix], near_recv.at[index], {"exp": at.near})
        for index, matrix in enumerate((at.near, at.cross))
    ]
    tick(2)
    attend_load.wait()
    first_grad = nt(turned_ref[0], attend_full[0])
    for matrix in range(1, 3):
        first_grad = first_grad + nt(turned_ref[matrix], attend_full[matrix])
    stream = tokens[...].astype(jnp.float32)
    scale = rms_factor(stream)
    gain_own[0:1, :] = jnp.sum(first_grad * (stream * scale), axis=0, keepdims=True)
    gain_moves = [links.copy(gain_own, gain_recv.at[me], {"exp": peer}) for peer in at.peers]
    gain_recv[me] = gain_own[...]
    input_grad_ref[...] += rms_back(stream, scale, first_grad * gains_full[0:1, :])
    for move in near_moves:
        move.wait_recv()
    far_send[...] = (
        attend_grad[at.far].astype(jnp.float32) + near_recv[1].astype(jnp.float32)
    ).astype(jnp.bfloat16)
    far_move = links.copy(far_send, far_recv, {"exp": at.far})
    tick(3)
    for moves in result_moves:
        for move in moves:
            move.wait_recv()
    result_load.wait()
    output = middle_ref[...]
    for member in range(members):
        output = output + result_recv[member].astype(jnp.float32)
    output_ref[...] = output
    for choice in range(2):
        route = routes[choice : choice + 1, :]
        found = jnp.zeros((1, length), jnp.float32)
        for member in range(members):
            found = jnp.where(route == member, gate_recv[member, 0:1, :], found)
        gate_grad_ref[choice : choice + 1, :] = found
    tick(4)
    for move in gain_moves:
        move.wait_recv()
    total = gain_recv[0]
    for member in range(1, members):
        total = total + gain_recv[member]
    gain_ring[at.group] = total
    far_move.wait_recv()
    attend_total[...] = (
        attend_grad[me].astype(jnp.float32)
        + near_recv[0].astype(jnp.float32)
        + far_recv[...].astype(jnp.float32)
    ).astype(jnp.bfloat16)

    half = block // 2
    small, gain_steps = [], []

    def advance_small():
        step = len(small)
        owners = (at.owner(-1 - step), at.owner(1 + step))
        made = []
        for side, target in enumerate((at.next, at.back)):
            spot = attend_total.at[rows(owners[side] * block + side * half, half), :]
            if step:
                small[-1][side].wait_recv()
                source = attend_recv.at[side, step - 1]
                added = source[...].astype(jnp.float32) + spot[...].astype(jnp.float32)
                if step < steps:
                    source[...] = added.astype(jnp.bfloat16)
                else:
                    for member in range(members // 2):
                        attend_back[side * (members // 2) + member] = added[
                            member * share : (member + 1) * share, :
                        ]
                spot = source
            if step < steps:
                made.append(links.copy(spot, attend_recv.at[side, step], target))
        if step:
            gain_steps[-1].wait_recv()
        if step < steps:
            owner = at.owner(-step)
            gain_steps.append(links.copy(gain_ring.at[owner], gain_ring.at[owner], at.next))
        small.append(made)

    advance_small()
    for step in range(5, steps):
        tick(step, between=3)
    while len(small) <= steps:
        advance_small()
    attend_moves = [
        links.copy(attend_back.at[peer], attend_sum.at[me], {"exp": peer}) for peer in at.peers
    ]
    attend_sum[me] = attend_back[me]
    total = gain_ring[0]
    for group in range(1, groups):
        total = total + gain_ring[group]
    count = gains_sum.shape[1]
    start = (at.group * members + me) * count
    gains_sum[...] = pltpu.roll(total, width - start, 1)[0:2, 0:count]
    tick(steps)
    for move in attend_moves:
        move.wait_recv()
    project_sum[...] = attend_sum[0:3]
    collect_sum[...] = attend_sum[3]
    for move in widen_moves:
        move.wait_recv()
    for matrix in range(2):
        for member in range(0, members, 2):
            found = joined_lanes(widen_home[member, matrix], widen_home[member + 1, matrix])
            for index, part in enumerate(found):
                start = index * 64 * members + member * 64
                widen_sum[matrix, :, start : start + 128] = part
    links.finish()


def update_kernel(rates, fixed, copies, *refs):
    count = len(rates)
    given, made = refs[: 4 * count + copies], refs[4 * count + copies :]
    for index in range(copies):
        made[index][...] = given[4 * count + index][...]

    def update(index):
        weight, moment, variance, gradient = given[4 * index : 4 * index + 4]
        grad = gradient[...]
        if len(weight.shape) < len(gradient.shape):
            grad = grad[3]
        elif weight.shape[0] < gradient.shape[0]:
            grad = grad[: weight.shape[0]]
        grad = 0.5 * grad
        level = 1.0 / (1.0 - 0.5**STEP)
        moment_new = 0.5 * moment[...] + grad
        variance_new = 0.5 * variance[...] + 2.0 * grad * grad
        kept = weight[...]
        stepped = moment_new * level / (jnp.sqrt(variance_new * level) + 1e-08) + 0.1 * kept
        made[copies + 3 * index][...] = moment_new
        made[copies + 3 * index + 1][...] = variance_new
        made[copies + 3 * index + 2][...] = kept - rates[index] * stepped

    for index in range(count):
        if fixed[index]:
            pl.when(pl.program_id(0) == 0)(functools.partial(update, index))
        else:
            update(index)


def update_all(*groups, passed):
    cuts = 4

    def spec(dims, cut):
        if cut is None:
            return pl.BlockSpec(dims, lambda step: (0,) * len(dims))
        block = tuple(size // cuts if at == cut else size for at, size in enumerate(dims))
        return pl.BlockSpec(
            block, lambda step: tuple(step if at == cut else 0 for at in range(len(dims)))
        )

    def cut_of(array):
        dims = array.shape
        for at in range(len(dims) - 1):
            if array.size > 100000 and dims[at] % (8 * cuts) == 0:
                return at
        return len(dims) - 1 if dims[-1] % (128 * cuts) == 0 else None

    given, specs, shapes, out_specs = [], [], [], []
    for _, weight, moment, variance, gradient in groups:
        cut = cut_of(weight)
        for array in (weight, moment, variance, gradient):
            given.append(array)
            specs.append(spec(array.shape, cut))
        for array in (weight, moment, variance):
            shapes.append(jax.ShapeDtypeStruct(array.shape, array.dtype))
            out_specs.append(spec(array.shape, cut))
    extra = [spec(array.shape, cut_of(array)) for array in passed]
    return pl.pallas_call(
        functools.partial(
            update_kernel,
            [group[0] for group in groups],
            [cut_of(group[1]) is None for group in groups],
            len(passed),
        ),
        grid=(cuts,),
        out_shape=[jax.ShapeDtypeStruct(array.shape, array.dtype) for array in passed] + shapes,
        in_specs=specs + extra,
        out_specs=extra + out_specs,
        compiler_params=pltpu.CompilerParams(vmem_limit_bytes=LIMIT),
    )(*given, *passed)


def rotary_lines(length):
    half = HEAD_FEATURES // 2
    freqs = np.exp(-np.log(10000.0) * np.arange(half) / half)
    angles = np.arange(length)[:, None] * freqs[None, :]
    cosines, sines = np.cos(angles), np.sin(angles)
    return (
        np.concatenate([cosines] * 4, axis=1).astype(np.float32),
        np.concatenate([-sines, sines] * 2, axis=1).astype(np.float32),
    )


def spaces(*names):
    kinds = {"v": pltpu.VMEM, "s": pltpu.SMEM, "a": pl.ANY}
    return [pl.BlockSpec(memory_space=kinds[name]) for name in "".join(names)]


def local(
    tokens,
    seq_lengths,
    deal_order,
    expert_routes,
    capacity_slots,
    gate_weights,
    cotangent,
    projector,
    projector_mean,
    projector_square,
    collector,
    collector_first_moment,
    collector_second_moment,
    widener,
    widener_mean,
    widener_square,
    narrower,
    narrower_mean,
    narrower_square,
    norm_gains,
    gains_mean,
    gains_square,
    expander,
    expander_mean,
    expander_square,
    reducer,
    reducer_mean,
    reducer_square,
):
    groups, members = lax.axis_size("grp"), lax.axis_size("exp")
    length, width = tokens.shape[1:]
    inner = expander.shape[3]
    piece = widener.shape[2] // members
    chunks = 1 + inner // piece
    capacity = 3 * length // members
    steps = groups - 1
    high, low, share = expander.shape[2], narrower.shape[0], projector.shape[1]
    bf16, f32 = jnp.bfloat16, jnp.float32
    shape = jax.ShapeDtypeStruct
    cosines, sines = (jnp.asarray(lines) for lines in rotary_lines(length))
    count = 16 * groups
    (
        wide_grads,
        down_grads,
        wide_first,
        down_first,
        attend_full,
        grads_all,
        saved,
        middle,
        soft,
        result_parts,
        back_parts,
        gains_full,
        gate_parts,
    ) = pl.pallas_call(
        functools.partial(gather_kernel, groups, members),
        out_shape=[
            shape((chunks, 2, width, piece), bf16),
            shape((chunks, piece, width), bf16),
            shape((chunks, 2, high, piece), bf16),
            shape((chunks, 2, low // 2, width), bf16),
            shape((4, width, width), bf16),
            shape((members, length, width), bf16),
            shape((5, length, width), bf16),
            shape((length, width), f32),
            shape((HEAD_COUNT, length, length), f32),
            shape((members, length, width), bf16),
            shape((members, length, width), bf16),
            shape((8, width), f32),
            shape((members, 8, length), f32),
        ],
        in_specs=spaces("ssvavvvvvvaaaavv"),
        out_specs=spaces("a" * 11, "vv"),
        scratch_shapes=[
            VMEM((length, width), f32),
            VMEM(widener.shape, f32),
            VMEM(narrower.shape, f32),
            VMEM(expander.shape[1:], f32),
            VMEM(reducer.shape[1:], f32),
            VMEM((members, length, width), bf16),
            VMEM((members, length, width), bf16),
            VMEM((4, width, width), bf16),
            VMEM((members, length, width), bf16),
            VMEM((5, length, width), bf16),
            VMEM((length, width), f32),
            VMEM((HEAD_COUNT, length, length), f32),
            VMEM((members, length, width), bf16),
            VMEM((members, 8, length), f32),
            VMEM((members, 8, length), f32),
            VMEM((4, share, width), f32),
            VMEM((4, share, width), f32),
            VMEM((members, 2, share, piece), f32),
            VMEM((members, 2, share, piece), f32),
            VMEM((8, width), f32),
            VMEM((members, 8, width), f32),
            VMEM((groups, 8, width), f32),
            VMEM((chunks, 2, width, piece), bf16),
            VMEM((chunks, piece, width), bf16),
            VMEM((chunks, 2, high, piece), bf16),
            VMEM((chunks, low, width), bf16),
            VMEM((members * length, width), bf16),
            VMEM((width, members * length), bf16),
            VMEM((members, length, width), f32),
            VMEM((members, length, width), f32),
            VMEM((members * capacity, width), bf16),
            VMEM((width, members * capacity), bf16),
            VMEM((members * capacity, width), bf16),
            VMEM((members * capacity, width), f32),
            VMEM((members * capacity, width), f32),
            pltpu.SemaphoreType.DMA((count,)),
            pltpu.SemaphoreType.DMA((count,)),
            pltpu.SemaphoreType.DMA((chunks * steps * 4,)),
            pltpu.SemaphoreType.DMA((chunks * steps * 4,)),
            pltpu.SemaphoreType.DMA((chunks * 4,)),
            pltpu.SemaphoreType.DMA((chunks * 4,)),
            pltpu.SemaphoreType.DMA((2 * chunks + 10 + 2 * members,)),
        ],
        compiler_params=pltpu.CompilerParams(
            collective_id=0, has_side_effects=True, vmem_limit_bytes=LIMIT
        ),
    )(
        seq_lengths,
        deal_order,
        tokens[0],
        cotangent[0],
        expert_routes[0].T,
        capacity_slots[0].T,
        gate_weights[0].T,
        norm_gains,
        projector,
        collector,
        widener,
        narrower,
        expander[0],
        reducer[0],
        cosines,
        sines,
    )
    count = 32 * groups
    (
        output,
        input_grad,
        gate_grad,
        expand_sum,
        reduce_sum,
        widen_sum,
        narrow_sum,
        project_sum,
        collect_sum,
        gains_sum,
    ) = pl.pallas_call(
        functools.partial(scatter_kernel, groups, members),
        out_shape=[
            shape((length, width), f32),
            shape((length, width), f32),
            shape((2, length), f32),
            shape((2, high, inner), f32),
            shape(reducer.shape[1:], f32),
            shape(widener.shape, f32),
            shape(narrower.shape, f32),
            shape(projector.shape, f32),
            shape(collector.shape, f32),
            shape(norm_gains.shape, f32),
        ],
        in_specs=spaces("s", "v" * 6, "a" * 11),
        out_specs=spaces("v" * 10),
        scratch_shapes=[
            VMEM((4, share, width), f32),
            VMEM((members, length, width), bf16),
            VMEM((length, width), f32),
            VMEM((4, width, width), bf16),
            VMEM((5, length, width), bf16),
            VMEM((HEAD_COUNT, length, length), f32),
            VMEM((members, 8, length), f32),
            VMEM((members, length, width), bf16),
            VMEM((members, length, width), bf16),
            VMEM((chunks, 2, width, piece), bf16),
            VMEM((chunks, piece, width), bf16),
            VMEM((chunks, 2, steps, high, piece), bf16),
            VMEM((chunks, 2, steps, low // 2, width), bf16),
            VMEM((chunks - 1, 2, high, piece), f32),
            VMEM((4, length, width), bf16),
            VMEM((4, width, width), bf16),
            VMEM((2, width, width), bf16),
            VMEM((width, width), bf16),
            VMEM((width, width), bf16),
            VMEM((width, width), bf16),
            VMEM((2, steps, high // 2, width), bf16),
            VMEM((4, share, width), f32),
            VMEM((members, 2, share, piece), f32),
            VMEM((members, 2, share, piece), f32),
            VMEM((8, width), f32),
            VMEM((members, 8, width), f32),
            VMEM((groups, 8, width), f32),
            pltpu.SemaphoreType.DMA((count,)),
            pltpu.SemaphoreType.DMA((count,)),
            pltpu.SemaphoreType.DMA((4 * groups + 16,)),
        ],
        compiler_params=pltpu.CompilerParams(
            collective_id=1, has_side_effects=True, vmem_limit_bytes=LIMIT
        ),
    )(
        deal_order,
        tokens[0],
        expert_routes[0].T,
        gains_full,
        cosines,
        sines,
        gate_parts,
        result_parts,
        back_parts,
        wide_grads,
        down_grads,
        wide_first,
        down_first,
        grads_all,
        middle,
        attend_full,
        saved,
        soft,
    )
    updated = update_all(
        (0.1, projector, projector_mean, projector_square, project_sum),
        (0.3, collector, collector_first_moment, collector_second_moment, collect_sum),
        (0.07, widener, widener_mean, widener_square, widen_sum),
        (0.045, narrower, narrower_mean, narrower_square, narrow_sum),
        (0.2, norm_gains, gains_mean, gains_square, gains_sum),
        (0.07, expander[0], expander_mean[0], expander_square[0], expand_sum),
        (0.045, reducer[0], reducer_mean[0], reducer_square[0], reduce_sum),
        passed=(output, input_grad),
    )
    return (
        updated[0][None],
        updated[1][None],
        gate_grad.T[None],
        *updated[2:17],
        *(found[None] for found in updated[17:]),
    )


def fits(mesh):
    groups, members = mesh.shape["grp"], mesh.shape["exp"]
    share = 64 * HEAD_COUNT // (groups * members)
    return members == 4 and groups % 2 == 0 and share % 8 == 0 and share * members // 2 % 16 == 0


def solution(mesh):
    placed = (
        P(("grp", "exp"), None, None),
        P("grp"),
        P("grp"),
        P(("grp", "exp"), None, None),
        P(("grp", "exp"), None, None),
        P(("grp", "exp"), None, None),
        P(("grp", "exp"), None, None),
        P(None, ("grp", "exp"), None),
        P(None, ("grp", "exp"), None),
        P(None, ("grp", "exp"), None),
        P(("grp", "exp"), None),
        P(("grp", "exp"), None),
        P(("grp", "exp"), None),
        P(None, ("grp", "exp"), None),
        P(None, ("grp", "exp"), None),
        P(None, ("grp", "exp"), None),
        P(("grp", "exp"), None),
        P(("grp", "exp"), None),
        P(("grp", "exp"), None),
        P(None, ("grp", "exp")),
        P(None, ("grp", "exp")),
        P(None, ("grp", "exp")),
        P("exp", None, "grp", None),
        P("exp", None, "grp", None),
        P("exp", None, "grp", None),
        P("exp", "grp", None),
        P("exp", "grp", None),
        P("exp", "grp", None),
    )
    return jax.shard_map(
        local if fits(mesh) else local_plain,
        mesh=mesh,
        in_specs=placed,
        out_specs=(
            P(("grp", "exp"), None, None),
            P(("grp", "exp"), None, None),
            P(("grp", "exp"), None, None),
            P(None, ("grp", "exp"), None),
            P(None, ("grp", "exp"), None),
            P(None, ("grp", "exp"), None),
            P(("grp", "exp"), None),
            P(("grp", "exp"), None),
            P(("grp", "exp"), None),
            P(None, ("grp", "exp"), None),
            P(None, ("grp", "exp"), None),
            P(None, ("grp", "exp"), None),
            P(("grp", "exp"), None),
            P(("grp", "exp"), None),
            P(("grp", "exp"), None),
            P(None, ("grp", "exp")),
            P(None, ("grp", "exp")),
            P(None, ("grp", "exp")),
            P("exp", None, "grp", None),
            P("exp", None, "grp", None),
            P("exp", None, "grp", None),
            P("exp", "grp", None),
            P("exp", "grp", None),
            P("exp", "grp", None),
        ),
        check_vma=False,
    )
```

```python
import functools

import jax
import jax.numpy as jnp
import numpy as np
from jax import lax
from jax.experimental import pallas as pl
from jax.experimental.pallas import tpu as pltpu
from jax.sharding import PartitionSpec as P

HEAD_COUNT = 12
HEAD_FEATURES = 64
STEP = 5


def rms_factor(values):
    return lax.rsqrt(jnp.mean(values * values, axis=-1, keepdims=True) + 1e-06)


def rms_back(values, factor, upstream):
    return factor * (
        upstream - values * factor * factor * jnp.mean(upstream * values, axis=-1, keepdims=True)
    )


def rotary(length):
    positions = jnp.arange(length, dtype=jnp.int32).astype(jnp.float32)
    half = HEAD_FEATURES // 2
    freqs = jnp.exp(
        -jnp.log(10000.0) * jnp.arange(half, dtype=jnp.int32).astype(jnp.float32) / half
    )
    angles = positions[:, None] * freqs[None, :]
    return (jnp.cos(angles)[:, None, :], jnp.sin(angles)[:, None, :])


def rotate(values, cosines, sines):
    half = values.shape[-1] // 2
    first = values[..., :half]
    second = values[..., half:]
    return jnp.concatenate(
        [first * cosines - second * sines, second * cosines + first * sines], axis=-1
    )


def rotate_back(values, cosines, sines):
    half = values.shape[-1] // 2
    first = values[..., :half]
    second = values[..., half:]
    return jnp.concatenate(
        [first * cosines + second * sines, second * cosines - first * sines], axis=-1
    )


def silu_slope(values):
    sigmoid_of = jax.nn.sigmoid(values)
    return sigmoid_of * (1.0 + values * (1.0 - sigmoid_of))


def matmul(left, right):
    return jnp.dot(left, right, preferred_element_type=jnp.float32)


def outer_sum(left, right):
    return jnp.einsum("ld,lf->df", left, right, preferred_element_type=jnp.float32)


def adamw_update(weight, moment, variance, gradient, rate):
    moment_new = 0.5 * moment + 0.5 * gradient
    variance_new = 0.5 * variance + 0.5 * gradient * gradient
    correct = 1.0 - 0.5**STEP
    stepped = moment_new / correct / (jnp.sqrt(variance_new / correct) + 1e-08) + 0.1 * weight
    return (moment_new, variance_new, weight - rate * stepped)


def local_plain(
    tokens,
    seq_lengths,
    deal_order,
    expert_routes,
    capacity_slots,
    gate_weights,
    cotangent,
    projector,
    projector_mean,
    projector_square,
    collector,
    collector_first_moment,
    collector_second_moment,
    widener,
    widener_mean,
    widener_square,
    narrower,
    narrower_mean,
    narrower_square,
    norm_gains,
    gains_mean,
    gains_square,
    expander,
    expander_mean,
    expander_square,
    reducer,
    reducer_mean,
    reducer_square,
):
    members = lax.axis_size("exp")
    member = lax.axis_index("exp")
    length_seq = tokens.shape[1]
    width = tokens.shape[2]
    local_experts = expander.shape[0]
    experts_all = local_experts * members
    capacity = 3 * length_seq // experts_all
    member_ids = jnp.arange(members, dtype=jnp.int32)
    source = deal_order[member]
    home_slot = jnp.sum(jnp.where(deal_order == member, member_ids, 0))
    seq_length = seq_lengths[source]
    piece = lax.all_gather(tokens, "exp", axis=0, tiled=True)
    chosen = jnp.arange(piece.shape[0], dtype=jnp.int32) == source
    dealt = jnp.sum(
        jnp.where(chosen[:, None, None], piece, jnp.zeros_like(piece)), axis=0, keepdims=True
    )
    residual_flow = dealt[0].astype(jnp.float32)
    project_full, collect_full, widen_full, narrow_full, gains_full = (
        lax.all_gather(projector.astype(jnp.bfloat16), ("grp", "exp"), axis=1, tiled=True),
        lax.all_gather(collector.astype(jnp.bfloat16), ("grp", "exp"), axis=0, tiled=True),
        lax.all_gather(widener.astype(jnp.bfloat16), ("grp", "exp"), axis=1, tiled=True),
        lax.all_gather(narrower.astype(jnp.bfloat16), ("grp", "exp"), axis=0, tiled=True),
        lax.all_gather(norm_gains.astype(jnp.bfloat16), ("grp", "exp"), axis=1, tiled=True),
    )
    expand_full, reduce_full = (
        lax.all_gather(expander.astype(jnp.bfloat16), "grp", axis=2, tiled=True),
        lax.all_gather(reducer.astype(jnp.bfloat16), "grp", axis=1, tiled=True),
    )
    gains_used = gains_full.astype(jnp.float32)
    cosines, sines = rotary(length_seq)
    scale_one = rms_factor(residual_flow)
    normed_one = residual_flow * scale_one
    first_input = (normed_one * gains_used[0]).astype(jnp.bfloat16)
    query_raw = matmul(first_input, project_full[0]).reshape(length_seq, HEAD_COUNT, HEAD_FEATURES)
    key_raw = matmul(first_input, project_full[1]).reshape(length_seq, HEAD_COUNT, HEAD_FEATURES)
    value_raw = matmul(first_input, project_full[2]).reshape(length_seq, HEAD_COUNT, HEAD_FEATURES)
    query_rot = rotate(query_raw, cosines, sines).astype(jnp.bfloat16)
    key_rot = rotate(key_raw, cosines, sines).astype(jnp.bfloat16)
    value_low = value_raw.astype(jnp.bfloat16)
    rows_at = jnp.arange(length_seq, dtype=jnp.int32)[:, None]
    cols_at = jnp.arange(length_seq, dtype=jnp.int32)[None, :]
    allowed = ((cols_at <= rows_at) & (cols_at < seq_length))[None]
    scores = (
        jnp.einsum("qhd,khd->hqk", query_rot, key_rot, preferred_element_type=jnp.float32) * 0.125
    )
    masked = jnp.where(allowed, scores, -1e30)
    top = jnp.max(masked, axis=-1, keepdims=True)
    expo = jnp.exp(masked - top)
    total = jnp.sum(expo, axis=-1, keepdims=True)
    soft = expo / total
    logsum = top + jnp.log(total)
    mixed_output = (
        jnp.einsum(
            "hqk,khd->qhd", soft.astype(jnp.bfloat16), value_low, preferred_element_type=jnp.float32
        )
        .reshape(length_seq, width)
        .astype(jnp.bfloat16)
    )
    middle_state = residual_flow + matmul(mixed_output, collect_full)
    scale_two = rms_factor(middle_state)
    normed_two = middle_state * scale_two
    second_input = (normed_two * gains_used[1]).astype(jnp.bfloat16)
    gating_scores = matmul(second_input, widen_full[0])
    upward_rows = matmul(second_input, widen_full[1])
    hidden_state = (jax.nn.silu(gating_scores) * upward_rows).astype(jnp.bfloat16)
    dense_branch = matmul(hidden_state, narrow_full)
    flat = (expert_routes[0] * capacity + capacity_slots[0]).reshape(-1)
    spread = jnp.repeat(second_input, 2, axis=0)
    dispatch = jnp.zeros((experts_all * capacity, width), jnp.bfloat16).at[flat].set(spread)
    dispatch = dispatch.reshape(experts_all, capacity, width)
    rows = lax.all_to_all(dispatch, "exp", split_axis=0, concat_axis=0, tiled=True)
    count = rows.shape[1]
    grouped = rows.reshape(members, local_experts, count, width)
    gate_pre = jnp.einsum(
        "sekd,edf->sekf", grouped, expand_full[:, 0], preferred_element_type=jnp.float32
    )
    up_pre = jnp.einsum(
        "sekd,edf->sekf", grouped, expand_full[:, 1], preferred_element_type=jnp.float32
    )
    hidden_rows = (jax.nn.silu(gate_pre) * up_pre).astype(jnp.bfloat16)
    result = jnp.einsum(
        "sekf,efd->sekd", hidden_rows, reduce_full, preferred_element_type=jnp.float32
    )
    result = result.astype(jnp.bfloat16).reshape(members * local_experts, count, width)
    returned_rows = lax.all_to_all(result, "exp", split_axis=0, concat_axis=0, tiled=True)
    outcome = (
        returned_rows,
        rows,
        gate_pre.reshape(members * local_experts, count, -1),
        up_pre.reshape(members * local_experts, count, -1),
    )
    returned, received, gate_kept, up_kept = outcome
    picked = (
        returned.reshape(experts_all * capacity, width)[flat]
        .reshape(length_seq, 2, width)
        .astype(jnp.float32)
    )
    gate_local = gate_weights[0]
    mixture = jnp.sum(gate_local[..., None] * picked, axis=1)
    layer_output = middle_state + dense_branch + mixture
    valid = (jnp.arange(length_seq, dtype=jnp.int32) < seq_length).astype(jnp.float32)
    grad_out = cotangent[0] * valid[:, None]
    grad_low = grad_out.astype(jnp.bfloat16)
    narrow_grad = outer_sum(hidden_state, grad_low)
    hidden_grad = jnp.einsum("ld,fd->lf", grad_low, narrow_full, preferred_element_type=jnp.float32)
    gating_grad = (hidden_grad * upward_rows * silu_slope(gating_scores)).astype(jnp.bfloat16)
    upward_grad = (hidden_grad * jax.nn.silu(gating_scores)).astype(jnp.bfloat16)
    widen_grad = jnp.stack(
        [outer_sum(second_input, gating_grad), outer_sum(second_input, upward_grad)]
    )
    second_grad = jnp.einsum(
        "lf,df->ld", gating_grad, widen_full[0], preferred_element_type=jnp.float32
    ) + jnp.einsum("lf,df->ld", upward_grad, widen_full[1], preferred_element_type=jnp.float32)
    gate_grad_local = jnp.sum(grad_out[:, None, :] * picked, axis=-1)
    result_grad = (
        (gate_local[..., None] * grad_out[:, None, :])
        .astype(jnp.bfloat16)
        .reshape(2 * length_seq, width)
    )
    grad_send = jnp.zeros((experts_all * capacity, width), jnp.bfloat16).at[flat].set(result_grad)
    grad_recv = lax.all_to_all(
        grad_send.reshape(experts_all, capacity, width),
        "exp",
        split_axis=0,
        concat_axis=0,
        tiled=True,
    )
    grad_group = grad_recv.reshape(members, local_experts, capacity, width)
    rows_group = received.reshape(members, local_experts, capacity, width)
    gate_pre = gate_kept.reshape(members, local_experts, capacity, -1)
    up_pre = up_kept.reshape(members, local_experts, capacity, -1)
    hidden_rows = (jax.nn.silu(gate_pre) * up_pre).astype(jnp.bfloat16)
    reduce_grad = jnp.einsum(
        "sekf,sekd->efd", hidden_rows, grad_group, preferred_element_type=jnp.float32
    )
    hidden_rows_grad = jnp.einsum(
        "sekd,efd->sekf", grad_group, reduce_full, preferred_element_type=jnp.float32
    )
    gate_rows_grad = (hidden_rows_grad * up_pre * silu_slope(gate_pre)).astype(jnp.bfloat16)
    up_rows_grad = (hidden_rows_grad * jax.nn.silu(gate_pre)).astype(jnp.bfloat16)
    expand_grad = jnp.stack(
        [
            jnp.einsum(
                "sekd,sekf->edf", rows_group, gate_rows_grad, preferred_element_type=jnp.float32
            ),
            jnp.einsum(
                "sekd,sekf->edf", rows_group, up_rows_grad, preferred_element_type=jnp.float32
            ),
        ],
        axis=1,
    )
    row_grads = jnp.einsum(
        "sekf,edf->sekd", gate_rows_grad, expand_full[:, 0], preferred_element_type=jnp.float32
    ) + jnp.einsum(
        "sekf,edf->sekd", up_rows_grad, expand_full[:, 1], preferred_element_type=jnp.float32
    )
    row_grads = row_grads.astype(jnp.bfloat16).reshape(experts_all, capacity, width)
    came_back = lax.all_to_all(row_grads, "exp", split_axis=0, concat_axis=0, tiled=True).reshape(
        experts_all * capacity, width
    )
    second_grad = second_grad + jnp.sum(
        came_back[flat].reshape(length_seq, 2, width).astype(jnp.float32), axis=1
    )
    gains_grad_two = jnp.sum(second_grad * normed_two, axis=0)
    middle_grad = grad_out + rms_back(middle_state, scale_two, second_grad * gains_used[1])
    middle_low = middle_grad.astype(jnp.bfloat16)
    collect_grad = outer_sum(mixed_output, middle_low)
    mixed_grad = jnp.einsum(
        "ld,ed->le", middle_low, collect_full, preferred_element_type=jnp.float32
    )
    mixed_grad = mixed_grad.astype(jnp.bfloat16).reshape(length_seq, HEAD_COUNT, HEAD_FEATURES)
    scores_again = (
        jnp.einsum("qhd,khd->hqk", query_rot, key_rot, preferred_element_type=jnp.float32) * 0.125
    )
    soft_again = jnp.where(allowed, jnp.exp(scores_again - logsum), 0.0)
    value_grad = jnp.einsum(
        "hqk,qhd->khd",
        soft_again.astype(jnp.bfloat16),
        mixed_grad,
        preferred_element_type=jnp.float32,
    )
    soft_grad = jnp.einsum(
        "qhd,khd->hqk", mixed_grad, value_low, preferred_element_type=jnp.float32
    )
    score_grad = (
        soft_again * (soft_grad - jnp.sum(soft_again * soft_grad, axis=-1, keepdims=True))
    ).astype(jnp.bfloat16)
    query_grad = (
        jnp.einsum("hqk,khd->qhd", score_grad, key_rot, preferred_element_type=jnp.float32) * 0.125
    )
    key_grad = (
        jnp.einsum("hqk,qhd->khd", score_grad, query_rot, preferred_element_type=jnp.float32)
        * 0.125
    )
    query_back = (
        rotate_back(query_grad, cosines, sines).reshape(length_seq, width).astype(jnp.bfloat16)
    )
    key_back = rotate_back(key_grad, cosines, sines).reshape(length_seq, width).astype(jnp.bfloat16)
    value_back = value_grad.reshape(length_seq, width).astype(jnp.bfloat16)
    project_grad = jnp.stack(
        [
            outer_sum(first_input, query_back),
            outer_sum(first_input, key_back),
            outer_sum(first_input, value_back),
        ]
    )
    first_grad = (
        jnp.einsum("le,de->ld", query_back, project_full[0], preferred_element_type=jnp.float32)
        + jnp.einsum("le,de->ld", key_back, project_full[1], preferred_element_type=jnp.float32)
        + jnp.einsum("le,de->ld", value_back, project_full[2], preferred_element_type=jnp.float32)
    )
    gains_grad_one = jnp.sum(first_grad * normed_one, axis=0)
    stream_grad = middle_grad + rms_back(residual_flow, scale_one, first_grad * gains_used[0])
    gains_grad = jnp.stack([gains_grad_one, gains_grad_two])
    project_part, collect_part, widen_part, narrow_part, gains_part = (
        lax.psum_scatter(project_grad, ("grp", "exp"), scatter_dimension=1, tiled=True),
        lax.psum_scatter(collect_grad, ("grp", "exp"), scatter_dimension=0, tiled=True),
        lax.psum_scatter(widen_grad, ("grp", "exp"), scatter_dimension=1, tiled=True),
        lax.psum_scatter(narrow_grad, ("grp", "exp"), scatter_dimension=0, tiled=True),
        lax.psum_scatter(gains_grad, ("grp", "exp"), scatter_dimension=1, tiled=True),
    )
    expand_part, reduce_part = (
        lax.psum_scatter(
            expand_grad.astype(jnp.bfloat16), "grp", scatter_dimension=2, tiled=True
        ).astype(jnp.float32),
        lax.psum_scatter(
            reduce_grad.astype(jnp.bfloat16), "grp", scatter_dimension=1, tiled=True
        ).astype(jnp.float32),
    )
    empty = jnp.zeros((1, length_seq, width), jnp.float32)
    pieces = (
        lax.all_gather(layer_output[None].astype(jnp.bfloat16), "exp", axis=0, tiled=True).astype(
            jnp.float32
        ),
        lax.all_gather(stream_grad[None].astype(jnp.bfloat16), "exp", axis=0, tiled=True).astype(
            jnp.float32
        ),
    )
    chosen = (jnp.arange(pieces[0].shape[0], dtype=jnp.int32) == home_slot)[:, None, None]
    homed_output = empty + jnp.sum(jnp.where(chosen, pieces[0], 0.0), axis=0, keepdims=True)
    homed_grad = empty + jnp.sum(jnp.where(chosen, pieces[1], 0.0), axis=0, keepdims=True)
    project_new = adamw_update(projector, projector_mean, projector_square, project_part, 0.1)
    collect_new = adamw_update(
        collector, collector_first_moment, collector_second_moment, collect_part, 0.3
    )
    widening_updated = adamw_update(widener, widener_mean, widener_square, widen_part, 0.07)
    narrowing_updated = adamw_update(narrower, narrower_mean, narrower_square, narrow_part, 0.045)
    gains_updated = adamw_update(norm_gains, gains_mean, gains_square, gains_part, 0.2)
    expansion_updated = adamw_update(expander, expander_mean, expander_square, expand_part, 0.07)
    reduction_updated = adamw_update(reducer, reducer_mean, reducer_square, reduce_part, 0.045)
    return (
        homed_output,
        homed_grad,
        gate_grad_local[None],
        project_new[0],
        project_new[1],
        project_new[2],
        collect_new[0],
        collect_new[1],
        collect_new[2],
        widening_updated[0],
        widening_updated[1],
        widening_updated[2],
        narrowing_updated[0],
        narrowing_updated[1],
        narrowing_updated[2],
        gains_updated[0],
        gains_updated[1],
        gains_updated[2],
        expansion_updated[0],
        expansion_updated[1],
        expansion_updated[2],
        reduction_updated[0],
        reduction_updated[1],
        reduction_updated[2],
    )


MESH = pl.DeviceIdType.MESH
VMEM = pltpu.VMEM
LIMIT = 60 * 1024 * 1024


def ring_place(index, groups):
    row, side = lax.div(index, 2), lax.rem(index, 2)
    return (1 - side) * row + side * (groups - 1 - row)


def ring_member(place, groups):
    side = lax.div(place, groups // 2)
    return 2 * ((1 - side) * place + side * (groups - 1 - place)) + side


def remote(source, target, sends, arrivals, at, device):
    return pltpu.make_async_remote_copy(
        src_ref=source,
        dst_ref=target,
        send_sem=sends.at[at],
        recv_sem=arrivals.at[at],
        device_id=device,
        device_id_type=MESH,
    )


class Links:
    def __init__(self, sends, arrivals):
        self.sends, self.arrivals, self.count, self.started = sends, arrivals, 0, []

    def copy(self, source, target, device):
        made = remote(source, target, self.sends, self.arrivals, self.count, device)
        self.count += 1
        made.start()
        self.started.append(made)
        return made

    def finish(self):
        for made in self.started:
            made.wait_send()


class Places:
    def __init__(self, groups, members):
        self.groups, self.members = groups, members
        self.group = lax.axis_index("grp")
        self.member = lax.axis_index("exp")
        self.place = ring_place(self.group, groups)
        self.next = {"grp": self.owner(1)}
        self.back = {"grp": self.owner(-1)}
        half = members // 2
        self.far = lax.rem(self.member + half, members)
        self.near = self.member + 1 - 2 * lax.rem(self.member, 2)
        self.cross = lax.rem(self.near + half, members)
        self.peers = [lax.rem(self.member + step, members) for step in range(1, members)]

    def owner(self, offset):
        place = lax.rem(self.place + offset + 2 * self.groups, self.groups)
        return ring_member(place, self.groups)

    def enter(self):
        barrier = pltpu.get_barrier_semaphore()
        partners = [self.next, self.back] + [{"exp": peer} for peer in self.peers]
        for partner in partners:
            pl.semaphore_signal(barrier, inc=1, device_id=partner, device_id_type=MESH)
        pl.semaphore_wait(barrier, len(partners))


def rows(start, count, align=16):
    return pl.ds(pl.multiple_of(start, align), count)


def first_half(shape):
    return lax.rem(lax.broadcasted_iota(jnp.int32, shape, len(shape) - 1), 128) < 64


def turned(values):
    lanes = lax.broadcasted_iota(jnp.int32, values.shape, 1)
    return jnp.where(
        lax.rem(lanes, HEAD_FEATURES) < HEAD_FEATURES // 2,
        pltpu.roll(values, 128 - HEAD_FEATURES // 2, 1),
        pltpu.roll(values, HEAD_FEATURES // 2, 1),
    )


def nt(left, right):
    return lax.dot_general(
        left, right, (((1,), (1,)), ((), ())), preferred_element_type=jnp.float32
    )


def tn(left, right):
    return lax.dot_general(
        left, right, (((0,), (0,)), ((), ())), preferred_element_type=jnp.float32
    )


def sigmoid(values):
    return 1.0 / (1.0 + jnp.exp(-values))


def same(length):
    shape = (length, length)
    return lax.broadcasted_iota(jnp.int32, shape, 0) == lax.broadcasted_iota(jnp.int32, shape, 1)


def upright(line):
    return jnp.sum(jnp.where(same(line.shape[1]), line, 0.0), axis=1, keepdims=True)


def lying(column):
    return jnp.sum(jnp.where(same(column.shape[0]), column, 0.0), axis=0, keepdims=True)


def slot_of(deal_ref, member):
    for _ in range(11):
        member = deal_ref[member]
    return member


def dealt_lanes(values, piece, pieces):
    low_lanes = lax.broadcasted_iota(jnp.int32, (values.shape[0], 128), 1) < 64
    found = []
    span = 64 * pieces
    for start in range(0, values.shape[1], 2 * span):
        start = start + piece // 2 * 128
        one, two = values[:, start : start + 128], values[:, start + span : start + span + 128]
        if piece % 2:
            one = pltpu.roll(one, 64, 1)
        else:
            two = pltpu.roll(two, 64, 1)
        found.append(jnp.where(low_lanes, one, two))
    return jnp.concatenate(found, axis=1)


def joined_lanes(even, odd):
    low_lanes = lax.broadcasted_iota(jnp.int32, (even.shape[0], 128), 1) < 64
    found = []
    for start in range(0, even.shape[1], 128):
        one, two = even[:, start : start + 128], odd[:, start : start + 128]
        found.append(jnp.where(low_lanes, one, pltpu.roll(two, 64, 1)))
        found.append(jnp.where(low_lanes, pltpu.roll(one, 64, 1), two))
    return found


def gather_kernel(
    groups,
    members,
    length_ref,
    deal_ref,
    tokens,
    cotangent_in,
    routes,
    places,
    gates,
    norm_gains,
    projector,
    collector,
    widener_in,
    narrower_in,
    expander_in,
    reducer_in,
    cos_ref,
    sin_ref,
    wide_grads,
    down_grads,
    wide_first,
    down_first,
    attend_out,
    grads_out,
    saved_out,
    middle_out,
    soft_out,
    result_out,
    back_out,
    gains_full,
    gate_ref,
    cotangent,
    widener,
    narrower,
    expander,
    reducer,
    result_ref,
    back_ref,
    attend_full,
    grads_all,
    saved,
    middle_ref,
    soft_ref,
    second_all,
    meta_send,
    meta_all,
    attend_send,
    attend_recv,
    widen_send,
    widen_recv,
    gains,
    gain_recv,
    gain_ring,
    wide_full,
    down_full,
    wide_own,
    down_own,
    inputs_ref,
    inputs_turned,
    dense_out,
    dense_back,
    rows_in,
    rows_turned,
    rows_grad,
    rows_out,
    rows_back,
    sends,
    arrivals,
    ring_sends,
    ring_arrivals,
    first_sends,
    first_arrivals,
    local_sems,
):
    at = Places(groups, members)
    links = Links(sends, arrivals)
    chunks, low = down_own.shape[:2]
    loads = {}
    for name, source, target in (
        ("expander", expander_in, expander),
        ("reducer", reducer_in, reducer),
        ("widener", widener_in, widener),
        ("narrower", narrower_in, narrower),
        ("cotangent", cotangent_in, cotangent),
    ):
        made = pltpu.make_async_copy(source, target, local_sems.at[2 * chunks + len(loads)])
        made.start(priority=1)
        loads[name] = made
    at.enter()
    me, steps = at.member, groups - 1
    share, width = projector.shape[1:]
    block = share * members
    length = tokens.shape[0]
    capacity = rows_in.shape[0] // members

    def ring_copy(chunk, step, side, piece):
        owner = at.owner(-step if side == 0 else step)
        if piece == 0:
            spot = wide_full.at[chunk, side, rows(owner * block, block), :]
            origin = wide_own.at[chunk, side]
        else:
            spot = down_full.at[chunk, rows(owner * low + side * (low // 2), low // 2), :]
            origin = down_own.at[chunk, pl.ds(side * (low // 2), low // 2), :]
        place = (chunk * steps + step) * 4 + side * 2 + piece
        return remote(
            spot if step else origin,
            spot,
            ring_sends,
            ring_arrivals,
            place,
            (at.next, at.back)[side],
        )

    def ring_step(chunk, step):
        for piece in range(2):
            for side in range(2):
                if step:
                    ring_copy(chunk, step - 1, side, piece).wait_recv()
                if step < steps:
                    ring_copy(chunk, step, side, piece).start()

    def tick(count):
        for chunk in range(chunks):
            if 0 <= count - 2 * chunk <= steps:
                ring_step(chunk, count - 2 * chunk)

    attend_send[0:3] = projector[...]
    attend_send[3] = collector[...]
    gains[...] = jnp.zeros_like(gains)
    gains[0:2, 0 : norm_gains.shape[1]] = norm_gains[...]
    gains[...] = pltpu.roll(gains[...], (at.group * members + me) * norm_gains.shape[1], 1)
    first_moves = [
        [
            links.copy(attend_send.at[peer], attend_recv.at[me], {"exp": peer}),
            links.copy(gains, gain_recv.at[me], {"exp": peer}),
        ]
        for peer in at.peers
    ]
    gain_recv[me] = gains[...]
    attend_recv[me] = attend_send[me]
    loads["widener"].wait()
    for matrix in range(2):
        for member in range(members):
            widen_send[member, matrix] = dealt_lanes(widener[matrix], member, members)
    widen_moves = [
        links.copy(widen_send.at[peer], widen_recv.at[me], {"exp": peer}) for peer in at.peers
    ]
    widen_recv[me] = widen_send[me]

    def stage(chunk):
        if chunk == 1:
            for matrix in range(2):
                wide_own[1, matrix] = jnp.concatenate(
                    [widen_recv[member, matrix] for member in range(members)], axis=0
                ).astype(jnp.bfloat16)
            down_own[1] = narrower[...].astype(jnp.bfloat16)
        else:
            index = max(chunk - 1, 0)
            for matrix in range(2):
                wide_own[chunk, matrix] = dealt_lanes(
                    expander[matrix], index, chunks - 1
                ).astype(jnp.bfloat16)
            down_own[chunk] = reducer[index * low : (index + 1) * low, :].astype(jnp.bfloat16)
        for side in range(2):
            wide_full[chunk, side, rows(at.group * block, block), :] = wide_own[chunk, side]
        down_full[chunk, rows(at.group * low, low), :] = down_own[chunk]

    loads["expander"].wait()
    loads["reducer"].wait()
    stage(0)
    tick(0)
    for moves in first_moves:
        for move in moves:
            move.wait_recv()
    attend_full[me, rows(at.group * block, block), :] = (
        attend_recv[...].reshape(block, width).astype(jnp.bfloat16)
    )
    total_gain = gain_recv[0]
    for member in range(1, members):
        total_gain = total_gain + gain_recv[member]
    gain_ring[at.group] = total_gain

    half = block // 2

    def unit(owner, side, matrix):
        return attend_full.at[matrix, rows(owner * block + side * half, half), :]

    def across(owner, side):
        spot = unit(owner, side, me)
        return (links.copy(spot, spot, {"exp": at.far}), links.copy(spot, spot, {"exp": at.near}))

    def onward(owner, side):
        spot = unit(owner, side, at.far)
        return links.copy(spot, spot, {"exp": at.near})

    ring, crossed, passed = [], [], []
    gain_moves = []
    for step in range(groups):
        owners = (at.owner(-step), at.owner(step))
        if step:
            for move in ring[-1]:
                move.wait_recv()
            gain_moves[-1].wait_recv()
        if step < steps:
            ring.append(
                [
                    links.copy(unit(owner, side, me), unit(owner, side, me), target)
                    for side, (owner, target) in enumerate(zip(owners, (at.next, at.back)))
                ]
            )
            gain_moves.append(
                links.copy(gain_ring.at[owners[0]], gain_ring.at[owners[0]], at.next)
            )
        crossed.append([across(owner, side) for side, owner in enumerate(owners)])
        if step:
            for side, owner in enumerate((at.owner(1 - step), at.owner(step - 1))):
                crossed[step - 1][side][0].wait_recv()
                passed.append(onward(owner, side))
        if step == 2:
            for move in widen_moves:
                move.wait_recv()
            loads["narrower"].wait()
            for chunk in range(1, chunks):
                stage(chunk)
        if step % 2:
            tick(step // 2 + 1)
    outgoing = []

    def hand_out(source, target):
        made = pltpu.make_async_copy(
            source, target, local_sems.at[2 * chunks + len(loads) + len(outgoing)]
        )
        made.start(priority=1)
        outgoing.append(made)

    loads["cotangent"].wait()
    valid = lax.broadcasted_iota(jnp.int32, (length, 1), 0) < length_ref[deal_ref[me]]
    grads_all[me] = jnp.where(valid, cotangent[...], 0.0).astype(jnp.bfloat16)
    route = [routes[choice : choice + 1, :] for choice in range(2)]
    place = [places[choice : choice + 1, :].astype(jnp.float32) for choice in range(2)]
    meta_send[...] = jnp.zeros_like(meta_send)
    for member in range(members):
        named = [chosen == member for chosen in route]
        meta_send[member, 0:1, :] = jnp.where(
            named[0], place[0], jnp.where(named[1], place[1], -1.0)
        )
        meta_send[member, 1:2, :] = jnp.where(
            named[0], gates[0:1, :], jnp.where(named[1], gates[1:2, :], 0.0)
        )
    meta_all[me] = meta_send[me]
    grad_moves = [
        [
            links.copy(grads_all.at[me], grads_all.at[me], {"exp": peer}),
            links.copy(meta_send.at[peer], meta_all.at[me], {"exp": peer}),
        ]
        for peer in at.peers
    ]
    for side, owner in enumerate((at.owner(-steps), at.owner(steps))):
        crossed[steps][side][0].wait_recv()
        passed.append(onward(owner, side))
    total_gain = gain_ring[0]
    for group in range(1, groups):
        total_gain = total_gain + gain_ring[group]
    gains_full[...] = total_gain.astype(jnp.bfloat16).astype(jnp.float32)
    stream = tokens[...].astype(jnp.float32)
    first_input = (stream * rms_factor(stream) * gains_full[0:1, :]).astype(jnp.bfloat16)
    saved[4] = first_input
    for moves in crossed:
        for move in moves:
            move[1].wait_recv()
    for move in passed:
        move.wait_recv()
    tick(5)
    hand_out(attend_full, attend_out)

    cosines, sines = cos_ref[...], sin_ref[...]
    for matrix in range(3):
        raw = matmul(first_input, attend_full[matrix])
        if matrix == 2:
            saved[2] = raw.astype(jnp.bfloat16)
        else:
            for start in range(0, width, 128):
                piece = raw[:, start : start + 128]
                saved[matrix, :, start : start + 128] = (
                    piece * cosines + turned(piece) * sines
                ).astype(jnp.bfloat16)
    tick(6)

    seq_length = length_ref[me]
    rows_at = lax.broadcasted_iota(jnp.int32, (length, length), 0)
    cols_at = lax.broadcasted_iota(jnp.int32, (length, length), 1)
    allowed = (cols_at <= rows_at) & (cols_at < seq_length)
    lower = first_half((length, 128))

    def heads(pair, carry):
        lanes = pl.ds(pl.multiple_of(pair * 128, 128), 128)
        query, key, value = saved[0, :, lanes], saved[1, :, lanes], saved[2, :, lanes]
        results = []
        for side in range(2):
            alone = jnp.where(lower == (side == 0), query, jnp.zeros_like(query))
            scores = jnp.where(allowed, nt(alone, key) * 0.125, -1e30)
            expo = jnp.exp(scores - jnp.max(scores, axis=-1, keepdims=True))
            soft = expo / jnp.sum(expo, axis=-1, keepdims=True)
            soft_ref[2 * pair + side] = soft
            results.append(matmul(soft.astype(jnp.bfloat16), value))
        saved[3, :, lanes] = jnp.where(lower, results[0], results[1]).astype(jnp.bfloat16)
        return carry

    lax.fori_loop(0, width // 128, heads, 0)
    hand_out(saved, saved_out)
    hand_out(soft_ref, soft_out)
    middle = tokens[...].astype(jnp.float32) + matmul(saved[3], attend_full[3])
    middle_ref[...] = middle
    hand_out(middle_ref, middle_out)
    second_all[me] = (middle * rms_factor(middle) * gains_full[1:2, :]).astype(jnp.bfloat16)
    second_moves = [
        links.copy(second_all.at[me], second_all.at[me], {"exp": peer}) for peer in at.peers
    ]
    for moves in grad_moves:
        for move in moves:
            move.wait_recv()
    hand_out(grads_all, grads_out)
    tick(7)

    def hits(slot, by_row):
        line = meta_all[slot, 0:1, :]
        if by_row:
            names = lax.broadcasted_iota(jnp.int32, (capacity, length), 0).astype(jnp.float32)
            hit = names == line
        else:
            names = lax.broadcasted_iota(jnp.int32, (length, capacity), 1).astype(jnp.float32)
            hit = names == upright(line)
        return jnp.where(hit, 1.0, 0.0).astype(jnp.bfloat16)

    def spot_of(slot):
        return slice(slot * capacity, (slot + 1) * capacity)

    def here_of(slot):
        return slice(slot * length, (slot + 1) * length)

    for slot in range(members):
        pick = hits(slot, True)
        gate = jnp.sum(pick.astype(jnp.float32) * meta_all[slot, 1:2, :], axis=1, keepdims=True)
        rows_grad[spot_of(slot), :] = (matmul(pick, grads_all[slot]) * gate).astype(jnp.bfloat16)
    for move in second_moves:
        move.wait_recv()
    for slot in range(members):
        inputs_ref[here_of(slot), :] = second_all[deal_ref[slot]]
        rows_in[spot_of(slot), :] = matmul(hits(slot, True), inputs_ref[here_of(slot), :]).astype(
            jnp.bfloat16
        )
    inputs_turned[...] = inputs_ref[...].T
    rows_turned[...] = rows_in[...].T
    dense_out[...] = jnp.zeros_like(dense_out)
    dense_back[...] = jnp.zeros_like(dense_back)
    rows_out[...] = jnp.zeros_like(rows_out)
    rows_back[...] = jnp.zeros_like(rows_back)

    def branch(chunk, inputs, turned_inputs, outer, out, back):
        for step in range(steps):
            for side in range(2):
                for piece in range(2):
                    ring_copy(chunk, step, side, piece).wait_send()

        def part(index, carry):
            lanes = pl.ds(pl.multiple_of(index * 256, 256), 256)
            gate = matmul(inputs[...], wide_full[chunk, 0, :, lanes])
            up = matmul(inputs[...], wide_full[chunk, 1, :, lanes])
            rise = sigmoid(gate)
            smooth = gate * rise
            hidden = (smooth * up).astype(jnp.bfloat16)
            hidden_grad = nt(outer[...], down_full[chunk, lanes, :])
            gate_grad = (hidden_grad * up * (rise * (1.0 + gate * (1.0 - rise)))).astype(
                jnp.bfloat16
            )
            up_grad = (hidden_grad * smooth).astype(jnp.bfloat16)
            out[...] += matmul(hidden, down_full[chunk, lanes, :])
            back[...] += nt(gate_grad, wide_full[chunk, 0, :, lanes]) + nt(
                up_grad, wide_full[chunk, 1, :, lanes]
            )
            down_full[chunk, lanes, :] = tn(hidden, outer[...]).astype(jnp.bfloat16)
            wide_full[chunk, 0, :, lanes] = matmul(turned_inputs[...], gate_grad).astype(
                jnp.bfloat16
            )
            wide_full[chunk, 1, :, lanes] = matmul(turned_inputs[...], up_grad).astype(
                jnp.bfloat16
            )

            @pl.when(index == 0)
            def _():
                for ahead in range(groups // 2):
                    @pl.when(chunk + 1 + ahead < chunks)
                    def _():
                        ring_step(chunk + 1 + ahead, steps - 1 - 2 * ahead)

            return carry

        lax.fori_loop(0, down_full.shape[1] // 256, part, 0)
        kept(chunk, 0).start(priority=1)
        kept(chunk, 1).start(priority=1)

    def kept(chunk, piece):
        source, target = ((wide_full, wide_grads), (down_full, down_grads))[piece]
        return pltpu.make_async_copy(
            source.at[chunk], target.at[chunk], local_sems.at[2 * chunk + piece]
        )

    outer_all = grads_all.reshape(members * length, width)
    flat = (members * length, width)
    dense = (
        inputs_ref,
        inputs_turned,
        outer_all,
        dense_out.reshape(flat),
        dense_back.reshape(flat),
    )

    def first_sum(chunk, side, piece):
        owner = at.owner(-1 if side == 0 else 1)
        if piece == 0:
            spot = wide_full.at[chunk, side, rows(owner * block, block), :]
        else:
            spot = down_full.at[chunk, rows(owner * low + side * (low // 2), low // 2), :]
        return remote(
            spot,
            (wide_first, down_first)[piece].at[chunk, side],
            first_sends,
            first_arrivals,
            chunk * 4 + side * 2 + piece,
            (at.next, at.back)[side],
        )

    early = chunks - 2

    def start_sums(chunk):
        for piece in range(2):
            for side in range(2):
                first_sum(chunk, side, piece).start()

    def next_chunk(chunk, carry):
        for ahead in range(groups // 2):
            @pl.when((chunk > 0) & (chunk + ahead < chunks))
            def _():
                ring_step(chunk + ahead, steps - 2 * ahead)

        @pl.when(chunk == chunks - 1)
        def _():
            for before in range(early):
                start_sums(before)

        @pl.when(chunk == 1)
        def _():
            branch(chunk, *dense)

        @pl.when(chunk != 1)
        def _():
            branch(chunk, rows_in, rows_turned, rows_grad, rows_out, rows_back)

        return carry

    lax.fori_loop(0, chunks, next_chunk, 0)

    for slot in range(members):
        inner = rows_back[spot_of(slot), :].astype(jnp.bfloat16)
        dense_back[slot] += matmul(hits(slot, False), inner)
    back_moves = []
    for member in range(members):
        back_ref[member] = dense_back[slot_of(deal_ref, member)].astype(jnp.bfloat16)
    for peer in at.peers:
        back_moves.append(links.copy(back_ref.at[peer], back_out.at[me], {"exp": peer}))
    hand_out(back_ref.at[me], back_out.at[me])
    for slot in range(members):
        gate = upright(meta_all[slot, 1:2, :])
        picked = matmul(hits(slot, False), rows_out[spot_of(slot), :].astype(jnp.bfloat16))
        dense_out[slot] += gate * picked
        score = jnp.sum(picked * grads_all[slot].astype(jnp.float32), axis=1, keepdims=True)
        gate_ref[slot] = jnp.broadcast_to(lying(score), gate_ref.shape[1:])
    for member in range(members):
        result_ref[member] = dense_out[slot_of(deal_ref, member)].astype(jnp.bfloat16)
        hand_out(result_ref.at[member], result_out.at[member])
    for chunk in range(chunks):
        kept(chunk, 0).wait()
        kept(chunk, 1).wait()
    for chunk in range(early):
        for piece in range(2):
            for side in range(2):
                first_sum(chunk, side, piece).wait()
    for move in back_moves:
        move.wait_recv()
    for made in outgoing:
        made.wait()
    links.finish()


def scatter_kernel(
    groups,
    members,
    deal_ref,
    tokens,
    routes,
    gains_full,
    cos_ref,
    sin_ref,
    gate_parts,
    result_parts,
    back_parts,
    wide_grads,
    down_grads,
    wide_first,
    down_first,
    grads_in,
    middle_in,
    attend_in,
    saved_in,
    soft_in,
    output_ref,
    input_grad_ref,
    gate_grad_ref,
    expand_sum,
    reduce_sum,
    widen_sum,
    narrow_sum,
    project_sum,
    collect_sum,
    gains_sum,
    attend_sum,
    grads_all,
    middle_ref,
    attend_full,
    saved,
    soft_ref,
    gate_recv,
    result_recv,
    back_recv,
    wide_own,
    down_own,
    wide_recv,
    down_recv,
    wide_sum,
    turned_ref,
    attend_grad,
    near_recv,
    far_recv,
    far_send,
    attend_total,
    attend_recv,
    attend_back,
    widen_back,
    widen_home,
    gain_own,
    gain_recv,
    gain_ring,
    sends,
    arrivals,
    local_sems,
):
    at = Places(groups, members)
    links = Links(sends, arrivals)
    at.enter()
    me, steps = at.member, groups - 1
    length, width = tokens.shape
    chunks, low = down_own.shape[0], narrow_sum.shape[0]
    share = attend_sum.shape[1]
    block = share * members

    moves_of = {}
    widen_moves = []

    def ring_step(chunk, step):
        made = []
        owners = (at.owner(-1 - step), at.owner(1 + step))
        for piece in range(2):
            for side, target in enumerate((at.next, at.back)):
                own = (wide_own, down_own)[piece]
                landing = (wide_recv, down_recv)[piece].at[chunk, side]
                if piece == 0:
                    spot = (chunk, side, rows(owners[side] * block, block))
                else:
                    spot = (chunk, rows(owners[side] * low + side * (low // 2), low // 2))
                if step == 0:
                    first = (wide_grads, down_grads)[piece]
                    made.append(links.copy(first.at[spot], landing.at[0], target))
                    continue
                if step > 1 or chunk >= early:
                    moves_of[chunk, step - 1][2 * piece + side].wait_recv()
                source = landing.at[step - 1]
                added = source[...].astype(jnp.float32) + own[spot].astype(jnp.float32)
                if step < steps:
                    source[...] = added.astype(jnp.bfloat16)
                elif piece == 0 and chunk != 1:
                    wide_sum[max(chunk - 1, 0), side] = added
                elif piece == 0:
                    for member in range(members):
                        widen_back[member, side] = added[member * share : (member + 1) * share, :]
                else:
                    start = side * (low // 2)
                    if chunk != 1:
                        start = start + max(chunk - 1, 0) * low
                        reduce_sum[start : start + low // 2, :] = added
                    else:
                        narrow_sum[start : start + low // 2, :] = added
                if step < steps:
                    made.append(links.copy(source, landing.at[step], target))
        moves_of[chunk, step] = made
        if step == steps and chunk == 1:
            widen_home[me] = widen_back[me]
            for peer in at.peers:
                widen_moves.append(
                    links.copy(widen_back.at[peer], widen_home.at[me], {"exp": peer})
                )
        if step == steps and chunk and chunk % 2 == 0:
            span = 64 * (chunks - 1)
            for side in range(2):
                found = joined_lanes(wide_sum[chunk - 2, side], wide_sum[chunk - 1, side])
                for index, part in enumerate(found):
                    start = index * span + (chunk - 2) * 64
                    expand_sum[side, :, start : start + 128] = part

    early = chunks - 2
    order = [(chunk, 0) for chunk in range(early, chunks)] + [
        (chunk, step) for step in range(1, groups) for chunk in (1, 0, *range(2, chunks))
    ]

    def poll(count):
        for _ in range(min(count, len(order))):
            chunk, step = order.pop(0)
            for made in own_loads.pop(step, ()):
                made.wait()
            ring_step(chunk, step)

    kept = []

    def load(source, target):
        made = pltpu.make_async_copy(source, target, local_sems.at[len(kept)])
        made.start(priority=1)
        kept.append(made)
        return made

    own_loads = {}

    def load_own(step):
        found = []
        for side, owner in enumerate((at.owner(-1 - step), at.owner(1 + step))):
            spot = rows(owner * block, block)
            found.append(load(wide_grads.at[:, side, spot], wide_own.at[:, side, spot]))
            spot = rows(owner * low + side * (low // 2), low // 2)
            found.append(load(down_grads.at[:, spot], down_own.at[:, spot]))
        own_loads[step] = found

    first_loads = [
        load(wide_first.at[:, side], wide_recv.at[0:early, side, 0]) for side in range(2)
    ] + [load(down_first.at[:, side], down_recv.at[0:early, side, 0]) for side in range(2)]
    load_own(1)
    poll(2)
    middle_loads = [
        load(back_parts, back_recv),
        load(middle_in, middle_ref),
        load(grads_in, grads_all),
        load(attend_in.at[3], attend_full.at[3]),
        load(saved_in, saved),
    ]
    soft_load = load(soft_in, soft_ref)
    load_own(2)
    attend_load = load(attend_in.at[0:3], attend_full.at[0:3])
    for step in range(3, groups):
        load_own(step)
    result_load = load(result_parts.at[me], result_recv.at[me])
    gate_recv[me] = gate_parts[me]
    for made in first_loads:
        made.wait()
    poll(3)
    result_moves = [
        [
            links.copy(result_parts.at[peer], result_recv.at[me], {"exp": peer}),
            links.copy(gate_parts.at[peer], gate_recv.at[me], {"exp": peer}),
        ]
        for peer in at.peers
    ]
    for made in middle_loads:
        made.wait()

    second_grad = back_recv[0].astype(jnp.float32)
    for member in range(1, members):
        second_grad = second_grad + back_recv[member].astype(jnp.float32)
    middle = middle_ref[...]
    scale = rms_factor(middle)
    gain_own[...] = jnp.zeros_like(gain_own)
    gain_own[1:2, :] = jnp.sum(second_grad * (middle * scale), axis=0, keepdims=True)
    input_grad_ref[...] = grads_all[slot_of(deal_ref, me)].astype(jnp.float32) + rms_back(
        middle, scale, second_grad * gains_full[1:2, :]
    )
    middle_low = input_grad_ref[...].astype(jnp.bfloat16)
    turned_ref[3] = nt(middle_low, attend_full[3]).astype(jnp.bfloat16)
    poll(2)
    cosines, sines = cos_ref[...], sin_ref[...]
    lower = first_half((length, 128))
    soft_load.wait()

    def heads(pair, carry):
        lanes = pl.ds(pl.multiple_of(pair * 128, 128), 128)
        query, key, value = saved[0, :, lanes], saved[1, :, lanes], saved[2, :, lanes]
        outer = turned_ref[3, :, lanes]
        made = []
        for side in range(2):
            soft = soft_ref[2 * pair + side]
            alone = jnp.where(lower == (side == 0), outer, jnp.zeros_like(outer))
            value_grad = tn(soft.astype(jnp.bfloat16), outer)
            soft_grad = nt(alone, value)
            score_grad = (
                soft * (soft_grad - jnp.sum(soft * soft_grad, axis=-1, keepdims=True))
            ).astype(jnp.bfloat16)
            made.append(
                (matmul(score_grad, key) * 0.125, tn(score_grad, query) * 0.125, value_grad)
            )
        for index in range(3):
            joined = jnp.where(lower, made[0][index], made[1][index])
            if index < 2:
                joined = joined * cosines - turned(joined) * sines
            turned_ref[index, :, lanes] = joined.astype(jnp.bfloat16)
        return carry

    attend_grad[3] = tn(saved[3], middle_low).astype(jnp.bfloat16)
    for third in range(3):
        lax.fori_loop(2 * third, 2 * third + 2, heads, 0)
        poll(2)
    for matrix in range(3):
        attend_grad[matrix] = tn(saved[4], turned_ref[matrix]).astype(jnp.bfloat16)
    near_moves = [
        links.copy(attend_grad.at[matrix], near_recv.at[index], {"exp": at.near})
        for index, matrix in enumerate((at.near, at.cross))
    ]
    poll(1)
    attend_load.wait()
    first_grad = nt(turned_ref[0], attend_full[0])
    for matrix in range(1, 3):
        first_grad = first_grad + nt(turned_ref[matrix], attend_full[matrix])
    stream = tokens[...].astype(jnp.float32)
    scale = rms_factor(stream)
    gain_own[0:1, :] = jnp.sum(first_grad * (stream * scale), axis=0, keepdims=True)
    gain_moves = [links.copy(gain_own, gain_recv.at[me], {"exp": peer}) for peer in at.peers]
    gain_recv[me] = gain_own[...]
    input_grad_ref[...] += rms_back(stream, scale, first_grad * gains_full[0:1, :])
    for move in near_moves:
        move.wait_recv()
    far_send[...] = (
        attend_grad[at.far].astype(jnp.float32) + near_recv[1].astype(jnp.float32)
    ).astype(jnp.bfloat16)
    far_move = links.copy(far_send, far_recv, {"exp": at.far})
    poll(2)
    for moves in result_moves:
        for move in moves:
            move.wait_recv()
    result_load.wait()
    output = middle_ref[...]
    for member in range(members):
        output = output + result_recv[member].astype(jnp.float32)
    output_ref[...] = output
    for choice in range(2):
        route = routes[choice : choice + 1, :]
        found = jnp.zeros((1, length), jnp.float32)
        for member in range(members):
            found = jnp.where(route == member, gate_recv[member, 0:1, :], found)
        gate_grad_ref[choice : choice + 1, :] = found
    poll(len(order) - 18)
    for move in gain_moves:
        move.wait_recv()
    total = gain_recv[0]
    for member in range(1, members):
        total = total + gain_recv[member]
    gain_ring[at.group] = total
    far_move.wait_recv()
    attend_total[...] = (
        attend_grad[me].astype(jnp.float32)
        + near_recv[0].astype(jnp.float32)
        + far_recv[...].astype(jnp.float32)
    ).astype(jnp.bfloat16)

    half = block // 2
    small, gain_steps = [], []

    def advance_small():
        step = len(small)
        owners = (at.owner(-1 - step), at.owner(1 + step))
        made = []
        for side, target in enumerate((at.next, at.back)):
            spot = attend_total.at[rows(owners[side] * block + side * half, half), :]
            if step:
                small[-1][side].wait_recv()
                source = attend_recv.at[side, step - 1]
                added = source[...].astype(jnp.float32) + spot[...].astype(jnp.float32)
                if step < steps:
                    source[...] = added.astype(jnp.bfloat16)
                else:
                    for member in range(members // 2):
                        attend_back[side * (members // 2) + member] = added[
                            member * share : (member + 1) * share, :
                        ]
                spot = source
            if step < steps:
                made.append(links.copy(spot, attend_recv.at[side, step], target))
        if step:
            gain_steps[-1].wait_recv()
        if step < steps:
            owner = at.owner(-step)
            gain_steps.append(links.copy(gain_ring.at[owner], gain_ring.at[owner], at.next))
        small.append(made)

    while len(small) <= steps:
        advance_small()
        poll(2)
    attend_moves = [
        links.copy(attend_back.at[peer], attend_sum.at[me], {"exp": peer}) for peer in at.peers
    ]
    attend_sum[me] = attend_back[me]
    total = gain_ring[0]
    for group in range(1, groups):
        total = total + gain_ring[group]
    count = gains_sum.shape[1]
    start = (at.group * members + me) * count
    gains_sum[...] = pltpu.roll(total, width - start, 1)[0:2, 0:count]
    poll(len(order))
    for move in attend_moves:
        move.wait_recv()
    project_sum[...] = attend_sum[0:3]
    collect_sum[...] = attend_sum[3]
    for move in widen_moves:
        move.wait_recv()
    for matrix in range(2):
        for member in range(0, members, 2):
            found = joined_lanes(widen_home[member, matrix], widen_home[member + 1, matrix])
            for index, part in enumerate(found):
                start = index * 64 * members + member * 64
                widen_sum[matrix, :, start : start + 128] = part
    links.finish()


def update_kernel(rates, fixed, copies, *refs):
    count = len(rates)
    given, made = refs[: 4 * count + copies], refs[4 * count + copies :]
    for index in range(copies):
        made[index][...] = given[4 * count + index][...]

    def update(index):
        weight, moment, variance, gradient = given[4 * index : 4 * index + 4]
        grad = gradient[...]
        if len(weight.shape) < len(gradient.shape):
            grad = grad[3]
        elif weight.shape[0] < gradient.shape[0]:
            grad = grad[: weight.shape[0]]
        grad = 0.5 * grad
        level = 1.0 / (1.0 - 0.5**STEP)
        moment_new = 0.5 * moment[...] + grad
        variance_new = 0.5 * variance[...] + 2.0 * grad * grad
        kept = weight[...]
        stepped = moment_new * level / (jnp.sqrt(variance_new * level) + 1e-08) + 0.1 * kept
        made[copies + 3 * index][...] = moment_new
        made[copies + 3 * index + 1][...] = variance_new
        made[copies + 3 * index + 2][...] = kept - rates[index] * stepped

    for index in range(count):
        if fixed[index]:
            pl.when(pl.program_id(0) == 0)(functools.partial(update, index))
        else:
            update(index)


def update_all(*groups, passed):
    cuts = 4

    def spec(dims, cut):
        if cut is None:
            return pl.BlockSpec(dims, lambda step: (0,) * len(dims))
        block = tuple(size // cuts if at == cut else size for at, size in enumerate(dims))
        return pl.BlockSpec(
            block, lambda step: tuple(step if at == cut else 0 for at in range(len(dims)))
        )

    def cut_of(array):
        dims = array.shape
        for at in range(len(dims) - 1):
            if array.size > 100000 and dims[at] % (8 * cuts) == 0:
                return at
        return len(dims) - 1 if dims[-1] % (128 * cuts) == 0 else None

    given, specs, shapes, out_specs = [], [], [], []
    for _, weight, moment, variance, gradient in groups:
        cut = cut_of(weight)
        for array in (weight, moment, variance, gradient):
            given.append(array)
            specs.append(spec(array.shape, cut))
        for array in (weight, moment, variance):
            shapes.append(jax.ShapeDtypeStruct(array.shape, array.dtype))
            out_specs.append(spec(array.shape, cut))
    extra = [spec(array.shape, cut_of(array)) for array in passed]
    return pl.pallas_call(
        functools.partial(
            update_kernel,
            [group[0] for group in groups],
            [cut_of(group[1]) is None for group in groups],
            len(passed),
        ),
        grid=(cuts,),
        out_shape=[jax.ShapeDtypeStruct(array.shape, array.dtype) for array in passed] + shapes,
        in_specs=specs + extra,
        out_specs=extra + out_specs,
        compiler_params=pltpu.CompilerParams(vmem_limit_bytes=LIMIT),
    )(*given, *passed)


def rotary_lines(length):
    half = HEAD_FEATURES // 2
    freqs = np.exp(-np.log(10000.0) * np.arange(half) / half)
    angles = np.arange(length)[:, None] * freqs[None, :]
    cosines, sines = np.cos(angles), np.sin(angles)
    return (
        np.concatenate([cosines] * 4, axis=1).astype(np.float32),
        np.concatenate([-sines, sines] * 2, axis=1).astype(np.float32),
    )


def spaces(*names):
    kinds = {"v": pltpu.VMEM, "s": pltpu.SMEM, "a": pl.ANY}
    return [pl.BlockSpec(memory_space=kinds[name]) for name in "".join(names)]


def local(
    tokens,
    seq_lengths,
    deal_order,
    expert_routes,
    capacity_slots,
    gate_weights,
    cotangent,
    projector,
    projector_mean,
    projector_square,
    collector,
    collector_first_moment,
    collector_second_moment,
    widener,
    widener_mean,
    widener_square,
    narrower,
    narrower_mean,
    narrower_square,
    norm_gains,
    gains_mean,
    gains_square,
    expander,
    expander_mean,
    expander_square,
    reducer,
    reducer_mean,
    reducer_square,
):
    groups, members = lax.axis_size("grp"), lax.axis_size("exp")
    length, width = tokens.shape[1:]
    inner = expander.shape[3]
    piece = widener.shape[2] // members
    chunks = 1 + inner // piece
    capacity = 3 * length // members
    steps = groups - 1
    high, low, share = expander.shape[2], narrower.shape[0], projector.shape[1]
    bf16, f32 = jnp.bfloat16, jnp.float32
    shape = jax.ShapeDtypeStruct
    cosines, sines = (jnp.asarray(lines) for lines in rotary_lines(length))
    count = 16 * groups
    (
        wide_grads,
        down_grads,
        wide_first,
        down_first,
        attend_full,
        grads_all,
        saved,
        middle,
        soft,
        result_parts,
        back_parts,
        gains_full,
        gate_parts,
    ) = pl.pallas_call(
        functools.partial(gather_kernel, groups, members),
        out_shape=[
            shape((chunks, 2, width, piece), bf16),
            shape((chunks, piece, width), bf16),
            shape((chunks - 2, 2, high, piece), bf16),
            shape((chunks - 2, 2, low // 2, width), bf16),
            shape((4, width, width), bf16),
            shape((members, length, width), bf16),
            shape((5, length, width), bf16),
            shape((length, width), f32),
            shape((HEAD_COUNT, length, length), f32),
            shape((members, length, width), bf16),
            shape((members, length, width), bf16),
            shape((8, width), f32),
            shape((members, 8, length), f32),
        ],
        in_specs=spaces("ssvavvvvvvaaaavv"),
        out_specs=spaces("a" * 11, "vv"),
        scratch_shapes=[
            VMEM((length, width), f32),
            VMEM(widener.shape, f32),
            VMEM(narrower.shape, f32),
            VMEM(expander.shape[1:], f32),
            VMEM(reducer.shape[1:], f32),
            VMEM((members, length, width), bf16),
            VMEM((members, length, width), bf16),
            VMEM((4, width, width), bf16),
            VMEM((members, length, width), bf16),
            VMEM((5, length, width), bf16),
            VMEM((length, width), f32),
            VMEM((HEAD_COUNT, length, length), f32),
            VMEM((members, length, width), bf16),
            VMEM((members, 8, length), f32),
            VMEM((members, 8, length), f32),
            VMEM((4, share, width), f32),
            VMEM((4, share, width), f32),
            VMEM((members, 2, share, piece), f32),
            VMEM((members, 2, share, piece), f32),
            VMEM((8, width), f32),
            VMEM((members, 8, width), f32),
            VMEM((groups, 8, width), f32),
            VMEM((chunks, 2, width, piece), bf16),
            VMEM((chunks, piece, width), bf16),
            VMEM((chunks, 2, high, piece), bf16),
            VMEM((chunks, low, width), bf16),
            VMEM((members * length, width), bf16),
            VMEM((width, members * length), bf16),
            VMEM((members, length, width), f32),
            VMEM((members, length, width), f32),
            VMEM((members * capacity, width), bf16),
            VMEM((width, members * capacity), bf16),
            VMEM((members * capacity, width), bf16),
            VMEM((members * capacity, width), f32),
            VMEM((members * capacity, width), f32),
            pltpu.SemaphoreType.DMA((count,)),
            pltpu.SemaphoreType.DMA((count,)),
            pltpu.SemaphoreType.DMA((chunks * steps * 4,)),
            pltpu.SemaphoreType.DMA((chunks * steps * 4,)),
            pltpu.SemaphoreType.DMA((chunks * 4,)),
            pltpu.SemaphoreType.DMA((chunks * 4,)),
            pltpu.SemaphoreType.DMA((2 * chunks + 10 + 2 * members,)),
        ],
        compiler_params=pltpu.CompilerParams(
            collective_id=0, has_side_effects=True, vmem_limit_bytes=LIMIT
        ),
    )(
        seq_lengths,
        deal_order,
        tokens[0],
        cotangent[0],
        expert_routes[0].T,
        capacity_slots[0].T,
        gate_weights[0].T,
        norm_gains,
        projector,
        collector,
        widener,
        narrower,
        expander[0],
        reducer[0],
        cosines,
        sines,
    )
    count = 32 * groups
    (
        output,
        input_grad,
        gate_grad,
        expand_sum,
        reduce_sum,
        widen_sum,
        narrow_sum,
        project_sum,
        collect_sum,
        gains_sum,
    ) = pl.pallas_call(
        functools.partial(scatter_kernel, groups, members),
        out_shape=[
            shape((length, width), f32),
            shape((length, width), f32),
            shape((2, length), f32),
            shape((2, high, inner), f32),
            shape(reducer.shape[1:], f32),
            shape(widener.shape, f32),
            shape(narrower.shape, f32),
            shape(projector.shape, f32),
            shape(collector.shape, f32),
            shape(norm_gains.shape, f32),
        ],
        in_specs=spaces("s", "v" * 6, "a" * 11),
        out_specs=spaces("v" * 10),
        scratch_shapes=[
            VMEM((4, share, width), f32),
            VMEM((members, length, width), bf16),
            VMEM((length, width), f32),
            VMEM((4, width, width), bf16),
            VMEM((5, length, width), bf16),
            VMEM((HEAD_COUNT, length, length), f32),
            VMEM((members, 8, length), f32),
            VMEM((members, length, width), bf16),
            VMEM((members, length, width), bf16),
            VMEM((chunks, 2, width, piece), bf16),
            VMEM((chunks, piece, width), bf16),
            VMEM((chunks, 2, steps, high, piece), bf16),
            VMEM((chunks, 2, steps, low // 2, width), bf16),
            VMEM((chunks - 1, 2, high, piece), f32),
            VMEM((4, length, width), bf16),
            VMEM((4, width, width), bf16),
            VMEM((2, width, width), bf16),
            VMEM((width, width), bf16),
            VMEM((width, width), bf16),
            VMEM((width, width), bf16),
            VMEM((2, steps, high // 2, width), bf16),
            VMEM((4, share, width), f32),
            VMEM((members, 2, share, piece), f32),
            VMEM((members, 2, share, piece), f32),
            VMEM((8, width), f32),
            VMEM((members, 8, width), f32),
            VMEM((groups, 8, width), f32),
            pltpu.SemaphoreType.DMA((count,)),
            pltpu.SemaphoreType.DMA((count,)),
            pltpu.SemaphoreType.DMA((4 * groups + 16,)),
        ],
        compiler_params=pltpu.CompilerParams(
            collective_id=1, has_side_effects=True, vmem_limit_bytes=LIMIT
        ),
    )(
        deal_order,
        tokens[0],
        expert_routes[0].T,
        gains_full,
        cosines,
        sines,
        gate_parts,
        result_parts,
        back_parts,
        wide_grads,
        down_grads,
        wide_first,
        down_first,
        grads_all,
        middle,
        attend_full,
        saved,
        soft,
    )
    updated = update_all(
        (0.1, projector, projector_mean, projector_square, project_sum),
        (0.3, collector, collector_first_moment, collector_second_moment, collect_sum),
        (0.07, widener, widener_mean, widener_square, widen_sum),
        (0.045, narrower, narrower_mean, narrower_square, narrow_sum),
        (0.2, norm_gains, gains_mean, gains_square, gains_sum),
        (0.07, expander[0], expander_mean[0], expander_square[0], expand_sum),
        (0.045, reducer[0], reducer_mean[0], reducer_square[0], reduce_sum),
        passed=(output, input_grad),
    )
    return (
        updated[0][None],
        updated[1][None],
        gate_grad.T[None],
        *updated[2:17],
        *(found[None] for found in updated[17:]),
    )


def fits(mesh):
    groups, members = mesh.shape["grp"], mesh.shape["exp"]
    share = 64 * HEAD_COUNT // (groups * members)
    return members == 4 and groups % 2 == 0 and share % 8 == 0 and share * members // 2 % 16 == 0


def solution(mesh):
    placed = (
        P(("grp", "exp"), None, None),
        P("grp"),
        P("grp"),
        P(("grp", "exp"), None, None),
        P(("grp", "exp"), None, None),
        P(("grp", "exp"), None, None),
        P(("grp", "exp"), None, None),
        P(None, ("grp", "exp"), None),
        P(None, ("grp", "exp"), None),
        P(None, ("grp", "exp"), None),
        P(("grp", "exp"), None),
        P(("grp", "exp"), None),
        P(("grp", "exp"), None),
        P(None, ("grp", "exp"), None),
        P(None, ("grp", "exp"), None),
        P(None, ("grp", "exp"), None),
        P(("grp", "exp"), None),
        P(("grp", "exp"), None),
        P(("grp", "exp"), None),
        P(None, ("grp", "exp")),
        P(None, ("grp", "exp")),
        P(None, ("grp", "exp")),
        P("exp", None, "grp", None),
        P("exp", None, "grp", None),
        P("exp", None, "grp", None),
        P("exp", "grp", None),
        P("exp", "grp", None),
        P("exp", "grp", None),
    )
    return jax.shard_map(
        local if fits(mesh) else local_plain,
        mesh=mesh,
        in_specs=placed,
        out_specs=(
            P(("grp", "exp"), None, None),
            P(("grp", "exp"), None, None),
            P(("grp", "exp"), None, None),
            P(None, ("grp", "exp"), None),
            P(None, ("grp", "exp"), None),
            P(None, ("grp", "exp"), None),
            P(("grp", "exp"), None),
            P(("grp", "exp"), None),
            P(("grp", "exp"), None),
            P(None, ("grp", "exp"), None),
            P(None, ("grp", "exp"), None),
            P(None, ("grp", "exp"), None),
            P(("grp", "exp"), None),
            P(("grp", "exp"), None),
            P(("grp", "exp"), None),
            P(None, ("grp", "exp")),
            P(None, ("grp", "exp")),
            P(None, ("grp", "exp")),
            P("exp", None, "grp", None),
            P("exp", None, "grp", None),
            P("exp", None, "grp", None),
            P("exp", "grp", None),
            P("exp", "grp", None),
            P("exp", "grp", None),
        ),
        check_vma=False,
    )
```

```python
import functools

import jax
import jax.numpy as jnp
import numpy as np
from jax import lax
from jax.experimental import pallas as pl
from jax.experimental.pallas import tpu as pltpu
from jax.sharding import PartitionSpec as P

HEAD_COUNT = 12
HEAD_FEATURES = 64
STEP = 5


def rms_factor(values):
    return lax.rsqrt(jnp.mean(values * values, axis=-1, keepdims=True) + 1e-06)


def rms_back(values, factor, upstream):
    return factor * (
        upstream - values * factor * factor * jnp.mean(upstream * values, axis=-1, keepdims=True)
    )


def rotary(length):
    positions = jnp.arange(length, dtype=jnp.int32).astype(jnp.float32)
    half = HEAD_FEATURES // 2
    freqs = jnp.exp(
        -jnp.log(10000.0) * jnp.arange(half, dtype=jnp.int32).astype(jnp.float32) / half
    )
    angles = positions[:, None] * freqs[None, :]
    return (jnp.cos(angles)[:, None, :], jnp.sin(angles)[:, None, :])


def rotate(values, cosines, sines):
    half = values.shape[-1] // 2
    first = values[..., :half]
    second = values[..., half:]
    return jnp.concatenate(
        [first * cosines - second * sines, second * cosines + first * sines], axis=-1
    )


def rotate_back(values, cosines, sines):
    half = values.shape[-1] // 2
    first = values[..., :half]
    second = values[..., half:]
    return jnp.concatenate(
        [first * cosines + second * sines, second * cosines - first * sines], axis=-1
    )


def silu_slope(values):
    sigmoid_of = jax.nn.sigmoid(values)
    return sigmoid_of * (1.0 + values * (1.0 - sigmoid_of))


def matmul(left, right):
    return jnp.dot(left, right, preferred_element_type=jnp.float32)


def outer_sum(left, right):
    return jnp.einsum("ld,lf->df", left, right, preferred_element_type=jnp.float32)


def adamw_update(weight, moment, variance, gradient, rate):
    moment_new = 0.5 * moment + 0.5 * gradient
    variance_new = 0.5 * variance + 0.5 * gradient * gradient
    correct = 1.0 - 0.5**STEP
    stepped = moment_new / correct / (jnp.sqrt(variance_new / correct) + 1e-08) + 0.1 * weight
    return (moment_new, variance_new, weight - rate * stepped)


def local_plain(
    tokens,
    seq_lengths,
    deal_order,
    expert_routes,
    capacity_slots,
    gate_weights,
    cotangent,
    projector,
    projector_mean,
    projector_square,
    collector,
    collector_first_moment,
    collector_second_moment,
    widener,
    widener_mean,
    widener_square,
    narrower,
    narrower_mean,
    narrower_square,
    norm_gains,
    gains_mean,
    gains_square,
    expander,
    expander_mean,
    expander_square,
    reducer,
    reducer_mean,
    reducer_square,
):
    members = lax.axis_size("exp")
    member = lax.axis_index("exp")
    length_seq = tokens.shape[1]
    width = tokens.shape[2]
    local_experts = expander.shape[0]
    experts_all = local_experts * members
    capacity = 3 * length_seq // experts_all
    member_ids = jnp.arange(members, dtype=jnp.int32)
    source = deal_order[member]
    home_slot = jnp.sum(jnp.where(deal_order == member, member_ids, 0))
    seq_length = seq_lengths[source]
    piece = lax.all_gather(tokens, "exp", axis=0, tiled=True)
    chosen = jnp.arange(piece.shape[0], dtype=jnp.int32) == source
    dealt = jnp.sum(
        jnp.where(chosen[:, None, None], piece, jnp.zeros_like(piece)), axis=0, keepdims=True
    )
    residual_flow = dealt[0].astype(jnp.float32)
    project_full, collect_full, widen_full, narrow_full, gains_full = (
        lax.all_gather(projector.astype(jnp.bfloat16), ("grp", "exp"), axis=1, tiled=True),
        lax.all_gather(collector.astype(jnp.bfloat16), ("grp", "exp"), axis=0, tiled=True),
        lax.all_gather(widener.astype(jnp.bfloat16), ("grp", "exp"), axis=1, tiled=True),
        lax.all_gather(narrower.astype(jnp.bfloat16), ("grp", "exp"), axis=0, tiled=True),
        lax.all_gather(norm_gains.astype(jnp.bfloat16), ("grp", "exp"), axis=1, tiled=True),
    )
    expand_full, reduce_full = (
        lax.all_gather(expander.astype(jnp.bfloat16), "grp", axis=2, tiled=True),
        lax.all_gather(reducer.astype(jnp.bfloat16), "grp", axis=1, tiled=True),
    )
    gains_used = gains_full.astype(jnp.float32)
    cosines, sines = rotary(length_seq)
    scale_one = rms_factor(residual_flow)
    normed_one = residual_flow * scale_one
    first_input = (normed_one * gains_used[0]).astype(jnp.bfloat16)
    query_raw = matmul(first_input, project_full[0]).reshape(length_seq, HEAD_COUNT, HEAD_FEATURES)
    key_raw = matmul(first_input, project_full[1]).reshape(length_seq, HEAD_COUNT, HEAD_FEATURES)
    value_raw = matmul(first_input, project_full[2]).reshape(length_seq, HEAD_COUNT, HEAD_FEATURES)
    query_rot = rotate(query_raw, cosines, sines).astype(jnp.bfloat16)
    key_rot = rotate(key_raw, cosines, sines).astype(jnp.bfloat16)
    value_low = value_raw.astype(jnp.bfloat16)
    rows_at = jnp.arange(length_seq, dtype=jnp.int32)[:, None]
    cols_at = jnp.arange(length_seq, dtype=jnp.int32)[None, :]
    allowed = ((cols_at <= rows_at) & (cols_at < seq_length))[None]
    scores = (
        jnp.einsum("qhd,khd->hqk", query_rot, key_rot, preferred_element_type=jnp.float32) * 0.125
    )
    masked = jnp.where(allowed, scores, -1e30)
    top = jnp.max(masked, axis=-1, keepdims=True)
    expo = jnp.exp(masked - top)
    total = jnp.sum(expo, axis=-1, keepdims=True)
    soft = expo / total
    logsum = top + jnp.log(total)
    mixed_output = (
        jnp.einsum(
            "hqk,khd->qhd", soft.astype(jnp.bfloat16), value_low, preferred_element_type=jnp.float32
        )
        .reshape(length_seq, width)
        .astype(jnp.bfloat16)
    )
    middle_state = residual_flow + matmul(mixed_output, collect_full)
    scale_two = rms_factor(middle_state)
    normed_two = middle_state * scale_two
    second_input = (normed_two * gains_used[1]).astype(jnp.bfloat16)
    gating_scores = matmul(second_input, widen_full[0])
    upward_rows = matmul(second_input, widen_full[1])
    hidden_state = (jax.nn.silu(gating_scores) * upward_rows).astype(jnp.bfloat16)
    dense_branch = matmul(hidden_state, narrow_full)
    flat = (expert_routes[0] * capacity + capacity_slots[0]).reshape(-1)
    spread = jnp.repeat(second_input, 2, axis=0)
    dispatch = jnp.zeros((experts_all * capacity, width), jnp.bfloat16).at[flat].set(spread)
    dispatch = dispatch.reshape(experts_all, capacity, width)
    rows = lax.all_to_all(dispatch, "exp", split_axis=0, concat_axis=0, tiled=True)
    count = rows.shape[1]
    grouped = rows.reshape(members, local_experts, count, width)
    gate_pre = jnp.einsum(
        "sekd,edf->sekf", grouped, expand_full[:, 0], preferred_element_type=jnp.float32
    )
    up_pre = jnp.einsum(
        "sekd,edf->sekf", grouped, expand_full[:, 1], preferred_element_type=jnp.float32
    )
    hidden_rows = (jax.nn.silu(gate_pre) * up_pre).astype(jnp.bfloat16)
    result = jnp.einsum(
        "sekf,efd->sekd", hidden_rows, reduce_full, preferred_element_type=jnp.float32
    )
    result = result.astype(jnp.bfloat16).reshape(members * local_experts, count, width)
    returned_rows = lax.all_to_all(result, "exp", split_axis=0, concat_axis=0, tiled=True)
    outcome = (
        returned_rows,
        rows,
        gate_pre.reshape(members * local_experts, count, -1),
        up_pre.reshape(members * local_experts, count, -1),
    )
    returned, received, gate_kept, up_kept = outcome
    picked = (
        returned.reshape(experts_all * capacity, width)[flat]
        .reshape(length_seq, 2, width)
        .astype(jnp.float32)
    )
    gate_local = gate_weights[0]
    mixture = jnp.sum(gate_local[..., None] * picked, axis=1)
    layer_output = middle_state + dense_branch + mixture
    valid = (jnp.arange(length_seq, dtype=jnp.int32) < seq_length).astype(jnp.float32)
    grad_out = cotangent[0] * valid[:, None]
    grad_low = grad_out.astype(jnp.bfloat16)
    narrow_grad = outer_sum(hidden_state, grad_low)
    hidden_grad = jnp.einsum("ld,fd->lf", grad_low, narrow_full, preferred_element_type=jnp.float32)
    gating_grad = (hidden_grad * upward_rows * silu_slope(gating_scores)).astype(jnp.bfloat16)
    upward_grad = (hidden_grad * jax.nn.silu(gating_scores)).astype(jnp.bfloat16)
    widen_grad = jnp.stack(
        [outer_sum(second_input, gating_grad), outer_sum(second_input, upward_grad)]
    )
    second_grad = jnp.einsum(
        "lf,df->ld", gating_grad, widen_full[0], preferred_element_type=jnp.float32
    ) + jnp.einsum("lf,df->ld", upward_grad, widen_full[1], preferred_element_type=jnp.float32)
    gate_grad_local = jnp.sum(grad_out[:, None, :] * picked, axis=-1)
    result_grad = (
        (gate_local[..., None] * grad_out[:, None, :])
        .astype(jnp.bfloat16)
        .reshape(2 * length_seq, width)
    )
    grad_send = jnp.zeros((experts_all * capacity, width), jnp.bfloat16).at[flat].set(result_grad)
    grad_recv = lax.all_to_all(
        grad_send.reshape(experts_all, capacity, width),
        "exp",
        split_axis=0,
        concat_axis=0,
        tiled=True,
    )
    grad_group = grad_recv.reshape(members, local_experts, capacity, width)
    rows_group = received.reshape(members, local_experts, capacity, width)
    gate_pre = gate_kept.reshape(members, local_experts, capacity, -1)
    up_pre = up_kept.reshape(members, local_experts, capacity, -1)
    hidden_rows = (jax.nn.silu(gate_pre) * up_pre).astype(jnp.bfloat16)
    reduce_grad = jnp.einsum(
        "sekf,sekd->efd", hidden_rows, grad_group, preferred_element_type=jnp.float32
    )
    hidden_rows_grad = jnp.einsum(
        "sekd,efd->sekf", grad_group, reduce_full, preferred_element_type=jnp.float32
    )
    gate_rows_grad = (hidden_rows_grad * up_pre * silu_slope(gate_pre)).astype(jnp.bfloat16)
    up_rows_grad = (hidden_rows_grad * jax.nn.silu(gate_pre)).astype(jnp.bfloat16)
    expand_grad = jnp.stack(
        [
            jnp.einsum(
                "sekd,sekf->edf", rows_group, gate_rows_grad, preferred_element_type=jnp.float32
            ),
            jnp.einsum(
                "sekd,sekf->edf", rows_group, up_rows_grad, preferred_element_type=jnp.float32
            ),
        ],
        axis=1,
    )
    row_grads = jnp.einsum(
        "sekf,edf->sekd", gate_rows_grad, expand_full[:, 0], preferred_element_type=jnp.float32
    ) + jnp.einsum(
        "sekf,edf->sekd", up_rows_grad, expand_full[:, 1], preferred_element_type=jnp.float32
    )
    row_grads = row_grads.astype(jnp.bfloat16).reshape(experts_all, capacity, width)
    came_back = lax.all_to_all(row_grads, "exp", split_axis=0, concat_axis=0, tiled=True).reshape(
        experts_all * capacity, width
    )
    second_grad = second_grad + jnp.sum(
        came_back[flat].reshape(length_seq, 2, width).astype(jnp.float32), axis=1
    )
    gains_grad_two = jnp.sum(second_grad * normed_two, axis=0)
    middle_grad = grad_out + rms_back(middle_state, scale_two, second_grad * gains_used[1])
    middle_low = middle_grad.astype(jnp.bfloat16)
    collect_grad = outer_sum(mixed_output, middle_low)
    mixed_grad = jnp.einsum(
        "ld,ed->le", middle_low, collect_full, preferred_element_type=jnp.float32
    )
    mixed_grad = mixed_grad.astype(jnp.bfloat16).reshape(length_seq, HEAD_COUNT, HEAD_FEATURES)
    scores_again = (
        jnp.einsum("qhd,khd->hqk", query_rot, key_rot, preferred_element_type=jnp.float32) * 0.125
    )
    soft_again = jnp.where(allowed, jnp.exp(scores_again - logsum), 0.0)
    value_grad = jnp.einsum(
        "hqk,qhd->khd",
        soft_again.astype(jnp.bfloat16),
        mixed_grad,
        preferred_element_type=jnp.float32,
    )
    soft_grad = jnp.einsum(
        "qhd,khd->hqk", mixed_grad, value_low, preferred_element_type=jnp.float32
    )
    score_grad = (
        soft_again * (soft_grad - jnp.sum(soft_again * soft_grad, axis=-1, keepdims=True))
    ).astype(jnp.bfloat16)
    query_grad = (
        jnp.einsum("hqk,khd->qhd", score_grad, key_rot, preferred_element_type=jnp.float32) * 0.125
    )
    key_grad = (
        jnp.einsum("hqk,qhd->khd", score_grad, query_rot, preferred_element_type=jnp.float32)
        * 0.125
    )
    query_back = (
        rotate_back(query_grad, cosines, sines).reshape(length_seq, width).astype(jnp.bfloat16)
    )
    key_back = rotate_back(key_grad, cosines, sines).reshape(length_seq, width).astype(jnp.bfloat16)
    value_back = value_grad.reshape(length_seq, width).astype(jnp.bfloat16)
    project_grad = jnp.stack(
        [
            outer_sum(first_input, query_back),
            outer_sum(first_input, key_back),
            outer_sum(first_input, value_back),
        ]
    )
    first_grad = (
        jnp.einsum("le,de->ld", query_back, project_full[0], preferred_element_type=jnp.float32)
        + jnp.einsum("le,de->ld", key_back, project_full[1], preferred_element_type=jnp.float32)
        + jnp.einsum("le,de->ld", value_back, project_full[2], preferred_element_type=jnp.float32)
    )
    gains_grad_one = jnp.sum(first_grad * normed_one, axis=0)
    stream_grad = middle_grad + rms_back(residual_flow, scale_one, first_grad * gains_used[0])
    gains_grad = jnp.stack([gains_grad_one, gains_grad_two])
    project_part, collect_part, widen_part, narrow_part, gains_part = (
        lax.psum_scatter(project_grad, ("grp", "exp"), scatter_dimension=1, tiled=True),
        lax.psum_scatter(collect_grad, ("grp", "exp"), scatter_dimension=0, tiled=True),
        lax.psum_scatter(widen_grad, ("grp", "exp"), scatter_dimension=1, tiled=True),
        lax.psum_scatter(narrow_grad, ("grp", "exp"), scatter_dimension=0, tiled=True),
        lax.psum_scatter(gains_grad, ("grp", "exp"), scatter_dimension=1, tiled=True),
    )
    expand_part, reduce_part = (
        lax.psum_scatter(
            expand_grad.astype(jnp.bfloat16), "grp", scatter_dimension=2, tiled=True
        ).astype(jnp.float32),
        lax.psum_scatter(
            reduce_grad.astype(jnp.bfloat16), "grp", scatter_dimension=1, tiled=True
        ).astype(jnp.float32),
    )
    empty = jnp.zeros((1, length_seq, width), jnp.float32)
    pieces = (
        lax.all_gather(layer_output[None].astype(jnp.bfloat16), "exp", axis=0, tiled=True).astype(
            jnp.float32
        ),
        lax.all_gather(stream_grad[None].astype(jnp.bfloat16), "exp", axis=0, tiled=True).astype(
            jnp.float32
        ),
    )
    chosen = (jnp.arange(pieces[0].shape[0], dtype=jnp.int32) == home_slot)[:, None, None]
    homed_output = empty + jnp.sum(jnp.where(chosen, pieces[0], 0.0), axis=0, keepdims=True)
    homed_grad = empty + jnp.sum(jnp.where(chosen, pieces[1], 0.0), axis=0, keepdims=True)
    project_new = adamw_update(projector, projector_mean, projector_square, project_part, 0.1)
    collect_new = adamw_update(
        collector, collector_first_moment, collector_second_moment, collect_part, 0.3
    )
    widening_updated = adamw_update(widener, widener_mean, widener_square, widen_part, 0.07)
    narrowing_updated = adamw_update(narrower, narrower_mean, narrower_square, narrow_part, 0.045)
    gains_updated = adamw_update(norm_gains, gains_mean, gains_square, gains_part, 0.2)
    expansion_updated = adamw_update(expander, expander_mean, expander_square, expand_part, 0.07)
    reduction_updated = adamw_update(reducer, reducer_mean, reducer_square, reduce_part, 0.045)
    return (
        homed_output,
        homed_grad,
        gate_grad_local[None],
        project_new[0],
        project_new[1],
        project_new[2],
        collect_new[0],
        collect_new[1],
        collect_new[2],
        widening_updated[0],
        widening_updated[1],
        widening_updated[2],
        narrowing_updated[0],
        narrowing_updated[1],
        narrowing_updated[2],
        gains_updated[0],
        gains_updated[1],
        gains_updated[2],
        expansion_updated[0],
        expansion_updated[1],
        expansion_updated[2],
        reduction_updated[0],
        reduction_updated[1],
        reduction_updated[2],
    )


MESH = pl.DeviceIdType.MESH
VMEM = pltpu.VMEM
LIMIT = 60 * 1024 * 1024


def ring_place(index, groups):
    row, side = lax.div(index, 2), lax.rem(index, 2)
    return (1 - side) * row + side * (groups - 1 - row)


def ring_member(place, groups):
    side = lax.div(place, groups // 2)
    return 2 * ((1 - side) * place + side * (groups - 1 - place)) + side


def remote(source, target, sends, arrivals, at, device):
    return pltpu.make_async_remote_copy(
        src_ref=source,
        dst_ref=target,
        send_sem=sends.at[at],
        recv_sem=arrivals.at[at],
        device_id=device,
        device_id_type=MESH,
    )


class Links:
    def __init__(self, sends, arrivals):
        self.sends, self.arrivals, self.count, self.started = sends, arrivals, 0, []

    def copy(self, source, target, device):
        made = remote(source, target, self.sends, self.arrivals, self.count, device)
        self.count += 1
        made.start()
        self.started.append(made)
        return made

    def finish(self):
        for made in self.started:
            made.wait_send()


class Places:
    def __init__(self, groups, members):
        self.groups, self.members = groups, members
        self.group = lax.axis_index("grp")
        self.member = lax.axis_index("exp")
        self.place = ring_place(self.group, groups)
        self.next = {"grp": self.owner(1)}
        self.back = {"grp": self.owner(-1)}
        half = members // 2
        self.far = lax.rem(self.member + half, members)
        self.near = self.member + 1 - 2 * lax.rem(self.member, 2)
        self.cross = lax.rem(self.near + half, members)
        self.peers = [lax.rem(self.member + step, members) for step in range(1, members)]
        self.others = [lax.rem(self.group + step, groups) for step in range(1, groups)]
        self.sources = [lax.rem(self.group + groups - step, groups) for step in range(1, groups)]

    def owner(self, offset):
        place = lax.rem(self.place + offset + 2 * self.groups, self.groups)
        return ring_member(place, self.groups)

    def enter(self):
        barrier = pltpu.get_barrier_semaphore()
        partners = [{"grp": other} for other in self.others]
        partners += [{"exp": peer} for peer in self.peers]
        for partner in partners:
            pl.semaphore_signal(barrier, inc=1, device_id=partner, device_id_type=MESH)
        pl.semaphore_wait(barrier, len(partners))


def rows(start, count, align=16):
    return pl.ds(pl.multiple_of(start, align), count)


def first_half(shape):
    return lax.rem(lax.broadcasted_iota(jnp.int32, shape, len(shape) - 1), 128) < 64


def turned(values):
    lanes = lax.broadcasted_iota(jnp.int32, values.shape, 1)
    return jnp.where(
        lax.rem(lanes, HEAD_FEATURES) < HEAD_FEATURES // 2,
        pltpu.roll(values, 128 - HEAD_FEATURES // 2, 1),
        pltpu.roll(values, HEAD_FEATURES // 2, 1),
    )


def nt(left, right):
    return lax.dot_general(
        left, right, (((1,), (1,)), ((), ())), preferred_element_type=jnp.float32
    )


def tn(left, right):
    return lax.dot_general(
        left, right, (((0,), (0,)), ((), ())), preferred_element_type=jnp.float32
    )


def sigmoid(values):
    return 1.0 / (1.0 + jnp.exp(-values))


def same(length):
    shape = (length, length)
    return lax.broadcasted_iota(jnp.int32, shape, 0) == lax.broadcasted_iota(jnp.int32, shape, 1)


def upright(line):
    return jnp.sum(jnp.where(same(line.shape[1]), line, 0.0), axis=1, keepdims=True)


def lying(column):
    return jnp.sum(jnp.where(same(column.shape[0]), column, 0.0), axis=0, keepdims=True)


def slot_of(deal_ref, member):
    for _ in range(11):
        member = deal_ref[member]
    return member


def dealt_lanes(values, piece, pieces):
    low_lanes = lax.broadcasted_iota(jnp.int32, (values.shape[0], 128), 1) < 64
    found = []
    span = 64 * pieces
    for start in range(0, values.shape[1], 2 * span):
        start = start + piece // 2 * 128
        one, two = values[:, start : start + 128], values[:, start + span : start + span + 128]
        if piece % 2:
            one = pltpu.roll(one, 64, 1)
        else:
            two = pltpu.roll(two, 64, 1)
        found.append(jnp.where(low_lanes, one, two))
    return jnp.concatenate(found, axis=1)


def joined_lanes(even, odd):
    low_lanes = lax.broadcasted_iota(jnp.int32, (even.shape[0], 128), 1) < 64
    found = []
    for start in range(0, even.shape[1], 128):
        one, two = even[:, start : start + 128], odd[:, start : start + 128]
        found.append(jnp.where(low_lanes, one, pltpu.roll(two, 64, 1)))
        found.append(jnp.where(low_lanes, pltpu.roll(one, 64, 1), two))
    return found


def gather_kernel(
    groups,
    members,
    length_ref,
    deal_ref,
    tokens,
    cotangent_in,
    routes,
    places,
    gates,
    norm_gains,
    projector,
    collector,
    widener_in,
    narrower_in,
    expander_in,
    reducer_in,
    cos_ref,
    sin_ref,
    wide_grads,
    down_grads,
    wide_first,
    down_first,
    attend_out,
    grads_out,
    saved_out,
    middle_out,
    soft_out,
    result_out,
    back_out,
    gains_full,
    gate_ref,
    cotangent,
    widener,
    narrower,
    expander,
    reducer,
    result_ref,
    back_ref,
    grads_home,
    attend_full,
    grads_all,
    saved,
    middle_ref,
    soft_ref,
    second_all,
    meta_send,
    meta_all,
    attend_send,
    attend_recv,
    widen_send,
    widen_recv,
    gains,
    gain_recv,
    gain_ring,
    wide_full,
    down_full,
    wide_own,
    down_own,
    inputs_ref,
    inputs_turned,
    dense_out,
    dense_back,
    rows_in,
    rows_turned,
    rows_grad,
    rows_out,
    rows_back,
    sends,
    arrivals,
    ring_sends,
    ring_arrivals,
    first_sends,
    first_arrivals,
    local_sems,
):
    at = Places(groups, members)
    links = Links(sends, arrivals)
    chunks, low = down_own.shape[:2]
    loads = {}
    for name, source, target in (
        ("expander", expander_in, expander),
        ("reducer", reducer_in, reducer),
        ("widener", widener_in, widener),
        ("narrower", narrower_in, narrower),
        ("cotangent", cotangent_in, cotangent),
    ):
        made = pltpu.make_async_copy(source, target, local_sems.at[2 * chunks + len(loads)])
        made.start(priority=1)
        loads[name] = made
    at.enter()
    me, steps = at.member, groups - 1
    share, width = projector.shape[1:]
    block = share * members
    length = tokens.shape[0]
    capacity = rows_in.shape[0] // members

    def ring_copy(chunk, step, side, piece):
        owner = at.owner(-step if side == 0 else step)
        if piece == 0:
            spot = wide_full.at[chunk, side, rows(owner * block, block), :]
            origin = wide_own.at[chunk, side]
        else:
            spot = down_full.at[chunk, rows(owner * low + side * (low // 2), low // 2), :]
            origin = down_own.at[chunk, pl.ds(side * (low // 2), low // 2), :]
        place = (chunk * steps + step) * 4 + side * 2 + piece
        return remote(
            spot if step else origin,
            spot,
            ring_sends,
            ring_arrivals,
            place,
            (at.next, at.back)[side],
        )

    def ring_step(chunk, step):
        for piece in range(2):
            for side in range(2):
                if step:
                    ring_copy(chunk, step - 1, side, piece).wait_recv()
                if step < steps:
                    ring_copy(chunk, step, side, piece).start()

    def tick(count):
        for chunk in range(chunks):
            if 0 <= count - 2 * chunk <= steps:
                ring_step(chunk, count - 2 * chunk)

    attend_send[0:3] = projector[...]
    attend_send[3] = collector[...]
    gains[...] = jnp.zeros_like(gains)
    gains[0:2, 0 : norm_gains.shape[1]] = norm_gains[...]
    gains[...] = pltpu.roll(gains[...], (at.group * members + me) * norm_gains.shape[1], 1)
    first_moves = [
        [
            links.copy(attend_send.at[peer], attend_recv.at[me], {"exp": peer}),
            links.copy(gains, gain_recv.at[me], {"exp": peer}),
        ]
        for peer in at.peers
    ]
    gain_recv[me] = gains[...]
    attend_recv[me] = attend_send[me]
    loads["widener"].wait()
    for matrix in range(2):
        for member in range(members):
            widen_send[member, matrix] = dealt_lanes(widener[matrix], member, members)
    widen_moves = [
        links.copy(widen_send.at[peer], widen_recv.at[me], {"exp": peer}) for peer in at.peers
    ]
    widen_recv[me] = widen_send[me]

    def stage(chunk):
        if chunk == 1:
            for matrix in range(2):
                wide_own[1, matrix] = jnp.concatenate(
                    [widen_recv[member, matrix] for member in range(members)], axis=0
                ).astype(jnp.bfloat16)
            down_own[1] = narrower[...].astype(jnp.bfloat16)
        else:
            index = max(chunk - 1, 0)
            for matrix in range(2):
                wide_own[chunk, matrix] = dealt_lanes(
                    expander[matrix], index, chunks - 1
                ).astype(jnp.bfloat16)
            down_own[chunk] = reducer[index * low : (index + 1) * low, :].astype(jnp.bfloat16)
        for side in range(2):
            wide_full[chunk, side, rows(at.group * block, block), :] = wide_own[chunk, side]
        down_full[chunk, rows(at.group * low, low), :] = down_own[chunk]

    loads["expander"].wait()
    loads["reducer"].wait()
    stage(0)
    tick(0)
    for moves in first_moves:
        for move in moves:
            move.wait_recv()
    attend_full[me, rows(at.group * block, block), :] = (
        attend_recv[...].reshape(block, width).astype(jnp.bfloat16)
    )
    total_gain = gain_recv[0]
    for member in range(1, members):
        total_gain = total_gain + gain_recv[member]
    gain_ring[at.group] = total_gain

    def unit(owner, matrix):
        return attend_full.at[matrix, rows(owner * block, block), :]

    own_unit = unit(at.group, me)
    gain_moves = [
        links.copy(gain_ring.at[at.group], gain_ring.at[at.group], {"grp": other})
        for other in at.others
    ]
    straight = [links.copy(own_unit, own_unit, {"grp": other}) for other in at.others]

    def across(owner):
        spot = unit(owner, me)
        return (links.copy(spot, spot, {"exp": at.far}), links.copy(spot, spot, {"exp": at.near}))

    crossed, passed = [across(at.group)], []

    def onward(owner):
        spot = unit(owner, at.far)
        crossed[len(passed)][0].wait_recv()
        passed.append(links.copy(spot, spot, {"exp": at.near}))

    for index, source in enumerate(at.sources):
        straight[index].wait_recv()
        crossed.append(across(source))
        onward((at.group, *at.sources)[index])
        if index == 1:
            for move in widen_moves:
                move.wait_recv()
            loads["narrower"].wait()
            for chunk in range(1, chunks):
                stage(chunk)
        if index in (2, 4, 6):
            tick(index // 2)
    for move in gain_moves:
        move.wait_recv()
    tick(4)
    outgoing = []

    def hand_out(source, target):
        made = pltpu.make_async_copy(
            source, target, local_sems.at[2 * chunks + len(loads) + len(outgoing)]
        )
        made.start(priority=1)
        outgoing.append(made)

    loads["cotangent"].wait()
    valid = lax.broadcasted_iota(jnp.int32, (length, 1), 0) < length_ref[deal_ref[me]]
    grads_all[me] = jnp.where(valid, cotangent[...], 0.0).astype(jnp.bfloat16)
    route = [routes[choice : choice + 1, :] for choice in range(2)]
    place = [places[choice : choice + 1, :].astype(jnp.float32) for choice in range(2)]
    meta_send[...] = jnp.zeros_like(meta_send)
    for member in range(members):
        named = [chosen == member for chosen in route]
        meta_send[member, 0:1, :] = jnp.where(
            named[0], place[0], jnp.where(named[1], place[1], -1.0)
        )
        meta_send[member, 1:2, :] = jnp.where(
            named[0], gates[0:1, :], jnp.where(named[1], gates[1:2, :], 0.0)
        )
    meta_all[me] = meta_send[me]
    grad_moves = [
        [
            links.copy(grads_all.at[me], grads_all.at[me], {"exp": peer}),
            links.copy(meta_send.at[peer], meta_all.at[me], {"exp": peer}),
        ]
        for peer in at.peers
    ]
    onward(at.sources[-1])
    total_gain = gain_ring[0]
    for group in range(1, groups):
        total_gain = total_gain + gain_ring[group]
    gains_full[...] = total_gain.astype(jnp.bfloat16).astype(jnp.float32)
    stream = tokens[...].astype(jnp.float32)
    first_input = (stream * rms_factor(stream) * gains_full[0:1, :]).astype(jnp.bfloat16)
    saved[4] = first_input
    for moves in crossed:
        moves[1].wait_recv()
    for move in passed:
        move.wait_recv()
    tick(5)
    hand_out(attend_full, attend_out)

    cosines, sines = cos_ref[...], sin_ref[...]
    for matrix in range(3):
        raw = matmul(first_input, attend_full[matrix])
        if matrix == 2:
            saved[2] = raw.astype(jnp.bfloat16)
        else:
            for start in range(0, width, 128):
                piece = raw[:, start : start + 128]
                saved[matrix, :, start : start + 128] = (
                    piece * cosines + turned(piece) * sines
                ).astype(jnp.bfloat16)
    tick(6)

    seq_length = length_ref[me]
    rows_at = lax.broadcasted_iota(jnp.int32, (length, length), 0)
    cols_at = lax.broadcasted_iota(jnp.int32, (length, length), 1)
    allowed = (cols_at <= rows_at) & (cols_at < seq_length)
    lower = first_half((length, 128))

    def heads(pair, carry):
        lanes = pl.ds(pl.multiple_of(pair * 128, 128), 128)
        query, key, value = saved[0, :, lanes], saved[1, :, lanes], saved[2, :, lanes]
        results = []
        for side in range(2):
            alone = jnp.where(lower == (side == 0), query, jnp.zeros_like(query))
            scores = jnp.where(allowed, nt(alone, key) * 0.125, -1e30)
            expo = jnp.exp(scores - jnp.max(scores, axis=-1, keepdims=True))
            soft = expo / jnp.sum(expo, axis=-1, keepdims=True)
            soft_ref[2 * pair + side] = soft
            results.append(matmul(soft.astype(jnp.bfloat16), value))
        saved[3, :, lanes] = jnp.where(lower, results[0], results[1]).astype(jnp.bfloat16)
        return carry

    lax.fori_loop(0, width // 128, heads, 0)
    hand_out(saved, saved_out)
    hand_out(soft_ref, soft_out)
    middle = tokens[...].astype(jnp.float32) + matmul(saved[3], attend_full[3])
    middle_ref[...] = middle
    hand_out(middle_ref, middle_out)
    second_all[me] = (middle * rms_factor(middle) * gains_full[1:2, :]).astype(jnp.bfloat16)
    second_moves = [
        links.copy(second_all.at[me], second_all.at[me], {"exp": peer}) for peer in at.peers
    ]
    for moves in grad_moves:
        for move in moves:
            move.wait_recv()
    grads_home[...] = grads_all[slot_of(deal_ref, me)]
    hand_out(grads_home, grads_out)
    tick(7)

    def hits(slot, by_row):
        line = meta_all[slot, 0:1, :]
        if by_row:
            names = lax.broadcasted_iota(jnp.int32, (capacity, length), 0).astype(jnp.float32)
            hit = names == line
        else:
            names = lax.broadcasted_iota(jnp.int32, (length, capacity), 1).astype(jnp.float32)
            hit = names == upright(line)
        return jnp.where(hit, 1.0, 0.0).astype(jnp.bfloat16)

    def spot_of(slot):
        return slice(slot * capacity, (slot + 1) * capacity)

    def here_of(slot):
        return slice(slot * length, (slot + 1) * length)

    for slot in range(members):
        pick = hits(slot, True)
        gate = jnp.sum(pick.astype(jnp.float32) * meta_all[slot, 1:2, :], axis=1, keepdims=True)
        rows_grad[spot_of(slot), :] = (matmul(pick, grads_all[slot]) * gate).astype(jnp.bfloat16)
    for move in second_moves:
        move.wait_recv()
    for slot in range(members):
        inputs_ref[here_of(slot), :] = second_all[deal_ref[slot]]
        rows_in[spot_of(slot), :] = matmul(hits(slot, True), inputs_ref[here_of(slot), :]).astype(
            jnp.bfloat16
        )
    inputs_turned[...] = inputs_ref[...].T
    rows_turned[...] = rows_in[...].T
    dense_out[...] = jnp.zeros_like(dense_out)
    dense_back[...] = jnp.zeros_like(dense_back)
    rows_out[...] = jnp.zeros_like(rows_out)
    rows_back[...] = jnp.zeros_like(rows_back)

    def branch(chunk, inputs, turned_inputs, outer, out, back):
        for step in range(steps):
            for side in range(2):
                for piece in range(2):
                    ring_copy(chunk, step, side, piece).wait_send()

        def part(index, carry):
            lanes = pl.ds(pl.multiple_of(index * 256, 256), 256)
            gate = matmul(inputs[...], wide_full[chunk, 0, :, lanes])
            up = matmul(inputs[...], wide_full[chunk, 1, :, lanes])
            rise = sigmoid(gate)
            smooth = gate * rise
            hidden = (smooth * up).astype(jnp.bfloat16)
            hidden_grad = nt(outer[...], down_full[chunk, lanes, :])
            gate_grad = (hidden_grad * up * (rise * (1.0 + gate * (1.0 - rise)))).astype(
                jnp.bfloat16
            )
            up_grad = (hidden_grad * smooth).astype(jnp.bfloat16)
            out[...] += matmul(hidden, down_full[chunk, lanes, :])
            back[...] += nt(gate_grad, wide_full[chunk, 0, :, lanes]) + nt(
                up_grad, wide_full[chunk, 1, :, lanes]
            )
            down_full[chunk, lanes, :] = tn(hidden, outer[...]).astype(jnp.bfloat16)
            wide_full[chunk, 0, :, lanes] = matmul(turned_inputs[...], gate_grad).astype(
                jnp.bfloat16
            )
            wide_full[chunk, 1, :, lanes] = matmul(turned_inputs[...], up_grad).astype(
                jnp.bfloat16
            )

            @pl.when(index == 0)
            def _():
                for ahead in range(groups // 2):
                    @pl.when(chunk + 1 + ahead < chunks)
                    def _():
                        ring_step(chunk + 1 + ahead, steps - 1 - 2 * ahead)

            return carry

        lax.fori_loop(0, down_full.shape[1] // 256, part, 0)
        kept(chunk, 0).start(priority=1)
        kept(chunk, 1).start(priority=1)

    def kept(chunk, piece):
        source, target = ((wide_full, wide_grads), (down_full, down_grads))[piece]
        return pltpu.make_async_copy(
            source.at[chunk], target.at[chunk], local_sems.at[2 * chunk + piece]
        )

    outer_all = grads_all.reshape(members * length, width)
    flat = (members * length, width)
    dense = (
        inputs_ref,
        inputs_turned,
        outer_all,
        dense_out.reshape(flat),
        dense_back.reshape(flat),
    )

    def first_sum(chunk, side, piece):
        owner = at.owner(-1 if side == 0 else 1)
        if piece == 0:
            spot = wide_full.at[chunk, side, rows(owner * block, block), :]
        else:
            spot = down_full.at[chunk, rows(owner * low + side * (low // 2), low // 2), :]
        return remote(
            spot,
            (wide_first, down_first)[piece].at[chunk, side],
            first_sends,
            first_arrivals,
            chunk * 4 + side * 2 + piece,
            (at.next, at.back)[side],
        )

    early = chunks - 2

    def start_sums(chunk):
        for piece in range(2):
            for side in range(2):
                first_sum(chunk, side, piece).start()

    def next_chunk(chunk, carry):
        for ahead in range(groups // 2):
            @pl.when((chunk > 0) & (chunk + ahead < chunks))
            def _():
                ring_step(chunk + ahead, steps - 2 * ahead)

        @pl.when(chunk == chunks - 1)
        def _():
            for before in range(early):
                start_sums(before)

        @pl.when(chunk == 1)
        def _():
            branch(chunk, *dense)

        @pl.when(chunk != 1)
        def _():
            branch(chunk, rows_in, rows_turned, rows_grad, rows_out, rows_back)

        return carry

    lax.fori_loop(0, chunks, next_chunk, 0)

    for slot in range(members):
        inner = rows_back[spot_of(slot), :].astype(jnp.bfloat16)
        dense_back[slot] += matmul(hits(slot, False), inner)
    back_moves = []
    for member in range(members):
        back_ref[member] = dense_back[slot_of(deal_ref, member)].astype(jnp.bfloat16)
    for peer in at.peers:
        back_moves.append(links.copy(back_ref.at[peer], back_out.at[me], {"exp": peer}))
    hand_out(back_ref.at[me], back_out.at[me])
    for slot in range(members):
        gate = upright(meta_all[slot, 1:2, :])
        picked = matmul(hits(slot, False), rows_out[spot_of(slot), :].astype(jnp.bfloat16))
        dense_out[slot] += gate * picked
        score = jnp.sum(picked * grads_all[slot].astype(jnp.float32), axis=1, keepdims=True)
        gate_ref[slot] = jnp.broadcast_to(lying(score), gate_ref.shape[1:])
    for member in range(members):
        result_ref[member] = dense_out[slot_of(deal_ref, member)].astype(jnp.bfloat16)
        hand_out(result_ref.at[member], result_out.at[member])
    for chunk in range(chunks):
        kept(chunk, 0).wait()
        kept(chunk, 1).wait()
    for chunk in range(early):
        for piece in range(2):
            for side in range(2):
                first_sum(chunk, side, piece).wait()
    for move in back_moves:
        move.wait_recv()
    for made in outgoing:
        made.wait()
    links.finish()


def scatter_kernel(
    groups,
    members,
    tokens,
    routes,
    gains_full,
    cos_ref,
    sin_ref,
    gate_parts,
    result_parts,
    back_parts,
    wide_grads,
    down_grads,
    wide_first,
    down_first,
    grads_in,
    middle_in,
    attend_in,
    saved_in,
    soft_in,
    output_ref,
    input_grad_ref,
    gate_grad_ref,
    expand_sum,
    reduce_sum,
    widen_sum,
    narrow_sum,
    project_sum,
    collect_sum,
    gains_sum,
    attend_sum,
    grads_home,
    middle_ref,
    attend_full,
    saved,
    soft_ref,
    gate_recv,
    result_recv,
    back_recv,
    wide_own,
    down_own,
    wide_recv,
    down_recv,
    wide_sum,
    turned_ref,
    attend_grad,
    near_recv,
    far_recv,
    far_send,
    attend_total,
    attend_recv,
    attend_back,
    widen_back,
    widen_home,
    gain_own,
    gain_recv,
    gain_ring,
    sends,
    arrivals,
    local_sems,
):
    at = Places(groups, members)
    links = Links(sends, arrivals)
    at.enter()
    me, steps = at.member, groups - 1
    length, width = tokens.shape
    chunks, low = down_own.shape[0], narrow_sum.shape[0]
    share = attend_sum.shape[1]
    block = share * members

    moves_of = {}
    widen_moves = []

    def ring_step(chunk, step):
        made = []
        owners = (at.owner(-1 - step), at.owner(1 + step))
        for piece in range(2):
            for side, target in enumerate((at.next, at.back)):
                own = (wide_own, down_own)[piece]
                landing = (wide_recv, down_recv)[piece].at[chunk, side]
                if piece == 0:
                    spot = (chunk, side, rows(owners[side] * block, block))
                else:
                    spot = (chunk, rows(owners[side] * low + side * (low // 2), low // 2))
                if step == 0:
                    first = (wide_grads, down_grads)[piece]
                    made.append(links.copy(first.at[spot], landing.at[0], target))
                    continue
                if step > 1 or chunk >= early:
                    moves_of[chunk, step - 1][2 * piece + side].wait_recv()
                source = landing.at[step - 1]
                added = source[...].astype(jnp.float32) + own[spot].astype(jnp.float32)
                if step < steps:
                    source[...] = added.astype(jnp.bfloat16)
                elif piece == 0 and chunk != 1:
                    wide_sum[max(chunk - 1, 0), side] = added
                elif piece == 0:
                    for member in range(members):
                        widen_back[member, side] = added[member * share : (member + 1) * share, :]
                else:
                    start = side * (low // 2)
                    if chunk != 1:
                        start = start + max(chunk - 1, 0) * low
                        reduce_sum[start : start + low // 2, :] = added
                    else:
                        narrow_sum[start : start + low // 2, :] = added
                if step < steps:
                    made.append(links.copy(source, landing.at[step], target))
        moves_of[chunk, step] = made
        if step == steps and chunk == 1:
            widen_home[me] = widen_back[me]
            for peer in at.peers:
                widen_moves.append(
                    links.copy(widen_back.at[peer], widen_home.at[me], {"exp": peer})
                )
        if step == steps and chunk and chunk % 2 == 0:
            span = 64 * (chunks - 1)
            for side in range(2):
                found = joined_lanes(wide_sum[chunk - 2, side], wide_sum[chunk - 1, side])
                for index, part in enumerate(found):
                    start = index * span + (chunk - 2) * 64
                    expand_sum[side, :, start : start + 128] = part

    early = chunks - 2
    order = [(chunk, 0) for chunk in range(early, chunks)] + [
        (chunk, step) for step in range(1, groups) for chunk in (1, 0, *range(2, chunks))
    ]

    def poll(count):
        for _ in range(min(count, len(order))):
            chunk, step = order.pop(0)
            for made in own_loads.pop(step, ()):
                made.wait()
            ring_step(chunk, step)

    kept = []

    def load(source, target):
        made = pltpu.make_async_copy(source, target, local_sems.at[len(kept)])
        made.start(priority=1)
        kept.append(made)
        return made

    own_loads = {}

    def load_own(step):
        found = []
        for side, owner in enumerate((at.owner(-1 - step), at.owner(1 + step))):
            spot = rows(owner * block, block)
            found.append(load(wide_grads.at[:, side, spot], wide_own.at[:, side, spot]))
            spot = rows(owner * low + side * (low // 2), low // 2)
            found.append(load(down_grads.at[:, spot], down_own.at[:, spot]))
        own_loads[step] = found

    poll(2)
    middle_loads = [
        load(back_parts, back_recv),
        load(middle_in, middle_ref),
        load(grads_in, grads_home),
        load(attend_in.at[3], attend_full.at[3]),
        load(saved_in, saved),
    ]
    first_loads = [
        load(wide_first.at[:, side], wide_recv.at[0:early, side, 0]) for side in range(2)
    ] + [load(down_first.at[:, side], down_recv.at[0:early, side, 0]) for side in range(2)]
    load_own(1)
    soft_load = load(soft_in, soft_ref)
    load_own(2)
    attend_load = load(attend_in.at[0:3], attend_full.at[0:3])
    for step in range(3, groups):
        load_own(step)
    result_load = load(result_parts.at[me], result_recv.at[me])
    gate_recv[me] = gate_parts[me]
    for made in middle_loads:
        made.wait()
    for made in first_loads:
        made.wait()
    poll(3)
    result_moves = [
        [
            links.copy(result_parts.at[peer], result_recv.at[me], {"exp": peer}),
            links.copy(gate_parts.at[peer], gate_recv.at[me], {"exp": peer}),
        ]
        for peer in at.peers
    ]

    second_grad = back_recv[0].astype(jnp.float32)
    for member in range(1, members):
        second_grad = second_grad + back_recv[member].astype(jnp.float32)
    middle = middle_ref[...]
    scale = rms_factor(middle)
    gain_own[...] = jnp.zeros_like(gain_own)
    gain_own[1:2, :] = jnp.sum(second_grad * (middle * scale), axis=0, keepdims=True)
    input_grad_ref[...] = grads_home[...].astype(jnp.float32) + rms_back(
        middle, scale, second_grad * gains_full[1:2, :]
    )
    middle_low = input_grad_ref[...].astype(jnp.bfloat16)
    turned_ref[3] = nt(middle_low, attend_full[3]).astype(jnp.bfloat16)
    poll(2)
    cosines, sines = cos_ref[...], sin_ref[...]
    lower = first_half((length, 128))
    soft_load.wait()

    def heads(pair, carry):
        lanes = pl.ds(pl.multiple_of(pair * 128, 128), 128)
        query, key, value = saved[0, :, lanes], saved[1, :, lanes], saved[2, :, lanes]
        outer = turned_ref[3, :, lanes]
        made = []
        for side in range(2):
            soft = soft_ref[2 * pair + side]
            alone = jnp.where(lower == (side == 0), outer, jnp.zeros_like(outer))
            value_grad = tn(soft.astype(jnp.bfloat16), outer)
            soft_grad = nt(alone, value)
            score_grad = (
                soft * (soft_grad - jnp.sum(soft * soft_grad, axis=-1, keepdims=True))
            ).astype(jnp.bfloat16)
            made.append(
                (matmul(score_grad, key) * 0.125, tn(score_grad, query) * 0.125, value_grad)
            )
        for index in range(3):
            joined = jnp.where(lower, made[0][index], made[1][index])
            if index < 2:
                joined = joined * cosines - turned(joined) * sines
            turned_ref[index, :, lanes] = joined.astype(jnp.bfloat16)
        return carry

    attend_grad[3] = tn(saved[3], middle_low).astype(jnp.bfloat16)
    for third in range(3):
        lax.fori_loop(2 * third, 2 * third + 2, heads, 0)
        poll(2)
    for matrix in range(3):
        attend_grad[matrix] = tn(saved[4], turned_ref[matrix]).astype(jnp.bfloat16)
    near_moves = [
        links.copy(attend_grad.at[matrix], near_recv.at[index], {"exp": at.near})
        for index, matrix in enumerate((at.near, at.cross))
    ]
    poll(1)
    attend_load.wait()
    first_grad = nt(turned_ref[0], attend_full[0])
    for matrix in range(1, 3):
        first_grad = first_grad + nt(turned_ref[matrix], attend_full[matrix])
    stream = tokens[...].astype(jnp.float32)
    scale = rms_factor(stream)
    gain_own[0:1, :] = jnp.sum(first_grad * (stream * scale), axis=0, keepdims=True)
    gain_moves = [links.copy(gain_own, gain_recv.at[me], {"exp": peer}) for peer in at.peers]
    gain_recv[me] = gain_own[...]
    input_grad_ref[...] += rms_back(stream, scale, first_grad * gains_full[0:1, :])
    for move in near_moves:
        move.wait_recv()
    far_send[...] = (
        attend_grad[at.far].astype(jnp.float32) + near_recv[1].astype(jnp.float32)
    ).astype(jnp.bfloat16)
    far_move = links.copy(far_send, far_recv, {"exp": at.far})
    poll(2)
    for moves in result_moves:
        for move in moves:
            move.wait_recv()
    result_load.wait()
    output = middle_ref[...]
    for member in range(members):
        output = output + result_recv[member].astype(jnp.float32)
    output_ref[...] = output
    for choice in range(2):
        route = routes[choice : choice + 1, :]
        found = jnp.zeros((1, length), jnp.float32)
        for member in range(members):
            found = jnp.where(route == member, gate_recv[member, 0:1, :], found)
        gate_grad_ref[choice : choice + 1, :] = found
    poll(5)
    for move in gain_moves:
        move.wait_recv()
    total = gain_recv[0]
    for member in range(1, members):
        total = total + gain_recv[member]
    gain_ring[at.group] = total
    gain_steps = [
        links.copy(gain_ring.at[at.group], gain_ring.at[at.group], {"grp": other})
        for other in at.others
    ]
    far_move.wait_recv()
    attend_total[...] = (
        attend_grad[me].astype(jnp.float32)
        + near_recv[0].astype(jnp.float32)
        + far_recv[...].astype(jnp.float32)
    ).astype(jnp.bfloat16)

    straight = [
        links.copy(
            attend_total.at[rows(other * block, block), :],
            attend_recv.at[at.group],
            {"grp": other},
        )
        for other in at.others
    ]
    attend_recv[at.group] = attend_total[rows(at.group * block, block), :]
    poll(9)
    for move in straight + gain_steps:
        move.wait_recv()
    added = attend_recv[0].astype(jnp.float32)
    for group in range(1, groups):
        added = added + attend_recv[group].astype(jnp.float32)
    for member in range(members):
        attend_back[member] = added[member * share : (member + 1) * share, :]
    attend_moves = [
        links.copy(attend_back.at[peer], attend_sum.at[me], {"exp": peer}) for peer in at.peers
    ]
    attend_sum[me] = attend_back[me]
    total = gain_ring[0]
    for group in range(1, groups):
        total = total + gain_ring[group]
    count = gains_sum.shape[1]
    start = (at.group * members + me) * count
    gains_sum[...] = pltpu.roll(total, width - start, 1)[0:2, 0:count]
    poll(len(order))
    for move in attend_moves:
        move.wait_recv()
    project_sum[...] = attend_sum[0:3]
    collect_sum[...] = attend_sum[3]
    for move in widen_moves:
        move.wait_recv()
    for matrix in range(2):
        for member in range(0, members, 2):
            found = joined_lanes(widen_home[member, matrix], widen_home[member + 1, matrix])
            for index, part in enumerate(found):
                start = index * 64 * members + member * 64
                widen_sum[matrix, :, start : start + 128] = part
    links.finish()


def update_kernel(rates, fixed, copies, *refs):
    count = len(rates)
    given, made = refs[: 4 * count + copies], refs[4 * count + copies :]
    for index in range(copies):
        made[index][...] = given[4 * count + index][...]

    def update(index):
        weight, moment, variance, gradient = given[4 * index : 4 * index + 4]
        grad = gradient[...]
        if len(weight.shape) < len(gradient.shape):
            grad = grad[3]
        elif weight.shape[0] < gradient.shape[0]:
            grad = grad[: weight.shape[0]]
        grad = 0.5 * grad
        level = 1.0 / (1.0 - 0.5**STEP)
        moment_new = 0.5 * moment[...] + grad
        variance_new = 0.5 * variance[...] + 2.0 * grad * grad
        kept = weight[...]
        stepped = moment_new * level / (jnp.sqrt(variance_new * level) + 1e-08) + 0.1 * kept
        made[copies + 3 * index][...] = moment_new
        made[copies + 3 * index + 1][...] = variance_new
        made[copies + 3 * index + 2][...] = kept - rates[index] * stepped

    for index in range(count):
        if fixed[index]:
            pl.when(pl.program_id(0) == 0)(functools.partial(update, index))
        else:
            update(index)


def update_all(*groups, passed):
    cuts = 4

    def spec(dims, cut):
        if cut is None:
            return pl.BlockSpec(dims, lambda step: (0,) * len(dims))
        block = tuple(size // cuts if at == cut else size for at, size in enumerate(dims))
        return pl.BlockSpec(
            block, lambda step: tuple(step if at == cut else 0 for at in range(len(dims)))
        )

    def cut_of(array):
        dims = array.shape
        for at in range(len(dims) - 1):
            if array.size > 100000 and dims[at] % (8 * cuts) == 0:
                return at
        return len(dims) - 1 if dims[-1] % (128 * cuts) == 0 else None

    given, specs, shapes, out_specs = [], [], [], []
    for _, weight, moment, variance, gradient in groups:
        cut = cut_of(weight)
        for array in (weight, moment, variance, gradient):
            given.append(array)
            specs.append(spec(array.shape, cut))
        for array in (weight, moment, variance):
            shapes.append(jax.ShapeDtypeStruct(array.shape, array.dtype))
            out_specs.append(spec(array.shape, cut))
    extra = [spec(array.shape, cut_of(array)) for array in passed]
    return pl.pallas_call(
        functools.partial(
            update_kernel,
            [group[0] for group in groups],
            [cut_of(group[1]) is None for group in groups],
            len(passed),
        ),
        grid=(cuts,),
        out_shape=[jax.ShapeDtypeStruct(array.shape, array.dtype) for array in passed] + shapes,
        in_specs=specs + extra,
        out_specs=extra + out_specs,
        compiler_params=pltpu.CompilerParams(vmem_limit_bytes=LIMIT),
    )(*given, *passed)


def rotary_lines(length):
    half = HEAD_FEATURES // 2
    freqs = np.exp(-np.log(10000.0) * np.arange(half) / half)
    angles = np.arange(length)[:, None] * freqs[None, :]
    cosines, sines = np.cos(angles), np.sin(angles)
    return (
        np.concatenate([cosines] * 4, axis=1).astype(np.float32),
        np.concatenate([-sines, sines] * 2, axis=1).astype(np.float32),
    )


def spaces(*names):
    kinds = {"v": pltpu.VMEM, "s": pltpu.SMEM, "a": pl.ANY}
    return [pl.BlockSpec(memory_space=kinds[name]) for name in "".join(names)]


def local(
    tokens,
    seq_lengths,
    deal_order,
    expert_routes,
    capacity_slots,
    gate_weights,
    cotangent,
    projector,
    projector_mean,
    projector_square,
    collector,
    collector_first_moment,
    collector_second_moment,
    widener,
    widener_mean,
    widener_square,
    narrower,
    narrower_mean,
    narrower_square,
    norm_gains,
    gains_mean,
    gains_square,
    expander,
    expander_mean,
    expander_square,
    reducer,
    reducer_mean,
    reducer_square,
):
    groups, members = lax.axis_size("grp"), lax.axis_size("exp")
    length, width = tokens.shape[1:]
    inner = expander.shape[3]
    piece = widener.shape[2] // members
    chunks = 1 + inner // piece
    capacity = 3 * length // members
    steps = groups - 1
    high, low, share = expander.shape[2], narrower.shape[0], projector.shape[1]
    bf16, f32 = jnp.bfloat16, jnp.float32
    shape = jax.ShapeDtypeStruct
    cosines, sines = (jnp.asarray(lines) for lines in rotary_lines(length))
    count = 16 * groups
    (
        wide_grads,
        down_grads,
        wide_first,
        down_first,
        attend_full,
        grads_all,
        saved,
        middle,
        soft,
        result_parts,
        back_parts,
        gains_full,
        gate_parts,
    ) = pl.pallas_call(
        functools.partial(gather_kernel, groups, members),
        out_shape=[
            shape((chunks, 2, width, piece), bf16),
            shape((chunks, piece, width), bf16),
            shape((chunks - 2, 2, high, piece), bf16),
            shape((chunks - 2, 2, low // 2, width), bf16),
            shape((4, width, width), bf16),
            shape((length, width), bf16),
            shape((5, length, width), bf16),
            shape((length, width), f32),
            shape((HEAD_COUNT, length, length), f32),
            shape((members, length, width), bf16),
            shape((members, length, width), bf16),
            shape((8, width), f32),
            shape((members, 8, length), f32),
        ],
        in_specs=spaces("ssvavvvvvvaaaavv"),
        out_specs=spaces("a" * 11, "vv"),
        scratch_shapes=[
            VMEM((length, width), f32),
            VMEM(widener.shape, f32),
            VMEM(narrower.shape, f32),
            VMEM(expander.shape[1:], f32),
            VMEM(reducer.shape[1:], f32),
            VMEM((members, length, width), bf16),
            VMEM((members, length, width), bf16),
            VMEM((length, width), bf16),
            VMEM((4, width, width), bf16),
            VMEM((members, length, width), bf16),
            VMEM((5, length, width), bf16),
            VMEM((length, width), f32),
            VMEM((HEAD_COUNT, length, length), f32),
            VMEM((members, length, width), bf16),
            VMEM((members, 8, length), f32),
            VMEM((members, 8, length), f32),
            VMEM((4, share, width), f32),
            VMEM((4, share, width), f32),
            VMEM((members, 2, share, piece), f32),
            VMEM((members, 2, share, piece), f32),
            VMEM((8, width), f32),
            VMEM((members, 8, width), f32),
            VMEM((groups, 8, width), f32),
            VMEM((chunks, 2, width, piece), bf16),
            VMEM((chunks, piece, width), bf16),
            VMEM((chunks, 2, high, piece), bf16),
            VMEM((chunks, low, width), bf16),
            VMEM((members * length, width), bf16),
            VMEM((width, members * length), bf16),
            VMEM((members, length, width), f32),
            VMEM((members, length, width), f32),
            VMEM((members * capacity, width), bf16),
            VMEM((width, members * capacity), bf16),
            VMEM((members * capacity, width), bf16),
            VMEM((members * capacity, width), f32),
            VMEM((members * capacity, width), f32),
            pltpu.SemaphoreType.DMA((count,)),
            pltpu.SemaphoreType.DMA((count,)),
            pltpu.SemaphoreType.DMA((chunks * steps * 4,)),
            pltpu.SemaphoreType.DMA((chunks * steps * 4,)),
            pltpu.SemaphoreType.DMA((chunks * 4,)),
            pltpu.SemaphoreType.DMA((chunks * 4,)),
            pltpu.SemaphoreType.DMA((2 * chunks + 10 + 2 * members,)),
        ],
        compiler_params=pltpu.CompilerParams(
            collective_id=0, has_side_effects=True, vmem_limit_bytes=LIMIT
        ),
    )(
        seq_lengths,
        deal_order,
        tokens[0],
        cotangent[0],
        expert_routes[0].T,
        capacity_slots[0].T,
        gate_weights[0].T,
        norm_gains,
        projector,
        collector,
        widener,
        narrower,
        expander[0],
        reducer[0],
        cosines,
        sines,
    )
    count = 32 * groups
    (
        output,
        input_grad,
        gate_grad,
        expand_sum,
        reduce_sum,
        widen_sum,
        narrow_sum,
        project_sum,
        collect_sum,
        gains_sum,
    ) = pl.pallas_call(
        functools.partial(scatter_kernel, groups, members),
        out_shape=[
            shape((length, width), f32),
            shape((length, width), f32),
            shape((2, length), f32),
            shape((2, high, inner), f32),
            shape(reducer.shape[1:], f32),
            shape(widener.shape, f32),
            shape(narrower.shape, f32),
            shape(projector.shape, f32),
            shape(collector.shape, f32),
            shape(norm_gains.shape, f32),
        ],
        in_specs=spaces("v" * 6, "a" * 11),
        out_specs=spaces("v" * 10),
        scratch_shapes=[
            VMEM((4, share, width), f32),
            VMEM((length, width), bf16),
            VMEM((length, width), f32),
            VMEM((4, width, width), bf16),
            VMEM((5, length, width), bf16),
            VMEM((HEAD_COUNT, length, length), f32),
            VMEM((members, 8, length), f32),
            VMEM((members, length, width), bf16),
            VMEM((members, length, width), bf16),
            VMEM((chunks, 2, width, piece), bf16),
            VMEM((chunks, piece, width), bf16),
            VMEM((chunks, 2, steps, high, piece), bf16),
            VMEM((chunks, 2, steps, low // 2, width), bf16),
            VMEM((chunks - 1, 2, high, piece), f32),
            VMEM((4, length, width), bf16),
            VMEM((4, width, width), bf16),
            VMEM((2, width, width), bf16),
            VMEM((width, width), bf16),
            VMEM((width, width), bf16),
            VMEM((width, width), bf16),
            VMEM((groups, high, width), bf16),
            VMEM((4, share, width), f32),
            VMEM((members, 2, share, piece), f32),
            VMEM((members, 2, share, piece), f32),
            VMEM((8, width), f32),
            VMEM((members, 8, width), f32),
            VMEM((groups, 8, width), f32),
            pltpu.SemaphoreType.DMA((count,)),
            pltpu.SemaphoreType.DMA((count,)),
            pltpu.SemaphoreType.DMA((4 * groups + 16,)),
        ],
        compiler_params=pltpu.CompilerParams(
            collective_id=1, has_side_effects=True, vmem_limit_bytes=LIMIT
        ),
    )(
        tokens[0],
        expert_routes[0].T,
        gains_full,
        cosines,
        sines,
        gate_parts,
        result_parts,
        back_parts,
        wide_grads,
        down_grads,
        wide_first,
        down_first,
        grads_all,
        middle,
        attend_full,
        saved,
        soft,
    )
    updated = update_all(
        (0.1, projector, projector_mean, projector_square, project_sum),
        (0.3, collector, collector_first_moment, collector_second_moment, collect_sum),
        (0.07, widener, widener_mean, widener_square, widen_sum),
        (0.045, narrower, narrower_mean, narrower_square, narrow_sum),
        (0.2, norm_gains, gains_mean, gains_square, gains_sum),
        (0.07, expander[0], expander_mean[0], expander_square[0], expand_sum),
        (0.045, reducer[0], reducer_mean[0], reducer_square[0], reduce_sum),
        passed=(output, input_grad),
    )
    return (
        updated[0][None],
        updated[1][None],
        gate_grad.T[None],
        *updated[2:17],
        *(found[None] for found in updated[17:]),
    )


def fits(mesh):
    groups, members = mesh.shape["grp"], mesh.shape["exp"]
    share = 64 * HEAD_COUNT // (groups * members)
    return members == 4 and groups % 2 == 0 and share % 8 == 0 and share * members // 2 % 16 == 0


def solution(mesh):
    placed = (
        P(("grp", "exp"), None, None),
        P("grp"),
        P("grp"),
        P(("grp", "exp"), None, None),
        P(("grp", "exp"), None, None),
        P(("grp", "exp"), None, None),
        P(("grp", "exp"), None, None),
        P(None, ("grp", "exp"), None),
        P(None, ("grp", "exp"), None),
        P(None, ("grp", "exp"), None),
        P(("grp", "exp"), None),
        P(("grp", "exp"), None),
        P(("grp", "exp"), None),
        P(None, ("grp", "exp"), None),
        P(None, ("grp", "exp"), None),
        P(None, ("grp", "exp"), None),
        P(("grp", "exp"), None),
        P(("grp", "exp"), None),
        P(("grp", "exp"), None),
        P(None, ("grp", "exp")),
        P(None, ("grp", "exp")),
        P(None, ("grp", "exp")),
        P("exp", None, "grp", None),
        P("exp", None, "grp", None),
        P("exp", None, "grp", None),
        P("exp", "grp", None),
        P("exp", "grp", None),
        P("exp", "grp", None),
    )
    return jax.shard_map(
        local if fits(mesh) else local_plain,
        mesh=mesh,
        in_specs=placed,
        out_specs=(
            P(("grp", "exp"), None, None),
            P(("grp", "exp"), None, None),
            P(("grp", "exp"), None, None),
            P(None, ("grp", "exp"), None),
            P(None, ("grp", "exp"), None),
            P(None, ("grp", "exp"), None),
            P(("grp", "exp"), None),
            P(("grp", "exp"), None),
            P(("grp", "exp"), None),
            P(None, ("grp", "exp"), None),
            P(None, ("grp", "exp"), None),
            P(None, ("grp", "exp"), None),
            P(("grp", "exp"), None),
            P(("grp", "exp"), None),
            P(("grp", "exp"), None),
            P(None, ("grp", "exp")),
            P(None, ("grp", "exp")),
            P(None, ("grp", "exp")),
            P("exp", None, "grp", None),
            P("exp", None, "grp", None),
            P("exp", None, "grp", None),
            P("exp", "grp", None),
            P("exp", "grp", None),
            P("exp", "grp", None),
        ),
        check_vma=False,
    )
```

```python
import functools

import jax
import jax.numpy as jnp
import numpy as np
from jax import lax
from jax.experimental import pallas as pl
from jax.experimental.pallas import tpu as pltpu
from jax.sharding import PartitionSpec as P

HEAD_COUNT = 12
HEAD_FEATURES = 64
STEP = 5


def rms_factor(values):
    return lax.rsqrt(jnp.mean(values * values, axis=-1, keepdims=True) + 1e-06)


def rms_back(values, factor, upstream):
    return factor * (
        upstream - values * factor * factor * jnp.mean(upstream * values, axis=-1, keepdims=True)
    )


def rotary(length):
    positions = jnp.arange(length, dtype=jnp.int32).astype(jnp.float32)
    half = HEAD_FEATURES // 2
    freqs = jnp.exp(
        -jnp.log(10000.0) * jnp.arange(half, dtype=jnp.int32).astype(jnp.float32) / half
    )
    angles = positions[:, None] * freqs[None, :]
    return (jnp.cos(angles)[:, None, :], jnp.sin(angles)[:, None, :])


def rotate(values, cosines, sines):
    half = values.shape[-1] // 2
    first = values[..., :half]
    second = values[..., half:]
    return jnp.concatenate(
        [first * cosines - second * sines, second * cosines + first * sines], axis=-1
    )


def rotate_back(values, cosines, sines):
    half = values.shape[-1] // 2
    first = values[..., :half]
    second = values[..., half:]
    return jnp.concatenate(
        [first * cosines + second * sines, second * cosines - first * sines], axis=-1
    )


def silu_slope(values):
    sigmoid_of = jax.nn.sigmoid(values)
    return sigmoid_of * (1.0 + values * (1.0 - sigmoid_of))


def matmul(left, right):
    return jnp.dot(left, right, preferred_element_type=jnp.float32)


def outer_sum(left, right):
    return jnp.einsum("ld,lf->df", left, right, preferred_element_type=jnp.float32)


def adamw_update(weight, moment, variance, gradient, rate):
    moment_new = 0.5 * moment + 0.5 * gradient
    variance_new = 0.5 * variance + 0.5 * gradient * gradient
    correct = 1.0 - 0.5**STEP
    stepped = moment_new / correct / (jnp.sqrt(variance_new / correct) + 1e-08) + 0.1 * weight
    return (moment_new, variance_new, weight - rate * stepped)


def local_plain(
    tokens,
    seq_lengths,
    deal_order,
    expert_routes,
    capacity_slots,
    gate_weights,
    cotangent,
    projector,
    projector_mean,
    projector_square,
    collector,
    collector_first_moment,
    collector_second_moment,
    widener,
    widener_mean,
    widener_square,
    narrower,
    narrower_mean,
    narrower_square,
    norm_gains,
    gains_mean,
    gains_square,
    expander,
    expander_mean,
    expander_square,
    reducer,
    reducer_mean,
    reducer_square,
):
    members = lax.axis_size("exp")
    member = lax.axis_index("exp")
    length_seq = tokens.shape[1]
    width = tokens.shape[2]
    local_experts = expander.shape[0]
    experts_all = local_experts * members
    capacity = 3 * length_seq // experts_all
    member_ids = jnp.arange(members, dtype=jnp.int32)
    source = deal_order[member]
    home_slot = jnp.sum(jnp.where(deal_order == member, member_ids, 0))
    seq_length = seq_lengths[source]
    piece = lax.all_gather(tokens, "exp", axis=0, tiled=True)
    chosen = jnp.arange(piece.shape[0], dtype=jnp.int32) == source
    dealt = jnp.sum(
        jnp.where(chosen[:, None, None], piece, jnp.zeros_like(piece)), axis=0, keepdims=True
    )
    residual_flow = dealt[0].astype(jnp.float32)
    project_full, collect_full, widen_full, narrow_full, gains_full = (
        lax.all_gather(projector.astype(jnp.bfloat16), ("grp", "exp"), axis=1, tiled=True),
        lax.all_gather(collector.astype(jnp.bfloat16), ("grp", "exp"), axis=0, tiled=True),
        lax.all_gather(widener.astype(jnp.bfloat16), ("grp", "exp"), axis=1, tiled=True),
        lax.all_gather(narrower.astype(jnp.bfloat16), ("grp", "exp"), axis=0, tiled=True),
        lax.all_gather(norm_gains.astype(jnp.bfloat16), ("grp", "exp"), axis=1, tiled=True),
    )
    expand_full, reduce_full = (
        lax.all_gather(expander.astype(jnp.bfloat16), "grp", axis=2, tiled=True),
        lax.all_gather(reducer.astype(jnp.bfloat16), "grp", axis=1, tiled=True),
    )
    gains_used = gains_full.astype(jnp.float32)
    cosines, sines = rotary(length_seq)
    scale_one = rms_factor(residual_flow)
    normed_one = residual_flow * scale_one
    first_input = (normed_one * gains_used[0]).astype(jnp.bfloat16)
    query_raw = matmul(first_input, project_full[0]).reshape(length_seq, HEAD_COUNT, HEAD_FEATURES)
    key_raw = matmul(first_input, project_full[1]).reshape(length_seq, HEAD_COUNT, HEAD_FEATURES)
    value_raw = matmul(first_input, project_full[2]).reshape(length_seq, HEAD_COUNT, HEAD_FEATURES)
    query_rot = rotate(query_raw, cosines, sines).astype(jnp.bfloat16)
    key_rot = rotate(key_raw, cosines, sines).astype(jnp.bfloat16)
    value_low = value_raw.astype(jnp.bfloat16)
    rows_at = jnp.arange(length_seq, dtype=jnp.int32)[:, None]
    cols_at = jnp.arange(length_seq, dtype=jnp.int32)[None, :]
    allowed = ((cols_at <= rows_at) & (cols_at < seq_length))[None]
    scores = (
        jnp.einsum("qhd,khd->hqk", query_rot, key_rot, preferred_element_type=jnp.float32) * 0.125
    )
    masked = jnp.where(allowed, scores, -1e30)
    top = jnp.max(masked, axis=-1, keepdims=True)
    expo = jnp.exp(masked - top)
    total = jnp.sum(expo, axis=-1, keepdims=True)
    soft = expo / total
    logsum = top + jnp.log(total)
    mixed_output = (
        jnp.einsum(
            "hqk,khd->qhd", soft.astype(jnp.bfloat16), value_low, preferred_element_type=jnp.float32
        )
        .reshape(length_seq, width)
        .astype(jnp.bfloat16)
    )
    middle_state = residual_flow + matmul(mixed_output, collect_full)
    scale_two = rms_factor(middle_state)
    normed_two = middle_state * scale_two
    second_input = (normed_two * gains_used[1]).astype(jnp.bfloat16)
    gating_scores = matmul(second_input, widen_full[0])
    upward_rows = matmul(second_input, widen_full[1])
    hidden_state = (jax.nn.silu(gating_scores) * upward_rows).astype(jnp.bfloat16)
    dense_branch = matmul(hidden_state, narrow_full)
    flat = (expert_routes[0] * capacity + capacity_slots[0]).reshape(-1)
    spread = jnp.repeat(second_input, 2, axis=0)
    dispatch = jnp.zeros((experts_all * capacity, width), jnp.bfloat16).at[flat].set(spread)
    dispatch = dispatch.reshape(experts_all, capacity, width)
    rows = lax.all_to_all(dispatch, "exp", split_axis=0, concat_axis=0, tiled=True)
    count = rows.shape[1]
    grouped = rows.reshape(members, local_experts, count, width)
    gate_pre = jnp.einsum(
        "sekd,edf->sekf", grouped, expand_full[:, 0], preferred_element_type=jnp.float32
    )
    up_pre = jnp.einsum(
        "sekd,edf->sekf", grouped, expand_full[:, 1], preferred_element_type=jnp.float32
    )
    hidden_rows = (jax.nn.silu(gate_pre) * up_pre).astype(jnp.bfloat16)
    result = jnp.einsum(
        "sekf,efd->sekd", hidden_rows, reduce_full, preferred_element_type=jnp.float32
    )
    result = result.astype(jnp.bfloat16).reshape(members * local_experts, count, width)
    returned_rows = lax.all_to_all(result, "exp", split_axis=0, concat_axis=0, tiled=True)
    outcome = (
        returned_rows,
        rows,
        gate_pre.reshape(members * local_experts, count, -1),
        up_pre.reshape(members * local_experts, count, -1),
    )
    returned, received, gate_kept, up_kept = outcome
    picked = (
        returned.reshape(experts_all * capacity, width)[flat]
        .reshape(length_seq, 2, width)
        .astype(jnp.float32)
    )
    gate_local = gate_weights[0]
    mixture = jnp.sum(gate_local[..., None] * picked, axis=1)
    layer_output = middle_state + dense_branch + mixture
    valid = (jnp.arange(length_seq, dtype=jnp.int32) < seq_length).astype(jnp.float32)
    grad_out = cotangent[0] * valid[:, None]
    grad_low = grad_out.astype(jnp.bfloat16)
    narrow_grad = outer_sum(hidden_state, grad_low)
    hidden_grad = jnp.einsum("ld,fd->lf", grad_low, narrow_full, preferred_element_type=jnp.float32)
    gating_grad = (hidden_grad * upward_rows * silu_slope(gating_scores)).astype(jnp.bfloat16)
    upward_grad = (hidden_grad * jax.nn.silu(gating_scores)).astype(jnp.bfloat16)
    widen_grad = jnp.stack(
        [outer_sum(second_input, gating_grad), outer_sum(second_input, upward_grad)]
    )
    second_grad = jnp.einsum(
        "lf,df->ld", gating_grad, widen_full[0], preferred_element_type=jnp.float32
    ) + jnp.einsum("lf,df->ld", upward_grad, widen_full[1], preferred_element_type=jnp.float32)
    gate_grad_local = jnp.sum(grad_out[:, None, :] * picked, axis=-1)
    result_grad = (
        (gate_local[..., None] * grad_out[:, None, :])
        .astype(jnp.bfloat16)
        .reshape(2 * length_seq, width)
    )
    grad_send = jnp.zeros((experts_all * capacity, width), jnp.bfloat16).at[flat].set(result_grad)
    grad_recv = lax.all_to_all(
        grad_send.reshape(experts_all, capacity, width),
        "exp",
        split_axis=0,
        concat_axis=0,
        tiled=True,
    )
    grad_group = grad_recv.reshape(members, local_experts, capacity, width)
    rows_group = received.reshape(members, local_experts, capacity, width)
    gate_pre = gate_kept.reshape(members, local_experts, capacity, -1)
    up_pre = up_kept.reshape(members, local_experts, capacity, -1)
    hidden_rows = (jax.nn.silu(gate_pre) * up_pre).astype(jnp.bfloat16)
    reduce_grad = jnp.einsum(
        "sekf,sekd->efd", hidden_rows, grad_group, preferred_element_type=jnp.float32
    )
    hidden_rows_grad = jnp.einsum(
        "sekd,efd->sekf", grad_group, reduce_full, preferred_element_type=jnp.float32
    )
    gate_rows_grad = (hidden_rows_grad * up_pre * silu_slope(gate_pre)).astype(jnp.bfloat16)
    up_rows_grad = (hidden_rows_grad * jax.nn.silu(gate_pre)).astype(jnp.bfloat16)
    expand_grad = jnp.stack(
        [
            jnp.einsum(
                "sekd,sekf->edf", rows_group, gate_rows_grad, preferred_element_type=jnp.float32
            ),
            jnp.einsum(
                "sekd,sekf->edf", rows_group, up_rows_grad, preferred_element_type=jnp.float32
            ),
        ],
        axis=1,
    )
    row_grads = jnp.einsum(
        "sekf,edf->sekd", gate_rows_grad, expand_full[:, 0], preferred_element_type=jnp.float32
    ) + jnp.einsum(
        "sekf,edf->sekd", up_rows_grad, expand_full[:, 1], preferred_element_type=jnp.float32
    )
    row_grads = row_grads.astype(jnp.bfloat16).reshape(experts_all, capacity, width)
    came_back = lax.all_to_all(row_grads, "exp", split_axis=0, concat_axis=0, tiled=True).reshape(
        experts_all * capacity, width
    )
    second_grad = second_grad + jnp.sum(
        came_back[flat].reshape(length_seq, 2, width).astype(jnp.float32), axis=1
    )
    gains_grad_two = jnp.sum(second_grad * normed_two, axis=0)
    middle_grad = grad_out + rms_back(middle_state, scale_two, second_grad * gains_used[1])
    middle_low = middle_grad.astype(jnp.bfloat16)
    collect_grad = outer_sum(mixed_output, middle_low)
    mixed_grad = jnp.einsum(
        "ld,ed->le", middle_low, collect_full, preferred_element_type=jnp.float32
    )
    mixed_grad = mixed_grad.astype(jnp.bfloat16).reshape(length_seq, HEAD_COUNT, HEAD_FEATURES)
    scores_again = (
        jnp.einsum("qhd,khd->hqk", query_rot, key_rot, preferred_element_type=jnp.float32) * 0.125
    )
    soft_again = jnp.where(allowed, jnp.exp(scores_again - logsum), 0.0)
    value_grad = jnp.einsum(
        "hqk,qhd->khd",
        soft_again.astype(jnp.bfloat16),
        mixed_grad,
        preferred_element_type=jnp.float32,
    )
    soft_grad = jnp.einsum(
        "qhd,khd->hqk", mixed_grad, value_low, preferred_element_type=jnp.float32
    )
    score_grad = (
        soft_again * (soft_grad - jnp.sum(soft_again * soft_grad, axis=-1, keepdims=True))
    ).astype(jnp.bfloat16)
    query_grad = (
        jnp.einsum("hqk,khd->qhd", score_grad, key_rot, preferred_element_type=jnp.float32) * 0.125
    )
    key_grad = (
        jnp.einsum("hqk,qhd->khd", score_grad, query_rot, preferred_element_type=jnp.float32)
        * 0.125
    )
    query_back = (
        rotate_back(query_grad, cosines, sines).reshape(length_seq, width).astype(jnp.bfloat16)
    )
    key_back = rotate_back(key_grad, cosines, sines).reshape(length_seq, width).astype(jnp.bfloat16)
    value_back = value_grad.reshape(length_seq, width).astype(jnp.bfloat16)
    project_grad = jnp.stack(
        [
            outer_sum(first_input, query_back),
            outer_sum(first_input, key_back),
            outer_sum(first_input, value_back),
        ]
    )
    first_grad = (
        jnp.einsum("le,de->ld", query_back, project_full[0], preferred_element_type=jnp.float32)
        + jnp.einsum("le,de->ld", key_back, project_full[1], preferred_element_type=jnp.float32)
        + jnp.einsum("le,de->ld", value_back, project_full[2], preferred_element_type=jnp.float32)
    )
    gains_grad_one = jnp.sum(first_grad * normed_one, axis=0)
    stream_grad = middle_grad + rms_back(residual_flow, scale_one, first_grad * gains_used[0])
    gains_grad = jnp.stack([gains_grad_one, gains_grad_two])
    project_part, collect_part, widen_part, narrow_part, gains_part = (
        lax.psum_scatter(project_grad, ("grp", "exp"), scatter_dimension=1, tiled=True),
        lax.psum_scatter(collect_grad, ("grp", "exp"), scatter_dimension=0, tiled=True),
        lax.psum_scatter(widen_grad, ("grp", "exp"), scatter_dimension=1, tiled=True),
        lax.psum_scatter(narrow_grad, ("grp", "exp"), scatter_dimension=0, tiled=True),
        lax.psum_scatter(gains_grad, ("grp", "exp"), scatter_dimension=1, tiled=True),
    )
    expand_part, reduce_part = (
        lax.psum_scatter(
            expand_grad.astype(jnp.bfloat16), "grp", scatter_dimension=2, tiled=True
        ).astype(jnp.float32),
        lax.psum_scatter(
            reduce_grad.astype(jnp.bfloat16), "grp", scatter_dimension=1, tiled=True
        ).astype(jnp.float32),
    )
    empty = jnp.zeros((1, length_seq, width), jnp.float32)
    pieces = (
        lax.all_gather(layer_output[None].astype(jnp.bfloat16), "exp", axis=0, tiled=True).astype(
            jnp.float32
        ),
        lax.all_gather(stream_grad[None].astype(jnp.bfloat16), "exp", axis=0, tiled=True).astype(
            jnp.float32
        ),
    )
    chosen = (jnp.arange(pieces[0].shape[0], dtype=jnp.int32) == home_slot)[:, None, None]
    homed_output = empty + jnp.sum(jnp.where(chosen, pieces[0], 0.0), axis=0, keepdims=True)
    homed_grad = empty + jnp.sum(jnp.where(chosen, pieces[1], 0.0), axis=0, keepdims=True)
    project_new = adamw_update(projector, projector_mean, projector_square, project_part, 0.1)
    collect_new = adamw_update(
        collector, collector_first_moment, collector_second_moment, collect_part, 0.3
    )
    widening_updated = adamw_update(widener, widener_mean, widener_square, widen_part, 0.07)
    narrowing_updated = adamw_update(narrower, narrower_mean, narrower_square, narrow_part, 0.045)
    gains_updated = adamw_update(norm_gains, gains_mean, gains_square, gains_part, 0.2)
    expansion_updated = adamw_update(expander, expander_mean, expander_square, expand_part, 0.07)
    reduction_updated = adamw_update(reducer, reducer_mean, reducer_square, reduce_part, 0.045)
    return (
        homed_output,
        homed_grad,
        gate_grad_local[None],
        project_new[0],
        project_new[1],
        project_new[2],
        collect_new[0],
        collect_new[1],
        collect_new[2],
        widening_updated[0],
        widening_updated[1],
        widening_updated[2],
        narrowing_updated[0],
        narrowing_updated[1],
        narrowing_updated[2],
        gains_updated[0],
        gains_updated[1],
        gains_updated[2],
        expansion_updated[0],
        expansion_updated[1],
        expansion_updated[2],
        reduction_updated[0],
        reduction_updated[1],
        reduction_updated[2],
    )


MESH = pl.DeviceIdType.MESH
VMEM = pltpu.VMEM
LIMIT = 60 * 1024 * 1024


def ring_place(index, groups):
    row, side = lax.div(index, 2), lax.rem(index, 2)
    return (1 - side) * row + side * (groups - 1 - row)


def ring_member(place, groups):
    side = lax.div(place, groups // 2)
    return 2 * ((1 - side) * place + side * (groups - 1 - place)) + side


def remote(source, target, sends, arrivals, at, device):
    return pltpu.make_async_remote_copy(
        src_ref=source,
        dst_ref=target,
        send_sem=sends.at[at],
        recv_sem=arrivals.at[at],
        device_id=device,
        device_id_type=MESH,
    )


class Links:
    def __init__(self, sends, arrivals):
        self.sends, self.arrivals, self.count, self.started = sends, arrivals, 0, []

    def copy(self, source, target, device):
        made = remote(source, target, self.sends, self.arrivals, self.count, device)
        self.count += 1
        made.start()
        self.started.append(made)
        return made

    def finish(self):
        for made in self.started:
            made.wait_send()


class Places:
    def __init__(self, groups, members):
        self.groups, self.members = groups, members
        self.group = lax.axis_index("grp")
        self.member = lax.axis_index("exp")
        self.place = ring_place(self.group, groups)
        self.next = {"grp": self.owner(1)}
        self.back = {"grp": self.owner(-1)}
        half = members // 2
        self.far = lax.rem(self.member + half, members)
        self.near = self.member + 1 - 2 * lax.rem(self.member, 2)
        self.cross = lax.rem(self.near + half, members)
        self.peers = [lax.rem(self.member + step, members) for step in range(1, members)]

    def owner(self, offset):
        place = lax.rem(self.place + offset + 2 * self.groups, self.groups)
        return ring_member(place, self.groups)

    def enter(self):
        barrier = pltpu.get_barrier_semaphore()
        partners = [self.next, self.back] + [{"exp": peer} for peer in self.peers]
        for partner in partners:
            pl.semaphore_signal(barrier, inc=1, device_id=partner, device_id_type=MESH)
        pl.semaphore_wait(barrier, len(partners))


def rows(start, count, align=16):
    return pl.ds(pl.multiple_of(start, align), count)


def first_half(shape):
    return lax.rem(lax.broadcasted_iota(jnp.int32, shape, len(shape) - 1), 128) < 64


def turned(values):
    lanes = lax.broadcasted_iota(jnp.int32, values.shape, 1)
    return jnp.where(
        lax.rem(lanes, HEAD_FEATURES) < HEAD_FEATURES // 2,
        pltpu.roll(values, 128 - HEAD_FEATURES // 2, 1),
        pltpu.roll(values, HEAD_FEATURES // 2, 1),
    )


def nt(left, right):
    return lax.dot_general(
        left, right, (((1,), (1,)), ((), ())), preferred_element_type=jnp.float32
    )


def tn(left, right):
    return lax.dot_general(
        left, right, (((0,), (0,)), ((), ())), preferred_element_type=jnp.float32
    )


def sigmoid(values):
    return 1.0 / (1.0 + jnp.exp(-values))


def same(length):
    shape = (length, length)
    return lax.broadcasted_iota(jnp.int32, shape, 0) == lax.broadcasted_iota(jnp.int32, shape, 1)


def upright(line):
    return jnp.sum(jnp.where(same(line.shape[1]), line, 0.0), axis=1, keepdims=True)


def lying(column):
    return jnp.sum(jnp.where(same(column.shape[0]), column, 0.0), axis=0, keepdims=True)


def slot_of(deal_ref, member):
    for _ in range(11):
        member = deal_ref[member]
    return member


def dealt_lanes(values, piece, pieces):
    low_lanes = lax.broadcasted_iota(jnp.int32, (values.shape[0], 128), 1) < 64
    found = []
    span = 64 * pieces
    for start in range(0, values.shape[1], 2 * span):
        start = start + piece // 2 * 128
        one, two = values[:, start : start + 128], values[:, start + span : start + span + 128]
        if piece % 2:
            one = pltpu.roll(one, 64, 1)
        else:
            two = pltpu.roll(two, 64, 1)
        found.append(jnp.where(low_lanes, one, two))
    return jnp.concatenate(found, axis=1)


def joined_lanes(even, odd):
    low_lanes = lax.broadcasted_iota(jnp.int32, (even.shape[0], 128), 1) < 64
    found = []
    for start in range(0, even.shape[1], 128):
        one, two = even[:, start : start + 128], odd[:, start : start + 128]
        found.append(jnp.where(low_lanes, one, pltpu.roll(two, 64, 1)))
        found.append(jnp.where(low_lanes, pltpu.roll(one, 64, 1), two))
    return found


def gather_kernel(
    groups,
    members,
    length_ref,
    deal_ref,
    tokens,
    cotangent_in,
    routes,
    places,
    gates,
    norm_gains,
    projector,
    collector,
    widener_in,
    narrower_in,
    expander_in,
    reducer_in,
    cos_ref,
    sin_ref,
    wide_grads,
    down_grads,
    wide_first,
    down_first,
    attend_out,
    grads_out,
    saved_out,
    middle_out,
    soft_out,
    result_out,
    back_out,
    gains_full,
    gate_ref,
    cotangent,
    widener,
    narrower,
    expander,
    reducer,
    result_ref,
    back_ref,
    grads_home,
    attend_full,
    grads_all,
    saved,
    middle_ref,
    soft_ref,
    second_all,
    meta_send,
    meta_all,
    attend_send,
    attend_recv,
    widen_send,
    widen_recv,
    gains,
    gain_recv,
    gain_ring,
    wide_full,
    down_full,
    wide_own,
    down_own,
    inputs_ref,
    inputs_turned,
    dense_out,
    dense_back,
    rows_in,
    rows_turned,
    rows_grad,
    rows_out,
    rows_back,
    sends,
    arrivals,
    ring_sends,
    ring_arrivals,
    first_sends,
    first_arrivals,
    local_sems,
):
    at = Places(groups, members)
    links = Links(sends, arrivals)
    chunks, low = down_own.shape[:2]
    loads = {}
    for name, source, target in (
        ("expander", expander_in, expander),
        ("reducer", reducer_in, reducer),
        ("widener", widener_in, widener),
        ("narrower", narrower_in, narrower),
        ("cotangent", cotangent_in, cotangent),
    ):
        made = pltpu.make_async_copy(source, target, local_sems.at[2 * chunks + len(loads)])
        made.start(priority=1)
        loads[name] = made
    at.enter()
    me, steps = at.member, groups - 1
    share, width = projector.shape[1:]
    block = share * members
    length = tokens.shape[0]
    capacity = rows_in.shape[0] // members

    def ring_copy(chunk, step, side, piece):
        owner = at.owner(-step if side == 0 else step)
        if piece == 0:
            spot = wide_full.at[chunk, side, rows(owner * block, block), :]
            origin = wide_own.at[chunk, side]
        else:
            spot = down_full.at[chunk, rows(owner * low + side * (low // 2), low // 2), :]
            origin = down_own.at[chunk, pl.ds(side * (low // 2), low // 2), :]
        place = (chunk * steps + step) * 4 + side * 2 + piece
        return remote(
            spot if step else origin,
            spot,
            ring_sends,
            ring_arrivals,
            place,
            (at.next, at.back)[side],
        )

    def ring_step(chunk, step):
        for piece in range(2):
            for side in range(2):
                if step:
                    ring_copy(chunk, step - 1, side, piece).wait_recv()
                if step < steps:
                    ring_copy(chunk, step, side, piece).start()

    def tick(count):
        for chunk in range(chunks):
            if 0 <= count - 2 * chunk <= steps:
                ring_step(chunk, count - 2 * chunk)

    attend_send[0:3] = projector[...]
    attend_send[3] = collector[...]
    gains[...] = jnp.zeros_like(gains)
    gains[0:2, 0 : norm_gains.shape[1]] = norm_gains[...]
    gains[...] = pltpu.roll(gains[...], (at.group * members + me) * norm_gains.shape[1], 1)
    first_moves = [
        [
            links.copy(attend_send.at[peer], attend_recv.at[me], {"exp": peer}),
            links.copy(gains, gain_recv.at[me], {"exp": peer}),
        ]
        for peer in at.peers
    ]
    gain_recv[me] = gains[...]
    attend_recv[me] = attend_send[me]
    loads["widener"].wait()
    for matrix in range(2):
        for member in range(members):
            widen_send[member, matrix] = dealt_lanes(widener[matrix], member, members)
    widen_moves = [
        links.copy(widen_send.at[peer], widen_recv.at[me], {"exp": peer}) for peer in at.peers
    ]
    widen_recv[me] = widen_send[me]

    def stage(chunk):
        if chunk == 1:
            for matrix in range(2):
                wide_own[1, matrix] = jnp.concatenate(
                    [widen_recv[member, matrix] for member in range(members)], axis=0
                ).astype(jnp.bfloat16)
            down_own[1] = narrower[...].astype(jnp.bfloat16)
        else:
            index = max(chunk - 1, 0)
            for matrix in range(2):
                wide_own[chunk, matrix] = dealt_lanes(
                    expander[matrix], index, chunks - 1
                ).astype(jnp.bfloat16)
            down_own[chunk] = reducer[index * low : (index + 1) * low, :].astype(jnp.bfloat16)
        for side in range(2):
            wide_full[chunk, side, rows(at.group * block, block), :] = wide_own[chunk, side]
        down_full[chunk, rows(at.group * low, low), :] = down_own[chunk]

    loads["expander"].wait()
    loads["reducer"].wait()
    stage(0)
    tick(0)
    for moves in first_moves:
        for move in moves:
            move.wait_recv()
    attend_full[me, rows(at.group * block, block), :] = (
        attend_recv[...].reshape(block, width).astype(jnp.bfloat16)
    )
    total_gain = gain_recv[0]
    for member in range(1, members):
        total_gain = total_gain + gain_recv[member]
    gain_ring[at.group] = total_gain

    half = block // 2

    def unit(owner, side, matrix):
        return attend_full.at[matrix, rows(owner * block + side * half, half), :]

    def across(owner, side):
        spot = unit(owner, side, me)
        return (links.copy(spot, spot, {"exp": at.far}), links.copy(spot, spot, {"exp": at.near}))

    def onward(owner, side):
        spot = unit(owner, side, at.far)
        return links.copy(spot, spot, {"exp": at.near})

    ring, crossed, passed = [], [], []
    gain_moves = []
    for step in range(groups):
        owners = (at.owner(-step), at.owner(step))
        if step:
            for move in ring[-1]:
                move.wait_recv()
            gain_moves[-1].wait_recv()
        if step < steps:
            ring.append(
                [
                    links.copy(unit(owner, side, me), unit(owner, side, me), target)
                    for side, (owner, target) in enumerate(zip(owners, (at.next, at.back)))
                ]
            )
            gain_moves.append(
                links.copy(gain_ring.at[owners[0]], gain_ring.at[owners[0]], at.next)
            )
        crossed.append([across(owner, side) for side, owner in enumerate(owners)])
        if step:
            for side, owner in enumerate((at.owner(1 - step), at.owner(step - 1))):
                crossed[step - 1][side][0].wait_recv()
                passed.append(onward(owner, side))
        if step == 2:
            for move in widen_moves:
                move.wait_recv()
            loads["narrower"].wait()
            for chunk in range(1, chunks):
                stage(chunk)
        if step % 2:
            tick(step // 2 + 1)
    outgoing = []

    def hand_out(source, target):
        made = pltpu.make_async_copy(
            source, target, local_sems.at[2 * chunks + len(loads) + len(outgoing)]
        )
        made.start(priority=1)
        outgoing.append(made)

    loads["cotangent"].wait()
    valid = lax.broadcasted_iota(jnp.int32, (length, 1), 0) < length_ref[deal_ref[me]]
    grads_all[me] = jnp.where(valid, cotangent[...], 0.0).astype(jnp.bfloat16)
    route = [routes[choice : choice + 1, :] for choice in range(2)]
    place = [places[choice : choice + 1, :].astype(jnp.float32) for choice in range(2)]
    meta_send[...] = jnp.zeros_like(meta_send)
    for member in range(members):
        named = [chosen == member for chosen in route]
        meta_send[member, 0:1, :] = jnp.where(
            named[0], place[0], jnp.where(named[1], place[1], -1.0)
        )
        meta_send[member, 1:2, :] = jnp.where(
            named[0], gates[0:1, :], jnp.where(named[1], gates[1:2, :], 0.0)
        )
    meta_all[me] = meta_send[me]
    grad_moves = [
        [
            links.copy(grads_all.at[me], grads_all.at[me], {"exp": peer}),
            links.copy(meta_send.at[peer], meta_all.at[me], {"exp": peer}),
        ]
        for peer in at.peers
    ]
    for side, owner in enumerate((at.owner(-steps), at.owner(steps))):
        crossed[steps][side][0].wait_recv()
        passed.append(onward(owner, side))
    total_gain = gain_ring[0]
    for group in range(1, groups):
        total_gain = total_gain + gain_ring[group]
    gains_full[...] = total_gain.astype(jnp.bfloat16).astype(jnp.float32)
    stream = tokens[...].astype(jnp.float32)
    first_input = (stream * rms_factor(stream) * gains_full[0:1, :]).astype(jnp.bfloat16)
    saved[4] = first_input
    for moves in crossed:
        for move in moves:
            move[1].wait_recv()
    for move in passed:
        move.wait_recv()
    tick(5)
    hand_out(attend_full, attend_out)

    cosines, sines = cos_ref[...], sin_ref[...]
    for matrix in range(3):
        raw = matmul(first_input, attend_full[matrix])
        if matrix == 2:
            saved[2] = raw.astype(jnp.bfloat16)
        else:
            for start in range(0, width, 128):
                piece = raw[:, start : start + 128]
                saved[matrix, :, start : start + 128] = (
                    piece * cosines + turned(piece) * sines
                ).astype(jnp.bfloat16)
    tick(6)

    seq_length = length_ref[me]
    rows_at = lax.broadcasted_iota(jnp.int32, (length, length), 0)
    cols_at = lax.broadcasted_iota(jnp.int32, (length, length), 1)
    allowed = (cols_at <= rows_at) & (cols_at < seq_length)
    lower = first_half((length, 128))

    def heads(pair, carry):
        lanes = pl.ds(pl.multiple_of(pair * 128, 128), 128)
        query, key, value = saved[0, :, lanes], saved[1, :, lanes], saved[2, :, lanes]
        results = []
        for side in range(2):
            alone = jnp.where(lower == (side == 0), query, jnp.zeros_like(query))
            scores = jnp.where(allowed, nt(alone, key) * 0.125, -1e30)
            expo = jnp.exp(scores - jnp.max(scores, axis=-1, keepdims=True))
            soft = expo / jnp.sum(expo, axis=-1, keepdims=True)
            soft_ref[2 * pair + side] = soft
            results.append(matmul(soft.astype(jnp.bfloat16), value))
        saved[3, :, lanes] = jnp.where(lower, results[0], results[1]).astype(jnp.bfloat16)
        return carry

    lax.fori_loop(0, width // 128, heads, 0)
    hand_out(saved, saved_out)
    hand_out(soft_ref, soft_out)
    middle = tokens[...].astype(jnp.float32) + matmul(saved[3], attend_full[3])
    middle_ref[...] = middle
    hand_out(middle_ref, middle_out)
    second_all[me] = (middle * rms_factor(middle) * gains_full[1:2, :]).astype(jnp.bfloat16)
    second_moves = [
        links.copy(second_all.at[me], second_all.at[me], {"exp": peer}) for peer in at.peers
    ]
    for moves in grad_moves:
        for move in moves:
            move.wait_recv()
    grads_home[...] = grads_all[slot_of(deal_ref, me)]
    hand_out(grads_home, grads_out)
    tick(7)

    def hits(slot, by_row):
        line = meta_all[slot, 0:1, :]
        if by_row:
            names = lax.broadcasted_iota(jnp.int32, (capacity, length), 0).astype(jnp.float32)
            hit = names == line
        else:
            names = lax.broadcasted_iota(jnp.int32, (length, capacity), 1).astype(jnp.float32)
            hit = names == upright(line)
        return jnp.where(hit, 1.0, 0.0).astype(jnp.bfloat16)

    def spot_of(slot):
        return slice(slot * capacity, (slot + 1) * capacity)

    def here_of(slot):
        return slice(slot * length, (slot + 1) * length)

    for slot in range(members):
        pick = hits(slot, True)
        gate = jnp.sum(pick.astype(jnp.float32) * meta_all[slot, 1:2, :], axis=1, keepdims=True)
        rows_grad[spot_of(slot), :] = (matmul(pick, grads_all[slot]) * gate).astype(jnp.bfloat16)
    for move in second_moves:
        move.wait_recv()
    for slot in range(members):
        inputs_ref[here_of(slot), :] = second_all[deal_ref[slot]]
        rows_in[spot_of(slot), :] = matmul(hits(slot, True), inputs_ref[here_of(slot), :]).astype(
            jnp.bfloat16
        )
    inputs_turned[...] = inputs_ref[...].T
    rows_turned[...] = rows_in[...].T
    dense_out[...] = jnp.zeros_like(dense_out)
    dense_back[...] = jnp.zeros_like(dense_back)
    rows_out[...] = jnp.zeros_like(rows_out)
    rows_back[...] = jnp.zeros_like(rows_back)

    def branch(chunk, inputs, turned_inputs, outer, out, back):
        for step in range(steps):
            for side in range(2):
                for piece in range(2):
                    ring_copy(chunk, step, side, piece).wait_send()

        def part(index, carry):
            lanes = pl.ds(pl.multiple_of(index * 256, 256), 256)
            gate = matmul(inputs[...], wide_full[chunk, 0, :, lanes])
            up = matmul(inputs[...], wide_full[chunk, 1, :, lanes])
            rise = sigmoid(gate)
            smooth = gate * rise
            hidden = (smooth * up).astype(jnp.bfloat16)
            hidden_grad = nt(outer[...], down_full[chunk, lanes, :])
            gate_grad = (hidden_grad * up * (rise * (1.0 + gate * (1.0 - rise)))).astype(
                jnp.bfloat16
            )
            up_grad = (hidden_grad * smooth).astype(jnp.bfloat16)
            out[...] += matmul(hidden, down_full[chunk, lanes, :])
            back[...] += nt(gate_grad, wide_full[chunk, 0, :, lanes]) + nt(
                up_grad, wide_full[chunk, 1, :, lanes]
            )
            down_full[chunk, lanes, :] = tn(hidden, outer[...]).astype(jnp.bfloat16)
            wide_full[chunk, 0, :, lanes] = matmul(turned_inputs[...], gate_grad).astype(
                jnp.bfloat16
            )
            wide_full[chunk, 1, :, lanes] = matmul(turned_inputs[...], up_grad).astype(
                jnp.bfloat16
            )

            @pl.when(index == 0)
            def _():
                for ahead in range(groups // 2):
                    @pl.when(chunk + 1 + ahead < chunks)
                    def _():
                        ring_step(chunk + 1 + ahead, steps - 1 - 2 * ahead)

            return carry

        lax.fori_loop(0, down_full.shape[1] // 256, part, 0)
        kept(chunk, 0).start(priority=1)
        kept(chunk, 1).start(priority=1)

    def kept(chunk, piece):
        source, target = ((wide_full, wide_grads), (down_full, down_grads))[piece]
        return pltpu.make_async_copy(
            source.at[chunk], target.at[chunk], local_sems.at[2 * chunk + piece]
        )

    outer_all = grads_all.reshape(members * length, width)
    flat = (members * length, width)
    dense = (
        inputs_ref,
        inputs_turned,
        outer_all,
        dense_out.reshape(flat),
        dense_back.reshape(flat),
    )

    def first_sum(chunk, side, piece):
        owner = at.owner(-1 if side == 0 else 1)
        if piece == 0:
            spot = wide_full.at[chunk, side, rows(owner * block, block), :]
        else:
            spot = down_full.at[chunk, rows(owner * low + side * (low // 2), low // 2), :]
        return remote(
            spot,
            (wide_first, down_first)[piece].at[chunk, side],
            first_sends,
            first_arrivals,
            chunk * 4 + side * 2 + piece,
            (at.next, at.back)[side],
        )

    early = chunks - 2

    def start_sums(chunk):
        for piece in range(2):
            for side in range(2):
                first_sum(chunk, side, piece).start()

    def next_chunk(chunk, carry):
        for ahead in range(groups // 2):
            @pl.when((chunk > 0) & (chunk + ahead < chunks))
            def _():
                ring_step(chunk + ahead, steps - 2 * ahead)

        @pl.when(chunk == chunks - 1)
        def _():
            for before in range(early):
                start_sums(before)

        @pl.when(chunk == 1)
        def _():
            branch(chunk, *dense)

        @pl.when(chunk != 1)
        def _():
            branch(chunk, rows_in, rows_turned, rows_grad, rows_out, rows_back)

        return carry

    lax.fori_loop(0, chunks, next_chunk, 0)

    for slot in range(members):
        inner = rows_back[spot_of(slot), :].astype(jnp.bfloat16)
        dense_back[slot] += matmul(hits(slot, False), inner)
    for member in range(members):
        back_ref[member] = dense_back[slot_of(deal_ref, member)].astype(jnp.bfloat16)
        hand_out(back_ref.at[member], back_out.at[member])
    for slot in range(members):
        gate = upright(meta_all[slot, 1:2, :])
        picked = matmul(hits(slot, False), rows_out[spot_of(slot), :].astype(jnp.bfloat16))
        dense_out[slot] += gate * picked
        score = jnp.sum(picked * grads_all[slot].astype(jnp.float32), axis=1, keepdims=True)
        gate_ref[slot] = jnp.broadcast_to(lying(score), gate_ref.shape[1:])
    for member in range(members):
        result_ref[member] = dense_out[slot_of(deal_ref, member)].astype(jnp.bfloat16)
        hand_out(result_ref.at[member], result_out.at[member])
    for chunk in range(chunks):
        kept(chunk, 0).wait()
        kept(chunk, 1).wait()
    for chunk in range(early):
        for piece in range(2):
            for side in range(2):
                first_sum(chunk, side, piece).wait()
    for made in outgoing:
        made.wait()
    links.finish()


def scatter_kernel(
    groups,
    members,
    tokens,
    routes,
    gains_full,
    cos_ref,
    sin_ref,
    gate_parts,
    result_parts,
    back_parts,
    wide_grads,
    down_grads,
    wide_first,
    down_first,
    grads_in,
    middle_in,
    attend_in,
    saved_in,
    soft_in,
    output_out,
    input_grad_out,
    expand_out,
    reduce_out,
    narrow_out,
    project_out,
    collect_out,
    gate_grad_ref,
    widen_sum,
    gains_sum,
    expand_sum,
    reduce_sum,
    narrow_sum,
    output_ref,
    input_grad_ref,
    attend_sum,
    grads_home,
    middle_ref,
    attend_full,
    saved,
    soft_ref,
    gate_recv,
    result_recv,
    back_recv,
    wide_own,
    down_own,
    wide_recv,
    down_recv,
    wide_sum,
    turned_ref,
    attend_grad,
    near_recv,
    far_recv,
    far_send,
    attend_total,
    attend_recv,
    attend_back,
    widen_back,
    widen_home,
    gain_own,
    gain_recv,
    gain_ring,
    sends,
    arrivals,
    local_sems,
):
    at = Places(groups, members)
    links = Links(sends, arrivals)
    at.enter()
    me, steps = at.member, groups - 1
    length, width = tokens.shape
    chunks, low = down_own.shape[0], narrow_sum.shape[0]
    share = attend_sum.shape[1]
    block = share * members

    moves_of = {}
    widen_moves = []

    def ring_step(chunk, step):
        made = []
        owners = (at.owner(-1 - step), at.owner(1 + step))
        for piece in range(2):
            for side, target in enumerate((at.next, at.back)):
                own = (wide_own, down_own)[piece]
                landing = (wide_recv, down_recv)[piece].at[chunk, side]
                if piece == 0:
                    spot = (chunk, side, rows(owners[side] * block, block))
                else:
                    spot = (chunk, rows(owners[side] * low + side * (low // 2), low // 2))
                if step == 0:
                    first = (wide_grads, down_grads)[piece]
                    made.append(links.copy(first.at[spot], landing.at[0], target))
                    continue
                if step > 1 or chunk >= early:
                    moves_of[chunk, step - 1][2 * piece + side].wait_recv()
                source = landing.at[step - 1]
                added = source[...].astype(jnp.float32) + own[spot].astype(jnp.float32)
                if step < steps:
                    source[...] = added.astype(jnp.bfloat16)
                elif piece == 0 and chunk != 1:
                    wide_sum[max(chunk - 1, 0), side] = added
                elif piece == 0:
                    for member in range(members):
                        widen_back[member, side] = added[member * share : (member + 1) * share, :]
                else:
                    start = side * (low // 2)
                    if chunk != 1:
                        start = start + max(chunk - 1, 0) * low
                        reduce_sum[start : start + low // 2, :] = added
                    else:
                        narrow_sum[start : start + low // 2, :] = added
                if step < steps:
                    made.append(links.copy(source, landing.at[step], target))
        moves_of[chunk, step] = made
        if step == steps and chunk == 1:
            widen_home[me] = widen_back[me]
            for peer in at.peers:
                widen_moves.append(
                    links.copy(widen_back.at[peer], widen_home.at[me], {"exp": peer})
                )
        if step == steps and chunk == 1:
            store(narrow_sum, narrow_out)
        elif step == steps:
            spot = rows(max(chunk - 1, 0) * low, low)
            store(reduce_sum.at[spot], reduce_out.at[spot])
        if step == steps and chunk and chunk % 2 == 0:
            pair = chunk // 2 - 1
            for side in range(2):
                found = joined_lanes(wide_sum[chunk - 2, side], wide_sum[chunk - 1, side])
                for index in range(0, len(found), 1):
                    expand_sum[pair, side, :, index * 128 : index * 128 + 128] = found[index]
            store(expand_sum.at[pair], expand_out.at[pair])

    early = chunks - 2
    order = [(chunk, 0) for chunk in range(early, chunks)] + [
        (chunk, step) for step in range(1, groups) for chunk in (1, 0, *range(2, chunks))
    ]

    def poll(count):
        for _ in range(min(count, len(order))):
            chunk, step = order.pop(0)
            for made in own_loads.pop(step, ()):
                made.wait()
            ring_step(chunk, step)

    kept, stored = [], []

    def store(source, target):
        made = pltpu.make_async_copy(source, target, local_sems.at[4 * groups + 14 + len(stored)])
        made.start(priority=1)
        stored.append(made)

    def load(source, target):
        made = pltpu.make_async_copy(source, target, local_sems.at[len(kept)])
        made.start(priority=1)
        kept.append(made)
        return made

    own_loads = {}

    def load_own(step):
        found = []
        for side, owner in enumerate((at.owner(-1 - step), at.owner(1 + step))):
            spot = rows(owner * block, block)
            found.append(load(wide_grads.at[:, side, spot], wide_own.at[:, side, spot]))
            spot = rows(owner * low + side * (low // 2), low // 2)
            found.append(load(down_grads.at[:, spot], down_own.at[:, spot]))
        own_loads[step] = found

    back_moves = [
        links.copy(back_parts.at[peer], back_recv.at[me], {"exp": peer}) for peer in at.peers
    ]
    first_loads = [
        load(wide_first.at[:, side], wide_recv.at[0:early, side, 0]) for side in range(2)
    ] + [load(down_first.at[:, side], down_recv.at[0:early, side, 0]) for side in range(2)]
    load_own(1)
    poll(2)
    middle_loads = [
        load(back_parts.at[me], back_recv.at[me]),
        load(middle_in, middle_ref),
        load(grads_in, grads_home),
        load(attend_in.at[3], attend_full.at[3]),
        load(saved_in, saved),
    ]
    soft_load = load(soft_in, soft_ref)
    load_own(2)
    attend_load = load(attend_in.at[0:3], attend_full.at[0:3])
    for step in range(3, groups):
        load_own(step)
    result_load = load(result_parts.at[me], result_recv.at[me])
    gate_recv[me] = gate_parts[me]
    for made in first_loads:
        made.wait()
    poll(3)
    result_moves = [
        [
            links.copy(result_parts.at[peer], result_recv.at[me], {"exp": peer}),
            links.copy(gate_parts.at[peer], gate_recv.at[me], {"exp": peer}),
        ]
        for peer in at.peers
    ]
    for made in middle_loads:
        made.wait()
    for move in back_moves:
        move.wait_recv()

    second_grad = back_recv[0].astype(jnp.float32)
    for member in range(1, members):
        second_grad = second_grad + back_recv[member].astype(jnp.float32)
    middle = middle_ref[...]
    scale = rms_factor(middle)
    gain_own[...] = jnp.zeros_like(gain_own)
    gain_own[1:2, :] = jnp.sum(second_grad * (middle * scale), axis=0, keepdims=True)
    input_grad_ref[...] = grads_home[...].astype(jnp.float32) + rms_back(
        middle, scale, second_grad * gains_full[1:2, :]
    )
    middle_low = input_grad_ref[...].astype(jnp.bfloat16)
    turned_ref[3] = nt(middle_low, attend_full[3]).astype(jnp.bfloat16)
    poll(2)
    cosines, sines = cos_ref[...], sin_ref[...]
    lower = first_half((length, 128))
    soft_load.wait()

    def heads(pair, carry):
        lanes = pl.ds(pl.multiple_of(pair * 128, 128), 128)
        query, key, value = saved[0, :, lanes], saved[1, :, lanes], saved[2, :, lanes]
        outer = turned_ref[3, :, lanes]
        made = []
        for side in range(2):
            soft = soft_ref[2 * pair + side]
            alone = jnp.where(lower == (side == 0), outer, jnp.zeros_like(outer))
            value_grad = tn(soft.astype(jnp.bfloat16), outer)
            soft_grad = nt(alone, value)
            score_grad = (
                soft * (soft_grad - jnp.sum(soft * soft_grad, axis=-1, keepdims=True))
            ).astype(jnp.bfloat16)
            made.append(
                (matmul(score_grad, key) * 0.125, tn(score_grad, query) * 0.125, value_grad)
            )
        for index in range(3):
            joined = jnp.where(lower, made[0][index], made[1][index])
            if index < 2:
                joined = joined * cosines - turned(joined) * sines
            turned_ref[index, :, lanes] = joined.astype(jnp.bfloat16)
        return carry

    attend_grad[3] = tn(saved[3], middle_low).astype(jnp.bfloat16)
    for third in range(3):
        lax.fori_loop(2 * third, 2 * third + 2, heads, 0)
        poll(2)
    for matrix in range(3):
        attend_grad[matrix] = tn(saved[4], turned_ref[matrix]).astype(jnp.bfloat16)
    near_moves = [
        links.copy(attend_grad.at[matrix], near_recv.at[index], {"exp": at.near})
        for index, matrix in enumerate((at.near, at.cross))
    ]
    poll(1)
    attend_load.wait()
    first_grad = nt(turned_ref[0], attend_full[0])
    for matrix in range(1, 3):
        first_grad = first_grad + nt(turned_ref[matrix], attend_full[matrix])
    stream = tokens[...].astype(jnp.float32)
    scale = rms_factor(stream)
    gain_own[0:1, :] = jnp.sum(first_grad * (stream * scale), axis=0, keepdims=True)
    gain_moves = [links.copy(gain_own, gain_recv.at[me], {"exp": peer}) for peer in at.peers]
    gain_recv[me] = gain_own[...]
    input_grad_ref[...] += rms_back(stream, scale, first_grad * gains_full[0:1, :])
    store(input_grad_ref, input_grad_out)
    for move in near_moves:
        move.wait_recv()
    far_send[...] = (
        attend_grad[at.far].astype(jnp.float32) + near_recv[1].astype(jnp.float32)
    ).astype(jnp.bfloat16)
    far_move = links.copy(far_send, far_recv, {"exp": at.far})
    poll(2)
    for moves in result_moves:
        for move in moves:
            move.wait_recv()
    result_load.wait()
    output = middle_ref[...]
    for member in range(members):
        output = output + result_recv[member].astype(jnp.float32)
    output_ref[...] = output
    store(output_ref, output_out)
    for choice in range(2):
        route = routes[choice : choice + 1, :]
        found = jnp.zeros((1, length), jnp.float32)
        for member in range(members):
            found = jnp.where(route == member, gate_recv[member, 0:1, :], found)
        gate_grad_ref[choice : choice + 1, :] = found
    poll(len(order) - 18)
    for move in gain_moves:
        move.wait_recv()
    total = gain_recv[0]
    for member in range(1, members):
        total = total + gain_recv[member]
    gain_ring[at.group] = total
    far_move.wait_recv()
    attend_total[...] = (
        attend_grad[me].astype(jnp.float32)
        + near_recv[0].astype(jnp.float32)
        + far_recv[...].astype(jnp.float32)
    ).astype(jnp.bfloat16)

    half = block // 2
    small, gain_steps = [], []

    def advance_small():
        step = len(small)
        owners = (at.owner(-1 - step), at.owner(1 + step))
        made = []
        for side, target in enumerate((at.next, at.back)):
            spot = attend_total.at[rows(owners[side] * block + side * half, half), :]
            if step:
                small[-1][side].wait_recv()
                source = attend_recv.at[side, step - 1]
                added = source[...].astype(jnp.float32) + spot[...].astype(jnp.float32)
                if step < steps:
                    source[...] = added.astype(jnp.bfloat16)
                else:
                    for member in range(members // 2):
                        attend_back[side * (members // 2) + member] = added[
                            member * share : (member + 1) * share, :
                        ]
                spot = source
            if step < steps:
                made.append(links.copy(spot, attend_recv.at[side, step], target))
        if step:
            gain_steps[-1].wait_recv()
        if step < steps:
            owner = at.owner(-step)
            gain_steps.append(links.copy(gain_ring.at[owner], gain_ring.at[owner], at.next))
        small.append(made)

    while len(small) <= steps:
        advance_small()
        poll(2)
    attend_moves = [
        links.copy(attend_back.at[peer], attend_sum.at[me], {"exp": peer}) for peer in at.peers
    ]
    attend_sum[me] = attend_back[me]
    total = gain_ring[0]
    for group in range(1, groups):
        total = total + gain_ring[group]
    count = gains_sum.shape[1]
    start = (at.group * members + me) * count
    gains_sum[...] = pltpu.roll(total, width - start, 1)[0:2, 0:count]
    poll(len(order) - 2)
    for move in attend_moves:
        move.wait_recv()
    store(attend_sum.at[0:3], project_out)
    store(attend_sum.at[3], collect_out)
    for move in widen_moves:
        move.wait_recv()
    for matrix in range(2):
        for member in range(0, members, 2):
            found = joined_lanes(widen_home[member, matrix], widen_home[member + 1, matrix])
            for index, part in enumerate(found):
                start = index * 64 * members + member * 64
                widen_sum[matrix, :, start : start + 128] = part
    poll(len(order))
    for made in stored:
        made.wait()
    links.finish()


def update_kernel(rates, fixed, copies, *refs):
    count = len(rates)
    given, made = refs[: 4 * count + copies], refs[4 * count + copies :]
    for index in range(copies):
        made[index][...] = given[4 * count + index][...]

    def update(index):
        weight, moment, variance, gradient = given[4 * index : 4 * index + 4]
        if len(gradient.shape) > len(weight.shape):
            grad = jnp.concatenate(
                [
                    gradient[at % 2, :, :, at // 2 * 128 : at // 2 * 128 + 128]
                    for at in range(weight.shape[-1] // 128)
                ],
                axis=2,
            )
        else:
            grad = gradient[...]
        grad = 0.5 * grad
        level = 1.0 / (1.0 - 0.5**STEP)
        moment_new = 0.5 * moment[...] + grad
        variance_new = 0.5 * variance[...] + 2.0 * grad * grad
        kept = weight[...]
        stepped = moment_new * level / (jnp.sqrt(variance_new * level) + 1e-08) + 0.1 * kept
        made[copies + 3 * index][...] = moment_new
        made[copies + 3 * index + 1][...] = variance_new
        made[copies + 3 * index + 2][...] = kept - rates[index] * stepped

    for index in range(count):
        if fixed[index]:
            pl.when(pl.program_id(0) == 0)(functools.partial(update, index))
        else:
            update(index)


def update_all(*groups, passed):
    cuts = 4

    def spec(dims, cut):
        if cut is None:
            return pl.BlockSpec(dims, lambda step: (0,) * len(dims))
        block = tuple(size // cuts if at == cut else size for at, size in enumerate(dims))
        return pl.BlockSpec(
            block, lambda step: tuple(step if at == cut else 0 for at in range(len(dims)))
        )

    def cut_of(array):
        dims = array.shape
        for at in range(len(dims) - 1):
            if array.size > 100000 and dims[at] % (8 * cuts) == 0:
                return at
        return len(dims) - 1 if dims[-1] % (128 * cuts) == 0 else None

    given, specs, shapes, out_specs = [], [], [], []
    for _, weight, moment, variance, gradient in groups:
        cut = cut_of(weight)
        for array in (weight, moment, variance, gradient):
            given.append(array)
            more = array.ndim - weight.ndim
            specs.append(spec(array.shape, None if cut is None else cut + more))
        for array in (weight, moment, variance):
            shapes.append(jax.ShapeDtypeStruct(array.shape, array.dtype))
            out_specs.append(spec(array.shape, cut))
    extra = [spec(array.shape, cut_of(array)) for array in passed]
    return pl.pallas_call(
        functools.partial(
            update_kernel,
            [group[0] for group in groups],
            [cut_of(group[1]) is None for group in groups],
            len(passed),
        ),
        grid=(cuts,),
        out_shape=[jax.ShapeDtypeStruct(array.shape, array.dtype) for array in passed] + shapes,
        in_specs=specs + extra,
        out_specs=extra + out_specs,
        compiler_params=pltpu.CompilerParams(vmem_limit_bytes=LIMIT),
    )(*given, *passed)


def rotary_lines(length):
    half = HEAD_FEATURES // 2
    freqs = np.exp(-np.log(10000.0) * np.arange(half) / half)
    angles = np.arange(length)[:, None] * freqs[None, :]
    cosines, sines = np.cos(angles), np.sin(angles)
    return (
        np.concatenate([cosines] * 4, axis=1).astype(np.float32),
        np.concatenate([-sines, sines] * 2, axis=1).astype(np.float32),
    )


def spaces(*names):
    kinds = {"v": pltpu.VMEM, "s": pltpu.SMEM, "a": pl.ANY}
    return [pl.BlockSpec(memory_space=kinds[name]) for name in "".join(names)]


def local(
    tokens,
    seq_lengths,
    deal_order,
    expert_routes,
    capacity_slots,
    gate_weights,
    cotangent,
    projector,
    projector_mean,
    projector_square,
    collector,
    collector_first_moment,
    collector_second_moment,
    widener,
    widener_mean,
    widener_square,
    narrower,
    narrower_mean,
    narrower_square,
    norm_gains,
    gains_mean,
    gains_square,
    expander,
    expander_mean,
    expander_square,
    reducer,
    reducer_mean,
    reducer_square,
):
    groups, members = lax.axis_size("grp"), lax.axis_size("exp")
    length, width = tokens.shape[1:]
    inner = expander.shape[3]
    piece = widener.shape[2] // members
    chunks = 1 + inner // piece
    capacity = 3 * length // members
    steps = groups - 1
    high, low, share = expander.shape[2], narrower.shape[0], projector.shape[1]
    bf16, f32 = jnp.bfloat16, jnp.float32
    shape = jax.ShapeDtypeStruct
    cosines, sines = (jnp.asarray(lines) for lines in rotary_lines(length))
    count = 16 * groups
    (
        wide_grads,
        down_grads,
        wide_first,
        down_first,
        attend_full,
        grads_all,
        saved,
        middle,
        soft,
        result_parts,
        back_parts,
        gains_full,
        gate_parts,
    ) = pl.pallas_call(
        functools.partial(gather_kernel, groups, members),
        out_shape=[
            shape((chunks, 2, width, piece), bf16),
            shape((chunks, piece, width), bf16),
            shape((chunks - 2, 2, high, piece), bf16),
            shape((chunks - 2, 2, low // 2, width), bf16),
            shape((4, width, width), bf16),
            shape((length, width), bf16),
            shape((5, length, width), bf16),
            shape((length, width), f32),
            shape((HEAD_COUNT, length, length), f32),
            shape((members, length, width), bf16),
            shape((members, length, width), bf16),
            shape((8, width), f32),
            shape((members, 8, length), f32),
        ],
        in_specs=spaces("ssvavvvvvvaaaavv"),
        out_specs=spaces("a" * 11, "vv"),
        scratch_shapes=[
            VMEM((length, width), f32),
            VMEM(widener.shape, f32),
            VMEM(narrower.shape, f32),
            VMEM(expander.shape[1:], f32),
            VMEM(reducer.shape[1:], f32),
            VMEM((members, length, width), bf16),
            VMEM((members, length, width), bf16),
            VMEM((length, width), bf16),
            VMEM((4, width, width), bf16),
            VMEM((members, length, width), bf16),
            VMEM((5, length, width), bf16),
            VMEM((length, width), f32),
            VMEM((HEAD_COUNT, length, length), f32),
            VMEM((members, length, width), bf16),
            VMEM((members, 8, length), f32),
            VMEM((members, 8, length), f32),
            VMEM((4, share, width), f32),
            VMEM((4, share, width), f32),
            VMEM((members, 2, share, piece), f32),
            VMEM((members, 2, share, piece), f32),
            VMEM((8, width), f32),
            VMEM((members, 8, width), f32),
            VMEM((groups, 8, width), f32),
            VMEM((chunks, 2, width, piece), bf16),
            VMEM((chunks, piece, width), bf16),
            VMEM((chunks, 2, high, piece), bf16),
            VMEM((chunks, low, width), bf16),
            VMEM((members * length, width), bf16),
            VMEM((width, members * length), bf16),
            VMEM((members, length, width), f32),
            VMEM((members, length, width), f32),
            VMEM((members * capacity, width), bf16),
            VMEM((width, members * capacity), bf16),
            VMEM((members * capacity, width), bf16),
            VMEM((members * capacity, width), f32),
            VMEM((members * capacity, width), f32),
            pltpu.SemaphoreType.DMA((count,)),
            pltpu.SemaphoreType.DMA((count,)),
            pltpu.SemaphoreType.DMA((chunks * steps * 4,)),
            pltpu.SemaphoreType.DMA((chunks * steps * 4,)),
            pltpu.SemaphoreType.DMA((chunks * 4,)),
            pltpu.SemaphoreType.DMA((chunks * 4,)),
            pltpu.SemaphoreType.DMA((2 * chunks + 10 + 2 * members,)),
        ],
        compiler_params=pltpu.CompilerParams(
            collective_id=0, has_side_effects=True, vmem_limit_bytes=LIMIT
        ),
    )(
        seq_lengths,
        deal_order,
        tokens[0],
        cotangent[0],
        expert_routes[0].T,
        capacity_slots[0].T,
        gate_weights[0].T,
        norm_gains,
        projector,
        collector,
        widener,
        narrower,
        expander[0],
        reducer[0],
        cosines,
        sines,
    )
    count = 32 * groups
    (
        output,
        input_grad,
        expand_sum,
        reduce_sum,
        narrow_sum,
        project_sum,
        collect_sum,
        gate_grad,
        widen_sum,
        gains_sum,
    ) = pl.pallas_call(
        functools.partial(scatter_kernel, groups, members),
        out_shape=[
            shape((length, width), f32),
            shape((length, width), f32),
            shape((2, 2, high, inner // 2), f32),
            shape(reducer.shape[1:], f32),
            shape(narrower.shape, f32),
            shape(projector.shape, f32),
            shape(collector.shape, f32),
            shape((2, length), f32),
            shape(widener.shape, f32),
            shape(norm_gains.shape, f32),
        ],
        in_specs=spaces("v" * 6, "a" * 11),
        out_specs=spaces("a" * 7, "vvv"),
        scratch_shapes=[
            VMEM((2, 2, high, inner // 2), f32),
            VMEM(reducer.shape[1:], f32),
            VMEM(narrower.shape, f32),
            VMEM((length, width), f32),
            VMEM((length, width), f32),
            VMEM((4, share, width), f32),
            VMEM((length, width), bf16),
            VMEM((length, width), f32),
            VMEM((4, width, width), bf16),
            VMEM((5, length, width), bf16),
            VMEM((HEAD_COUNT, length, length), f32),
            VMEM((members, 8, length), f32),
            VMEM((members, length, width), bf16),
            VMEM((members, length, width), bf16),
            VMEM((chunks, 2, width, piece), bf16),
            VMEM((chunks, piece, width), bf16),
            VMEM((chunks, 2, steps, high, piece), bf16),
            VMEM((chunks, 2, steps, low // 2, width), bf16),
            VMEM((chunks - 1, 2, high, piece), f32),
            VMEM((4, length, width), bf16),
            VMEM((4, width, width), bf16),
            VMEM((2, width, width), bf16),
            VMEM((width, width), bf16),
            VMEM((width, width), bf16),
            VMEM((width, width), bf16),
            VMEM((2, steps, high // 2, width), bf16),
            VMEM((4, share, width), f32),
            VMEM((members, 2, share, piece), f32),
            VMEM((members, 2, share, piece), f32),
            VMEM((8, width), f32),
            VMEM((members, 8, width), f32),
            VMEM((groups, 8, width), f32),
            pltpu.SemaphoreType.DMA((count,)),
            pltpu.SemaphoreType.DMA((count,)),
            pltpu.SemaphoreType.DMA((4 * groups + 32,)),
        ],
        compiler_params=pltpu.CompilerParams(
            collective_id=1, has_side_effects=True, vmem_limit_bytes=LIMIT
        ),
    )(
        tokens[0],
        expert_routes[0].T,
        gains_full,
        cosines,
        sines,
        gate_parts,
        result_parts,
        back_parts,
        wide_grads,
        down_grads,
        wide_first,
        down_first,
        grads_all,
        middle,
        attend_full,
        saved,
        soft,
    )
    updated = update_all(
        (0.1, projector, projector_mean, projector_square, project_sum),
        (0.3, collector, collector_first_moment, collector_second_moment, collect_sum),
        (0.07, widener, widener_mean, widener_square, widen_sum),
        (0.045, narrower, narrower_mean, narrower_square, narrow_sum),
        (0.2, norm_gains, gains_mean, gains_square, gains_sum),
        (0.07, expander[0], expander_mean[0], expander_square[0], expand_sum),
        (0.045, reducer[0], reducer_mean[0], reducer_square[0], reduce_sum),
        passed=(output, input_grad),
    )
    return (
        updated[0][None],
        updated[1][None],
        gate_grad.T[None],
        *updated[2:17],
        *(found[None] for found in updated[17:]),
    )


def fits(mesh):
    groups, members = mesh.shape["grp"], mesh.shape["exp"]
    share = 64 * HEAD_COUNT // (groups * members)
    return members == 4 and groups % 2 == 0 and share % 8 == 0 and share * members // 2 % 16 == 0


def solution(mesh):
    placed = (
        P(("grp", "exp"), None, None),
        P("grp"),
        P("grp"),
        P(("grp", "exp"), None, None),
        P(("grp", "exp"), None, None),
        P(("grp", "exp"), None, None),
        P(("grp", "exp"), None, None),
        P(None, ("grp", "exp"), None),
        P(None, ("grp", "exp"), None),
        P(None, ("grp", "exp"), None),
        P(("grp", "exp"), None),
        P(("grp", "exp"), None),
        P(("grp", "exp"), None),
        P(None, ("grp", "exp"), None),
        P(None, ("grp", "exp"), None),
        P(None, ("grp", "exp"), None),
        P(("grp", "exp"), None),
        P(("grp", "exp"), None),
        P(("grp", "exp"), None),
        P(None, ("grp", "exp")),
        P(None, ("grp", "exp")),
        P(None, ("grp", "exp")),
        P("exp", None, "grp", None),
        P("exp", None, "grp", None),
        P("exp", None, "grp", None),
        P("exp", "grp", None),
        P("exp", "grp", None),
        P("exp", "grp", None),
    )
    return jax.shard_map(
        local if fits(mesh) else local_plain,
        mesh=mesh,
        in_specs=placed,
        out_specs=(
            P(("grp", "exp"), None, None),
            P(("grp", "exp"), None, None),
            P(("grp", "exp"), None, None),
            P(None, ("grp", "exp"), None),
            P(None, ("grp", "exp"), None),
            P(None, ("grp", "exp"), None),
            P(("grp", "exp"), None),
            P(("grp", "exp"), None),
            P(("grp", "exp"), None),
            P(None, ("grp", "exp"), None),
            P(None, ("grp", "exp"), None),
            P(None, ("grp", "exp"), None),
            P(("grp", "exp"), None),
            P(("grp", "exp"), None),
            P(("grp", "exp"), None),
            P(None, ("grp", "exp")),
            P(None, ("grp", "exp")),
            P(None, ("grp", "exp")),
            P("exp", None, "grp", None),
            P("exp", None, "grp", None),
            P("exp", None, "grp", None),
            P("exp", "grp", None),
            P("exp", "grp", None),
            P("exp", "grp", None),
        ),
        check_vma=False,
    )
```

```python
import functools

import jax
import jax.numpy as jnp
import numpy as np
from jax import lax
from jax.experimental import pallas as pl
from jax.experimental.pallas import tpu as pltpu
from jax.sharding import PartitionSpec as P

HEAD_COUNT = 12
HEAD_FEATURES = 64
STEP = 5


def rms_factor(values):
    return lax.rsqrt(jnp.mean(values * values, axis=-1, keepdims=True) + 1e-06)


def rms_back(values, factor, upstream):
    return factor * (
        upstream - values * factor * factor * jnp.mean(upstream * values, axis=-1, keepdims=True)
    )


def rotary(length):
    positions = jnp.arange(length, dtype=jnp.int32).astype(jnp.float32)
    half = HEAD_FEATURES // 2
    freqs = jnp.exp(
        -jnp.log(10000.0) * jnp.arange(half, dtype=jnp.int32).astype(jnp.float32) / half
    )
    angles = positions[:, None] * freqs[None, :]
    return (jnp.cos(angles)[:, None, :], jnp.sin(angles)[:, None, :])


def rotate(values, cosines, sines):
    half = values.shape[-1] // 2
    first = values[..., :half]
    second = values[..., half:]
    return jnp.concatenate(
        [first * cosines - second * sines, second * cosines + first * sines], axis=-1
    )


def rotate_back(values, cosines, sines):
    half = values.shape[-1] // 2
    first = values[..., :half]
    second = values[..., half:]
    return jnp.concatenate(
        [first * cosines + second * sines, second * cosines - first * sines], axis=-1
    )


def silu_slope(values):
    sigmoid_of = jax.nn.sigmoid(values)
    return sigmoid_of * (1.0 + values * (1.0 - sigmoid_of))


def matmul(left, right):
    return jnp.dot(left, right, preferred_element_type=jnp.float32)


def outer_sum(left, right):
    return jnp.einsum("ld,lf->df", left, right, preferred_element_type=jnp.float32)


def adamw_update(weight, moment, variance, gradient, rate):
    moment_new = 0.5 * moment + 0.5 * gradient
    variance_new = 0.5 * variance + 0.5 * gradient * gradient
    correct = 1.0 - 0.5**STEP
    stepped = moment_new / correct / (jnp.sqrt(variance_new / correct) + 1e-08) + 0.1 * weight
    return (moment_new, variance_new, weight - rate * stepped)


def local_plain(
    tokens,
    seq_lengths,
    deal_order,
    expert_routes,
    capacity_slots,
    gate_weights,
    cotangent,
    projector,
    projector_mean,
    projector_square,
    collector,
    collector_first_moment,
    collector_second_moment,
    widener,
    widener_mean,
    widener_square,
    narrower,
    narrower_mean,
    narrower_square,
    norm_gains,
    gains_mean,
    gains_square,
    expander,
    expander_mean,
    expander_square,
    reducer,
    reducer_mean,
    reducer_square,
):
    members = lax.axis_size("exp")
    member = lax.axis_index("exp")
    length_seq = tokens.shape[1]
    width = tokens.shape[2]
    local_experts = expander.shape[0]
    experts_all = local_experts * members
    capacity = 3 * length_seq // experts_all
    member_ids = jnp.arange(members, dtype=jnp.int32)
    source = deal_order[member]
    home_slot = jnp.sum(jnp.where(deal_order == member, member_ids, 0))
    seq_length = seq_lengths[source]
    piece = lax.all_gather(tokens, "exp", axis=0, tiled=True)
    chosen = jnp.arange(piece.shape[0], dtype=jnp.int32) == source
    dealt = jnp.sum(
        jnp.where(chosen[:, None, None], piece, jnp.zeros_like(piece)), axis=0, keepdims=True
    )
    residual_flow = dealt[0].astype(jnp.float32)
    project_full, collect_full, widen_full, narrow_full, gains_full = (
        lax.all_gather(projector.astype(jnp.bfloat16), ("grp", "exp"), axis=1, tiled=True),
        lax.all_gather(collector.astype(jnp.bfloat16), ("grp", "exp"), axis=0, tiled=True),
        lax.all_gather(widener.astype(jnp.bfloat16), ("grp", "exp"), axis=1, tiled=True),
        lax.all_gather(narrower.astype(jnp.bfloat16), ("grp", "exp"), axis=0, tiled=True),
        lax.all_gather(norm_gains.astype(jnp.bfloat16), ("grp", "exp"), axis=1, tiled=True),
    )
    expand_full, reduce_full = (
        lax.all_gather(expander.astype(jnp.bfloat16), "grp", axis=2, tiled=True),
        lax.all_gather(reducer.astype(jnp.bfloat16), "grp", axis=1, tiled=True),
    )
    gains_used = gains_full.astype(jnp.float32)
    cosines, sines = rotary(length_seq)
    scale_one = rms_factor(residual_flow)
    normed_one = residual_flow * scale_one
    first_input = (normed_one * gains_used[0]).astype(jnp.bfloat16)
    query_raw = matmul(first_input, project_full[0]).reshape(length_seq, HEAD_COUNT, HEAD_FEATURES)
    key_raw = matmul(first_input, project_full[1]).reshape(length_seq, HEAD_COUNT, HEAD_FEATURES)
    value_raw = matmul(first_input, project_full[2]).reshape(length_seq, HEAD_COUNT, HEAD_FEATURES)
    query_rot = rotate(query_raw, cosines, sines).astype(jnp.bfloat16)
    key_rot = rotate(key_raw, cosines, sines).astype(jnp.bfloat16)
    value_low = value_raw.astype(jnp.bfloat16)
    rows_at = jnp.arange(length_seq, dtype=jnp.int32)[:, None]
    cols_at = jnp.arange(length_seq, dtype=jnp.int32)[None, :]
    allowed = ((cols_at <= rows_at) & (cols_at < seq_length))[None]
    scores = (
        jnp.einsum("qhd,khd->hqk", query_rot, key_rot, preferred_element_type=jnp.float32) * 0.125
    )
    masked = jnp.where(allowed, scores, -1e30)
    top = jnp.max(masked, axis=-1, keepdims=True)
    expo = jnp.exp(masked - top)
    total = jnp.sum(expo, axis=-1, keepdims=True)
    soft = expo / total
    logsum = top + jnp.log(total)
    mixed_output = (
        jnp.einsum(
            "hqk,khd->qhd", soft.astype(jnp.bfloat16), value_low, preferred_element_type=jnp.float32
        )
        .reshape(length_seq, width)
        .astype(jnp.bfloat16)
    )
    middle_state = residual_flow + matmul(mixed_output, collect_full)
    scale_two = rms_factor(middle_state)
    normed_two = middle_state * scale_two
    second_input = (normed_two * gains_used[1]).astype(jnp.bfloat16)
    gating_scores = matmul(second_input, widen_full[0])
    upward_rows = matmul(second_input, widen_full[1])
    hidden_state = (jax.nn.silu(gating_scores) * upward_rows).astype(jnp.bfloat16)
    dense_branch = matmul(hidden_state, narrow_full)
    flat = (expert_routes[0] * capacity + capacity_slots[0]).reshape(-1)
    spread = jnp.repeat(second_input, 2, axis=0)
    dispatch = jnp.zeros((experts_all * capacity, width), jnp.bfloat16).at[flat].set(spread)
    dispatch = dispatch.reshape(experts_all, capacity, width)
    rows = lax.all_to_all(dispatch, "exp", split_axis=0, concat_axis=0, tiled=True)
    count = rows.shape[1]
    grouped = rows.reshape(members, local_experts, count, width)
    gate_pre = jnp.einsum(
        "sekd,edf->sekf", grouped, expand_full[:, 0], preferred_element_type=jnp.float32
    )
    up_pre = jnp.einsum(
        "sekd,edf->sekf", grouped, expand_full[:, 1], preferred_element_type=jnp.float32
    )
    hidden_rows = (jax.nn.silu(gate_pre) * up_pre).astype(jnp.bfloat16)
    result = jnp.einsum(
        "sekf,efd->sekd", hidden_rows, reduce_full, preferred_element_type=jnp.float32
    )
    result = result.astype(jnp.bfloat16).reshape(members * local_experts, count, width)
    returned_rows = lax.all_to_all(result, "exp", split_axis=0, concat_axis=0, tiled=True)
    outcome = (
        returned_rows,
        rows,
        gate_pre.reshape(members * local_experts, count, -1),
        up_pre.reshape(members * local_experts, count, -1),
    )
    returned, received, gate_kept, up_kept = outcome
    picked = (
        returned.reshape(experts_all * capacity, width)[flat]
        .reshape(length_seq, 2, width)
        .astype(jnp.float32)
    )
    gate_local = gate_weights[0]
    mixture = jnp.sum(gate_local[..., None] * picked, axis=1)
    layer_output = middle_state + dense_branch + mixture
    valid = (jnp.arange(length_seq, dtype=jnp.int32) < seq_length).astype(jnp.float32)
    grad_out = cotangent[0] * valid[:, None]
    grad_low = grad_out.astype(jnp.bfloat16)
    narrow_grad = outer_sum(hidden_state, grad_low)
    hidden_grad = jnp.einsum("ld,fd->lf", grad_low, narrow_full, preferred_element_type=jnp.float32)
    gating_grad = (hidden_grad * upward_rows * silu_slope(gating_scores)).astype(jnp.bfloat16)
    upward_grad = (hidden_grad * jax.nn.silu(gating_scores)).astype(jnp.bfloat16)
    widen_grad = jnp.stack(
        [outer_sum(second_input, gating_grad), outer_sum(second_input, upward_grad)]
    )
    second_grad = jnp.einsum(
        "lf,df->ld", gating_grad, widen_full[0], preferred_element_type=jnp.float32
    ) + jnp.einsum("lf,df->ld", upward_grad, widen_full[1], preferred_element_type=jnp.float32)
    gate_grad_local = jnp.sum(grad_out[:, None, :] * picked, axis=-1)
    result_grad = (
        (gate_local[..., None] * grad_out[:, None, :])
        .astype(jnp.bfloat16)
        .reshape(2 * length_seq, width)
    )
    grad_send = jnp.zeros((experts_all * capacity, width), jnp.bfloat16).at[flat].set(result_grad)
    grad_recv = lax.all_to_all(
        grad_send.reshape(experts_all, capacity, width),
        "exp",
        split_axis=0,
        concat_axis=0,
        tiled=True,
    )
    grad_group = grad_recv.reshape(members, local_experts, capacity, width)
    rows_group = received.reshape(members, local_experts, capacity, width)
    gate_pre = gate_kept.reshape(members, local_experts, capacity, -1)
    up_pre = up_kept.reshape(members, local_experts, capacity, -1)
    hidden_rows = (jax.nn.silu(gate_pre) * up_pre).astype(jnp.bfloat16)
    reduce_grad = jnp.einsum(
        "sekf,sekd->efd", hidden_rows, grad_group, preferred_element_type=jnp.float32
    )
    hidden_rows_grad = jnp.einsum(
        "sekd,efd->sekf", grad_group, reduce_full, preferred_element_type=jnp.float32
    )
    gate_rows_grad = (hidden_rows_grad * up_pre * silu_slope(gate_pre)).astype(jnp.bfloat16)
    up_rows_grad = (hidden_rows_grad * jax.nn.silu(gate_pre)).astype(jnp.bfloat16)
    expand_grad = jnp.stack(
        [
            jnp.einsum(
                "sekd,sekf->edf", rows_group, gate_rows_grad, preferred_element_type=jnp.float32
            ),
            jnp.einsum(
                "sekd,sekf->edf", rows_group, up_rows_grad, preferred_element_type=jnp.float32
            ),
        ],
        axis=1,
    )
    row_grads = jnp.einsum(
        "sekf,edf->sekd", gate_rows_grad, expand_full[:, 0], preferred_element_type=jnp.float32
    ) + jnp.einsum(
        "sekf,edf->sekd", up_rows_grad, expand_full[:, 1], preferred_element_type=jnp.float32
    )
    row_grads = row_grads.astype(jnp.bfloat16).reshape(experts_all, capacity, width)
    came_back = lax.all_to_all(row_grads, "exp", split_axis=0, concat_axis=0, tiled=True).reshape(
        experts_all * capacity, width
    )
    second_grad = second_grad + jnp.sum(
        came_back[flat].reshape(length_seq, 2, width).astype(jnp.float32), axis=1
    )
    gains_grad_two = jnp.sum(second_grad * normed_two, axis=0)
    middle_grad = grad_out + rms_back(middle_state, scale_two, second_grad * gains_used[1])
    middle_low = middle_grad.astype(jnp.bfloat16)
    collect_grad = outer_sum(mixed_output, middle_low)
    mixed_grad = jnp.einsum(
        "ld,ed->le", middle_low, collect_full, preferred_element_type=jnp.float32
    )
    mixed_grad = mixed_grad.astype(jnp.bfloat16).reshape(length_seq, HEAD_COUNT, HEAD_FEATURES)
    scores_again = (
        jnp.einsum("qhd,khd->hqk", query_rot, key_rot, preferred_element_type=jnp.float32) * 0.125
    )
    soft_again = jnp.where(allowed, jnp.exp(scores_again - logsum), 0.0)
    value_grad = jnp.einsum(
        "hqk,qhd->khd",
        soft_again.astype(jnp.bfloat16),
        mixed_grad,
        preferred_element_type=jnp.float32,
    )
    soft_grad = jnp.einsum(
        "qhd,khd->hqk", mixed_grad, value_low, preferred_element_type=jnp.float32
    )
    score_grad = (
        soft_again * (soft_grad - jnp.sum(soft_again * soft_grad, axis=-1, keepdims=True))
    ).astype(jnp.bfloat16)
    query_grad = (
        jnp.einsum("hqk,khd->qhd", score_grad, key_rot, preferred_element_type=jnp.float32) * 0.125
    )
    key_grad = (
        jnp.einsum("hqk,qhd->khd", score_grad, query_rot, preferred_element_type=jnp.float32)
        * 0.125
    )
    query_back = (
        rotate_back(query_grad, cosines, sines).reshape(length_seq, width).astype(jnp.bfloat16)
    )
    key_back = rotate_back(key_grad, cosines, sines).reshape(length_seq, width).astype(jnp.bfloat16)
    value_back = value_grad.reshape(length_seq, width).astype(jnp.bfloat16)
    project_grad = jnp.stack(
        [
            outer_sum(first_input, query_back),
            outer_sum(first_input, key_back),
            outer_sum(first_input, value_back),
        ]
    )
    first_grad = (
        jnp.einsum("le,de->ld", query_back, project_full[0], preferred_element_type=jnp.float32)
        + jnp.einsum("le,de->ld", key_back, project_full[1], preferred_element_type=jnp.float32)
        + jnp.einsum("le,de->ld", value_back, project_full[2], preferred_element_type=jnp.float32)
    )
    gains_grad_one = jnp.sum(first_grad * normed_one, axis=0)
    stream_grad = middle_grad + rms_back(residual_flow, scale_one, first_grad * gains_used[0])
    gains_grad = jnp.stack([gains_grad_one, gains_grad_two])
    project_part, collect_part, widen_part, narrow_part, gains_part = (
        lax.psum_scatter(project_grad, ("grp", "exp"), scatter_dimension=1, tiled=True),
        lax.psum_scatter(collect_grad, ("grp", "exp"), scatter_dimension=0, tiled=True),
        lax.psum_scatter(widen_grad, ("grp", "exp"), scatter_dimension=1, tiled=True),
        lax.psum_scatter(narrow_grad, ("grp", "exp"), scatter_dimension=0, tiled=True),
        lax.psum_scatter(gains_grad, ("grp", "exp"), scatter_dimension=1, tiled=True),
    )
    expand_part, reduce_part = (
        lax.psum_scatter(
            expand_grad.astype(jnp.bfloat16), "grp", scatter_dimension=2, tiled=True
        ).astype(jnp.float32),
        lax.psum_scatter(
            reduce_grad.astype(jnp.bfloat16), "grp", scatter_dimension=1, tiled=True
        ).astype(jnp.float32),
    )
    empty = jnp.zeros((1, length_seq, width), jnp.float32)
    pieces = (
        lax.all_gather(layer_output[None].astype(jnp.bfloat16), "exp", axis=0, tiled=True).astype(
            jnp.float32
        ),
        lax.all_gather(stream_grad[None].astype(jnp.bfloat16), "exp", axis=0, tiled=True).astype(
            jnp.float32
        ),
    )
    chosen = (jnp.arange(pieces[0].shape[0], dtype=jnp.int32) == home_slot)[:, None, None]
    homed_output = empty + jnp.sum(jnp.where(chosen, pieces[0], 0.0), axis=0, keepdims=True)
    homed_grad = empty + jnp.sum(jnp.where(chosen, pieces[1], 0.0), axis=0, keepdims=True)
    project_new = adamw_update(projector, projector_mean, projector_square, project_part, 0.1)
    collect_new = adamw_update(
        collector, collector_first_moment, collector_second_moment, collect_part, 0.3
    )
    widening_updated = adamw_update(widener, widener_mean, widener_square, widen_part, 0.07)
    narrowing_updated = adamw_update(narrower, narrower_mean, narrower_square, narrow_part, 0.045)
    gains_updated = adamw_update(norm_gains, gains_mean, gains_square, gains_part, 0.2)
    expansion_updated = adamw_update(expander, expander_mean, expander_square, expand_part, 0.07)
    reduction_updated = adamw_update(reducer, reducer_mean, reducer_square, reduce_part, 0.045)
    return (
        homed_output,
        homed_grad,
        gate_grad_local[None],
        project_new[0],
        project_new[1],
        project_new[2],
        collect_new[0],
        collect_new[1],
        collect_new[2],
        widening_updated[0],
        widening_updated[1],
        widening_updated[2],
        narrowing_updated[0],
        narrowing_updated[1],
        narrowing_updated[2],
        gains_updated[0],
        gains_updated[1],
        gains_updated[2],
        expansion_updated[0],
        expansion_updated[1],
        expansion_updated[2],
        reduction_updated[0],
        reduction_updated[1],
        reduction_updated[2],
    )


MESH = pl.DeviceIdType.MESH
VMEM = pltpu.VMEM
LIMIT = 60 * 1024 * 1024


def ring_place(index, groups):
    row, side = lax.div(index, 2), lax.rem(index, 2)
    return (1 - side) * row + side * (groups - 1 - row)


def ring_member(place, groups):
    side = lax.div(place, groups // 2)
    return 2 * ((1 - side) * place + side * (groups - 1 - place)) + side


def remote(source, target, sends, arrivals, at, device):
    return pltpu.make_async_remote_copy(
        src_ref=source,
        dst_ref=target,
        send_sem=sends.at[at],
        recv_sem=arrivals.at[at],
        device_id=device,
        device_id_type=MESH,
    )


class Links:
    def __init__(self, sends, arrivals):
        self.sends, self.arrivals, self.count, self.started = sends, arrivals, 0, []

    def copy(self, source, target, device):
        made = remote(source, target, self.sends, self.arrivals, self.count, device)
        self.count += 1
        made.start()
        self.started.append(made)
        return made

    def finish(self):
        for made in self.started:
            made.wait_send()


class Places:
    def __init__(self, groups, members):
        self.groups, self.members = groups, members
        self.group = lax.axis_index("grp")
        self.member = lax.axis_index("exp")
        self.place = ring_place(self.group, groups)
        self.next = {"grp": self.owner(1)}
        self.back = {"grp": self.owner(-1)}
        half = members // 2
        self.far = lax.rem(self.member + half, members)
        self.near = self.member + 1 - 2 * lax.rem(self.member, 2)
        self.cross = lax.rem(self.near + half, members)
        self.peers = [lax.rem(self.member + step, members) for step in range(1, members)]

    def owner(self, offset):
        place = lax.rem(self.place + offset + 2 * self.groups, self.groups)
        return ring_member(place, self.groups)

    def enter(self):
        barrier = pltpu.get_barrier_semaphore()
        partners = [self.next, self.back] + [{"exp": peer} for peer in self.peers]
        for partner in partners:
            pl.semaphore_signal(barrier, inc=1, device_id=partner, device_id_type=MESH)
        pl.semaphore_wait(barrier, len(partners))


def rows(start, count, align=16):
    return pl.ds(pl.multiple_of(start, align), count)


def first_half(shape):
    return lax.rem(lax.broadcasted_iota(jnp.int32, shape, len(shape) - 1), 128) < 64


def turned(values):
    lanes = lax.broadcasted_iota(jnp.int32, values.shape, 1)
    return jnp.where(
        lax.rem(lanes, HEAD_FEATURES) < HEAD_FEATURES // 2,
        pltpu.roll(values, 128 - HEAD_FEATURES // 2, 1),
        pltpu.roll(values, HEAD_FEATURES // 2, 1),
    )


def nt(left, right):
    return lax.dot_general(
        left, right, (((1,), (1,)), ((), ())), preferred_element_type=jnp.float32
    )


def tn(left, right):
    return lax.dot_general(
        left, right, (((0,), (0,)), ((), ())), preferred_element_type=jnp.float32
    )


def sigmoid(values):
    return 1.0 / (1.0 + jnp.exp(-values))


def same(length):
    shape = (length, length)
    return lax.broadcasted_iota(jnp.int32, shape, 0) == lax.broadcasted_iota(jnp.int32, shape, 1)


def upright(line):
    return jnp.sum(jnp.where(same(line.shape[1]), line, 0.0), axis=1, keepdims=True)


def lying(column):
    return jnp.sum(jnp.where(same(column.shape[0]), column, 0.0), axis=0, keepdims=True)


def slot_of(deal_ref, member):
    for _ in range(11):
        member = deal_ref[member]
    return member


def dealt_lanes(values, piece, pieces):
    low_lanes = lax.broadcasted_iota(jnp.int32, (values.shape[0], 128), 1) < 64
    found = []
    span = 64 * pieces
    for start in range(0, values.shape[1], 2 * span):
        start = start + piece // 2 * 128
        one, two = values[:, start : start + 128], values[:, start + span : start + span + 128]
        if piece % 2:
            one = pltpu.roll(one, 64, 1)
        else:
            two = pltpu.roll(two, 64, 1)
        found.append(jnp.where(low_lanes, one, two))
    return jnp.concatenate(found, axis=1)


def joined_lanes(even, odd):
    low_lanes = lax.broadcasted_iota(jnp.int32, (even.shape[0], 128), 1) < 64
    found = []
    for start in range(0, even.shape[1], 128):
        one, two = even[:, start : start + 128], odd[:, start : start + 128]
        found.append(jnp.where(low_lanes, one, pltpu.roll(two, 64, 1)))
        found.append(jnp.where(low_lanes, pltpu.roll(one, 64, 1), two))
    return found


def gather_kernel(
    groups,
    members,
    length_ref,
    deal_ref,
    tokens,
    cotangent_in,
    routes,
    places,
    gates,
    norm_gains,
    projector,
    collector,
    widener_in,
    narrower_in,
    expander_in,
    reducer_in,
    cos_ref,
    sin_ref,
    wide_grads,
    down_grads,
    wide_first,
    down_first,
    attend_out,
    grads_out,
    saved_out,
    middle_out,
    soft_out,
    result_out,
    back_out,
    gains_full,
    gate_ref,
    cotangent,
    widener,
    narrower,
    expander,
    reducer,
    result_ref,
    back_ref,
    grads_home,
    attend_full,
    grads_all,
    saved,
    middle_ref,
    soft_ref,
    second_all,
    meta_send,
    meta_all,
    attend_send,
    attend_recv,
    widen_send,
    widen_recv,
    gains,
    gain_recv,
    gain_ring,
    wide_full,
    down_full,
    wide_own,
    down_own,
    inputs_ref,
    inputs_turned,
    dense_out,
    dense_back,
    rows_in,
    rows_turned,
    rows_grad,
    rows_out,
    rows_back,
    sends,
    arrivals,
    ring_sends,
    ring_arrivals,
    first_sends,
    first_arrivals,
    local_sems,
):
    at = Places(groups, members)
    links = Links(sends, arrivals)
    chunks, low = down_own.shape[:2]
    loads = {}
    for name, source, target in (
        ("expander", expander_in, expander),
        ("reducer", reducer_in, reducer),
        ("widener", widener_in, widener),
        ("narrower", narrower_in, narrower),
        ("cotangent", cotangent_in, cotangent),
    ):
        made = pltpu.make_async_copy(source, target, local_sems.at[2 * chunks + len(loads)])
        made.start(priority=1)
        loads[name] = made
    at.enter()
    me, steps = at.member, groups - 1
    share, width = projector.shape[1:]
    block = share * members
    length = tokens.shape[0]
    capacity = rows_in.shape[0] // members

    def ring_copy(chunk, step, side, piece):
        owner = at.owner(-step if side == 0 else step)
        if piece == 0:
            spot = wide_full.at[chunk, side, rows(owner * block, block), :]
            origin = wide_own.at[chunk, side]
        else:
            spot = down_full.at[chunk, rows(owner * low + side * (low // 2), low // 2), :]
            origin = down_own.at[chunk, pl.ds(side * (low // 2), low // 2), :]
        place = (chunk * steps + step) * 4 + side * 2 + piece
        return remote(
            spot if step else origin,
            spot,
            ring_sends,
            ring_arrivals,
            place,
            (at.next, at.back)[side],
        )

    def ring_step(chunk, step):
        for piece in range(2):
            for side in range(2):
                if step:
                    ring_copy(chunk, step - 1, side, piece).wait_recv()
                if step < steps:
                    ring_copy(chunk, step, side, piece).start()

    def tick(count):
        for chunk in range(chunks):
            if 0 <= count - 2 * chunk <= steps:
                ring_step(chunk, count - 2 * chunk)

    attend_send[0:3] = projector[...]
    attend_send[3] = collector[...]
    gains[...] = jnp.zeros_like(gains)
    gains[0:2, 0 : norm_gains.shape[1]] = norm_gains[...]
    gains[...] = pltpu.roll(gains[...], (at.group * members + me) * norm_gains.shape[1], 1)
    first_moves = [
        [
            links.copy(attend_send.at[peer], attend_recv.at[me], {"exp": peer}),
            links.copy(gains, gain_recv.at[me], {"exp": peer}),
        ]
        for peer in at.peers
    ]
    gain_recv[me] = gains[...]
    attend_recv[me] = attend_send[me]
    loads["widener"].wait()
    for matrix in range(2):
        for member in range(members):
            widen_send[member, matrix] = dealt_lanes(widener[matrix], member, members)
    widen_moves = [
        links.copy(widen_send.at[peer], widen_recv.at[me], {"exp": peer}) for peer in at.peers
    ]
    widen_recv[me] = widen_send[me]

    def stage(chunk):
        if chunk == 1:
            for matrix in range(2):
                wide_own[1, matrix] = jnp.concatenate(
                    [widen_recv[member, matrix] for member in range(members)], axis=0
                ).astype(jnp.bfloat16)
            down_own[1] = narrower[...].astype(jnp.bfloat16)
        else:
            index = max(chunk - 1, 0)
            for matrix in range(2):
                wide_own[chunk, matrix] = dealt_lanes(
                    expander[matrix], index, chunks - 1
                ).astype(jnp.bfloat16)
            down_own[chunk] = reducer[index * low : (index + 1) * low, :].astype(jnp.bfloat16)
        for side in range(2):
            wide_full[chunk, side, rows(at.group * block, block), :] = wide_own[chunk, side]
        down_full[chunk, rows(at.group * low, low), :] = down_own[chunk]

    loads["expander"].wait()
    loads["reducer"].wait()
    stage(0)
    tick(0)
    for moves in first_moves:
        for move in moves:
            move.wait_recv()
    attend_full[me, rows(at.group * block, block), :] = (
        attend_recv[...].reshape(block, width).astype(jnp.bfloat16)
    )
    total_gain = gain_recv[0]
    for member in range(1, members):
        total_gain = total_gain + gain_recv[member]
    gain_ring[at.group] = total_gain

    reach = (groups // 2, groups - 1 - groups // 2)

    def unit(owner, matrix):
        return attend_full.at[matrix, rows(owner * block, block), :]

    def across(owner):
        spot = unit(owner, me)
        return (links.copy(spot, spot, {"exp": at.far}), links.copy(spot, spot, {"exp": at.near}))

    crossed, passed, owners_seen = [], [], []

    def onward():
        spot = unit(owners_seen[len(passed)], at.far)
        crossed[len(passed)][0].wait_recv()
        passed.append(links.copy(spot, spot, {"exp": at.near}))

    ring = {}
    for step in range(reach[0] + 1):
        fresh = []
        for side, target in enumerate((at.next, at.back)):
            if step > reach[side]:
                continue
            owner = at.owner(-step if side == 0 else step)
            if step:
                for move in ring[step - 1, side]:
                    move.wait_recv()
            if step < reach[side]:
                spot, line = unit(owner, me), gain_ring.at[owner]
                ring[step, side] = (
                    links.copy(spot, spot, target),
                    links.copy(line, line, target),
                )
            if step or side == 0:
                fresh.append(owner)
        waiting = len(owners_seen) - len(passed)
        for owner in fresh:
            owners_seen.append(owner)
            crossed.append(across(owner))
        for _ in range(waiting):
            onward()
        if step == 1:
            for move in widen_moves:
                move.wait_recv()
            loads["narrower"].wait()
            for chunk in range(1, chunks):
                stage(chunk)
        if step:
            tick(step)
    outgoing = []

    def hand_out(source, target):
        made = pltpu.make_async_copy(
            source, target, local_sems.at[2 * chunks + len(loads) + len(outgoing)]
        )
        made.start(priority=1)
        outgoing.append(made)

    loads["cotangent"].wait()
    valid = lax.broadcasted_iota(jnp.int32, (length, 1), 0) < length_ref[deal_ref[me]]
    grads_all[me] = jnp.where(valid, cotangent[...], 0.0).astype(jnp.bfloat16)
    route = [routes[choice : choice + 1, :] for choice in range(2)]
    place = [places[choice : choice + 1, :].astype(jnp.float32) for choice in range(2)]
    meta_send[...] = jnp.zeros_like(meta_send)
    for member in range(members):
        named = [chosen == member for chosen in route]
        meta_send[member, 0:1, :] = jnp.where(
            named[0], place[0], jnp.where(named[1], place[1], -1.0)
        )
        meta_send[member, 1:2, :] = jnp.where(
            named[0], gates[0:1, :], jnp.where(named[1], gates[1:2, :], 0.0)
        )
    meta_all[me] = meta_send[me]
    grad_moves = [
        [
            links.copy(grads_all.at[me], grads_all.at[me], {"exp": peer}),
            links.copy(meta_send.at[peer], meta_all.at[me], {"exp": peer}),
        ]
        for peer in at.peers
    ]
    while len(passed) < groups:
        onward()
    total_gain = gain_ring[0]
    for group in range(1, groups):
        total_gain = total_gain + gain_ring[group]
    gains_full[...] = total_gain.astype(jnp.bfloat16).astype(jnp.float32)
    stream = tokens[...].astype(jnp.float32)
    first_input = (stream * rms_factor(stream) * gains_full[0:1, :]).astype(jnp.bfloat16)
    saved[4] = first_input
    for moves in crossed:
        moves[1].wait_recv()
    for move in passed:
        move.wait_recv()
    tick(5)
    hand_out(attend_full, attend_out)

    cosines, sines = cos_ref[...], sin_ref[...]
    for matrix in range(3):
        raw = matmul(first_input, attend_full[matrix])
        if matrix == 2:
            saved[2] = raw.astype(jnp.bfloat16)
        else:
            for start in range(0, width, 128):
                piece = raw[:, start : start + 128]
                saved[matrix, :, start : start + 128] = (
                    piece * cosines + turned(piece) * sines
                ).astype(jnp.bfloat16)
    tick(6)

    seq_length = length_ref[me]
    rows_at = lax.broadcasted_iota(jnp.int32, (length, length), 0)
    cols_at = lax.broadcasted_iota(jnp.int32, (length, length), 1)
    allowed = (cols_at <= rows_at) & (cols_at < seq_length)
    lower = first_half((length, 128))

    def heads(pair, carry):
        lanes = pl.ds(pl.multiple_of(pair * 128, 128), 128)
        query, key, value = saved[0, :, lanes], saved[1, :, lanes], saved[2, :, lanes]
        results = []
        for side in range(2):
            alone = jnp.where(lower == (side == 0), query, jnp.zeros_like(query))
            scores = jnp.where(allowed, nt(alone, key) * 0.125, -1e30)
            expo = jnp.exp(scores - jnp.max(scores, axis=-1, keepdims=True))
            soft = expo / jnp.sum(expo, axis=-1, keepdims=True)
            soft_ref[2 * pair + side] = soft
            results.append(matmul(soft.astype(jnp.bfloat16), value))
        saved[3, :, lanes] = jnp.where(lower, results[0], results[1]).astype(jnp.bfloat16)
        return carry

    lax.fori_loop(0, width // 128, heads, 0)
    hand_out(saved, saved_out)
    hand_out(soft_ref, soft_out)
    middle = tokens[...].astype(jnp.float32) + matmul(saved[3], attend_full[3])
    middle_ref[...] = middle
    hand_out(middle_ref, middle_out)
    second_all[me] = (middle * rms_factor(middle) * gains_full[1:2, :]).astype(jnp.bfloat16)
    second_moves = [
        links.copy(second_all.at[me], second_all.at[me], {"exp": peer}) for peer in at.peers
    ]
    for moves in grad_moves:
        for move in moves:
            move.wait_recv()
    grads_home[...] = grads_all[slot_of(deal_ref, me)]
    hand_out(grads_home, grads_out)
    tick(7)

    def hits(slot, by_row):
        line = meta_all[slot, 0:1, :]
        if by_row:
            names = lax.broadcasted_iota(jnp.int32, (capacity, length), 0).astype(jnp.float32)
            hit = names == line
        else:
            names = lax.broadcasted_iota(jnp.int32, (length, capacity), 1).astype(jnp.float32)
            hit = names == upright(line)
        return jnp.where(hit, 1.0, 0.0).astype(jnp.bfloat16)

    def spot_of(slot):
        return slice(slot * capacity, (slot + 1) * capacity)

    def here_of(slot):
        return slice(slot * length, (slot + 1) * length)

    for slot in range(members):
        pick = hits(slot, True)
        gate = jnp.sum(pick.astype(jnp.float32) * meta_all[slot, 1:2, :], axis=1, keepdims=True)
        rows_grad[spot_of(slot), :] = (matmul(pick, grads_all[slot]) * gate).astype(jnp.bfloat16)
    for move in second_moves:
        move.wait_recv()
    for slot in range(members):
        inputs_ref[here_of(slot), :] = second_all[deal_ref[slot]]
        rows_in[spot_of(slot), :] = matmul(hits(slot, True), inputs_ref[here_of(slot), :]).astype(
            jnp.bfloat16
        )
    inputs_turned[...] = inputs_ref[...].T
    rows_turned[...] = rows_in[...].T
    dense_out[...] = jnp.zeros_like(dense_out)
    dense_back[...] = jnp.zeros_like(dense_back)
    rows_out[...] = jnp.zeros_like(rows_out)
    rows_back[...] = jnp.zeros_like(rows_back)

    def branch(chunk, inputs, turned_inputs, outer, out, back):
        for step in range(steps):
            for side in range(2):
                for piece in range(2):
                    ring_copy(chunk, step, side, piece).wait_send()

        def part(index, carry):
            lanes = pl.ds(pl.multiple_of(index * 256, 256), 256)
            gate = matmul(inputs[...], wide_full[chunk, 0, :, lanes])
            up = matmul(inputs[...], wide_full[chunk, 1, :, lanes])
            rise = sigmoid(gate)
            smooth = gate * rise
            hidden = (smooth * up).astype(jnp.bfloat16)
            hidden_grad = nt(outer[...], down_full[chunk, lanes, :])
            gate_grad = (hidden_grad * up * (rise * (1.0 + gate * (1.0 - rise)))).astype(
                jnp.bfloat16
            )
            up_grad = (hidden_grad * smooth).astype(jnp.bfloat16)
            out[...] += matmul(hidden, down_full[chunk, lanes, :])
            back[...] += nt(gate_grad, wide_full[chunk, 0, :, lanes]) + nt(
                up_grad, wide_full[chunk, 1, :, lanes]
            )
            down_full[chunk, lanes, :] = tn(hidden, outer[...]).astype(jnp.bfloat16)
            wide_full[chunk, 0, :, lanes] = matmul(turned_inputs[...], gate_grad).astype(
                jnp.bfloat16
            )
            wide_full[chunk, 1, :, lanes] = matmul(turned_inputs[...], up_grad).astype(
                jnp.bfloat16
            )

            @pl.when(index == 0)
            def _():
                for ahead in range(groups // 2):
                    @pl.when(chunk + 1 + ahead < chunks)
                    def _():
                        ring_step(chunk + 1 + ahead, steps - 1 - 2 * ahead)

            return carry

        lax.fori_loop(0, down_full.shape[1] // 256, part, 0)
        kept(chunk, 0).start(priority=1)
        kept(chunk, 1).start(priority=1)

    def kept(chunk, piece):
        source, target = ((wide_full, wide_grads), (down_full, down_grads))[piece]
        return pltpu.make_async_copy(
            source.at[chunk], target.at[chunk], local_sems.at[2 * chunk + piece]
        )

    outer_all = grads_all.reshape(members * length, width)
    flat = (members * length, width)
    dense = (
        inputs_ref,
        inputs_turned,
        outer_all,
        dense_out.reshape(flat),
        dense_back.reshape(flat),
    )

    def first_sum(chunk, side, piece):
        owner = at.owner(-1 if side == 0 else 1)
        if piece == 0:
            spot = wide_full.at[chunk, side, rows(owner * block, block), :]
        else:
            spot = down_full.at[chunk, rows(owner * low + side * (low // 2), low // 2), :]
        return remote(
            spot,
            (wide_first, down_first)[piece].at[chunk, side],
            first_sends,
            first_arrivals,
            chunk * 4 + side * 2 + piece,
            (at.next, at.back)[side],
        )

    early = chunks - 2

    def start_sums(chunk):
        for piece in range(2):
            for side in range(2):
                first_sum(chunk, side, piece).start()

    def next_chunk(chunk, carry):
        for ahead in range(groups // 2):
            @pl.when((chunk > 0) & (chunk + ahead < chunks))
            def _():
                ring_step(chunk + ahead, steps - 2 * ahead)

        @pl.when(chunk == chunks - 1)
        def _():
            for before in range(early):
                start_sums(before)

        @pl.when(chunk == 1)
        def _():
            branch(chunk, *dense)

        @pl.when(chunk != 1)
        def _():
            branch(chunk, rows_in, rows_turned, rows_grad, rows_out, rows_back)

        return carry

    lax.fori_loop(0, chunks, next_chunk, 0)

    for slot in range(members):
        inner = rows_back[spot_of(slot), :].astype(jnp.bfloat16)
        dense_back[slot] += matmul(hits(slot, False), inner)
    for member in range(members):
        back_ref[member] = dense_back[slot_of(deal_ref, member)].astype(jnp.bfloat16)
        hand_out(back_ref.at[member], back_out.at[member])
    for slot in range(members):
        gate = upright(meta_all[slot, 1:2, :])
        picked = matmul(hits(slot, False), rows_out[spot_of(slot), :].astype(jnp.bfloat16))
        dense_out[slot] += gate * picked
        score = jnp.sum(picked * grads_all[slot].astype(jnp.float32), axis=1, keepdims=True)
        gate_ref[slot] = jnp.broadcast_to(lying(score), gate_ref.shape[1:])
    for member in range(members):
        result_ref[member] = dense_out[slot_of(deal_ref, member)].astype(jnp.bfloat16)
        hand_out(result_ref.at[member], result_out.at[member])
    for chunk in range(chunks):
        kept(chunk, 0).wait()
        kept(chunk, 1).wait()
    for chunk in range(early):
        for piece in range(2):
            for side in range(2):
                first_sum(chunk, side, piece).wait()
    for made in outgoing:
        made.wait()
    links.finish()


def scatter_kernel(
    groups,
    members,
    tokens,
    routes,
    gains_full,
    cos_ref,
    sin_ref,
    gate_parts,
    result_parts,
    back_parts,
    wide_grads,
    down_grads,
    wide_first,
    down_first,
    grads_in,
    middle_in,
    attend_in,
    saved_in,
    soft_in,
    output_out,
    input_grad_out,
    expand_out,
    reduce_out,
    narrow_out,
    project_out,
    collect_out,
    gate_grad_ref,
    widen_sum,
    gains_sum,
    expand_sum,
    reduce_sum,
    narrow_sum,
    output_ref,
    input_grad_ref,
    attend_sum,
    grads_home,
    middle_ref,
    attend_full,
    saved,
    soft_ref,
    gate_recv,
    result_recv,
    back_recv,
    wide_own,
    down_own,
    wide_recv,
    down_recv,
    wide_sum,
    turned_ref,
    attend_grad,
    near_recv,
    far_recv,
    far_send,
    attend_total,
    attend_recv,
    attend_back,
    widen_back,
    widen_home,
    gain_own,
    gain_recv,
    gain_ring,
    sends,
    arrivals,
    local_sems,
):
    at = Places(groups, members)
    links = Links(sends, arrivals)
    at.enter()
    me, steps = at.member, groups - 1
    length, width = tokens.shape
    chunks, low = down_own.shape[0], narrow_sum.shape[0]
    share = attend_sum.shape[1]
    block = share * members

    moves_of = {}
    widen_moves = []

    def ring_step(chunk, step):
        made = []
        owners = (at.owner(-1 - step), at.owner(1 + step))
        for piece in range(2):
            for side, target in enumerate((at.next, at.back)):
                own = (wide_own, down_own)[piece]
                landing = (wide_recv, down_recv)[piece].at[chunk, side]
                if piece == 0:
                    spot = (chunk, side, rows(owners[side] * block, block))
                else:
                    spot = (chunk, rows(owners[side] * low + side * (low // 2), low // 2))
                if step == 0:
                    first = (wide_grads, down_grads)[piece]
                    made.append(links.copy(first.at[spot], landing.at[0], target))
                    continue
                if step > 1 or chunk >= early:
                    moves_of[chunk, step - 1][2 * piece + side].wait_recv()
                source = landing.at[step - 1]
                added = source[...].astype(jnp.float32) + own[spot].astype(jnp.float32)
                if step < steps:
                    source[...] = added.astype(jnp.bfloat16)
                elif piece == 0 and chunk != 1:
                    wide_sum[max(chunk - 1, 0), side] = added
                elif piece == 0:
                    for member in range(members):
                        widen_back[member, side] = added[member * share : (member + 1) * share, :]
                else:
                    start = side * (low // 2)
                    if chunk != 1:
                        start = start + max(chunk - 1, 0) * low
                        reduce_sum[start : start + low // 2, :] = added
                    else:
                        narrow_sum[start : start + low // 2, :] = added
                if step < steps:
                    made.append(links.copy(source, landing.at[step], target))
        moves_of[chunk, step] = made
        if step == steps and chunk == 1:
            widen_home[me] = widen_back[me]
            for peer in at.peers:
                widen_moves.append(
                    links.copy(widen_back.at[peer], widen_home.at[me], {"exp": peer})
                )
        if step == steps and chunk == 1:
            store(narrow_sum, narrow_out)
        elif step == steps:
            spot = rows(max(chunk - 1, 0) * low, low)
            store(reduce_sum.at[spot], reduce_out.at[spot])
        if step == steps and chunk and chunk % 2 == 0:
            pair = chunk // 2 - 1
            for side in range(2):
                found = joined_lanes(wide_sum[chunk - 2, side], wide_sum[chunk - 1, side])
                for index in range(0, len(found), 1):
                    expand_sum[pair, side, :, index * 128 : index * 128 + 128] = found[index]
            store(expand_sum.at[pair], expand_out.at[pair])

    early = chunks - 2
    order = [(chunk, 0) for chunk in range(early, chunks)] + [
        (chunk, step) for step in range(1, groups) for chunk in (1, 0, *range(2, chunks))
    ]

    def poll(count):
        for _ in range(min(count, len(order))):
            chunk, step = order.pop(0)
            for made in own_loads.pop(step, ()):
                made.wait()
            ring_step(chunk, step)

    kept, stored = [], []

    def store(source, target):
        made = pltpu.make_async_copy(source, target, local_sems.at[4 * groups + 14 + len(stored)])
        made.start(priority=1)
        stored.append(made)

    def load(source, target):
        made = pltpu.make_async_copy(source, target, local_sems.at[len(kept)])
        made.start(priority=1)
        kept.append(made)
        return made

    own_loads = {}

    def load_own(step):
        found = []
        for side, owner in enumerate((at.owner(-1 - step), at.owner(1 + step))):
            spot = rows(owner * block, block)
            found.append(load(wide_grads.at[:, side, spot], wide_own.at[:, side, spot]))
            spot = rows(owner * low + side * (low // 2), low // 2)
            found.append(load(down_grads.at[:, spot], down_own.at[:, spot]))
        own_loads[step] = found

    back_moves = [
        links.copy(back_parts.at[peer], back_recv.at[me], {"exp": peer}) for peer in at.peers
    ]
    first_loads = [
        load(wide_first.at[:, side], wide_recv.at[0:early, side, 0]) for side in range(2)
    ] + [load(down_first.at[:, side], down_recv.at[0:early, side, 0]) for side in range(2)]
    load_own(1)
    poll(2)
    middle_loads = [
        load(back_parts.at[me], back_recv.at[me]),
        load(middle_in, middle_ref),
        load(grads_in, grads_home),
        load(attend_in.at[3], attend_full.at[3]),
        load(saved_in, saved),
    ]
    soft_load = load(soft_in, soft_ref)
    load_own(2)
    attend_load = load(attend_in.at[0:3], attend_full.at[0:3])
    for step in range(3, groups):
        load_own(step)
    result_load = load(result_parts.at[me], result_recv.at[me])
    gate_recv[me] = gate_parts[me]
    for made in first_loads:
        made.wait()
    poll(3)
    result_moves = [
        [
            links.copy(result_parts.at[peer], result_recv.at[me], {"exp": peer}),
            links.copy(gate_parts.at[peer], gate_recv.at[me], {"exp": peer}),
        ]
        for peer in at.peers
    ]
    for made in middle_loads:
        made.wait()
    for move in back_moves:
        move.wait_recv()

    second_grad = back_recv[0].astype(jnp.float32)
    for member in range(1, members):
        second_grad = second_grad + back_recv[member].astype(jnp.float32)
    middle = middle_ref[...]
    scale = rms_factor(middle)
    gain_own[...] = jnp.zeros_like(gain_own)
    gain_own[1:2, :] = jnp.sum(second_grad * (middle * scale), axis=0, keepdims=True)
    input_grad_ref[...] = grads_home[...].astype(jnp.float32) + rms_back(
        middle, scale, second_grad * gains_full[1:2, :]
    )
    middle_low = input_grad_ref[...].astype(jnp.bfloat16)
    turned_ref[3] = nt(middle_low, attend_full[3]).astype(jnp.bfloat16)
    poll(2)
    cosines, sines = cos_ref[...], sin_ref[...]
    lower = first_half((length, 128))
    soft_load.wait()

    def heads(pair, carry):
        lanes = pl.ds(pl.multiple_of(pair * 128, 128), 128)
        query, key, value = saved[0, :, lanes], saved[1, :, lanes], saved[2, :, lanes]
        outer = turned_ref[3, :, lanes]
        made = []
        for side in range(2):
            soft = soft_ref[2 * pair + side]
            alone = jnp.where(lower == (side == 0), outer, jnp.zeros_like(outer))
            value_grad = tn(soft.astype(jnp.bfloat16), outer)
            soft_grad = nt(alone, value)
            score_grad = (
                soft * (soft_grad - jnp.sum(soft * soft_grad, axis=-1, keepdims=True))
            ).astype(jnp.bfloat16)
            made.append(
                (matmul(score_grad, key) * 0.125, tn(score_grad, query) * 0.125, value_grad)
            )
        for index in range(3):
            joined = jnp.where(lower, made[0][index], made[1][index])
            if index < 2:
                joined = joined * cosines - turned(joined) * sines
            turned_ref[index, :, lanes] = joined.astype(jnp.bfloat16)
        return carry

    attend_grad[3] = tn(saved[3], middle_low).astype(jnp.bfloat16)
    for third in range(3):
        lax.fori_loop(2 * third, 2 * third + 2, heads, 0)
        poll(2)
    for matrix in range(3):
        attend_grad[matrix] = tn(saved[4], turned_ref[matrix]).astype(jnp.bfloat16)
    near_moves = [
        links.copy(attend_grad.at[matrix], near_recv.at[index], {"exp": at.near})
        for index, matrix in enumerate((at.near, at.cross))
    ]
    poll(1)
    attend_load.wait()
    first_grad = nt(turned_ref[0], attend_full[0])
    for matrix in range(1, 3):
        first_grad = first_grad + nt(turned_ref[matrix], attend_full[matrix])
    stream = tokens[...].astype(jnp.float32)
    scale = rms_factor(stream)
    gain_own[0:1, :] = jnp.sum(first_grad * (stream * scale), axis=0, keepdims=True)
    gain_moves = [links.copy(gain_own, gain_recv.at[me], {"exp": peer}) for peer in at.peers]
    gain_recv[me] = gain_own[...]
    input_grad_ref[...] += rms_back(stream, scale, first_grad * gains_full[0:1, :])
    store(input_grad_ref, input_grad_out)
    for move in near_moves:
        move.wait_recv()
    far_send[...] = (
        attend_grad[at.far].astype(jnp.float32) + near_recv[1].astype(jnp.float32)
    ).astype(jnp.bfloat16)
    far_move = links.copy(far_send, far_recv, {"exp": at.far})
    poll(2)
    for moves in result_moves:
        for move in moves:
            move.wait_recv()
    result_load.wait()
    output = middle_ref[...]
    for member in range(members):
        output = output + result_recv[member].astype(jnp.float32)
    output_ref[...] = output
    store(output_ref, output_out)
    for choice in range(2):
        route = routes[choice : choice + 1, :]
        found = jnp.zeros((1, length), jnp.float32)
        for member in range(members):
            found = jnp.where(route == member, gate_recv[member, 0:1, :], found)
        gate_grad_ref[choice : choice + 1, :] = found
    poll(7)
    for move in gain_moves:
        move.wait_recv()
    total = gain_recv[0]
    for member in range(1, members):
        total = total + gain_recv[member]
    gain_ring[at.group] = total
    far_move.wait_recv()
    attend_total[...] = (
        attend_grad[me].astype(jnp.float32)
        + near_recv[0].astype(jnp.float32)
        + far_recv[...].astype(jnp.float32)
    ).astype(jnp.bfloat16)

    reach = (groups // 2, groups - 1 - groups // 2)
    small = {}

    def advance_small(step):
        for side, target in enumerate((at.next, at.back)):
            if step > reach[side]:
                continue
            owner = at.owner(reach[side] - step if side == 0 else step - reach[side])
            spot = attend_total.at[rows(owner * block, block), :]
            if step:
                for move in small[step - 1, side]:
                    move.wait_recv()
            if step < reach[side]:
                source = spot
                if step:
                    source = attend_recv.at[side, step - 1]
                    source[...] = (
                        source[...].astype(jnp.float32) + spot[...].astype(jnp.float32)
                    ).astype(jnp.bfloat16)
                line = gain_ring.at[at.owner(-step if side == 0 else step)]
                small[step, side] = (
                    links.copy(source, attend_recv.at[side, step], target),
                    links.copy(line, line, target),
                )

    for step in range(reach[0] + 1):
        advance_small(step)
        poll(2)
    added = attend_total[rows(at.group * block, block), :].astype(jnp.float32)
    for side in range(2):
        added = added + attend_recv[side, reach[side] - 1].astype(jnp.float32)
    for member in range(members):
        attend_back[member] = added[member * share : (member + 1) * share, :]
    attend_moves = [
        links.copy(attend_back.at[peer], attend_sum.at[me], {"exp": peer}) for peer in at.peers
    ]
    attend_sum[me] = attend_back[me]
    total = gain_ring[0]
    for group in range(1, groups):
        total = total + gain_ring[group]
    count = gains_sum.shape[1]
    start = (at.group * members + me) * count
    gains_sum[...] = pltpu.roll(total, width - start, 1)[0:2, 0:count]
    poll(len(order) - 2)
    for move in attend_moves:
        move.wait_recv()
    store(attend_sum.at[0:3], project_out)
    store(attend_sum.at[3], collect_out)
    for move in widen_moves:
        move.wait_recv()
    for matrix in range(2):
        for member in range(0, members, 2):
            found = joined_lanes(widen_home[member, matrix], widen_home[member + 1, matrix])
            for index, part in enumerate(found):
                start = index * 64 * members + member * 64
                widen_sum[matrix, :, start : start + 128] = part
    poll(len(order))
    for made in stored:
        made.wait()
    links.finish()


def update_kernel(rates, fixed, copies, *refs):
    count = len(rates)
    given, made = refs[: 4 * count + copies], refs[4 * count + copies :]
    for index in range(copies):
        made[index][...] = given[4 * count + index][...]

    def update(index):
        weight, moment, variance, gradient = given[4 * index : 4 * index + 4]
        if len(gradient.shape) > len(weight.shape):
            grad = jnp.concatenate(
                [
                    gradient[at % 2, :, :, at // 2 * 128 : at // 2 * 128 + 128]
                    for at in range(weight.shape[-1] // 128)
                ],
                axis=2,
            )
        else:
            grad = gradient[...]
        grad = 0.5 * grad
        level = 1.0 / (1.0 - 0.5**STEP)
        moment_new = 0.5 * moment[...] + grad
        variance_new = 0.5 * variance[...] + 2.0 * grad * grad
        kept = weight[...]
        stepped = moment_new * level / (jnp.sqrt(variance_new * level) + 1e-08) + 0.1 * kept
        made[copies + 3 * index][...] = moment_new
        made[copies + 3 * index + 1][...] = variance_new
        made[copies + 3 * index + 2][...] = kept - rates[index] * stepped

    for index in range(count):
        if fixed[index]:
            pl.when(pl.program_id(0) == 0)(functools.partial(update, index))
        else:
            update(index)


def update_all(*groups, passed):
    cuts = 4

    def spec(dims, cut):
        if cut is None:
            return pl.BlockSpec(dims, lambda step: (0,) * len(dims))
        block = tuple(size // cuts if at == cut else size for at, size in enumerate(dims))
        return pl.BlockSpec(
            block, lambda step: tuple(step if at == cut else 0 for at in range(len(dims)))
        )

    def cut_of(array):
        dims = array.shape
        for at in range(len(dims) - 1):
            if array.size > 100000 and dims[at] % (8 * cuts) == 0:
                return at
        return len(dims) - 1 if dims[-1] % (128 * cuts) == 0 else None

    given, specs, shapes, out_specs = [], [], [], []
    for _, weight, moment, variance, gradient in groups:
        cut = cut_of(weight)
        for array in (weight, moment, variance, gradient):
            given.append(array)
            more = array.ndim - weight.ndim
            specs.append(spec(array.shape, None if cut is None else cut + more))
        for array in (weight, moment, variance):
            shapes.append(jax.ShapeDtypeStruct(array.shape, array.dtype))
            out_specs.append(spec(array.shape, cut))
    extra = [spec(array.shape, cut_of(array)) for array in passed]
    return pl.pallas_call(
        functools.partial(
            update_kernel,
            [group[0] for group in groups],
            [cut_of(group[1]) is None for group in groups],
            len(passed),
        ),
        grid=(cuts,),
        out_shape=[jax.ShapeDtypeStruct(array.shape, array.dtype) for array in passed] + shapes,
        in_specs=specs + extra,
        out_specs=extra + out_specs,
        compiler_params=pltpu.CompilerParams(vmem_limit_bytes=LIMIT),
    )(*given, *passed)


def rotary_lines(length):
    half = HEAD_FEATURES // 2
    freqs = np.exp(-np.log(10000.0) * np.arange(half) / half)
    angles = np.arange(length)[:, None] * freqs[None, :]
    cosines, sines = np.cos(angles), np.sin(angles)
    return (
        np.concatenate([cosines] * 4, axis=1).astype(np.float32),
        np.concatenate([-sines, sines] * 2, axis=1).astype(np.float32),
    )


def spaces(*names):
    kinds = {"v": pltpu.VMEM, "s": pltpu.SMEM, "a": pl.ANY}
    return [pl.BlockSpec(memory_space=kinds[name]) for name in "".join(names)]


def local(
    tokens,
    seq_lengths,
    deal_order,
    expert_routes,
    capacity_slots,
    gate_weights,
    cotangent,
    projector,
    projector_mean,
    projector_square,
    collector,
    collector_first_moment,
    collector_second_moment,
    widener,
    widener_mean,
    widener_square,
    narrower,
    narrower_mean,
    narrower_square,
    norm_gains,
    gains_mean,
    gains_square,
    expander,
    expander_mean,
    expander_square,
    reducer,
    reducer_mean,
    reducer_square,
):
    groups, members = lax.axis_size("grp"), lax.axis_size("exp")
    length, width = tokens.shape[1:]
    inner = expander.shape[3]
    piece = widener.shape[2] // members
    chunks = 1 + inner // piece
    capacity = 3 * length // members
    steps = groups - 1
    high, low, share = expander.shape[2], narrower.shape[0], projector.shape[1]
    bf16, f32 = jnp.bfloat16, jnp.float32
    shape = jax.ShapeDtypeStruct
    cosines, sines = (jnp.asarray(lines) for lines in rotary_lines(length))
    count = 16 * groups
    (
        wide_grads,
        down_grads,
        wide_first,
        down_first,
        attend_full,
        grads_all,
        saved,
        middle,
        soft,
        result_parts,
        back_parts,
        gains_full,
        gate_parts,
    ) = pl.pallas_call(
        functools.partial(gather_kernel, groups, members),
        out_shape=[
            shape((chunks, 2, width, piece), bf16),
            shape((chunks, piece, width), bf16),
            shape((chunks - 2, 2, high, piece), bf16),
            shape((chunks - 2, 2, low // 2, width), bf16),
            shape((4, width, width), bf16),
            shape((length, width), bf16),
            shape((5, length, width), bf16),
            shape((length, width), f32),
            shape((HEAD_COUNT, length, length), f32),
            shape((members, length, width), bf16),
            shape((members, length, width), bf16),
            shape((8, width), f32),
            shape((members, 8, length), f32),
        ],
        in_specs=spaces("ssvavvvvvvaaaavv"),
        out_specs=spaces("a" * 11, "vv"),
        scratch_shapes=[
            VMEM((length, width), f32),
            VMEM(widener.shape, f32),
            VMEM(narrower.shape, f32),
            VMEM(expander.shape[1:], f32),
            VMEM(reducer.shape[1:], f32),
            VMEM((members, length, width), bf16),
            VMEM((members, length, width), bf16),
            VMEM((length, width), bf16),
            VMEM((4, width, width), bf16),
            VMEM((members, length, width), bf16),
            VMEM((5, length, width), bf16),
            VMEM((length, width), f32),
            VMEM((HEAD_COUNT, length, length), f32),
            VMEM((members, length, width), bf16),
            VMEM((members, 8, length), f32),
            VMEM((members, 8, length), f32),
            VMEM((4, share, width), f32),
            VMEM((4, share, width), f32),
            VMEM((members, 2, share, piece), f32),
            VMEM((members, 2, share, piece), f32),
            VMEM((8, width), f32),
            VMEM((members, 8, width), f32),
            VMEM((groups, 8, width), f32),
            VMEM((chunks, 2, width, piece), bf16),
            VMEM((chunks, piece, width), bf16),
            VMEM((chunks, 2, high, piece), bf16),
            VMEM((chunks, low, width), bf16),
            VMEM((members * length, width), bf16),
            VMEM((width, members * length), bf16),
            VMEM((members, length, width), f32),
            VMEM((members, length, width), f32),
            VMEM((members * capacity, width), bf16),
            VMEM((width, members * capacity), bf16),
            VMEM((members * capacity, width), bf16),
            VMEM((members * capacity, width), f32),
            VMEM((members * capacity, width), f32),
            pltpu.SemaphoreType.DMA((count,)),
            pltpu.SemaphoreType.DMA((count,)),
            pltpu.SemaphoreType.DMA((chunks * steps * 4,)),
            pltpu.SemaphoreType.DMA((chunks * steps * 4,)),
            pltpu.SemaphoreType.DMA((chunks * 4,)),
            pltpu.SemaphoreType.DMA((chunks * 4,)),
            pltpu.SemaphoreType.DMA((2 * chunks + 10 + 2 * members,)),
        ],
        compiler_params=pltpu.CompilerParams(
            collective_id=0, has_side_effects=True, vmem_limit_bytes=LIMIT
        ),
    )(
        seq_lengths,
        deal_order,
        tokens[0],
        cotangent[0],
        expert_routes[0].T,
        capacity_slots[0].T,
        gate_weights[0].T,
        norm_gains,
        projector,
        collector,
        widener,
        narrower,
        expander[0],
        reducer[0],
        cosines,
        sines,
    )
    count = 32 * groups
    (
        output,
        input_grad,
        expand_sum,
        reduce_sum,
        narrow_sum,
        project_sum,
        collect_sum,
        gate_grad,
        widen_sum,
        gains_sum,
    ) = pl.pallas_call(
        functools.partial(scatter_kernel, groups, members),
        out_shape=[
            shape((length, width), f32),
            shape((length, width), f32),
            shape((2, 2, high, inner // 2), f32),
            shape(reducer.shape[1:], f32),
            shape(narrower.shape, f32),
            shape(projector.shape, f32),
            shape(collector.shape, f32),
            shape((2, length), f32),
            shape(widener.shape, f32),
            shape(norm_gains.shape, f32),
        ],
        in_specs=spaces("v" * 6, "a" * 11),
        out_specs=spaces("a" * 7, "vvv"),
        scratch_shapes=[
            VMEM((2, 2, high, inner // 2), f32),
            VMEM(reducer.shape[1:], f32),
            VMEM(narrower.shape, f32),
            VMEM((length, width), f32),
            VMEM((length, width), f32),
            VMEM((4, share, width), f32),
            VMEM((length, width), bf16),
            VMEM((length, width), f32),
            VMEM((4, width, width), bf16),
            VMEM((5, length, width), bf16),
            VMEM((HEAD_COUNT, length, length), f32),
            VMEM((members, 8, length), f32),
            VMEM((members, length, width), bf16),
            VMEM((members, length, width), bf16),
            VMEM((chunks, 2, width, piece), bf16),
            VMEM((chunks, piece, width), bf16),
            VMEM((chunks, 2, steps, high, piece), bf16),
            VMEM((chunks, 2, steps, low // 2, width), bf16),
            VMEM((chunks - 1, 2, high, piece), f32),
            VMEM((4, length, width), bf16),
            VMEM((4, width, width), bf16),
            VMEM((2, width, width), bf16),
            VMEM((width, width), bf16),
            VMEM((width, width), bf16),
            VMEM((width, width), bf16),
            VMEM((2, groups // 2, high, width), bf16),
            VMEM((4, share, width), f32),
            VMEM((members, 2, share, piece), f32),
            VMEM((members, 2, share, piece), f32),
            VMEM((8, width), f32),
            VMEM((members, 8, width), f32),
            VMEM((groups, 8, width), f32),
            pltpu.SemaphoreType.DMA((count,)),
            pltpu.SemaphoreType.DMA((count,)),
            pltpu.SemaphoreType.DMA((4 * groups + 32,)),
        ],
        compiler_params=pltpu.CompilerParams(
            collective_id=1, has_side_effects=True, vmem_limit_bytes=LIMIT
        ),
    )(
        tokens[0],
        expert_routes[0].T,
        gains_full,
        cosines,
        sines,
        gate_parts,
        result_parts,
        back_parts,
        wide_grads,
        down_grads,
        wide_first,
        down_first,
        grads_all,
        middle,
        attend_full,
        saved,
        soft,
    )
    updated = update_all(
        (0.1, projector, projector_mean, projector_square, project_sum),
        (0.3, collector, collector_first_moment, collector_second_moment, collect_sum),
        (0.07, widener, widener_mean, widener_square, widen_sum),
        (0.045, narrower, narrower_mean, narrower_square, narrow_sum),
        (0.2, norm_gains, gains_mean, gains_square, gains_sum),
        (0.07, expander[0], expander_mean[0], expander_square[0], expand_sum),
        (0.045, reducer[0], reducer_mean[0], reducer_square[0], reduce_sum),
        passed=(output, input_grad),
    )
    return (
        updated[0][None],
        updated[1][None],
        gate_grad.T[None],
        *updated[2:17],
        *(found[None] for found in updated[17:]),
    )


def fits(mesh):
    groups, members = mesh.shape["grp"], mesh.shape["exp"]
    share = 64 * HEAD_COUNT // (groups * members)
    return members == 4 and groups % 2 == 0 and share % 8 == 0 and share * members // 2 % 16 == 0


def solution(mesh):
    placed = (
        P(("grp", "exp"), None, None),
        P("grp"),
        P("grp"),
        P(("grp", "exp"), None, None),
        P(("grp", "exp"), None, None),
        P(("grp", "exp"), None, None),
        P(("grp", "exp"), None, None),
        P(None, ("grp", "exp"), None),
        P(None, ("grp", "exp"), None),
        P(None, ("grp", "exp"), None),
        P(("grp", "exp"), None),
        P(("grp", "exp"), None),
        P(("grp", "exp"), None),
        P(None, ("grp", "exp"), None),
        P(None, ("grp", "exp"), None),
        P(None, ("grp", "exp"), None),
        P(("grp", "exp"), None),
        P(("grp", "exp"), None),
        P(("grp", "exp"), None),
        P(None, ("grp", "exp")),
        P(None, ("grp", "exp")),
        P(None, ("grp", "exp")),
        P("exp", None, "grp", None),
        P("exp", None, "grp", None),
        P("exp", None, "grp", None),
        P("exp", "grp", None),
        P("exp", "grp", None),
        P("exp", "grp", None),
    )
    return jax.shard_map(
        local if fits(mesh) else local_plain,
        mesh=mesh,
        in_specs=placed,
        out_specs=(
            P(("grp", "exp"), None, None),
            P(("grp", "exp"), None, None),
            P(("grp", "exp"), None, None),
            P(None, ("grp", "exp"), None),
            P(None, ("grp", "exp"), None),
            P(None, ("grp", "exp"), None),
            P(("grp", "exp"), None),
            P(("grp", "exp"), None),
            P(("grp", "exp"), None),
            P(None, ("grp", "exp"), None),
            P(None, ("grp", "exp"), None),
            P(None, ("grp", "exp"), None),
            P(("grp", "exp"), None),
            P(("grp", "exp"), None),
            P(("grp", "exp"), None),
            P(None, ("grp", "exp")),
            P(None, ("grp", "exp")),
            P(None, ("grp", "exp")),
            P("exp", None, "grp", None),
            P("exp", None, "grp", None),
            P("exp", None, "grp", None),
            P("exp", "grp", None),
            P("exp", "grp", None),
            P("exp", "grp", None),
        ),
        check_vma=False,
    )
```

```python
import functools

import jax
import jax.numpy as jnp
import numpy as np
from jax import lax
from jax.experimental import pallas as pl
from jax.experimental.pallas import tpu as pltpu
from jax.sharding import PartitionSpec as P

HEAD_COUNT = 12
HEAD_FEATURES = 64
STEP = 5


def rms_factor(values):
    return lax.rsqrt(jnp.mean(values * values, axis=-1, keepdims=True) + 1e-06)


def rms_back(values, factor, upstream):
    return factor * (
        upstream - values * factor * factor * jnp.mean(upstream * values, axis=-1, keepdims=True)
    )


def rotary(length):
    positions = jnp.arange(length, dtype=jnp.int32).astype(jnp.float32)
    half = HEAD_FEATURES // 2
    freqs = jnp.exp(
        -jnp.log(10000.0) * jnp.arange(half, dtype=jnp.int32).astype(jnp.float32) / half
    )
    angles = positions[:, None] * freqs[None, :]
    return (jnp.cos(angles)[:, None, :], jnp.sin(angles)[:, None, :])


def rotate(values, cosines, sines):
    half = values.shape[-1] // 2
    first = values[..., :half]
    second = values[..., half:]
    return jnp.concatenate(
        [first * cosines - second * sines, second * cosines + first * sines], axis=-1
    )


def rotate_back(values, cosines, sines):
    half = values.shape[-1] // 2
    first = values[..., :half]
    second = values[..., half:]
    return jnp.concatenate(
        [first * cosines + second * sines, second * cosines - first * sines], axis=-1
    )


def silu_slope(values):
    sigmoid_of = jax.nn.sigmoid(values)
    return sigmoid_of * (1.0 + values * (1.0 - sigmoid_of))


def matmul(left, right):
    return jnp.dot(left, right, preferred_element_type=jnp.float32)


def outer_sum(left, right):
    return jnp.einsum("ld,lf->df", left, right, preferred_element_type=jnp.float32)


def adamw_update(weight, moment, variance, gradient, rate):
    moment_new = 0.5 * moment + 0.5 * gradient
    variance_new = 0.5 * variance + 0.5 * gradient * gradient
    correct = 1.0 - 0.5**STEP
    stepped = moment_new / correct / (jnp.sqrt(variance_new / correct) + 1e-08) + 0.1 * weight
    return (moment_new, variance_new, weight - rate * stepped)


def local_plain(
    tokens,
    seq_lengths,
    deal_order,
    expert_routes,
    capacity_slots,
    gate_weights,
    cotangent,
    projector,
    projector_mean,
    projector_square,
    collector,
    collector_first_moment,
    collector_second_moment,
    widener,
    widener_mean,
    widener_square,
    narrower,
    narrower_mean,
    narrower_square,
    norm_gains,
    gains_mean,
    gains_square,
    expander,
    expander_mean,
    expander_square,
    reducer,
    reducer_mean,
    reducer_square,
):
    members = lax.axis_size("exp")
    member = lax.axis_index("exp")
    length_seq = tokens.shape[1]
    width = tokens.shape[2]
    local_experts = expander.shape[0]
    experts_all = local_experts * members
    capacity = 3 * length_seq // experts_all
    member_ids = jnp.arange(members, dtype=jnp.int32)
    source = deal_order[member]
    home_slot = jnp.sum(jnp.where(deal_order == member, member_ids, 0))
    seq_length = seq_lengths[source]
    piece = lax.all_gather(tokens, "exp", axis=0, tiled=True)
    chosen = jnp.arange(piece.shape[0], dtype=jnp.int32) == source
    dealt = jnp.sum(
        jnp.where(chosen[:, None, None], piece, jnp.zeros_like(piece)), axis=0, keepdims=True
    )
    residual_flow = dealt[0].astype(jnp.float32)
    project_full, collect_full, widen_full, narrow_full, gains_full = (
        lax.all_gather(projector.astype(jnp.bfloat16), ("grp", "exp"), axis=1, tiled=True),
        lax.all_gather(collector.astype(jnp.bfloat16), ("grp", "exp"), axis=0, tiled=True),
        lax.all_gather(widener.astype(jnp.bfloat16), ("grp", "exp"), axis=1, tiled=True),
        lax.all_gather(narrower.astype(jnp.bfloat16), ("grp", "exp"), axis=0, tiled=True),
        lax.all_gather(norm_gains.astype(jnp.bfloat16), ("grp", "exp"), axis=1, tiled=True),
    )
    expand_full, reduce_full = (
        lax.all_gather(expander.astype(jnp.bfloat16), "grp", axis=2, tiled=True),
        lax.all_gather(reducer.astype(jnp.bfloat16), "grp", axis=1, tiled=True),
    )
    gains_used = gains_full.astype(jnp.float32)
    cosines, sines = rotary(length_seq)
    scale_one = rms_factor(residual_flow)
    normed_one = residual_flow * scale_one
    first_input = (normed_one * gains_used[0]).astype(jnp.bfloat16)
    query_raw = matmul(first_input, project_full[0]).reshape(length_seq, HEAD_COUNT, HEAD_FEATURES)
    key_raw = matmul(first_input, project_full[1]).reshape(length_seq, HEAD_COUNT, HEAD_FEATURES)
    value_raw = matmul(first_input, project_full[2]).reshape(length_seq, HEAD_COUNT, HEAD_FEATURES)
    query_rot = rotate(query_raw, cosines, sines).astype(jnp.bfloat16)
    key_rot = rotate(key_raw, cosines, sines).astype(jnp.bfloat16)
    value_low = value_raw.astype(jnp.bfloat16)
    rows_at = jnp.arange(length_seq, dtype=jnp.int32)[:, None]
    cols_at = jnp.arange(length_seq, dtype=jnp.int32)[None, :]
    allowed = ((cols_at <= rows_at) & (cols_at < seq_length))[None]
    scores = (
        jnp.einsum("qhd,khd->hqk", query_rot, key_rot, preferred_element_type=jnp.float32) * 0.125
    )
    masked = jnp.where(allowed, scores, -1e30)
    top = jnp.max(masked, axis=-1, keepdims=True)
    expo = jnp.exp(masked - top)
    total = jnp.sum(expo, axis=-1, keepdims=True)
    soft = expo / total
    logsum = top + jnp.log(total)
    mixed_output = (
        jnp.einsum(
            "hqk,khd->qhd", soft.astype(jnp.bfloat16), value_low, preferred_element_type=jnp.float32
        )
        .reshape(length_seq, width)
        .astype(jnp.bfloat16)
    )
    middle_state = residual_flow + matmul(mixed_output, collect_full)
    scale_two = rms_factor(middle_state)
    normed_two = middle_state * scale_two
    second_input = (normed_two * gains_used[1]).astype(jnp.bfloat16)
    gating_scores = matmul(second_input, widen_full[0])
    upward_rows = matmul(second_input, widen_full[1])
    hidden_state = (jax.nn.silu(gating_scores) * upward_rows).astype(jnp.bfloat16)
    dense_branch = matmul(hidden_state, narrow_full)
    flat = (expert_routes[0] * capacity + capacity_slots[0]).reshape(-1)
    spread = jnp.repeat(second_input, 2, axis=0)
    dispatch = jnp.zeros((experts_all * capacity, width), jnp.bfloat16).at[flat].set(spread)
    dispatch = dispatch.reshape(experts_all, capacity, width)
    rows = lax.all_to_all(dispatch, "exp", split_axis=0, concat_axis=0, tiled=True)
    count = rows.shape[1]
    grouped = rows.reshape(members, local_experts, count, width)
    gate_pre = jnp.einsum(
        "sekd,edf->sekf", grouped, expand_full[:, 0], preferred_element_type=jnp.float32
    )
    up_pre = jnp.einsum(
        "sekd,edf->sekf", grouped, expand_full[:, 1], preferred_element_type=jnp.float32
    )
    hidden_rows = (jax.nn.silu(gate_pre) * up_pre).astype(jnp.bfloat16)
    result = jnp.einsum(
        "sekf,efd->sekd", hidden_rows, reduce_full, preferred_element_type=jnp.float32
    )
    result = result.astype(jnp.bfloat16).reshape(members * local_experts, count, width)
    returned_rows = lax.all_to_all(result, "exp", split_axis=0, concat_axis=0, tiled=True)
    outcome = (
        returned_rows,
        rows,
        gate_pre.reshape(members * local_experts, count, -1),
        up_pre.reshape(members * local_experts, count, -1),
    )
    returned, received, gate_kept, up_kept = outcome
    picked = (
        returned.reshape(experts_all * capacity, width)[flat]
        .reshape(length_seq, 2, width)
        .astype(jnp.float32)
    )
    gate_local = gate_weights[0]
    mixture = jnp.sum(gate_local[..., None] * picked, axis=1)
    layer_output = middle_state + dense_branch + mixture
    valid = (jnp.arange(length_seq, dtype=jnp.int32) < seq_length).astype(jnp.float32)
    grad_out = cotangent[0] * valid[:, None]
    grad_low = grad_out.astype(jnp.bfloat16)
    narrow_grad = outer_sum(hidden_state, grad_low)
    hidden_grad = jnp.einsum("ld,fd->lf", grad_low, narrow_full, preferred_element_type=jnp.float32)
    gating_grad = (hidden_grad * upward_rows * silu_slope(gating_scores)).astype(jnp.bfloat16)
    upward_grad = (hidden_grad * jax.nn.silu(gating_scores)).astype(jnp.bfloat16)
    widen_grad = jnp.stack(
        [outer_sum(second_input, gating_grad), outer_sum(second_input, upward_grad)]
    )
    second_grad = jnp.einsum(
        "lf,df->ld", gating_grad, widen_full[0], preferred_element_type=jnp.float32
    ) + jnp.einsum("lf,df->ld", upward_grad, widen_full[1], preferred_element_type=jnp.float32)
    gate_grad_local = jnp.sum(grad_out[:, None, :] * picked, axis=-1)
    result_grad = (
        (gate_local[..., None] * grad_out[:, None, :])
        .astype(jnp.bfloat16)
        .reshape(2 * length_seq, width)
    )
    grad_send = jnp.zeros((experts_all * capacity, width), jnp.bfloat16).at[flat].set(result_grad)
    grad_recv = lax.all_to_all(
        grad_send.reshape(experts_all, capacity, width),
        "exp",
        split_axis=0,
        concat_axis=0,
        tiled=True,
    )
    grad_group = grad_recv.reshape(members, local_experts, capacity, width)
    rows_group = received.reshape(members, local_experts, capacity, width)
    gate_pre = gate_kept.reshape(members, local_experts, capacity, -1)
    up_pre = up_kept.reshape(members, local_experts, capacity, -1)
    hidden_rows = (jax.nn.silu(gate_pre) * up_pre).astype(jnp.bfloat16)
    reduce_grad = jnp.einsum(
        "sekf,sekd->efd", hidden_rows, grad_group, preferred_element_type=jnp.float32
    )
    hidden_rows_grad = jnp.einsum(
        "sekd,efd->sekf", grad_group, reduce_full, preferred_element_type=jnp.float32
    )
    gate_rows_grad = (hidden_rows_grad * up_pre * silu_slope(gate_pre)).astype(jnp.bfloat16)
    up_rows_grad = (hidden_rows_grad * jax.nn.silu(gate_pre)).astype(jnp.bfloat16)
    expand_grad = jnp.stack(
        [
            jnp.einsum(
                "sekd,sekf->edf", rows_group, gate_rows_grad, preferred_element_type=jnp.float32
            ),
            jnp.einsum(
                "sekd,sekf->edf", rows_group, up_rows_grad, preferred_element_type=jnp.float32
            ),
        ],
        axis=1,
    )
    row_grads = jnp.einsum(
        "sekf,edf->sekd", gate_rows_grad, expand_full[:, 0], preferred_element_type=jnp.float32
    ) + jnp.einsum(
        "sekf,edf->sekd", up_rows_grad, expand_full[:, 1], preferred_element_type=jnp.float32
    )
    row_grads = row_grads.astype(jnp.bfloat16).reshape(experts_all, capacity, width)
    came_back = lax.all_to_all(row_grads, "exp", split_axis=0, concat_axis=0, tiled=True).reshape(
        experts_all * capacity, width
    )
    second_grad = second_grad + jnp.sum(
        came_back[flat].reshape(length_seq, 2, width).astype(jnp.float32), axis=1
    )
    gains_grad_two = jnp.sum(second_grad * normed_two, axis=0)
    middle_grad = grad_out + rms_back(middle_state, scale_two, second_grad * gains_used[1])
    middle_low = middle_grad.astype(jnp.bfloat16)
    collect_grad = outer_sum(mixed_output, middle_low)
    mixed_grad = jnp.einsum(
        "ld,ed->le", middle_low, collect_full, preferred_element_type=jnp.float32
    )
    mixed_grad = mixed_grad.astype(jnp.bfloat16).reshape(length_seq, HEAD_COUNT, HEAD_FEATURES)
    scores_again = (
        jnp.einsum("qhd,khd->hqk", query_rot, key_rot, preferred_element_type=jnp.float32) * 0.125
    )
    soft_again = jnp.where(allowed, jnp.exp(scores_again - logsum), 0.0)
    value_grad = jnp.einsum(
        "hqk,qhd->khd",
        soft_again.astype(jnp.bfloat16),
        mixed_grad,
        preferred_element_type=jnp.float32,
    )
    soft_grad = jnp.einsum(
        "qhd,khd->hqk", mixed_grad, value_low, preferred_element_type=jnp.float32
    )
    score_grad = (
        soft_again * (soft_grad - jnp.sum(soft_again * soft_grad, axis=-1, keepdims=True))
    ).astype(jnp.bfloat16)
    query_grad = (
        jnp.einsum("hqk,khd->qhd", score_grad, key_rot, preferred_element_type=jnp.float32) * 0.125
    )
    key_grad = (
        jnp.einsum("hqk,qhd->khd", score_grad, query_rot, preferred_element_type=jnp.float32)
        * 0.125
    )
    query_back = (
        rotate_back(query_grad, cosines, sines).reshape(length_seq, width).astype(jnp.bfloat16)
    )
    key_back = rotate_back(key_grad, cosines, sines).reshape(length_seq, width).astype(jnp.bfloat16)
    value_back = value_grad.reshape(length_seq, width).astype(jnp.bfloat16)
    project_grad = jnp.stack(
        [
            outer_sum(first_input, query_back),
            outer_sum(first_input, key_back),
            outer_sum(first_input, value_back),
        ]
    )
    first_grad = (
        jnp.einsum("le,de->ld", query_back, project_full[0], preferred_element_type=jnp.float32)
        + jnp.einsum("le,de->ld", key_back, project_full[1], preferred_element_type=jnp.float32)
        + jnp.einsum("le,de->ld", value_back, project_full[2], preferred_element_type=jnp.float32)
    )
    gains_grad_one = jnp.sum(first_grad * normed_one, axis=0)
    stream_grad = middle_grad + rms_back(residual_flow, scale_one, first_grad * gains_used[0])
    gains_grad = jnp.stack([gains_grad_one, gains_grad_two])
    project_part, collect_part, widen_part, narrow_part, gains_part = (
        lax.psum_scatter(project_grad, ("grp", "exp"), scatter_dimension=1, tiled=True),
        lax.psum_scatter(collect_grad, ("grp", "exp"), scatter_dimension=0, tiled=True),
        lax.psum_scatter(widen_grad, ("grp", "exp"), scatter_dimension=1, tiled=True),
        lax.psum_scatter(narrow_grad, ("grp", "exp"), scatter_dimension=0, tiled=True),
        lax.psum_scatter(gains_grad, ("grp", "exp"), scatter_dimension=1, tiled=True),
    )
    expand_part, reduce_part = (
        lax.psum_scatter(
            expand_grad.astype(jnp.bfloat16), "grp", scatter_dimension=2, tiled=True
        ).astype(jnp.float32),
        lax.psum_scatter(
            reduce_grad.astype(jnp.bfloat16), "grp", scatter_dimension=1, tiled=True
        ).astype(jnp.float32),
    )
    empty = jnp.zeros((1, length_seq, width), jnp.float32)
    pieces = (
        lax.all_gather(layer_output[None].astype(jnp.bfloat16), "exp", axis=0, tiled=True).astype(
            jnp.float32
        ),
        lax.all_gather(stream_grad[None].astype(jnp.bfloat16), "exp", axis=0, tiled=True).astype(
            jnp.float32
        ),
    )
    chosen = (jnp.arange(pieces[0].shape[0], dtype=jnp.int32) == home_slot)[:, None, None]
    homed_output = empty + jnp.sum(jnp.where(chosen, pieces[0], 0.0), axis=0, keepdims=True)
    homed_grad = empty + jnp.sum(jnp.where(chosen, pieces[1], 0.0), axis=0, keepdims=True)
    project_new = adamw_update(projector, projector_mean, projector_square, project_part, 0.1)
    collect_new = adamw_update(
        collector, collector_first_moment, collector_second_moment, collect_part, 0.3
    )
    widening_updated = adamw_update(widener, widener_mean, widener_square, widen_part, 0.07)
    narrowing_updated = adamw_update(narrower, narrower_mean, narrower_square, narrow_part, 0.045)
    gains_updated = adamw_update(norm_gains, gains_mean, gains_square, gains_part, 0.2)
    expansion_updated = adamw_update(expander, expander_mean, expander_square, expand_part, 0.07)
    reduction_updated = adamw_update(reducer, reducer_mean, reducer_square, reduce_part, 0.045)
    return (
        homed_output,
        homed_grad,
        gate_grad_local[None],
        project_new[0],
        project_new[1],
        project_new[2],
        collect_new[0],
        collect_new[1],
        collect_new[2],
        widening_updated[0],
        widening_updated[1],
        widening_updated[2],
        narrowing_updated[0],
        narrowing_updated[1],
        narrowing_updated[2],
        gains_updated[0],
        gains_updated[1],
        gains_updated[2],
        expansion_updated[0],
        expansion_updated[1],
        expansion_updated[2],
        reduction_updated[0],
        reduction_updated[1],
        reduction_updated[2],
    )


MESH = pl.DeviceIdType.MESH
VMEM = pltpu.VMEM
LIMIT = 60 * 1024 * 1024


def ring_place(index, groups):
    row, side = lax.div(index, 2), lax.rem(index, 2)
    return (1 - side) * row + side * (groups - 1 - row)


def ring_member(place, groups):
    side = lax.div(place, groups // 2)
    return 2 * ((1 - side) * place + side * (groups - 1 - place)) + side


def remote(source, target, sends, arrivals, at, device):
    return pltpu.make_async_remote_copy(
        src_ref=source,
        dst_ref=target,
        send_sem=sends.at[at],
        recv_sem=arrivals.at[at],
        device_id=device,
        device_id_type=MESH,
    )


class Links:
    def __init__(self, sends, arrivals):
        self.sends, self.arrivals, self.count, self.started = sends, arrivals, 0, []

    def copy(self, source, target, device):
        made = remote(source, target, self.sends, self.arrivals, self.count, device)
        self.count += 1
        made.start()
        self.started.append(made)
        return made

    def finish(self):
        for made in self.started:
            made.wait_send()


class Places:
    def __init__(self, groups, members):
        self.groups, self.members = groups, members
        self.group = lax.axis_index("grp")
        self.member = lax.axis_index("exp")
        self.place = ring_place(self.group, groups)
        self.next = {"grp": self.owner(1)}
        self.back = {"grp": self.owner(-1)}
        half = members // 2
        self.far = lax.rem(self.member + half, members)
        self.near = self.member + 1 - 2 * lax.rem(self.member, 2)
        self.cross = lax.rem(self.near + half, members)
        self.peers = [lax.rem(self.member + step, members) for step in range(1, members)]

    def owner(self, offset):
        place = lax.rem(self.place + offset + 2 * self.groups, self.groups)
        return ring_member(place, self.groups)

    def enter(self):
        barrier = pltpu.get_barrier_semaphore()
        partners = [self.next, self.back] + [{"exp": peer} for peer in self.peers]
        for partner in partners:
            pl.semaphore_signal(barrier, inc=1, device_id=partner, device_id_type=MESH)
        pl.semaphore_wait(barrier, len(partners))


def rows(start, count, align=16):
    return pl.ds(pl.multiple_of(start, align), count)


def first_half(shape):
    return lax.rem(lax.broadcasted_iota(jnp.int32, shape, len(shape) - 1), 128) < 64


def turned(values):
    lanes = lax.broadcasted_iota(jnp.int32, values.shape, 1)
    return jnp.where(
        lax.rem(lanes, HEAD_FEATURES) < HEAD_FEATURES // 2,
        pltpu.roll(values, 128 - HEAD_FEATURES // 2, 1),
        pltpu.roll(values, HEAD_FEATURES // 2, 1),
    )


def nt(left, right):
    return lax.dot_general(
        left, right, (((1,), (1,)), ((), ())), preferred_element_type=jnp.float32
    )


def tn(left, right):
    return lax.dot_general(
        left, right, (((0,), (0,)), ((), ())), preferred_element_type=jnp.float32
    )


def sigmoid(values):
    return 1.0 / (1.0 + jnp.exp(-values))


def same(length):
    shape = (length, length)
    return lax.broadcasted_iota(jnp.int32, shape, 0) == lax.broadcasted_iota(jnp.int32, shape, 1)


def upright(line):
    return jnp.sum(jnp.where(same(line.shape[1]), line, 0.0), axis=1, keepdims=True)


def lying(column):
    return jnp.sum(jnp.where(same(column.shape[0]), column, 0.0), axis=0, keepdims=True)


def slot_of(deal_ref, member):
    for _ in range(11):
        member = deal_ref[member]
    return member


def dealt_lanes(values, piece, pieces):
    low_lanes = lax.broadcasted_iota(jnp.int32, (values.shape[0], 128), 1) < 64
    found = []
    span = 64 * pieces
    for start in range(0, values.shape[1], 2 * span):
        start = start + piece // 2 * 128
        one, two = values[:, start : start + 128], values[:, start + span : start + span + 128]
        if piece % 2:
            one = pltpu.roll(one, 64, 1)
        else:
            two = pltpu.roll(two, 64, 1)
        found.append(jnp.where(low_lanes, one, two))
    return jnp.concatenate(found, axis=1)


def joined_lanes(even, odd):
    low_lanes = lax.broadcasted_iota(jnp.int32, (even.shape[0], 128), 1) < 64
    found = []
    for start in range(0, even.shape[1], 128):
        one, two = even[:, start : start + 128], odd[:, start : start + 128]
        found.append(jnp.where(low_lanes, one, pltpu.roll(two, 64, 1)))
        found.append(jnp.where(low_lanes, pltpu.roll(one, 64, 1), two))
    return found


def gather_kernel(
    groups,
    members,
    length_ref,
    deal_ref,
    tokens,
    cotangent_in,
    routes,
    places,
    gates,
    norm_gains,
    projector,
    collector,
    widener_in,
    narrower_in,
    expander_in,
    reducer_in,
    cos_ref,
    sin_ref,
    wide_grads,
    down_grads,
    wide_first,
    down_first,
    attend_out,
    grads_out,
    saved_out,
    middle_out,
    soft_out,
    result_out,
    back_out,
    gains_full,
    gate_ref,
    cotangent,
    widener,
    narrower,
    expander,
    reducer,
    result_ref,
    back_ref,
    grads_home,
    attend_full,
    grads_all,
    saved,
    middle_ref,
    soft_ref,
    second_all,
    meta_send,
    meta_all,
    attend_send,
    attend_recv,
    widen_send,
    widen_recv,
    gains,
    gain_recv,
    gain_ring,
    wide_full,
    down_full,
    wide_own,
    down_own,
    inputs_ref,
    inputs_turned,
    dense_out,
    dense_back,
    rows_in,
    rows_turned,
    rows_grad,
    rows_out,
    rows_back,
    sends,
    arrivals,
    ring_sends,
    ring_arrivals,
    first_sends,
    first_arrivals,
    local_sems,
):
    at = Places(groups, members)
    links = Links(sends, arrivals)
    chunks, low = down_own.shape[:2]
    loads = {}
    for name, source, target in (
        ("expander", expander_in, expander),
        ("reducer", reducer_in, reducer),
        ("widener", widener_in, widener),
        ("narrower", narrower_in, narrower),
        ("cotangent", cotangent_in, cotangent),
    ):
        made = pltpu.make_async_copy(source, target, local_sems.at[2 * chunks + len(loads)])
        made.start(priority=1)
        loads[name] = made
    at.enter()
    me, steps = at.member, groups - 1
    share, width = projector.shape[1:]
    block = share * members
    length = tokens.shape[0]
    capacity = rows_in.shape[0] // members

    def ring_copy(chunk, step, side, piece):
        owner = at.owner(-step if side == 0 else step)
        if piece == 0:
            spot = wide_full.at[chunk, side, rows(owner * block, block), :]
            origin = wide_own.at[chunk, side]
        else:
            spot = down_full.at[chunk, rows(owner * low + side * (low // 2), low // 2), :]
            origin = down_own.at[chunk, pl.ds(side * (low // 2), low // 2), :]
        place = (chunk * steps + step) * 4 + side * 2 + piece
        return remote(
            spot if step else origin,
            spot,
            ring_sends,
            ring_arrivals,
            place,
            (at.next, at.back)[side],
        )

    def ring_step(chunk, step):
        for piece in range(2):
            for side in range(2):
                if step:
                    ring_copy(chunk, step - 1, side, piece).wait_recv()
                if step < steps:
                    ring_copy(chunk, step, side, piece).start()

    def tick(count):
        for chunk in range(chunks):
            if 0 <= count - 2 * chunk <= steps:
                ring_step(chunk, count - 2 * chunk)

    attend_send[0:3] = projector[...]
    attend_send[3] = collector[...]
    gains[...] = jnp.zeros_like(gains)
    gains[0:2, 0 : norm_gains.shape[1]] = norm_gains[...]
    gains[...] = pltpu.roll(gains[...], (at.group * members + me) * norm_gains.shape[1], 1)
    first_moves = [
        [
            links.copy(attend_send.at[peer], attend_recv.at[me], {"exp": peer}),
            links.copy(gains, gain_recv.at[me], {"exp": peer}),
        ]
        for peer in at.peers
    ]
    gain_recv[me] = gains[...]
    attend_recv[me] = attend_send[me]
    def stage(chunk):
        if chunk == 1:
            for matrix in range(2):
                wide_own[1, matrix] = jnp.concatenate(
                    [widen_recv[member, matrix] for member in range(members)], axis=0
                ).astype(jnp.bfloat16)
            down_own[1] = narrower[...].astype(jnp.bfloat16)
        else:
            index = max(chunk - 1, 0)
            for matrix in range(2):
                wide_own[chunk, matrix] = dealt_lanes(
                    expander[matrix], index, chunks - 1
                ).astype(jnp.bfloat16)
            down_own[chunk] = reducer[index * low : (index + 1) * low, :].astype(jnp.bfloat16)
        for side in range(2):
            wide_full[chunk, side, rows(at.group * block, block), :] = wide_own[chunk, side]
        down_full[chunk, rows(at.group * low, low), :] = down_own[chunk]

    for moves in first_moves:
        for move in moves:
            move.wait_recv()
    attend_full[me, rows(at.group * block, block), :] = (
        attend_recv[...].reshape(block, width).astype(jnp.bfloat16)
    )
    total_gain = gain_recv[0]
    for member in range(1, members):
        total_gain = total_gain + gain_recv[member]
    gain_ring[at.group] = total_gain

    reach = (groups // 2, groups - 1 - groups // 2)

    def unit(owner, matrix):
        return attend_full.at[matrix, rows(owner * block, block), :]

    def across(owner):
        spot = unit(owner, me)
        return (links.copy(spot, spot, {"exp": at.far}), links.copy(spot, spot, {"exp": at.near}))

    crossed, passed, owners_seen = [], [], []

    def onward():
        spot = unit(owners_seen[len(passed)], at.far)
        crossed[len(passed)][0].wait_recv()
        passed.append(links.copy(spot, spot, {"exp": at.near}))

    ring = {}
    for step in range(reach[0] + 1):
        fresh = []
        for side, target in enumerate((at.next, at.back)):
            if step > reach[side]:
                continue
            owner = at.owner(-step if side == 0 else step)
            if step:
                for move in ring[step - 1, side]:
                    move.wait_recv()
            if step < reach[side]:
                spot, line = unit(owner, me), gain_ring.at[owner]
                ring[step, side] = (
                    links.copy(spot, spot, target),
                    links.copy(line, line, target),
                )
            if step or side == 0:
                fresh.append(owner)
        waiting = len(owners_seen) - len(passed)
        for owner in fresh:
            owners_seen.append(owner)
            crossed.append(across(owner))
        for _ in range(waiting):
            onward()
        if step == 0:
            loads["expander"].wait()
            loads["reducer"].wait()
            stage(0)
            tick(0)
            loads["widener"].wait()
            for matrix in range(2):
                for member in range(members):
                    widen_send[member, matrix] = dealt_lanes(widener[matrix], member, members)
            widen_moves = [
                links.copy(widen_send.at[peer], widen_recv.at[me], {"exp": peer}) for peer in at.peers
            ]
            widen_recv[me] = widen_send[me]
        if step == 1:
            for move in widen_moves:
                move.wait_recv()
            loads["narrower"].wait()
            for chunk in range(1, chunks):
                stage(chunk)
        if step:
            tick(step)
    outgoing = []

    def hand_out(source, target):
        made = pltpu.make_async_copy(
            source, target, local_sems.at[2 * chunks + len(loads) + len(outgoing)]
        )
        made.start(priority=1)
        outgoing.append(made)

    loads["cotangent"].wait()
    valid = lax.broadcasted_iota(jnp.int32, (length, 1), 0) < length_ref[deal_ref[me]]
    grads_all[me] = jnp.where(valid, cotangent[...], 0.0).astype(jnp.bfloat16)
    route = [routes[choice : choice + 1, :] for choice in range(2)]
    place = [places[choice : choice + 1, :].astype(jnp.float32) for choice in range(2)]
    meta_send[...] = jnp.zeros_like(meta_send)
    for member in range(members):
        named = [chosen == member for chosen in route]
        meta_send[member, 0:1, :] = jnp.where(
            named[0], place[0], jnp.where(named[1], place[1], -1.0)
        )
        meta_send[member, 1:2, :] = jnp.where(
            named[0], gates[0:1, :], jnp.where(named[1], gates[1:2, :], 0.0)
        )
    meta_all[me] = meta_send[me]
    grad_moves = [
        [
            links.copy(grads_all.at[me], grads_all.at[me], {"exp": peer}),
            links.copy(meta_send.at[peer], meta_all.at[me], {"exp": peer}),
        ]
        for peer in at.peers
    ]
    while len(passed) < groups:
        onward()
    total_gain = gain_ring[0]
    for group in range(1, groups):
        total_gain = total_gain + gain_ring[group]
    gains_full[...] = total_gain.astype(jnp.bfloat16).astype(jnp.float32)
    stream = tokens[...].astype(jnp.float32)
    first_input = (stream * rms_factor(stream) * gains_full[0:1, :]).astype(jnp.bfloat16)
    saved[4] = first_input
    for moves in crossed:
        moves[1].wait_recv()
    for move in passed:
        move.wait_recv()
    tick(5)
    hand_out(attend_full, attend_out)

    cosines, sines = cos_ref[...], sin_ref[...]
    for matrix in range(3):
        raw = matmul(first_input, attend_full[matrix])
        if matrix == 2:
            saved[2] = raw.astype(jnp.bfloat16)
        else:
            for start in range(0, width, 128):
                piece = raw[:, start : start + 128]
                saved[matrix, :, start : start + 128] = (
                    piece * cosines + turned(piece) * sines
                ).astype(jnp.bfloat16)
    tick(6)

    seq_length = length_ref[me]
    rows_at = lax.broadcasted_iota(jnp.int32, (length, length), 0)
    cols_at = lax.broadcasted_iota(jnp.int32, (length, length), 1)
    allowed = (cols_at <= rows_at) & (cols_at < seq_length)
    lower = first_half((length, 128))

    def heads(pair, carry):
        lanes = pl.ds(pl.multiple_of(pair * 128, 128), 128)
        query, key, value = saved[0, :, lanes], saved[1, :, lanes], saved[2, :, lanes]
        results = []
        for side in range(2):
            alone = jnp.where(lower == (side == 0), query, jnp.zeros_like(query))
            scores = jnp.where(allowed, nt(alone, key) * 0.125, -1e30)
            expo = jnp.exp(scores - jnp.max(scores, axis=-1, keepdims=True))
            soft = expo / jnp.sum(expo, axis=-1, keepdims=True)
            soft_ref[2 * pair + side] = soft
            results.append(matmul(soft.astype(jnp.bfloat16), value))
        saved[3, :, lanes] = jnp.where(lower, results[0], results[1]).astype(jnp.bfloat16)
        return carry

    lax.fori_loop(0, width // 128, heads, 0)
    hand_out(saved, saved_out)
    hand_out(soft_ref, soft_out)
    middle = tokens[...].astype(jnp.float32) + matmul(saved[3], attend_full[3])
    middle_ref[...] = middle
    hand_out(middle_ref, middle_out)
    second_all[me] = (middle * rms_factor(middle) * gains_full[1:2, :]).astype(jnp.bfloat16)
    second_moves = [
        links.copy(second_all.at[me], second_all.at[me], {"exp": peer}) for peer in at.peers
    ]
    for moves in grad_moves:
        for move in moves:
            move.wait_recv()
    grads_home[...] = grads_all[slot_of(deal_ref, me)]
    hand_out(grads_home, grads_out)
    tick(7)

    def hits(slot, by_row):
        line = meta_all[slot, 0:1, :]
        if by_row:
            names = lax.broadcasted_iota(jnp.int32, (capacity, length), 0).astype(jnp.float32)
            hit = names == line
        else:
            names = lax.broadcasted_iota(jnp.int32, (length, capacity), 1).astype(jnp.float32)
            hit = names == upright(line)
        return jnp.where(hit, 1.0, 0.0).astype(jnp.bfloat16)

    def spot_of(slot):
        return slice(slot * capacity, (slot + 1) * capacity)

    def here_of(slot):
        return slice(slot * length, (slot + 1) * length)

    for slot in range(members):
        pick = hits(slot, True)
        gate = jnp.sum(pick.astype(jnp.float32) * meta_all[slot, 1:2, :], axis=1, keepdims=True)
        rows_grad[spot_of(slot), :] = (matmul(pick, grads_all[slot]) * gate).astype(jnp.bfloat16)
    for move in second_moves:
        move.wait_recv()
    for slot in range(members):
        inputs_ref[here_of(slot), :] = second_all[deal_ref[slot]]
        rows_in[spot_of(slot), :] = matmul(hits(slot, True), inputs_ref[here_of(slot), :]).astype(
            jnp.bfloat16
        )
    inputs_turned[...] = inputs_ref[...].T
    rows_turned[...] = rows_in[...].T
    dense_out[...] = jnp.zeros_like(dense_out)
    dense_back[...] = jnp.zeros_like(dense_back)
    rows_out[...] = jnp.zeros_like(rows_out)
    rows_back[...] = jnp.zeros_like(rows_back)

    def branch(chunk, inputs, turned_inputs, outer, out, back):
        for step in range(steps):
            for side in range(2):
                for piece in range(2):
                    ring_copy(chunk, step, side, piece).wait_send()

        def part(index, carry):
            lanes = pl.ds(pl.multiple_of(index * 256, 256), 256)
            gate = matmul(inputs[...], wide_full[chunk, 0, :, lanes])
            up = matmul(inputs[...], wide_full[chunk, 1, :, lanes])
            rise = sigmoid(gate)
            smooth = gate * rise
            hidden = (smooth * up).astype(jnp.bfloat16)
            hidden_grad = nt(outer[...], down_full[chunk, lanes, :])
            gate_grad = (hidden_grad * up * (rise * (1.0 + gate * (1.0 - rise)))).astype(
                jnp.bfloat16
            )
            up_grad = (hidden_grad * smooth).astype(jnp.bfloat16)
            out[...] += matmul(hidden, down_full[chunk, lanes, :])
            back[...] += nt(gate_grad, wide_full[chunk, 0, :, lanes]) + nt(
                up_grad, wide_full[chunk, 1, :, lanes]
            )
            down_full[chunk, lanes, :] = tn(hidden, outer[...]).astype(jnp.bfloat16)
            wide_full[chunk, 0, :, lanes] = matmul(turned_inputs[...], gate_grad).astype(
                jnp.bfloat16
            )
            wide_full[chunk, 1, :, lanes] = matmul(turned_inputs[...], up_grad).astype(
                jnp.bfloat16
            )

            @pl.when(index == 0)
            def _():
                for ahead in range(groups // 2):
                    @pl.when(chunk + 1 + ahead < chunks)
                    def _():
                        ring_step(chunk + 1 + ahead, steps - 1 - 2 * ahead)

            return carry

        lax.fori_loop(0, down_full.shape[1] // 256, part, 0)
        kept(chunk, 0).start(priority=1)
        kept(chunk, 1).start(priority=1)

    def kept(chunk, piece):
        source, target = ((wide_full, wide_grads), (down_full, down_grads))[piece]
        return pltpu.make_async_copy(
            source.at[chunk], target.at[chunk], local_sems.at[2 * chunk + piece]
        )

    outer_all = grads_all.reshape(members * length, width)
    flat = (members * length, width)
    dense = (
        inputs_ref,
        inputs_turned,
        outer_all,
        dense_out.reshape(flat),
        dense_back.reshape(flat),
    )

    def first_sum(chunk, side, piece):
        owner = at.owner(-1 if side == 0 else 1)
        if piece == 0:
            spot = wide_full.at[chunk, side, rows(owner * block, block), :]
        else:
            spot = down_full.at[chunk, rows(owner * low + side * (low // 2), low // 2), :]
        return remote(
            spot,
            (wide_first, down_first)[piece].at[chunk, side],
            first_sends,
            first_arrivals,
            chunk * 4 + side * 2 + piece,
            (at.next, at.back)[side],
        )

    early = chunks - 2

    def start_sums(chunk):
        for piece in range(2):
            for side in range(2):
                first_sum(chunk, side, piece).start()

    def next_chunk(chunk, carry):
        for ahead in range(groups // 2):
            @pl.when((chunk > 0) & (chunk + ahead < chunks))
            def _():
                ring_step(chunk + ahead, steps - 2 * ahead)

        @pl.when(chunk == chunks - 1)
        def _():
            for before in range(early):
                start_sums(before)

        @pl.when(chunk == 1)
        def _():
            branch(chunk, *dense)

        @pl.when(chunk != 1)
        def _():
            branch(chunk, rows_in, rows_turned, rows_grad, rows_out, rows_back)

        return carry

    lax.fori_loop(0, chunks, next_chunk, 0)

    for slot in range(members):
        inner = rows_back[spot_of(slot), :].astype(jnp.bfloat16)
        dense_back[slot] += matmul(hits(slot, False), inner)
    for member in range(members):
        back_ref[member] = dense_back[slot_of(deal_ref, member)].astype(jnp.bfloat16)
        hand_out(back_ref.at[member], back_out.at[member])
    for slot in range(members):
        gate = upright(meta_all[slot, 1:2, :])
        picked = matmul(hits(slot, False), rows_out[spot_of(slot), :].astype(jnp.bfloat16))
        dense_out[slot] += gate * picked
        score = jnp.sum(picked * grads_all[slot].astype(jnp.float32), axis=1, keepdims=True)
        gate_ref[slot] = jnp.broadcast_to(lying(score), gate_ref.shape[1:])
    for member in range(members):
        result_ref[member] = dense_out[slot_of(deal_ref, member)].astype(jnp.bfloat16)
        hand_out(result_ref.at[member], result_out.at[member])
    for chunk in range(chunks):
        kept(chunk, 0).wait()
        kept(chunk, 1).wait()
    for chunk in range(early):
        for piece in range(2):
            for side in range(2):
                first_sum(chunk, side, piece).wait()
    for made in outgoing:
        made.wait()
    links.finish()


def scatter_kernel(
    groups,
    members,
    tokens,
    routes,
    gains_full,
    cos_ref,
    sin_ref,
    gate_parts,
    result_parts,
    back_parts,
    wide_grads,
    down_grads,
    wide_first,
    down_first,
    grads_in,
    middle_in,
    attend_in,
    saved_in,
    soft_in,
    output_out,
    input_grad_out,
    expand_out,
    reduce_out,
    narrow_out,
    project_out,
    collect_out,
    gate_grad_ref,
    widen_sum,
    gains_sum,
    expand_sum,
    reduce_sum,
    narrow_sum,
    output_ref,
    input_grad_ref,
    attend_sum,
    grads_home,
    middle_ref,
    attend_full,
    saved,
    soft_ref,
    gate_recv,
    result_recv,
    back_recv,
    wide_own,
    down_own,
    wide_recv,
    down_recv,
    wide_sum,
    turned_ref,
    attend_grad,
    near_recv,
    far_recv,
    far_send,
    attend_total,
    attend_recv,
    attend_back,
    widen_back,
    widen_home,
    gain_own,
    gain_recv,
    gain_ring,
    sends,
    arrivals,
    local_sems,
):
    at = Places(groups, members)
    links = Links(sends, arrivals)
    at.enter()
    me, steps = at.member, groups - 1
    length, width = tokens.shape
    chunks, low = down_own.shape[0], narrow_sum.shape[0]
    share = attend_sum.shape[1]
    block = share * members

    moves_of = {}
    widen_moves = []

    def ring_step(chunk, step):
        made = []
        owners = (at.owner(-1 - step), at.owner(1 + step))
        for piece in range(2):
            for side, target in enumerate((at.next, at.back)):
                own = (wide_own, down_own)[piece]
                landing = (wide_recv, down_recv)[piece].at[chunk, side]
                if piece == 0:
                    spot = (chunk, side, rows(owners[side] * block, block))
                else:
                    spot = (chunk, rows(owners[side] * low + side * (low // 2), low // 2))
                if step == 0:
                    first = (wide_grads, down_grads)[piece]
                    made.append(links.copy(first.at[spot], landing.at[0], target))
                    continue
                if step > 1 or chunk >= early:
                    moves_of[chunk, step - 1][2 * piece + side].wait_recv()
                source = landing.at[step - 1]
                added = source[...].astype(jnp.float32) + own[spot].astype(jnp.float32)
                if step < steps:
                    source[...] = added.astype(jnp.bfloat16)
                elif piece == 0 and chunk != 1:
                    wide_sum[max(chunk - 1, 0), side] = added
                elif piece == 0:
                    for member in range(members):
                        widen_back[member, side] = added[member * share : (member + 1) * share, :]
                else:
                    start = side * (low // 2)
                    if chunk != 1:
                        start = start + max(chunk - 1, 0) * low
                        reduce_sum[start : start + low // 2, :] = added
                    else:
                        narrow_sum[start : start + low // 2, :] = added
                if step < steps:
                    made.append(links.copy(source, landing.at[step], target))
        moves_of[chunk, step] = made
        if step == steps and chunk == 1:
            widen_home[me] = widen_back[me]
            for peer in at.peers:
                widen_moves.append(
                    links.copy(widen_back.at[peer], widen_home.at[me], {"exp": peer})
                )
        if step == steps and chunk == 1:
            store(narrow_sum, narrow_out)
        elif step == steps:
            spot = rows(max(chunk - 1, 0) * low, low)
            store(reduce_sum.at[spot], reduce_out.at[spot])
        if step == steps and chunk and chunk % 2 == 0:
            pair = chunk // 2 - 1
            for side in range(2):
                found = joined_lanes(wide_sum[chunk - 2, side], wide_sum[chunk - 1, side])
                for index in range(0, len(found), 1):
                    expand_sum[pair, side, :, index * 128 : index * 128 + 128] = found[index]
            store(expand_sum.at[pair], expand_out.at[pair])

    early = chunks - 2
    order = [(chunk, 0) for chunk in range(early, chunks)] + [
        (chunk, step) for step in range(1, groups) for chunk in (1, 0, *range(2, chunks))
    ]

    def poll(count):
        for _ in range(min(count, len(order))):
            chunk, step = order.pop(0)
            for made in own_loads.pop(step, ()):
                made.wait()
            ring_step(chunk, step)

    kept, stored = [], []

    def store(source, target):
        made = pltpu.make_async_copy(source, target, local_sems.at[4 * groups + 14 + len(stored)])
        made.start(priority=1)
        stored.append(made)

    def load(source, target):
        made = pltpu.make_async_copy(source, target, local_sems.at[len(kept)])
        made.start(priority=1)
        kept.append(made)
        return made

    own_loads = {}

    def load_own(step):
        found = []
        for side, owner in enumerate((at.owner(-1 - step), at.owner(1 + step))):
            spot = rows(owner * block, block)
            found.append(load(wide_grads.at[:, side, spot], wide_own.at[:, side, spot]))
            spot = rows(owner * low + side * (low // 2), low // 2)
            found.append(load(down_grads.at[:, spot], down_own.at[:, spot]))
        own_loads[step] = found

    back_moves = [
        links.copy(back_parts.at[peer], back_recv.at[me], {"exp": peer}) for peer in at.peers
    ]
    first_loads = [
        load(wide_first.at[:, side], wide_recv.at[0:early, side, 0]) for side in range(2)
    ] + [load(down_first.at[:, side], down_recv.at[0:early, side, 0]) for side in range(2)]
    load_own(1)
    poll(2)
    middle_loads = [
        load(back_parts.at[me], back_recv.at[me]),
        load(middle_in, middle_ref),
        load(grads_in, grads_home),
        load(attend_in.at[3], attend_full.at[3]),
        load(saved_in, saved),
    ]
    soft_load = load(soft_in, soft_ref)
    load_own(2)
    attend_load = load(attend_in.at[0:3], attend_full.at[0:3])
    for step in range(3, groups):
        load_own(step)
    result_load = load(result_parts.at[me], result_recv.at[me])
    gate_recv[me] = gate_parts[me]
    for made in first_loads:
        made.wait()
    poll(3)
    result_moves = [
        [
            links.copy(result_parts.at[peer], result_recv.at[me], {"exp": peer}),
            links.copy(gate_parts.at[peer], gate_recv.at[me], {"exp": peer}),
        ]
        for peer in at.peers
    ]
    for made in middle_loads:
        made.wait()
    for move in back_moves:
        move.wait_recv()

    second_grad = back_recv[0].astype(jnp.float32)
    for member in range(1, members):
        second_grad = second_grad + back_recv[member].astype(jnp.float32)
    middle = middle_ref[...]
    scale = rms_factor(middle)
    gain_own[...] = jnp.zeros_like(gain_own)
    gain_own[1:2, :] = jnp.sum(second_grad * (middle * scale), axis=0, keepdims=True)
    input_grad_ref[...] = grads_home[...].astype(jnp.float32) + rms_back(
        middle, scale, second_grad * gains_full[1:2, :]
    )
    middle_low = input_grad_ref[...].astype(jnp.bfloat16)
    turned_ref[3] = nt(middle_low, attend_full[3]).astype(jnp.bfloat16)
    poll(3)
    cosines, sines = cos_ref[...], sin_ref[...]
    lower = first_half((length, 128))
    soft_load.wait()

    def heads(pair, carry):
        lanes = pl.ds(pl.multiple_of(pair * 128, 128), 128)
        query, key, value = saved[0, :, lanes], saved[1, :, lanes], saved[2, :, lanes]
        outer = turned_ref[3, :, lanes]
        made = []
        for side in range(2):
            soft = soft_ref[2 * pair + side]
            alone = jnp.where(lower == (side == 0), outer, jnp.zeros_like(outer))
            value_grad = tn(soft.astype(jnp.bfloat16), outer)
            soft_grad = nt(alone, value)
            score_grad = (
                soft * (soft_grad - jnp.sum(soft * soft_grad, axis=-1, keepdims=True))
            ).astype(jnp.bfloat16)
            made.append(
                (matmul(score_grad, key) * 0.125, tn(score_grad, query) * 0.125, value_grad)
            )
        for index in range(3):
            joined = jnp.where(lower, made[0][index], made[1][index])
            if index < 2:
                joined = joined * cosines - turned(joined) * sines
            turned_ref[index, :, lanes] = joined.astype(jnp.bfloat16)
        return carry

    attend_grad[3] = tn(saved[3], middle_low).astype(jnp.bfloat16)
    for third in range(3):
        lax.fori_loop(2 * third, 2 * third + 2, heads, 0)
        poll(3)
    for matrix in range(3):
        attend_grad[matrix] = tn(saved[4], turned_ref[matrix]).astype(jnp.bfloat16)
    near_moves = [
        links.copy(attend_grad.at[matrix], near_recv.at[index], {"exp": at.near})
        for index, matrix in enumerate((at.near, at.cross))
    ]
    poll(1)
    attend_load.wait()
    first_grad = nt(turned_ref[0], attend_full[0])
    for matrix in range(1, 3):
        first_grad = first_grad + nt(turned_ref[matrix], attend_full[matrix])
    stream = tokens[...].astype(jnp.float32)
    scale = rms_factor(stream)
    gain_own[0:1, :] = jnp.sum(first_grad * (stream * scale), axis=0, keepdims=True)
    gain_moves = [links.copy(gain_own, gain_recv.at[me], {"exp": peer}) for peer in at.peers]
    gain_recv[me] = gain_own[...]
    input_grad_ref[...] += rms_back(stream, scale, first_grad * gains_full[0:1, :])
    store(input_grad_ref, input_grad_out)
    for move in near_moves:
        move.wait_recv()
    far_send[...] = (
        attend_grad[at.far].astype(jnp.float32) + near_recv[1].astype(jnp.float32)
    ).astype(jnp.bfloat16)
    far_move = links.copy(far_send, far_recv, {"exp": at.far})
    poll(2)
    for moves in result_moves:
        for move in moves:
            move.wait_recv()
    result_load.wait()
    output = middle_ref[...]
    for member in range(members):
        output = output + result_recv[member].astype(jnp.float32)
    output_ref[...] = output
    store(output_ref, output_out)
    for choice in range(2):
        route = routes[choice : choice + 1, :]
        found = jnp.zeros((1, length), jnp.float32)
        for member in range(members):
            found = jnp.where(route == member, gate_recv[member, 0:1, :], found)
        gate_grad_ref[choice : choice + 1, :] = found
    poll(3)
    for move in gain_moves:
        move.wait_recv()
    total = gain_recv[0]
    for member in range(1, members):
        total = total + gain_recv[member]
    gain_ring[at.group] = total
    far_move.wait_recv()
    attend_total[...] = (
        attend_grad[me].astype(jnp.float32)
        + near_recv[0].astype(jnp.float32)
        + far_recv[...].astype(jnp.float32)
    ).astype(jnp.bfloat16)

    reach = (groups // 2, groups - 1 - groups // 2)
    small = {}

    def advance_small(step):
        for side, target in enumerate((at.next, at.back)):
            if step > reach[side]:
                continue
            owner = at.owner(reach[side] - step if side == 0 else step - reach[side])
            spot = attend_total.at[rows(owner * block, block), :]
            if step:
                for move in small[step - 1, side]:
                    move.wait_recv()
            if step < reach[side]:
                source = spot
                if step:
                    source = attend_recv.at[side, step - 1]
                    source[...] = (
                        source[...].astype(jnp.float32) + spot[...].astype(jnp.float32)
                    ).astype(jnp.bfloat16)
                line = gain_ring.at[at.owner(-step if side == 0 else step)]
                small[step, side] = (
                    links.copy(source, attend_recv.at[side, step], target),
                    links.copy(line, line, target),
                )

    for step in range(reach[0] + 1):
        advance_small(step)
        poll(2)
    added = attend_total[rows(at.group * block, block), :].astype(jnp.float32)
    for side in range(2):
        added = added + attend_recv[side, reach[side] - 1].astype(jnp.float32)
    for member in range(members):
        attend_back[member] = added[member * share : (member + 1) * share, :]
    attend_moves = [
        links.copy(attend_back.at[peer], attend_sum.at[me], {"exp": peer}) for peer in at.peers
    ]
    attend_sum[me] = attend_back[me]
    total = gain_ring[0]
    for group in range(1, groups):
        total = total + gain_ring[group]
    count = gains_sum.shape[1]
    start = (at.group * members + me) * count
    gains_sum[...] = pltpu.roll(total, width - start, 1)[0:2, 0:count]
    poll(len(order) - 2)
    for move in attend_moves:
        move.wait_recv()
    store(attend_sum.at[0:3], project_out)
    store(attend_sum.at[3], collect_out)
    for move in widen_moves:
        move.wait_recv()
    for matrix in range(2):
        for member in range(0, members, 2):
            found = joined_lanes(widen_home[member, matrix], widen_home[member + 1, matrix])
            for index, part in enumerate(found):
                start = index * 64 * members + member * 64
                widen_sum[matrix, :, start : start + 128] = part
    poll(len(order))
    for made in stored:
        made.wait()
    links.finish()


def update_kernel(rates, fixed, copies, *refs):
    count = len(rates)
    given, made = refs[: 4 * count + copies], refs[4 * count + copies :]
    for index in range(copies):
        made[index][...] = given[4 * count + index][...]

    def update(index):
        weight, moment, variance, gradient = given[4 * index : 4 * index + 4]
        if len(gradient.shape) > len(weight.shape):
            grad = jnp.concatenate(
                [
                    gradient[at % 2, :, :, at // 2 * 128 : at // 2 * 128 + 128]
                    for at in range(weight.shape[-1] // 128)
                ],
                axis=2,
            )
        else:
            grad = gradient[...]
        grad = 0.5 * grad
        level = 1.0 / (1.0 - 0.5**STEP)
        moment_new = 0.5 * moment[...] + grad
        variance_new = 0.5 * variance[...] + 2.0 * grad * grad
        kept = weight[...]
        stepped = moment_new * level / (jnp.sqrt(variance_new * level) + 1e-08) + 0.1 * kept
        made[copies + 3 * index][...] = moment_new
        made[copies + 3 * index + 1][...] = variance_new
        made[copies + 3 * index + 2][...] = kept - rates[index] * stepped

    for index in range(count):
        if fixed[index]:
            pl.when(pl.program_id(0) == 0)(functools.partial(update, index))
        else:
            update(index)


def update_all(*groups, passed):
    cuts = 4

    def spec(dims, cut):
        if cut is None:
            return pl.BlockSpec(dims, lambda step: (0,) * len(dims))
        block = tuple(size // cuts if at == cut else size for at, size in enumerate(dims))
        return pl.BlockSpec(
            block, lambda step: tuple(step if at == cut else 0 for at in range(len(dims)))
        )

    def cut_of(array):
        dims = array.shape
        for at in range(len(dims) - 1):
            if array.size > 100000 and dims[at] % (8 * cuts) == 0:
                return at
        return len(dims) - 1 if dims[-1] % (128 * cuts) == 0 else None

    given, specs, shapes, out_specs = [], [], [], []
    for _, weight, moment, variance, gradient in groups:
        cut = cut_of(weight)
        for array in (weight, moment, variance, gradient):
            given.append(array)
            more = array.ndim - weight.ndim
            specs.append(spec(array.shape, None if cut is None else cut + more))
        for array in (weight, moment, variance):
            shapes.append(jax.ShapeDtypeStruct(array.shape, array.dtype))
            out_specs.append(spec(array.shape, cut))
    extra = [spec(array.shape, cut_of(array)) for array in passed]
    return pl.pallas_call(
        functools.partial(
            update_kernel,
            [group[0] for group in groups],
            [cut_of(group[1]) is None for group in groups],
            len(passed),
        ),
        grid=(cuts,),
        out_shape=[jax.ShapeDtypeStruct(array.shape, array.dtype) for array in passed] + shapes,
        in_specs=specs + extra,
        out_specs=extra + out_specs,
        compiler_params=pltpu.CompilerParams(vmem_limit_bytes=LIMIT),
    )(*given, *passed)


def rotary_lines(length):
    half = HEAD_FEATURES // 2
    freqs = np.exp(-np.log(10000.0) * np.arange(half) / half)
    angles = np.arange(length)[:, None] * freqs[None, :]
    cosines, sines = np.cos(angles), np.sin(angles)
    return (
        np.concatenate([cosines] * 4, axis=1).astype(np.float32),
        np.concatenate([-sines, sines] * 2, axis=1).astype(np.float32),
    )


def spaces(*names):
    kinds = {"v": pltpu.VMEM, "s": pltpu.SMEM, "a": pl.ANY}
    return [pl.BlockSpec(memory_space=kinds[name]) for name in "".join(names)]


def local(
    tokens,
    seq_lengths,
    deal_order,
    expert_routes,
    capacity_slots,
    gate_weights,
    cotangent,
    projector,
    projector_mean,
    projector_square,
    collector,
    collector_first_moment,
    collector_second_moment,
    widener,
    widener_mean,
    widener_square,
    narrower,
    narrower_mean,
    narrower_square,
    norm_gains,
    gains_mean,
    gains_square,
    expander,
    expander_mean,
    expander_square,
    reducer,
    reducer_mean,
    reducer_square,
):
    groups, members = lax.axis_size("grp"), lax.axis_size("exp")
    length, width = tokens.shape[1:]
    inner = expander.shape[3]
    piece = widener.shape[2] // members
    chunks = 1 + inner // piece
    capacity = 3 * length // members
    steps = groups - 1
    high, low, share = expander.shape[2], narrower.shape[0], projector.shape[1]
    bf16, f32 = jnp.bfloat16, jnp.float32
    shape = jax.ShapeDtypeStruct
    cosines, sines = (jnp.asarray(lines) for lines in rotary_lines(length))
    count = 16 * groups
    (
        wide_grads,
        down_grads,
        wide_first,
        down_first,
        attend_full,
        grads_all,
        saved,
        middle,
        soft,
        result_parts,
        back_parts,
        gains_full,
        gate_parts,
    ) = pl.pallas_call(
        functools.partial(gather_kernel, groups, members),
        out_shape=[
            shape((chunks, 2, width, piece), bf16),
            shape((chunks, piece, width), bf16),
            shape((chunks - 2, 2, high, piece), bf16),
            shape((chunks - 2, 2, low // 2, width), bf16),
            shape((4, width, width), bf16),
            shape((length, width), bf16),
            shape((5, length, width), bf16),
            shape((length, width), f32),
            shape((HEAD_COUNT, length, length), f32),
            shape((members, length, width), bf16),
            shape((members, length, width), bf16),
            shape((8, width), f32),
            shape((members, 8, length), f32),
        ],
        in_specs=spaces("ssvavvvvvvaaaavv"),
        out_specs=spaces("a" * 11, "vv"),
        scratch_shapes=[
            VMEM((length, width), f32),
            VMEM(widener.shape, f32),
            VMEM(narrower.shape, f32),
            VMEM(expander.shape[1:], f32),
            VMEM(reducer.shape[1:], f32),
            VMEM((members, length, width), bf16),
            VMEM((members, length, width), bf16),
            VMEM((length, width), bf16),
            VMEM((4, width, width), bf16),
            VMEM((members, length, width), bf16),
            VMEM((5, length, width), bf16),
            VMEM((length, width), f32),
            VMEM((HEAD_COUNT, length, length), f32),
            VMEM((members, length, width), bf16),
            VMEM((members, 8, length), f32),
            VMEM((members, 8, length), f32),
            VMEM((4, share, width), f32),
            VMEM((4, share, width), f32),
            VMEM((members, 2, share, piece), f32),
            VMEM((members, 2, share, piece), f32),
            VMEM((8, width), f32),
            VMEM((members, 8, width), f32),
            VMEM((groups, 8, width), f32),
            VMEM((chunks, 2, width, piece), bf16),
            VMEM((chunks, piece, width), bf16),
            VMEM((chunks, 2, high, piece), bf16),
            VMEM((chunks, low, width), bf16),
            VMEM((members * length, width), bf16),
            VMEM((width, members * length), bf16),
            VMEM((members, length, width), f32),
            VMEM((members, length, width), f32),
            VMEM((members * capacity, width), bf16),
            VMEM((width, members * capacity), bf16),
            VMEM((members * capacity, width), bf16),
            VMEM((members * capacity, width), f32),
            VMEM((members * capacity, width), f32),
            pltpu.SemaphoreType.DMA((count,)),
            pltpu.SemaphoreType.DMA((count,)),
            pltpu.SemaphoreType.DMA((chunks * steps * 4,)),
            pltpu.SemaphoreType.DMA((chunks * steps * 4,)),
            pltpu.SemaphoreType.DMA((chunks * 4,)),
            pltpu.SemaphoreType.DMA((chunks * 4,)),
            pltpu.SemaphoreType.DMA((2 * chunks + 10 + 2 * members,)),
        ],
        compiler_params=pltpu.CompilerParams(
            collective_id=0, has_side_effects=True, vmem_limit_bytes=LIMIT
        ),
    )(
        seq_lengths,
        deal_order,
        tokens[0],
        cotangent[0],
        expert_routes[0].T,
        capacity_slots[0].T,
        gate_weights[0].T,
        norm_gains,
        projector,
        collector,
        widener,
        narrower,
        expander[0],
        reducer[0],
        cosines,
        sines,
    )
    count = 32 * groups
    (
        output,
        input_grad,
        expand_sum,
        reduce_sum,
        narrow_sum,
        project_sum,
        collect_sum,
        gate_grad,
        widen_sum,
        gains_sum,
    ) = pl.pallas_call(
        functools.partial(scatter_kernel, groups, members),
        out_shape=[
            shape((length, width), f32),
            shape((length, width), f32),
            shape((2, 2, high, inner // 2), f32),
            shape(reducer.shape[1:], f32),
            shape(narrower.shape, f32),
            shape(projector.shape, f32),
            shape(collector.shape, f32),
            shape((2, length), f32),
            shape(widener.shape, f32),
            shape(norm_gains.shape, f32),
        ],
        in_specs=spaces("v" * 6, "a" * 11),
        out_specs=spaces("a" * 7, "vvv"),
        scratch_shapes=[
            VMEM((2, 2, high, inner // 2), f32),
            VMEM(reducer.shape[1:], f32),
            VMEM(narrower.shape, f32),
            VMEM((length, width), f32),
            VMEM((length, width), f32),
            VMEM((4, share, width), f32),
            VMEM((length, width), bf16),
            VMEM((length, width), f32),
            VMEM((4, width, width), bf16),
            VMEM((5, length, width), bf16),
            VMEM((HEAD_COUNT, length, length), f32),
            VMEM((members, 8, length), f32),
            VMEM((members, length, width), bf16),
            VMEM((members, length, width), bf16),
            VMEM((chunks, 2, width, piece), bf16),
            VMEM((chunks, piece, width), bf16),
            VMEM((chunks, 2, steps, high, piece), bf16),
            VMEM((chunks, 2, steps, low // 2, width), bf16),
            VMEM((chunks - 1, 2, high, piece), f32),
            VMEM((4, length, width), bf16),
            VMEM((4, width, width), bf16),
            VMEM((2, width, width), bf16),
            VMEM((width, width), bf16),
            VMEM((width, width), bf16),
            VMEM((width, width), bf16),
            VMEM((2, groups // 2, high, width), bf16),
            VMEM((4, share, width), f32),
            VMEM((members, 2, share, piece), f32),
            VMEM((members, 2, share, piece), f32),
            VMEM((8, width), f32),
            VMEM((members, 8, width), f32),
            VMEM((groups, 8, width), f32),
            pltpu.SemaphoreType.DMA((count,)),
            pltpu.SemaphoreType.DMA((count,)),
            pltpu.SemaphoreType.DMA((4 * groups + 32,)),
        ],
        compiler_params=pltpu.CompilerParams(
            collective_id=1, has_side_effects=True, vmem_limit_bytes=LIMIT
        ),
    )(
        tokens[0],
        expert_routes[0].T,
        gains_full,
        cosines,
        sines,
        gate_parts,
        result_parts,
        back_parts,
        wide_grads,
        down_grads,
        wide_first,
        down_first,
        grads_all,
        middle,
        attend_full,
        saved,
        soft,
    )
    updated = update_all(
        (0.1, projector, projector_mean, projector_square, project_sum),
        (0.3, collector, collector_first_moment, collector_second_moment, collect_sum),
        (0.07, widener, widener_mean, widener_square, widen_sum),
        (0.045, narrower, narrower_mean, narrower_square, narrow_sum),
        (0.2, norm_gains, gains_mean, gains_square, gains_sum),
        (0.07, expander[0], expander_mean[0], expander_square[0], expand_sum),
        (0.045, reducer[0], reducer_mean[0], reducer_square[0], reduce_sum),
        passed=(output, input_grad),
    )
    return (
        updated[0][None],
        updated[1][None],
        gate_grad.T[None],
        *updated[2:17],
        *(found[None] for found in updated[17:]),
    )


def fits(mesh):
    groups, members = mesh.shape["grp"], mesh.shape["exp"]
    share = 64 * HEAD_COUNT // (groups * members)
    return members == 4 and groups % 2 == 0 and share % 8 == 0 and share * members // 2 % 16 == 0


def solution(mesh):
    placed = (
        P(("grp", "exp"), None, None),
        P("grp"),
        P("grp"),
        P(("grp", "exp"), None, None),
        P(("grp", "exp"), None, None),
        P(("grp", "exp"), None, None),
        P(("grp", "exp"), None, None),
        P(None, ("grp", "exp"), None),
        P(None, ("grp", "exp"), None),
        P(None, ("grp", "exp"), None),
        P(("grp", "exp"), None),
        P(("grp", "exp"), None),
        P(("grp", "exp"), None),
        P(None, ("grp", "exp"), None),
        P(None, ("grp", "exp"), None),
        P(None, ("grp", "exp"), None),
        P(("grp", "exp"), None),
        P(("grp", "exp"), None),
        P(("grp", "exp"), None),
        P(None, ("grp", "exp")),
        P(None, ("grp", "exp")),
        P(None, ("grp", "exp")),
        P("exp", None, "grp", None),
        P("exp", None, "grp", None),
        P("exp", None, "grp", None),
        P("exp", "grp", None),
        P("exp", "grp", None),
        P("exp", "grp", None),
    )
    return jax.shard_map(
        local if fits(mesh) else local_plain,
        mesh=mesh,
        in_specs=placed,
        out_specs=(
            P(("grp", "exp"), None, None),
            P(("grp", "exp"), None, None),
            P(("grp", "exp"), None, None),
            P(None, ("grp", "exp"), None),
            P(None, ("grp", "exp"), None),
            P(None, ("grp", "exp"), None),
            P(("grp", "exp"), None),
            P(("grp", "exp"), None),
            P(("grp", "exp"), None),
            P(None, ("grp", "exp"), None),
            P(None, ("grp", "exp"), None),
            P(None, ("grp", "exp"), None),
            P(("grp", "exp"), None),
            P(("grp", "exp"), None),
            P(("grp", "exp"), None),
            P(None, ("grp", "exp")),
            P(None, ("grp", "exp")),
            P(None, ("grp", "exp")),
            P("exp", None, "grp", None),
            P("exp", None, "grp", None),
            P("exp", None, "grp", None),
            P("exp", "grp", None),
            P("exp", "grp", None),
            P("exp", "grp", None),
        ),
        check_vma=False,
    )
```

```python
import functools

import jax
import jax.numpy as jnp
import numpy as np
from jax import lax
from jax.experimental import pallas as pl
from jax.experimental.pallas import tpu as pltpu
from jax.sharding import PartitionSpec as P

HEAD_COUNT = 12
HEAD_FEATURES = 64
STEP = 5


def rms_factor(values):
    return lax.rsqrt(jnp.mean(values * values, axis=-1, keepdims=True) + 1e-06)


def rms_back(values, factor, upstream):
    return factor * (
        upstream - values * factor * factor * jnp.mean(upstream * values, axis=-1, keepdims=True)
    )


def rotary(length):
    positions = jnp.arange(length, dtype=jnp.int32).astype(jnp.float32)
    half = HEAD_FEATURES // 2
    freqs = jnp.exp(
        -jnp.log(10000.0) * jnp.arange(half, dtype=jnp.int32).astype(jnp.float32) / half
    )
    angles = positions[:, None] * freqs[None, :]
    return (jnp.cos(angles)[:, None, :], jnp.sin(angles)[:, None, :])


def rotate(values, cosines, sines):
    half = values.shape[-1] // 2
    first = values[..., :half]
    second = values[..., half:]
    return jnp.concatenate(
        [first * cosines - second * sines, second * cosines + first * sines], axis=-1
    )


def rotate_back(values, cosines, sines):
    half = values.shape[-1] // 2
    first = values[..., :half]
    second = values[..., half:]
    return jnp.concatenate(
        [first * cosines + second * sines, second * cosines - first * sines], axis=-1
    )


def silu_slope(values):
    sigmoid_of = jax.nn.sigmoid(values)
    return sigmoid_of * (1.0 + values * (1.0 - sigmoid_of))


def matmul(left, right):
    return jnp.dot(left, right, preferred_element_type=jnp.float32)


def outer_sum(left, right):
    return jnp.einsum("ld,lf->df", left, right, preferred_element_type=jnp.float32)


def adamw_update(weight, moment, variance, gradient, rate):
    moment_new = 0.5 * moment + 0.5 * gradient
    variance_new = 0.5 * variance + 0.5 * gradient * gradient
    correct = 1.0 - 0.5**STEP
    stepped = moment_new / correct / (jnp.sqrt(variance_new / correct) + 1e-08) + 0.1 * weight
    return (moment_new, variance_new, weight - rate * stepped)


def local_plain(
    tokens,
    seq_lengths,
    deal_order,
    expert_routes,
    capacity_slots,
    gate_weights,
    cotangent,
    projector,
    projector_mean,
    projector_square,
    collector,
    collector_first_moment,
    collector_second_moment,
    widener,
    widener_mean,
    widener_square,
    narrower,
    narrower_mean,
    narrower_square,
    norm_gains,
    gains_mean,
    gains_square,
    expander,
    expander_mean,
    expander_square,
    reducer,
    reducer_mean,
    reducer_square,
):
    members = lax.axis_size("exp")
    member = lax.axis_index("exp")
    length_seq = tokens.shape[1]
    width = tokens.shape[2]
    local_experts = expander.shape[0]
    experts_all = local_experts * members
    capacity = 3 * length_seq // experts_all
    member_ids = jnp.arange(members, dtype=jnp.int32)
    source = deal_order[member]
    home_slot = jnp.sum(jnp.where(deal_order == member, member_ids, 0))
    seq_length = seq_lengths[source]
    piece = lax.all_gather(tokens, "exp", axis=0, tiled=True)
    chosen = jnp.arange(piece.shape[0], dtype=jnp.int32) == source
    dealt = jnp.sum(
        jnp.where(chosen[:, None, None], piece, jnp.zeros_like(piece)), axis=0, keepdims=True
    )
    residual_flow = dealt[0].astype(jnp.float32)
    project_full, collect_full, widen_full, narrow_full, gains_full = (
        lax.all_gather(projector.astype(jnp.bfloat16), ("grp", "exp"), axis=1, tiled=True),
        lax.all_gather(collector.astype(jnp.bfloat16), ("grp", "exp"), axis=0, tiled=True),
        lax.all_gather(widener.astype(jnp.bfloat16), ("grp", "exp"), axis=1, tiled=True),
        lax.all_gather(narrower.astype(jnp.bfloat16), ("grp", "exp"), axis=0, tiled=True),
        lax.all_gather(norm_gains.astype(jnp.bfloat16), ("grp", "exp"), axis=1, tiled=True),
    )
    expand_full, reduce_full = (
        lax.all_gather(expander.astype(jnp.bfloat16), "grp", axis=2, tiled=True),
        lax.all_gather(reducer.astype(jnp.bfloat16), "grp", axis=1, tiled=True),
    )
    gains_used = gains_full.astype(jnp.float32)
    cosines, sines = rotary(length_seq)
    scale_one = rms_factor(residual_flow)
    normed_one = residual_flow * scale_one
    first_input = (normed_one * gains_used[0]).astype(jnp.bfloat16)
    query_raw = matmul(first_input, project_full[0]).reshape(length_seq, HEAD_COUNT, HEAD_FEATURES)
    key_raw = matmul(first_input, project_full[1]).reshape(length_seq, HEAD_COUNT, HEAD_FEATURES)
    value_raw = matmul(first_input, project_full[2]).reshape(length_seq, HEAD_COUNT, HEAD_FEATURES)
    query_rot = rotate(query_raw, cosines, sines).astype(jnp.bfloat16)
    key_rot = rotate(key_raw, cosines, sines).astype(jnp.bfloat16)
    value_low = value_raw.astype(jnp.bfloat16)
    rows_at = jnp.arange(length_seq, dtype=jnp.int32)[:, None]
    cols_at = jnp.arange(length_seq, dtype=jnp.int32)[None, :]
    allowed = ((cols_at <= rows_at) & (cols_at < seq_length))[None]
    scores = (
        jnp.einsum("qhd,khd->hqk", query_rot, key_rot, preferred_element_type=jnp.float32) * 0.125
    )
    masked = jnp.where(allowed, scores, -1e30)
    top = jnp.max(masked, axis=-1, keepdims=True)
    expo = jnp.exp(masked - top)
    total = jnp.sum(expo, axis=-1, keepdims=True)
    soft = expo / total
    logsum = top + jnp.log(total)
    mixed_output = (
        jnp.einsum(
            "hqk,khd->qhd", soft.astype(jnp.bfloat16), value_low, preferred_element_type=jnp.float32
        )
        .reshape(length_seq, width)
        .astype(jnp.bfloat16)
    )
    middle_state = residual_flow + matmul(mixed_output, collect_full)
    scale_two = rms_factor(middle_state)
    normed_two = middle_state * scale_two
    second_input = (normed_two * gains_used[1]).astype(jnp.bfloat16)
    gating_scores = matmul(second_input, widen_full[0])
    upward_rows = matmul(second_input, widen_full[1])
    hidden_state = (jax.nn.silu(gating_scores) * upward_rows).astype(jnp.bfloat16)
    dense_branch = matmul(hidden_state, narrow_full)
    flat = (expert_routes[0] * capacity + capacity_slots[0]).reshape(-1)
    spread = jnp.repeat(second_input, 2, axis=0)
    dispatch = jnp.zeros((experts_all * capacity, width), jnp.bfloat16).at[flat].set(spread)
    dispatch = dispatch.reshape(experts_all, capacity, width)
    rows = lax.all_to_all(dispatch, "exp", split_axis=0, concat_axis=0, tiled=True)
    count = rows.shape[1]
    grouped = rows.reshape(members, local_experts, count, width)
    gate_pre = jnp.einsum(
        "sekd,edf->sekf", grouped, expand_full[:, 0], preferred_element_type=jnp.float32
    )
    up_pre = jnp.einsum(
        "sekd,edf->sekf", grouped, expand_full[:, 1], preferred_element_type=jnp.float32
    )
    hidden_rows = (jax.nn.silu(gate_pre) * up_pre).astype(jnp.bfloat16)
    result = jnp.einsum(
        "sekf,efd->sekd", hidden_rows, reduce_full, preferred_element_type=jnp.float32
    )
    result = result.astype(jnp.bfloat16).reshape(members * local_experts, count, width)
    returned_rows = lax.all_to_all(result, "exp", split_axis=0, concat_axis=0, tiled=True)
    outcome = (
        returned_rows,
        rows,
        gate_pre.reshape(members * local_experts, count, -1),
        up_pre.reshape(members * local_experts, count, -1),
    )
    returned, received, gate_kept, up_kept = outcome
    picked = (
        returned.reshape(experts_all * capacity, width)[flat]
        .reshape(length_seq, 2, width)
        .astype(jnp.float32)
    )
    gate_local = gate_weights[0]
    mixture = jnp.sum(gate_local[..., None] * picked, axis=1)
    layer_output = middle_state + dense_branch + mixture
    valid = (jnp.arange(length_seq, dtype=jnp.int32) < seq_length).astype(jnp.float32)
    grad_out = cotangent[0] * valid[:, None]
    grad_low = grad_out.astype(jnp.bfloat16)
    narrow_grad = outer_sum(hidden_state, grad_low)
    hidden_grad = jnp.einsum("ld,fd->lf", grad_low, narrow_full, preferred_element_type=jnp.float32)
    gating_grad = (hidden_grad * upward_rows * silu_slope(gating_scores)).astype(jnp.bfloat16)
    upward_grad = (hidden_grad * jax.nn.silu(gating_scores)).astype(jnp.bfloat16)
    widen_grad = jnp.stack(
        [outer_sum(second_input, gating_grad), outer_sum(second_input, upward_grad)]
    )
    second_grad = jnp.einsum(
        "lf,df->ld", gating_grad, widen_full[0], preferred_element_type=jnp.float32
    ) + jnp.einsum("lf,df->ld", upward_grad, widen_full[1], preferred_element_type=jnp.float32)
    gate_grad_local = jnp.sum(grad_out[:, None, :] * picked, axis=-1)
    result_grad = (
        (gate_local[..., None] * grad_out[:, None, :])
        .astype(jnp.bfloat16)
        .reshape(2 * length_seq, width)
    )
    grad_send = jnp.zeros((experts_all * capacity, width), jnp.bfloat16).at[flat].set(result_grad)
    grad_recv = lax.all_to_all(
        grad_send.reshape(experts_all, capacity, width),
        "exp",
        split_axis=0,
        concat_axis=0,
        tiled=True,
    )
    grad_group = grad_recv.reshape(members, local_experts, capacity, width)
    rows_group = received.reshape(members, local_experts, capacity, width)
    gate_pre = gate_kept.reshape(members, local_experts, capacity, -1)
    up_pre = up_kept.reshape(members, local_experts, capacity, -1)
    hidden_rows = (jax.nn.silu(gate_pre) * up_pre).astype(jnp.bfloat16)
    reduce_grad = jnp.einsum(
        "sekf,sekd->efd", hidden_rows, grad_group, preferred_element_type=jnp.float32
    )
    hidden_rows_grad = jnp.einsum(
        "sekd,efd->sekf", grad_group, reduce_full, preferred_element_type=jnp.float32
    )
    gate_rows_grad = (hidden_rows_grad * up_pre * silu_slope(gate_pre)).astype(jnp.bfloat16)
    up_rows_grad = (hidden_rows_grad * jax.nn.silu(gate_pre)).astype(jnp.bfloat16)
    expand_grad = jnp.stack(
        [
            jnp.einsum(
                "sekd,sekf->edf", rows_group, gate_rows_grad, preferred_element_type=jnp.float32
            ),
            jnp.einsum(
                "sekd,sekf->edf", rows_group, up_rows_grad, preferred_element_type=jnp.float32
            ),
        ],
        axis=1,
    )
    row_grads = jnp.einsum(
        "sekf,edf->sekd", gate_rows_grad, expand_full[:, 0], preferred_element_type=jnp.float32
    ) + jnp.einsum(
        "sekf,edf->sekd", up_rows_grad, expand_full[:, 1], preferred_element_type=jnp.float32
    )
    row_grads = row_grads.astype(jnp.bfloat16).reshape(experts_all, capacity, width)
    came_back = lax.all_to_all(row_grads, "exp", split_axis=0, concat_axis=0, tiled=True).reshape(
        experts_all * capacity, width
    )
    second_grad = second_grad + jnp.sum(
        came_back[flat].reshape(length_seq, 2, width).astype(jnp.float32), axis=1
    )
    gains_grad_two = jnp.sum(second_grad * normed_two, axis=0)
    middle_grad = grad_out + rms_back(middle_state, scale_two, second_grad * gains_used[1])
    middle_low = middle_grad.astype(jnp.bfloat16)
    collect_grad = outer_sum(mixed_output, middle_low)
    mixed_grad = jnp.einsum(
        "ld,ed->le", middle_low, collect_full, preferred_element_type=jnp.float32
    )
    mixed_grad = mixed_grad.astype(jnp.bfloat16).reshape(length_seq, HEAD_COUNT, HEAD_FEATURES)
    scores_again = (
        jnp.einsum("qhd,khd->hqk", query_rot, key_rot, preferred_element_type=jnp.float32) * 0.125
    )
    soft_again = jnp.where(allowed, jnp.exp(scores_again - logsum), 0.0)
    value_grad = jnp.einsum(
        "hqk,qhd->khd",
        soft_again.astype(jnp.bfloat16),
        mixed_grad,
        preferred_element_type=jnp.float32,
    )
    soft_grad = jnp.einsum(
        "qhd,khd->hqk", mixed_grad, value_low, preferred_element_type=jnp.float32
    )
    score_grad = (
        soft_again * (soft_grad - jnp.sum(soft_again * soft_grad, axis=-1, keepdims=True))
    ).astype(jnp.bfloat16)
    query_grad = (
        jnp.einsum("hqk,khd->qhd", score_grad, key_rot, preferred_element_type=jnp.float32) * 0.125
    )
    key_grad = (
        jnp.einsum("hqk,qhd->khd", score_grad, query_rot, preferred_element_type=jnp.float32)
        * 0.125
    )
    query_back = (
        rotate_back(query_grad, cosines, sines).reshape(length_seq, width).astype(jnp.bfloat16)
    )
    key_back = rotate_back(key_grad, cosines, sines).reshape(length_seq, width).astype(jnp.bfloat16)
    value_back = value_grad.reshape(length_seq, width).astype(jnp.bfloat16)
    project_grad = jnp.stack(
        [
            outer_sum(first_input, query_back),
            outer_sum(first_input, key_back),
            outer_sum(first_input, value_back),
        ]
    )
    first_grad = (
        jnp.einsum("le,de->ld", query_back, project_full[0], preferred_element_type=jnp.float32)
        + jnp.einsum("le,de->ld", key_back, project_full[1], preferred_element_type=jnp.float32)
        + jnp.einsum("le,de->ld", value_back, project_full[2], preferred_element_type=jnp.float32)
    )
    gains_grad_one = jnp.sum(first_grad * normed_one, axis=0)
    stream_grad = middle_grad + rms_back(residual_flow, scale_one, first_grad * gains_used[0])
    gains_grad = jnp.stack([gains_grad_one, gains_grad_two])
    project_part, collect_part, widen_part, narrow_part, gains_part = (
        lax.psum_scatter(project_grad, ("grp", "exp"), scatter_dimension=1, tiled=True),
        lax.psum_scatter(collect_grad, ("grp", "exp"), scatter_dimension=0, tiled=True),
        lax.psum_scatter(widen_grad, ("grp", "exp"), scatter_dimension=1, tiled=True),
        lax.psum_scatter(narrow_grad, ("grp", "exp"), scatter_dimension=0, tiled=True),
        lax.psum_scatter(gains_grad, ("grp", "exp"), scatter_dimension=1, tiled=True),
    )
    expand_part, reduce_part = (
        lax.psum_scatter(
            expand_grad.astype(jnp.bfloat16), "grp", scatter_dimension=2, tiled=True
        ).astype(jnp.float32),
        lax.psum_scatter(
            reduce_grad.astype(jnp.bfloat16), "grp", scatter_dimension=1, tiled=True
        ).astype(jnp.float32),
    )
    empty = jnp.zeros((1, length_seq, width), jnp.float32)
    pieces = (
        lax.all_gather(layer_output[None].astype(jnp.bfloat16), "exp", axis=0, tiled=True).astype(
            jnp.float32
        ),
        lax.all_gather(stream_grad[None].astype(jnp.bfloat16), "exp", axis=0, tiled=True).astype(
            jnp.float32
        ),
    )
    chosen = (jnp.arange(pieces[0].shape[0], dtype=jnp.int32) == home_slot)[:, None, None]
    homed_output = empty + jnp.sum(jnp.where(chosen, pieces[0], 0.0), axis=0, keepdims=True)
    homed_grad = empty + jnp.sum(jnp.where(chosen, pieces[1], 0.0), axis=0, keepdims=True)
    project_new = adamw_update(projector, projector_mean, projector_square, project_part, 0.1)
    collect_new = adamw_update(
        collector, collector_first_moment, collector_second_moment, collect_part, 0.3
    )
    widening_updated = adamw_update(widener, widener_mean, widener_square, widen_part, 0.07)
    narrowing_updated = adamw_update(narrower, narrower_mean, narrower_square, narrow_part, 0.045)
    gains_updated = adamw_update(norm_gains, gains_mean, gains_square, gains_part, 0.2)
    expansion_updated = adamw_update(expander, expander_mean, expander_square, expand_part, 0.07)
    reduction_updated = adamw_update(reducer, reducer_mean, reducer_square, reduce_part, 0.045)
    return (
        homed_output,
        homed_grad,
        gate_grad_local[None],
        project_new[0],
        project_new[1],
        project_new[2],
        collect_new[0],
        collect_new[1],
        collect_new[2],
        widening_updated[0],
        widening_updated[1],
        widening_updated[2],
        narrowing_updated[0],
        narrowing_updated[1],
        narrowing_updated[2],
        gains_updated[0],
        gains_updated[1],
        gains_updated[2],
        expansion_updated[0],
        expansion_updated[1],
        expansion_updated[2],
        reduction_updated[0],
        reduction_updated[1],
        reduction_updated[2],
    )


MESH = pl.DeviceIdType.MESH
VMEM = pltpu.VMEM
LIMIT = 60 * 1024 * 1024


def ring_place(index, groups):
    row, side = lax.div(index, 2), lax.rem(index, 2)
    return (1 - side) * row + side * (groups - 1 - row)


def ring_member(place, groups):
    side = lax.div(place, groups // 2)
    return 2 * ((1 - side) * place + side * (groups - 1 - place)) + side


def remote(source, target, sends, arrivals, at, device):
    return pltpu.make_async_remote_copy(
        src_ref=source,
        dst_ref=target,
        send_sem=sends.at[at],
        recv_sem=arrivals.at[at],
        device_id=device,
        device_id_type=MESH,
    )


class Links:
    def __init__(self, sends, arrivals):
        self.sends, self.arrivals, self.count, self.started = sends, arrivals, 0, []

    def copy(self, source, target, device):
        made = remote(source, target, self.sends, self.arrivals, self.count, device)
        self.count += 1
        made.start()
        self.started.append(made)
        return made

    def finish(self):
        for made in self.started:
            made.wait_send()


class Places:
    def __init__(self, groups, members):
        self.groups, self.members = groups, members
        self.group = lax.axis_index("grp")
        self.member = lax.axis_index("exp")
        self.place = ring_place(self.group, groups)
        self.next = {"grp": self.owner(1)}
        self.back = {"grp": self.owner(-1)}
        half = members // 2
        self.far = lax.rem(self.member + half, members)
        self.near = self.member + 1 - 2 * lax.rem(self.member, 2)
        self.cross = lax.rem(self.near + half, members)
        self.peers = [lax.rem(self.member + step, members) for step in range(1, members)]

    def owner(self, offset):
        place = lax.rem(self.place + offset + 2 * self.groups, self.groups)
        return ring_member(place, self.groups)

    def enter(self):
        barrier = pltpu.get_barrier_semaphore()
        partners = [self.next, self.back] + [{"exp": peer} for peer in self.peers]
        for partner in partners:
            pl.semaphore_signal(barrier, inc=1, device_id=partner, device_id_type=MESH)
        pl.semaphore_wait(barrier, len(partners))


def rows(start, count, align=16):
    return pl.ds(pl.multiple_of(start, align), count)


def first_half(shape):
    return lax.rem(lax.broadcasted_iota(jnp.int32, shape, len(shape) - 1), 128) < 64


def turned(values):
    lanes = lax.broadcasted_iota(jnp.int32, values.shape, 1)
    return jnp.where(
        lax.rem(lanes, HEAD_FEATURES) < HEAD_FEATURES // 2,
        pltpu.roll(values, 128 - HEAD_FEATURES // 2, 1),
        pltpu.roll(values, HEAD_FEATURES // 2, 1),
    )


def nt(left, right):
    return lax.dot_general(
        left, right, (((1,), (1,)), ((), ())), preferred_element_type=jnp.float32
    )


def tn(left, right):
    return lax.dot_general(
        left, right, (((0,), (0,)), ((), ())), preferred_element_type=jnp.float32
    )


def sigmoid(values):
    return 1.0 / (1.0 + jnp.exp(-values))


def same(length):
    shape = (length, length)
    return lax.broadcasted_iota(jnp.int32, shape, 0) == lax.broadcasted_iota(jnp.int32, shape, 1)


def upright(line):
    return jnp.sum(jnp.where(same(line.shape[1]), line, 0.0), axis=1, keepdims=True)


def lying(column):
    return jnp.sum(jnp.where(same(column.shape[0]), column, 0.0), axis=0, keepdims=True)


def slot_of(deal_ref, member):
    for _ in range(11):
        member = deal_ref[member]
    return member


def dealt_lanes(values, piece, pieces):
    low_lanes = lax.broadcasted_iota(jnp.int32, (values.shape[0], 128), 1) < 64
    found = []
    span = 64 * pieces
    for start in range(0, values.shape[1], 2 * span):
        start = start + piece // 2 * 128
        one, two = values[:, start : start + 128], values[:, start + span : start + span + 128]
        if piece % 2:
            one = pltpu.roll(one, 64, 1)
        else:
            two = pltpu.roll(two, 64, 1)
        found.append(jnp.where(low_lanes, one, two))
    return jnp.concatenate(found, axis=1)


def joined_lanes(even, odd):
    low_lanes = lax.broadcasted_iota(jnp.int32, (even.shape[0], 128), 1) < 64
    found = []
    for start in range(0, even.shape[1], 128):
        one, two = even[:, start : start + 128], odd[:, start : start + 128]
        found.append(jnp.where(low_lanes, one, pltpu.roll(two, 64, 1)))
        found.append(jnp.where(low_lanes, pltpu.roll(one, 64, 1), two))
    return found


def gather_kernel(
    groups,
    members,
    length_ref,
    deal_ref,
    tokens,
    cotangent_in,
    routes,
    places,
    gates,
    norm_gains,
    projector,
    collector,
    widener_in,
    narrower_in,
    expander_in,
    reducer_in,
    cos_ref,
    sin_ref,
    wide_grads,
    down_grads,
    wide_first,
    down_first,
    attend_out,
    grads_out,
    saved_out,
    middle_out,
    soft_out,
    result_out,
    back_out,
    gains_full,
    gate_ref,
    cotangent,
    widener,
    narrower,
    expander,
    reducer,
    result_ref,
    back_ref,
    grads_home,
    attend_full,
    grads_all,
    saved,
    middle_ref,
    soft_ref,
    second_all,
    meta_send,
    meta_all,
    attend_send,
    attend_recv,
    widen_send,
    widen_recv,
    gains,
    gain_recv,
    gain_ring,
    wide_full,
    down_full,
    wide_own,
    down_own,
    inputs_ref,
    inputs_turned,
    dense_out,
    dense_back,
    rows_in,
    rows_turned,
    rows_grad,
    rows_out,
    rows_back,
    sends,
    arrivals,
    ring_sends,
    ring_arrivals,
    first_sends,
    first_arrivals,
    local_sems,
):
    at = Places(groups, members)
    links = Links(sends, arrivals)
    chunks, low = down_own.shape[:2]
    loads = {}
    for name, source, target in (
        ("expander", expander_in, expander),
        ("reducer", reducer_in, reducer),
        ("widener", widener_in, widener),
        ("narrower", narrower_in, narrower),
        ("cotangent", cotangent_in, cotangent),
    ):
        made = pltpu.make_async_copy(source, target, local_sems.at[2 * chunks + len(loads)])
        made.start(priority=1)
        loads[name] = made
    at.enter()
    me, steps = at.member, groups - 1
    share, width = projector.shape[1:]
    block = share * members
    length = tokens.shape[0]
    capacity = rows_in.shape[0] // members

    def ring_copy(chunk, step, side, piece):
        owner = at.owner(-step if side == 0 else step)
        if piece == 0:
            spot = wide_full.at[chunk, side, rows(owner * block, block), :]
            origin = wide_own.at[chunk, side]
        else:
            spot = down_full.at[chunk, rows(owner * low + side * (low // 2), low // 2), :]
            origin = down_own.at[chunk, pl.ds(side * (low // 2), low // 2), :]
        place = (chunk * steps + step) * 4 + side * 2 + piece
        return remote(
            spot if step else origin,
            spot,
            ring_sends,
            ring_arrivals,
            place,
            (at.next, at.back)[side],
        )

    def ring_step(chunk, step):
        for piece in range(2):
            for side in range(2):
                if step:
                    ring_copy(chunk, step - 1, side, piece).wait_recv()
                if step < steps:
                    ring_copy(chunk, step, side, piece).start()

    def tick(count):
        for chunk in range(chunks):
            if 0 <= count - 2 * chunk <= steps:
                ring_step(chunk, count - 2 * chunk)

    attend_send[0:3] = projector[...]
    attend_send[3] = collector[...]
    gains[...] = jnp.zeros_like(gains)
    gains[0:2, 0 : norm_gains.shape[1]] = norm_gains[...]
    gains[...] = pltpu.roll(gains[...], (at.group * members + me) * norm_gains.shape[1], 1)
    first_moves = [
        [
            links.copy(attend_send.at[peer], attend_recv.at[me], {"exp": peer}),
            links.copy(gains, gain_recv.at[me], {"exp": peer}),
        ]
        for peer in at.peers
    ]
    gain_recv[me] = gains[...]
    attend_recv[me] = attend_send[me]
    loads["widener"].wait()
    for matrix in range(2):
        for member in range(members):
            widen_send[member, matrix] = dealt_lanes(widener[matrix], member, members)
    widen_moves = [
        links.copy(widen_send.at[peer], widen_recv.at[me], {"exp": peer}) for peer in at.peers
    ]
    widen_recv[me] = widen_send[me]

    def stage(chunk):
        if chunk == 1:
            for matrix in range(2):
                wide_own[1, matrix] = jnp.concatenate(
                    [widen_recv[member, matrix] for member in range(members)], axis=0
                ).astype(jnp.bfloat16)
            down_own[1] = narrower[...].astype(jnp.bfloat16)
        else:
            index = max(chunk - 1, 0)
            for matrix in range(2):
                wide_own[chunk, matrix] = dealt_lanes(
                    expander[matrix], index, chunks - 1
                ).astype(jnp.bfloat16)
            down_own[chunk] = reducer[index * low : (index + 1) * low, :].astype(jnp.bfloat16)
        for side in range(2):
            wide_full[chunk, side, rows(at.group * block, block), :] = wide_own[chunk, side]
        down_full[chunk, rows(at.group * low, low), :] = down_own[chunk]

    loads["expander"].wait()
    loads["reducer"].wait()
    stage(0)
    tick(0)
    for moves in first_moves:
        for move in moves:
            move.wait_recv()
    attend_full[me, rows(at.group * block, block), :] = (
        attend_recv[...].reshape(block, width).astype(jnp.bfloat16)
    )
    total_gain = gain_recv[0]
    for member in range(1, members):
        total_gain = total_gain + gain_recv[member]
    gain_ring[at.group] = total_gain

    reach = (groups // 2, groups - 1 - groups // 2)

    def unit(owner, matrix):
        return attend_full.at[matrix, rows(owner * block, block), :]

    def across(owner):
        spot = unit(owner, me)
        return (links.copy(spot, spot, {"exp": at.far}), links.copy(spot, spot, {"exp": at.near}))

    crossed, passed, owners_seen = [], [], []

    def onward():
        spot = unit(owners_seen[len(passed)], at.far)
        crossed[len(passed)][0].wait_recv()
        passed.append(links.copy(spot, spot, {"exp": at.near}))

    ring = {}
    for step in range(reach[0] + 1):
        fresh = []
        for side, target in enumerate((at.next, at.back)):
            if step > reach[side]:
                continue
            owner = at.owner(-step if side == 0 else step)
            if step:
                for move in ring[step - 1, side]:
                    move.wait_recv()
            if step < reach[side]:
                spot, line = unit(owner, me), gain_ring.at[owner]
                ring[step, side] = (
                    links.copy(spot, spot, target),
                    links.copy(line, line, target),
                )
            if step or side == 0:
                fresh.append(owner)
        waiting = len(owners_seen) - len(passed)
        for owner in fresh:
            owners_seen.append(owner)
            crossed.append(across(owner))
        for _ in range(waiting):
            onward()
        if step == 1:
            for move in widen_moves:
                move.wait_recv()
            loads["narrower"].wait()
            for chunk in range(1, chunks):
                stage(chunk)
        if step:
            tick(step)
    outgoing = []

    def hand_out(source, target):
        made = pltpu.make_async_copy(
            source, target, local_sems.at[2 * chunks + len(loads) + len(outgoing)]
        )
        made.start(priority=1)
        outgoing.append(made)

    loads["cotangent"].wait()
    valid = lax.broadcasted_iota(jnp.int32, (length, 1), 0) < length_ref[deal_ref[me]]
    grads_all[me] = jnp.where(valid, cotangent[...], 0.0).astype(jnp.bfloat16)
    route = [routes[choice : choice + 1, :] for choice in range(2)]
    place = [places[choice : choice + 1, :].astype(jnp.float32) for choice in range(2)]
    meta_send[...] = jnp.zeros_like(meta_send)
    for member in range(members):
        named = [chosen == member for chosen in route]
        meta_send[member, 0:1, :] = jnp.where(
            named[0], place[0], jnp.where(named[1], place[1], -1.0)
        )
        meta_send[member, 1:2, :] = jnp.where(
            named[0], gates[0:1, :], jnp.where(named[1], gates[1:2, :], 0.0)
        )
    meta_all[me] = meta_send[me]
    grad_moves = [
        [
            links.copy(grads_all.at[me], grads_all.at[me], {"exp": peer}),
            links.copy(meta_send.at[peer], meta_all.at[me], {"exp": peer}),
        ]
        for peer in at.peers
    ]
    while len(passed) < groups:
        onward()
    total_gain = gain_ring[0]
    for group in range(1, groups):
        total_gain = total_gain + gain_ring[group]
    gains_full[...] = total_gain.astype(jnp.bfloat16).astype(jnp.float32)
    stream = tokens[...].astype(jnp.float32)
    first_input = (stream * rms_factor(stream) * gains_full[0:1, :]).astype(jnp.bfloat16)
    saved[4] = first_input
    for moves in crossed:
        moves[1].wait_recv()
    for move in passed:
        move.wait_recv()
    tick(5)
    hand_out(attend_full, attend_out)

    cosines, sines = cos_ref[...], sin_ref[...]
    for matrix in range(3):
        raw = matmul(first_input, attend_full[matrix])
        if matrix == 2:
            saved[2] = raw.astype(jnp.bfloat16)
        else:
            for start in range(0, width, 128):
                piece = raw[:, start : start + 128]
                saved[matrix, :, start : start + 128] = (
                    piece * cosines + turned(piece) * sines
                ).astype(jnp.bfloat16)
    tick(6)

    seq_length = length_ref[me]
    rows_at = lax.broadcasted_iota(jnp.int32, (length, length), 0)
    cols_at = lax.broadcasted_iota(jnp.int32, (length, length), 1)
    allowed = (cols_at <= rows_at) & (cols_at < seq_length)
    lower = first_half((length, 128))

    def heads(pair, carry):
        lanes = pl.ds(pl.multiple_of(pair * 128, 128), 128)
        query, key, value = saved[0, :, lanes], saved[1, :, lanes], saved[2, :, lanes]
        results = []
        for side in range(2):
            alone = jnp.where(lower == (side == 0), query, jnp.zeros_like(query))
            scores = jnp.where(allowed, nt(alone, key) * 0.125, -1e30)
            expo = jnp.exp(scores - jnp.max(scores, axis=-1, keepdims=True))
            soft = expo / jnp.sum(expo, axis=-1, keepdims=True)
            soft_ref[2 * pair + side] = soft
            results.append(matmul(soft.astype(jnp.bfloat16), value))
        saved[3, :, lanes] = jnp.where(lower, results[0], results[1]).astype(jnp.bfloat16)
        return carry

    lax.fori_loop(0, width // 128, heads, 0)
    hand_out(saved, saved_out)
    hand_out(soft_ref, soft_out)
    middle = tokens[...].astype(jnp.float32) + matmul(saved[3], attend_full[3])
    middle_ref[...] = middle
    hand_out(middle_ref, middle_out)
    second_all[me] = (middle * rms_factor(middle) * gains_full[1:2, :]).astype(jnp.bfloat16)
    second_moves = [
        links.copy(second_all.at[me], second_all.at[me], {"exp": peer}) for peer in at.peers
    ]
    for moves in grad_moves:
        for move in moves:
            move.wait_recv()
    grads_home[...] = grads_all[slot_of(deal_ref, me)]
    hand_out(grads_home, grads_out)
    tick(7)

    def hits(slot, by_row):
        line = meta_all[slot, 0:1, :]
        if by_row:
            names = lax.broadcasted_iota(jnp.int32, (capacity, length), 0).astype(jnp.float32)
            hit = names == line
        else:
            names = lax.broadcasted_iota(jnp.int32, (length, capacity), 1).astype(jnp.float32)
            hit = names == upright(line)
        return jnp.where(hit, 1.0, 0.0).astype(jnp.bfloat16)

    def spot_of(slot):
        return slice(slot * capacity, (slot + 1) * capacity)

    def here_of(slot):
        return slice(slot * length, (slot + 1) * length)

    for slot in range(members):
        pick = hits(slot, True)
        gate = jnp.sum(pick.astype(jnp.float32) * meta_all[slot, 1:2, :], axis=1, keepdims=True)
        rows_grad[spot_of(slot), :] = (matmul(pick, grads_all[slot]) * gate).astype(jnp.bfloat16)
    for move in second_moves:
        move.wait_recv()
    for slot in range(members):
        inputs_ref[here_of(slot), :] = second_all[deal_ref[slot]]
        rows_in[spot_of(slot), :] = matmul(hits(slot, True), inputs_ref[here_of(slot), :]).astype(
            jnp.bfloat16
        )
    inputs_turned[...] = inputs_ref[...].T
    rows_turned[...] = rows_in[...].T
    dense_out[...] = jnp.zeros_like(dense_out)
    dense_back[...] = jnp.zeros_like(dense_back)
    rows_out[...] = jnp.zeros_like(rows_out)
    rows_back[...] = jnp.zeros_like(rows_back)

    def branch(chunk, inputs, turned_inputs, outer, out, back):
        for step in range(steps):
            for side in range(2):
                for piece in range(2):
                    ring_copy(chunk, step, side, piece).wait_send()

        def part(index, carry):
            lanes = pl.ds(pl.multiple_of(index * 256, 256), 256)
            gate = matmul(inputs[...], wide_full[chunk, 0, :, lanes])
            up = matmul(inputs[...], wide_full[chunk, 1, :, lanes])
            rise = sigmoid(gate)
            smooth = gate * rise
            hidden = (smooth * up).astype(jnp.bfloat16)
            hidden_grad = nt(outer[...], down_full[chunk, lanes, :])
            gate_grad = (hidden_grad * up * (rise * (1.0 + gate * (1.0 - rise)))).astype(
                jnp.bfloat16
            )
            up_grad = (hidden_grad * smooth).astype(jnp.bfloat16)
            out[...] += matmul(hidden, down_full[chunk, lanes, :])
            back[...] += nt(gate_grad, wide_full[chunk, 0, :, lanes]) + nt(
                up_grad, wide_full[chunk, 1, :, lanes]
            )
            down_full[chunk, lanes, :] = tn(hidden, outer[...]).astype(jnp.bfloat16)
            wide_full[chunk, 0, :, lanes] = matmul(turned_inputs[...], gate_grad).astype(
                jnp.bfloat16
            )
            wide_full[chunk, 1, :, lanes] = matmul(turned_inputs[...], up_grad).astype(
                jnp.bfloat16
            )

            @pl.when(index == 0)
            def _():
                for ahead in range(groups // 2):
                    @pl.when(chunk + 1 + ahead < chunks)
                    def _():
                        ring_step(chunk + 1 + ahead, steps - 1 - 2 * ahead)

            return carry

        lax.fori_loop(0, down_full.shape[1] // 256, part, 0)
        kept(chunk, 0).start(priority=1)
        kept(chunk, 1).start(priority=1)

    def kept(chunk, piece):
        source, target = ((wide_full, wide_grads), (down_full, down_grads))[piece]
        return pltpu.make_async_copy(
            source.at[chunk], target.at[chunk], local_sems.at[2 * chunk + piece]
        )

    outer_all = grads_all.reshape(members * length, width)
    flat = (members * length, width)
    dense = (
        inputs_ref,
        inputs_turned,
        outer_all,
        dense_out.reshape(flat),
        dense_back.reshape(flat),
    )

    def first_sum(chunk, side, piece):
        owner = at.owner(-1 if side == 0 else 1)
        if piece == 0:
            spot = wide_full.at[chunk, side, rows(owner * block, block), :]
        else:
            spot = down_full.at[chunk, rows(owner * low + side * (low // 2), low // 2), :]
        return remote(
            spot,
            (wide_first, down_first)[piece].at[chunk, side],
            first_sends,
            first_arrivals,
            chunk * 4 + side * 2 + piece,
            (at.next, at.back)[side],
        )

    early = chunks - 1

    def start_sums(chunk):
        for piece in range(2):
            for side in range(2):
                first_sum(chunk, side, piece).start()

    def next_chunk(chunk, carry):
        for ahead in range(groups // 2):
            @pl.when((chunk > 0) & (chunk + ahead < chunks))
            def _():
                ring_step(chunk + ahead, steps - 2 * ahead)

        @pl.when(chunk == chunks - 1)
        def _():
            for before in range(early):
                start_sums(before)

        @pl.when(chunk == 1)
        def _():
            branch(chunk, *dense)

        @pl.when(chunk != 1)
        def _():
            branch(chunk, rows_in, rows_turned, rows_grad, rows_out, rows_back)

        return carry

    lax.fori_loop(0, chunks, next_chunk, 0)

    for slot in range(members):
        inner = rows_back[spot_of(slot), :].astype(jnp.bfloat16)
        dense_back[slot] += matmul(hits(slot, False), inner)
    for member in range(members):
        back_ref[member] = dense_back[slot_of(deal_ref, member)].astype(jnp.bfloat16)
        hand_out(back_ref.at[member], back_out.at[member])
    for slot in range(members):
        gate = upright(meta_all[slot, 1:2, :])
        picked = matmul(hits(slot, False), rows_out[spot_of(slot), :].astype(jnp.bfloat16))
        dense_out[slot] += gate * picked
        score = jnp.sum(picked * grads_all[slot].astype(jnp.float32), axis=1, keepdims=True)
        gate_ref[slot] = jnp.broadcast_to(lying(score), gate_ref.shape[1:])
    for member in range(members):
        result_ref[member] = dense_out[slot_of(deal_ref, member)].astype(jnp.bfloat16)
        hand_out(result_ref.at[member], result_out.at[member])
    for chunk in range(chunks):
        kept(chunk, 0).wait()
        kept(chunk, 1).wait()
    for chunk in range(early):
        for piece in range(2):
            for side in range(2):
                first_sum(chunk, side, piece).wait()
    for made in outgoing:
        made.wait()
    links.finish()


def scatter_kernel(
    groups,
    members,
    tokens,
    routes,
    gains_full,
    cos_ref,
    sin_ref,
    gate_parts,
    result_parts,
    back_parts,
    wide_grads,
    down_grads,
    wide_first,
    down_first,
    grads_in,
    middle_in,
    attend_in,
    saved_in,
    soft_in,
    output_out,
    input_grad_out,
    expand_out,
    reduce_out,
    narrow_out,
    project_out,
    collect_out,
    gate_grad_ref,
    widen_sum,
    gains_sum,
    expand_sum,
    reduce_sum,
    narrow_sum,
    output_ref,
    input_grad_ref,
    attend_sum,
    grads_home,
    middle_ref,
    attend_full,
    saved,
    soft_ref,
    gate_recv,
    result_recv,
    back_recv,
    wide_own,
    down_own,
    wide_recv,
    down_recv,
    wide_sum,
    turned_ref,
    attend_grad,
    near_recv,
    far_recv,
    far_send,
    attend_total,
    attend_recv,
    attend_back,
    widen_back,
    widen_home,
    gain_own,
    gain_recv,
    gain_ring,
    sends,
    arrivals,
    local_sems,
):
    at = Places(groups, members)
    links = Links(sends, arrivals)
    at.enter()
    me, steps = at.member, groups - 1
    length, width = tokens.shape
    chunks, low = down_own.shape[0], narrow_sum.shape[0]
    share = attend_sum.shape[1]
    block = share * members

    moves_of = {}
    widen_moves = []

    def ring_step(chunk, step):
        made = []
        owners = (at.owner(-1 - step), at.owner(1 + step))
        for piece in range(2):
            for side, target in enumerate((at.next, at.back)):
                own = (wide_own, down_own)[piece]
                landing = (wide_recv, down_recv)[piece].at[chunk, side]
                if piece == 0:
                    spot = (chunk, side, rows(owners[side] * block, block))
                else:
                    spot = (chunk, rows(owners[side] * low + side * (low // 2), low // 2))
                if step == 0:
                    first = (wide_grads, down_grads)[piece]
                    made.append(links.copy(first.at[spot], landing.at[0], target))
                    continue
                if step > 1 or chunk >= early:
                    moves_of[chunk, step - 1][2 * piece + side].wait_recv()
                source = landing.at[step - 1]
                added = source[...].astype(jnp.float32) + own[spot].astype(jnp.float32)
                if step < steps:
                    source[...] = added.astype(jnp.bfloat16)
                elif piece == 0 and chunk != 1:
                    wide_sum[max(chunk - 1, 0), side] = added
                elif piece == 0:
                    for member in range(members):
                        widen_back[member, side] = added[member * share : (member + 1) * share, :]
                else:
                    start = side * (low // 2)
                    if chunk != 1:
                        start = start + max(chunk - 1, 0) * low
                        reduce_sum[start : start + low // 2, :] = added
                    else:
                        narrow_sum[start : start + low // 2, :] = added
                if step < steps:
                    made.append(links.copy(source, landing.at[step], target))
        moves_of[chunk, step] = made
        if step == steps and chunk == 1:
            widen_home[me] = widen_back[me]
            for peer in at.peers:
                widen_moves.append(
                    links.copy(widen_back.at[peer], widen_home.at[me], {"exp": peer})
                )
        if step == steps and chunk == 1:
            store(narrow_sum, narrow_out)
        elif step == steps:
            spot = rows(max(chunk - 1, 0) * low, low)
            store(reduce_sum.at[spot], reduce_out.at[spot])
        if step == steps and chunk and chunk % 2 == 0:
            pair = chunk // 2 - 1
            for side in range(2):
                found = joined_lanes(wide_sum[chunk - 2, side], wide_sum[chunk - 1, side])
                for index in range(0, len(found), 1):
                    expand_sum[pair, side, :, index * 128 : index * 128 + 128] = found[index]
            store(expand_sum.at[pair], expand_out.at[pair])

    early = chunks - 1
    order = [(chunk, 0) for chunk in range(early, chunks)] + [
        (chunk, step) for step in range(1, groups) for chunk in (1, 0, *range(2, chunks))
    ]

    def poll(count):
        for _ in range(min(count, len(order))):
            chunk, step = order.pop(0)
            for made in own_loads.pop(step, ()):
                made.wait()
            ring_step(chunk, step)

    kept, stored = [], []

    def store(source, target):
        made = pltpu.make_async_copy(source, target, local_sems.at[4 * groups + 14 + len(stored)])
        made.start(priority=1)
        stored.append(made)

    def load(source, target):
        made = pltpu.make_async_copy(source, target, local_sems.at[len(kept)])
        made.start(priority=1)
        kept.append(made)
        return made

    own_loads = {}

    def load_own(step):
        found = []
        for side, owner in enumerate((at.owner(-1 - step), at.owner(1 + step))):
            spot = rows(owner * block, block)
            found.append(load(wide_grads.at[:, side, spot], wide_own.at[:, side, spot]))
            spot = rows(owner * low + side * (low // 2), low // 2)
            found.append(load(down_grads.at[:, spot], down_own.at[:, spot]))
        own_loads[step] = found

    back_moves = [
        links.copy(back_parts.at[peer], back_recv.at[me], {"exp": peer}) for peer in at.peers
    ]
    first_loads = [
        load(wide_first.at[:, side], wide_recv.at[0:early, side, 0]) for side in range(2)
    ] + [load(down_first.at[:, side], down_recv.at[0:early, side, 0]) for side in range(2)]
    load_own(1)
    poll(1)
    middle_loads = [
        load(back_parts.at[me], back_recv.at[me]),
        load(middle_in, middle_ref),
        load(grads_in, grads_home),
        load(attend_in.at[3], attend_full.at[3]),
        load(saved_in, saved),
    ]
    soft_load = load(soft_in, soft_ref)
    load_own(2)
    attend_load = load(attend_in.at[0:3], attend_full.at[0:3])
    for step in range(3, groups):
        load_own(step)
    result_load = load(result_parts.at[me], result_recv.at[me])
    gate_recv[me] = gate_parts[me]
    for made in first_loads:
        made.wait()
    poll(4)
    result_moves = [
        [
            links.copy(result_parts.at[peer], result_recv.at[me], {"exp": peer}),
            links.copy(gate_parts.at[peer], gate_recv.at[me], {"exp": peer}),
        ]
        for peer in at.peers
    ]
    for made in middle_loads:
        made.wait()
    for move in back_moves:
        move.wait_recv()

    second_grad = back_recv[0].astype(jnp.float32)
    for member in range(1, members):
        second_grad = second_grad + back_recv[member].astype(jnp.float32)
    middle = middle_ref[...]
    scale = rms_factor(middle)
    gain_own[...] = jnp.zeros_like(gain_own)
    gain_own[1:2, :] = jnp.sum(second_grad * (middle * scale), axis=0, keepdims=True)
    input_grad_ref[...] = grads_home[...].astype(jnp.float32) + rms_back(
        middle, scale, second_grad * gains_full[1:2, :]
    )
    middle_low = input_grad_ref[...].astype(jnp.bfloat16)
    turned_ref[3] = nt(middle_low, attend_full[3]).astype(jnp.bfloat16)
    poll(3)
    cosines, sines = cos_ref[...], sin_ref[...]
    lower = first_half((length, 128))
    soft_load.wait()

    def heads(pair, carry):
        lanes = pl.ds(pl.multiple_of(pair * 128, 128), 128)
        query, key, value = saved[0, :, lanes], saved[1, :, lanes], saved[2, :, lanes]
        outer = turned_ref[3, :, lanes]
        made = []
        for side in range(2):
            soft = soft_ref[2 * pair + side]
            alone = jnp.where(lower == (side == 0), outer, jnp.zeros_like(outer))
            value_grad = tn(soft.astype(jnp.bfloat16), outer)
            soft_grad = nt(alone, value)
            score_grad = (
                soft * (soft_grad - jnp.sum(soft * soft_grad, axis=-1, keepdims=True))
            ).astype(jnp.bfloat16)
            made.append(
                (matmul(score_grad, key) * 0.125, tn(score_grad, query) * 0.125, value_grad)
            )
        for index in range(3):
            joined = jnp.where(lower, made[0][index], made[1][index])
            if index < 2:
                joined = joined * cosines - turned(joined) * sines
            turned_ref[index, :, lanes] = joined.astype(jnp.bfloat16)
        return carry

    attend_grad[3] = tn(saved[3], middle_low).astype(jnp.bfloat16)
    for third in range(3):
        lax.fori_loop(2 * third, 2 * third + 2, heads, 0)
        poll(3)
    for matrix in range(3):
        attend_grad[matrix] = tn(saved[4], turned_ref[matrix]).astype(jnp.bfloat16)
    near_moves = [
        links.copy(attend_grad.at[matrix], near_recv.at[index], {"exp": at.near})
        for index, matrix in enumerate((at.near, at.cross))
    ]
    poll(1)
    attend_load.wait()
    first_grad = nt(turned_ref[0], attend_full[0])
    for matrix in range(1, 3):
        first_grad = first_grad + nt(turned_ref[matrix], attend_full[matrix])
    stream = tokens[...].astype(jnp.float32)
    scale = rms_factor(stream)
    gain_own[0:1, :] = jnp.sum(first_grad * (stream * scale), axis=0, keepdims=True)
    gain_moves = [links.copy(gain_own, gain_recv.at[me], {"exp": peer}) for peer in at.peers]
    gain_recv[me] = gain_own[...]
    input_grad_ref[...] += rms_back(stream, scale, first_grad * gains_full[0:1, :])
    store(input_grad_ref, input_grad_out)
    for move in near_moves:
        move.wait_recv()
    far_send[...] = (
        attend_grad[at.far].astype(jnp.float32) + near_recv[1].astype(jnp.float32)
    ).astype(jnp.bfloat16)
    far_move = links.copy(far_send, far_recv, {"exp": at.far})
    poll(2)
    for moves in result_moves:
        for move in moves:
            move.wait_recv()
    result_load.wait()
    output = middle_ref[...]
    for member in range(members):
        output = output + result_recv[member].astype(jnp.float32)
    output_ref[...] = output
    store(output_ref, output_out)
    for choice in range(2):
        route = routes[choice : choice + 1, :]
        found = jnp.zeros((1, length), jnp.float32)
        for member in range(members):
            found = jnp.where(route == member, gate_recv[member, 0:1, :], found)
        gate_grad_ref[choice : choice + 1, :] = found
    poll(3)
    for move in gain_moves:
        move.wait_recv()
    total = gain_recv[0]
    for member in range(1, members):
        total = total + gain_recv[member]
    gain_ring[at.group] = total
    far_move.wait_recv()
    attend_total[...] = (
        attend_grad[me].astype(jnp.float32)
        + near_recv[0].astype(jnp.float32)
        + far_recv[...].astype(jnp.float32)
    ).astype(jnp.bfloat16)

    reach = (groups // 2, groups - 1 - groups // 2)
    small = {}

    def advance_small(step):
        for side, target in enumerate((at.next, at.back)):
            if step > reach[side]:
                continue
            owner = at.owner(reach[side] - step if side == 0 else step - reach[side])
            spot = attend_total.at[rows(owner * block, block), :]
            if step:
                for move in small[step - 1, side]:
                    move.wait_recv()
            if step < reach[side]:
                source = spot
                if step:
                    source = attend_recv.at[side, step - 1]
                    source[...] = (
                        source[...].astype(jnp.float32) + spot[...].astype(jnp.float32)
                    ).astype(jnp.bfloat16)
                line = gain_ring.at[at.owner(-step if side == 0 else step)]
                small[step, side] = (
                    links.copy(source, attend_recv.at[side, step], target),
                    links.copy(line, line, target),
                )

    for step in range(reach[0] + 1):
        advance_small(step)
        poll(2)
    added = attend_total[rows(at.group * block, block), :].astype(jnp.float32)
    for side in range(2):
        added = added + attend_recv[side, reach[side] - 1].astype(jnp.float32)
    for member in range(members):
        attend_back[member] = added[member * share : (member + 1) * share, :]
    attend_moves = [
        links.copy(attend_back.at[peer], attend_sum.at[me], {"exp": peer}) for peer in at.peers
    ]
    attend_sum[me] = attend_back[me]
    total = gain_ring[0]
    for group in range(1, groups):
        total = total + gain_ring[group]
    count = gains_sum.shape[1]
    start = (at.group * members + me) * count
    gains_sum[...] = pltpu.roll(total, width - start, 1)[0:2, 0:count]
    poll(len(order) - 2)
    for move in attend_moves:
        move.wait_recv()
    store(attend_sum.at[0:3], project_out)
    store(attend_sum.at[3], collect_out)
    for move in widen_moves:
        move.wait_recv()
    for matrix in range(2):
        for member in range(0, members, 2):
            found = joined_lanes(widen_home[member, matrix], widen_home[member + 1, matrix])
            for index, part in enumerate(found):
                start = index * 64 * members + member * 64
                widen_sum[matrix, :, start : start + 128] = part
    poll(len(order))
    for made in stored:
        made.wait()
    links.finish()


def update_kernel(rates, fixed, copies, *refs):
    count = len(rates)
    given, made = refs[: 4 * count + copies], refs[4 * count + copies :]
    for index in range(copies):
        made[index][...] = given[4 * count + index][...]

    def update(index):
        weight, moment, variance, gradient = given[4 * index : 4 * index + 4]
        if len(gradient.shape) > len(weight.shape):
            grad = jnp.concatenate(
                [
                    gradient[at % 2, :, :, at // 2 * 128 : at // 2 * 128 + 128]
                    for at in range(weight.shape[-1] // 128)
                ],
                axis=2,
            )
        else:
            grad = gradient[...]
        grad = 0.5 * grad
        level = 1.0 / (1.0 - 0.5**STEP)
        moment_new = 0.5 * moment[...] + grad
        variance_new = 0.5 * variance[...] + 2.0 * grad * grad
        kept = weight[...]
        stepped = moment_new * level / (jnp.sqrt(variance_new * level) + 1e-08) + 0.1 * kept
        made[copies + 3 * index][...] = moment_new
        made[copies + 3 * index + 1][...] = variance_new
        made[copies + 3 * index + 2][...] = kept - rates[index] * stepped

    for index in range(count):
        if fixed[index]:
            pl.when(pl.program_id(0) == 0)(functools.partial(update, index))
        else:
            update(index)


def update_all(*groups, passed):
    cuts = 4

    def spec(dims, cut):
        if cut is None:
            return pl.BlockSpec(dims, lambda step: (0,) * len(dims))
        block = tuple(size // cuts if at == cut else size for at, size in enumerate(dims))
        return pl.BlockSpec(
            block, lambda step: tuple(step if at == cut else 0 for at in range(len(dims)))
        )

    def cut_of(array):
        dims = array.shape
        for at in range(len(dims) - 1):
            if array.size > 100000 and dims[at] % (8 * cuts) == 0:
                return at
        return len(dims) - 1 if dims[-1] % (128 * cuts) == 0 else None

    given, specs, shapes, out_specs = [], [], [], []
    for _, weight, moment, variance, gradient in groups:
        cut = cut_of(weight)
        for array in (weight, moment, variance, gradient):
            given.append(array)
            more = array.ndim - weight.ndim
            specs.append(spec(array.shape, None if cut is None else cut + more))
        for array in (weight, moment, variance):
            shapes.append(jax.ShapeDtypeStruct(array.shape, array.dtype))
            out_specs.append(spec(array.shape, cut))
    extra = [spec(array.shape, cut_of(array)) for array in passed]
    return pl.pallas_call(
        functools.partial(
            update_kernel,
            [group[0] for group in groups],
            [cut_of(group[1]) is None for group in groups],
            len(passed),
        ),
        grid=(cuts,),
        out_shape=[jax.ShapeDtypeStruct(array.shape, array.dtype) for array in passed] + shapes,
        in_specs=specs + extra,
        out_specs=extra + out_specs,
        compiler_params=pltpu.CompilerParams(vmem_limit_bytes=LIMIT),
    )(*given, *passed)


def rotary_lines(length):
    half = HEAD_FEATURES // 2
    freqs = np.exp(-np.log(10000.0) * np.arange(half) / half)
    angles = np.arange(length)[:, None] * freqs[None, :]
    cosines, sines = np.cos(angles), np.sin(angles)
    return (
        np.concatenate([cosines] * 4, axis=1).astype(np.float32),
        np.concatenate([-sines, sines] * 2, axis=1).astype(np.float32),
    )


def spaces(*names):
    kinds = {"v": pltpu.VMEM, "s": pltpu.SMEM, "a": pl.ANY}
    return [pl.BlockSpec(memory_space=kinds[name]) for name in "".join(names)]


def local(
    tokens,
    seq_lengths,
    deal_order,
    expert_routes,
    capacity_slots,
    gate_weights,
    cotangent,
    projector,
    projector_mean,
    projector_square,
    collector,
    collector_first_moment,
    collector_second_moment,
    widener,
    widener_mean,
    widener_square,
    narrower,
    narrower_mean,
    narrower_square,
    norm_gains,
    gains_mean,
    gains_square,
    expander,
    expander_mean,
    expander_square,
    reducer,
    reducer_mean,
    reducer_square,
):
    groups, members = lax.axis_size("grp"), lax.axis_size("exp")
    length, width = tokens.shape[1:]
    inner = expander.shape[3]
    piece = widener.shape[2] // members
    chunks = 1 + inner // piece
    capacity = 3 * length // members
    steps = groups - 1
    high, low, share = expander.shape[2], narrower.shape[0], projector.shape[1]
    bf16, f32 = jnp.bfloat16, jnp.float32
    shape = jax.ShapeDtypeStruct
    cosines, sines = (jnp.asarray(lines) for lines in rotary_lines(length))
    count = 16 * groups
    (
        wide_grads,
        down_grads,
        wide_first,
        down_first,
        attend_full,
        grads_all,
        saved,
        middle,
        soft,
        result_parts,
        back_parts,
        gains_full,
        gate_parts,
    ) = pl.pallas_call(
        functools.partial(gather_kernel, groups, members),
        out_shape=[
            shape((chunks, 2, width, piece), bf16),
            shape((chunks, piece, width), bf16),
            shape((chunks - 1, 2, high, piece), bf16),
            shape((chunks - 1, 2, low // 2, width), bf16),
            shape((4, width, width), bf16),
            shape((length, width), bf16),
            shape((5, length, width), bf16),
            shape((length, width), f32),
            shape((HEAD_COUNT, length, length), f32),
            shape((members, length, width), bf16),
            shape((members, length, width), bf16),
            shape((8, width), f32),
            shape((members, 8, length), f32),
        ],
        in_specs=spaces("ssvavvvvvvaaaavv"),
        out_specs=spaces("a" * 11, "vv"),
        scratch_shapes=[
            VMEM((length, width), f32),
            VMEM(widener.shape, f32),
            VMEM(narrower.shape, f32),
            VMEM(expander.shape[1:], f32),
            VMEM(reducer.shape[1:], f32),
            VMEM((members, length, width), bf16),
            VMEM((members, length, width), bf16),
            VMEM((length, width), bf16),
            VMEM((4, width, width), bf16),
            VMEM((members, length, width), bf16),
            VMEM((5, length, width), bf16),
            VMEM((length, width), f32),
            VMEM((HEAD_COUNT, length, length), f32),
            VMEM((members, length, width), bf16),
            VMEM((members, 8, length), f32),
            VMEM((members, 8, length), f32),
            VMEM((4, share, width), f32),
            VMEM((4, share, width), f32),
            VMEM((members, 2, share, piece), f32),
            VMEM((members, 2, share, piece), f32),
            VMEM((8, width), f32),
            VMEM((members, 8, width), f32),
            VMEM((groups, 8, width), f32),
            VMEM((chunks, 2, width, piece), bf16),
            VMEM((chunks, piece, width), bf16),
            VMEM((chunks, 2, high, piece), bf16),
            VMEM((chunks, low, width), bf16),
            VMEM((members * length, width), bf16),
            VMEM((width, members * length), bf16),
            VMEM((members, length, width), f32),
            VMEM((members, length, width), f32),
            VMEM((members * capacity, width), bf16),
            VMEM((width, members * capacity), bf16),
            VMEM((members * capacity, width), bf16),
            VMEM((members * capacity, width), f32),
            VMEM((members * capacity, width), f32),
            pltpu.SemaphoreType.DMA((count,)),
            pltpu.SemaphoreType.DMA((count,)),
            pltpu.SemaphoreType.DMA((chunks * steps * 4,)),
            pltpu.SemaphoreType.DMA((chunks * steps * 4,)),
            pltpu.SemaphoreType.DMA((chunks * 4,)),
            pltpu.SemaphoreType.DMA((chunks * 4,)),
            pltpu.SemaphoreType.DMA((2 * chunks + 10 + 2 * members,)),
        ],
        compiler_params=pltpu.CompilerParams(
            collective_id=0, has_side_effects=True, vmem_limit_bytes=LIMIT
        ),
    )(
        seq_lengths,
        deal_order,
        tokens[0],
        cotangent[0],
        expert_routes[0].T,
        capacity_slots[0].T,
        gate_weights[0].T,
        norm_gains,
        projector,
        collector,
        widener,
        narrower,
        expander[0],
        reducer[0],
        cosines,
        sines,
    )
    count = 32 * groups
    (
        output,
        input_grad,
        expand_sum,
        reduce_sum,
        narrow_sum,
        project_sum,
        collect_sum,
        gate_grad,
        widen_sum,
        gains_sum,
    ) = pl.pallas_call(
        functools.partial(scatter_kernel, groups, members),
        out_shape=[
            shape((length, width), f32),
            shape((length, width), f32),
            shape((2, 2, high, inner // 2), f32),
            shape(reducer.shape[1:], f32),
            shape(narrower.shape, f32),
            shape(projector.shape, f32),
            shape(collector.shape, f32),
            shape((2, length), f32),
            shape(widener.shape, f32),
            shape(norm_gains.shape, f32),
        ],
        in_specs=spaces("v" * 6, "a" * 11),
        out_specs=spaces("a" * 7, "vvv"),
        scratch_shapes=[
            VMEM((2, 2, high, inner // 2), f32),
            VMEM(reducer.shape[1:], f32),
            VMEM(narrower.shape, f32),
            VMEM((length, width), f32),
            VMEM((length, width), f32),
            VMEM((4, share, width), f32),
            VMEM((length, width), bf16),
            VMEM((length, width), f32),
            VMEM((4, width, width), bf16),
            VMEM((5, length, width), bf16),
            VMEM((HEAD_COUNT, length, length), f32),
            VMEM((members, 8, length), f32),
            VMEM((members, length, width), bf16),
            VMEM((members, length, width), bf16),
            VMEM((chunks, 2, width, piece), bf16),
            VMEM((chunks, piece, width), bf16),
            VMEM((chunks, 2, steps, high, piece), bf16),
            VMEM((chunks, 2, steps, low // 2, width), bf16),
            VMEM((chunks - 1, 2, high, piece), f32),
            VMEM((4, length, width), bf16),
            VMEM((4, width, width), bf16),
            VMEM((2, width, width), bf16),
            VMEM((width, width), bf16),
            VMEM((width, width), bf16),
            VMEM((width, width), bf16),
            VMEM((2, groups // 2, high, width), bf16),
            VMEM((4, share, width), f32),
            VMEM((members, 2, share, piece), f32),
            VMEM((members, 2, share, piece), f32),
            VMEM((8, width), f32),
            VMEM((members, 8, width), f32),
            VMEM((groups, 8, width), f32),
            pltpu.SemaphoreType.DMA((count,)),
            pltpu.SemaphoreType.DMA((count,)),
            pltpu.SemaphoreType.DMA((4 * groups + 32,)),
        ],
        compiler_params=pltpu.CompilerParams(
            collective_id=1, has_side_effects=True, vmem_limit_bytes=LIMIT
        ),
    )(
        tokens[0],
        expert_routes[0].T,
        gains_full,
        cosines,
        sines,
        gate_parts,
        result_parts,
        back_parts,
        wide_grads,
        down_grads,
        wide_first,
        down_first,
        grads_all,
        middle,
        attend_full,
        saved,
        soft,
    )
    updated = update_all(
        (0.1, projector, projector_mean, projector_square, project_sum),
        (0.3, collector, collector_first_moment, collector_second_moment, collect_sum),
        (0.07, widener, widener_mean, widener_square, widen_sum),
        (0.045, narrower, narrower_mean, narrower_square, narrow_sum),
        (0.2, norm_gains, gains_mean, gains_square, gains_sum),
        (0.07, expander[0], expander_mean[0], expander_square[0], expand_sum),
        (0.045, reducer[0], reducer_mean[0], reducer_square[0], reduce_sum),
        passed=(output, input_grad),
    )
    return (
        updated[0][None],
        updated[1][None],
        gate_grad.T[None],
        *updated[2:17],
        *(found[None] for found in updated[17:]),
    )


def fits(mesh):
    groups, members = mesh.shape["grp"], mesh.shape["exp"]
    share = 64 * HEAD_COUNT // (groups * members)
    return members == 4 and groups % 2 == 0 and share % 8 == 0 and share * members // 2 % 16 == 0


def solution(mesh):
    placed = (
        P(("grp", "exp"), None, None),
        P("grp"),
        P("grp"),
        P(("grp", "exp"), None, None),
        P(("grp", "exp"), None, None),
        P(("grp", "exp"), None, None),
        P(("grp", "exp"), None, None),
        P(None, ("grp", "exp"), None),
        P(None, ("grp", "exp"), None),
        P(None, ("grp", "exp"), None),
        P(("grp", "exp"), None),
        P(("grp", "exp"), None),
        P(("grp", "exp"), None),
        P(None, ("grp", "exp"), None),
        P(None, ("grp", "exp"), None),
        P(None, ("grp", "exp"), None),
        P(("grp", "exp"), None),
        P(("grp", "exp"), None),
        P(("grp", "exp"), None),
        P(None, ("grp", "exp")),
        P(None, ("grp", "exp")),
        P(None, ("grp", "exp")),
        P("exp", None, "grp", None),
        P("exp", None, "grp", None),
        P("exp", None, "grp", None),
        P("exp", "grp", None),
        P("exp", "grp", None),
        P("exp", "grp", None),
    )
    return jax.shard_map(
        local if fits(mesh) else local_plain,
        mesh=mesh,
        in_specs=placed,
        out_specs=(
            P(("grp", "exp"), None, None),
            P(("grp", "exp"), None, None),
            P(("grp", "exp"), None, None),
            P(None, ("grp", "exp"), None),
            P(None, ("grp", "exp"), None),
            P(None, ("grp", "exp"), None),
            P(("grp", "exp"), None),
            P(("grp", "exp"), None),
            P(("grp", "exp"), None),
            P(None, ("grp", "exp"), None),
            P(None, ("grp", "exp"), None),
            P(None, ("grp", "exp"), None),
            P(("grp", "exp"), None),
            P(("grp", "exp"), None),
            P(("grp", "exp"), None),
            P(None, ("grp", "exp")),
            P(None, ("grp", "exp")),
            P(None, ("grp", "exp")),
            P("exp", None, "grp", None),
            P("exp", None, "grp", None),
            P("exp", None, "grp", None),
            P("exp", "grp", None),
            P("exp", "grp", None),
            P("exp", "grp", None),
        ),
        check_vma=False,
    )
```
